32 devices in a mesh: pipe: 2 (over core), tensor: 16 (over z, y, x).
Axes of the slice: x: 2, y: 2, z: 4, core: 2. Of those that a mesh axis runs over, the one named last changes fastest.
Arguments:
- output_gradient: bfloat16 [2, 16, 2, 256, 1024], P('pipe', 'tensor'), may hold values from -6 to 6
- forward_input: bfloat16 [2, 2, 512, 8192], P('pipe', None, None, 'tensor'), may hold values from -6 to 6
- saved_rank_outputs: bfloat16 [2, 2, 512, 64], P('pipe', None, 'tensor'), may hold values from -6 to 6
- projection_weight: bfloat16 [2, 16, 4096, 1024], P('pipe', 'tensor'), may hold values from -0.0625 to 0.0625
- adapter_down_maps: bfloat16 [2, 8, 64, 8192], P('pipe', None, None, 'tensor'), may hold values from -0.75 to 0.75
- adapter_up_maps: bfloat16 [2, 16, 8, 32, 1024], P('pipe', 'tensor'), may hold values from -0.0625 to 0.0625
- segment_adapter_class: int32 [2, 2, 4], P('pipe'), may hold values from 0 to 7
- live_segment_table: int32 [2, 2], P('pipe'), may hold values from 1 to 4, as said below
Outputs:
- grad_prev: bfloat16 [2, 2, 512, 8192], P('pipe', None, None, 'tensor')
- down_map_gradient: bfloat16 [2, 8, 64, 8192], P('pipe', None, None, 'tensor')
- up_map_gradient: bfloat16 [2, 16, 8, 32, 1024], P('pipe', 'tensor')
The draws below stay inside these ranges and needn't reach their ends.
Inputs may be any that keep to these rules, and one draw needn't show every extreme that they name: The first live_segment_table segments of a microbatch are live; some microbatch has all 4 live.
All inputs are finite; a program needn't handle non-finite values.
Results may differ from the reference program's by a relative error of at most 0.0049.
Values may be sent and summed in bfloat16 or wider, within the bound.
No kernel may reach another device: no remote copies, remote signals or barrier semaphores. Data moves between devices by JAX's collectives and lax.ppermute only.
A program may use at most 128 MiB of HBM per device.

```python
import jax
import jax.numpy as jnp
from jax import lax

MODEL_WIDTH = 8192
ADAPTER_RANK = 64
SEG = 128
SEG_MB = 4
MICRO = 2
CLASS_ADAPTERS = 8
LOWER_GROUPS = 8
UPPER_GROUPS = 2
ROWS_MB = 512
ROWS = 1024
RELAY_SECTIONS = 2
N_TENSOR = 16


def draw_live_segment_table(key, part):
    first_key, second_key = jax.random.split(jax.random.fold_in(key, 17))
    values = jax.random.randint(first_key, (RELAY_SECTIONS * MICRO,), 1, SEG_MB + 1)
    picked = jax.random.randint(second_key, (), 0, RELAY_SECTIONS * MICRO)
    values = jnp.where(jnp.arange(RELAY_SECTIONS * MICRO) == picked, SEG_MB, values)
    return values.reshape(RELAY_SECTIONS, MICRO).astype(jnp.int32)


def touch_ends(values, own_key, low, largest):
    index_at = [jax.random.randint(jax.random.fold_in(own_key, axis), (), 0, length) for axis, length in enumerate(values.shape)]
    main_axis = values.shape.index(max(values.shape))
    neighbour = index_at[:main_axis] + [(index_at[main_axis] + 1) % values.shape[main_axis]] + index_at[main_axis + 1:]
    return values.at[tuple(index_at)].set(low).at[tuple(neighbour)].set(largest)


def levels(rng, extent, cuts, least, top_value):
    def one(position, shards_of):
        draws = jax.random.uniform(jax.random.fold_in(jax.random.fold_in(rng, 6), position), (shards_of,), jnp.float32, least / len(cuts), top_value / len(cuts))
        return jnp.repeat(jnp.exp(draws), extent[position] // shards_of).reshape((-1,) + (1,) * (len(extent) - position - 1))

    loudness = one(*cuts[0])
    for cut in cuts[1:]:
        loudness = loudness * one(*cut)
    return loudness


def scatter_about(key, extent, width, bound, shards=(), held_as=jnp.bfloat16):
    entries = jax.random.normal(key, extent, jnp.float32) * width
    if len(shards) > 0:
        entries = levels(key, extent, shards, -0.22, 0.18) * entries
    return jnp.clip(entries, min=-bound, max=bound).astype(held_as)


def setup_inputs(seed: int = 0) -> dict:
    streams_of = jax.random.split(jax.random.key(seed), 9)
    return {
        "output_gradient": scatter_about(streams_of[0], (RELAY_SECTIONS, N_TENSOR, MICRO, ROWS_MB // UPPER_GROUPS, MODEL_WIDTH // LOWER_GROUPS), 1.0, 6.0, ((0, 2), (1, 16))),
        "forward_input": scatter_about(streams_of[1], (RELAY_SECTIONS, MICRO, ROWS_MB, MODEL_WIDTH), 1.0, 6.0, ((0, 2), (3, 16))),
        "saved_rank_outputs": scatter_about(streams_of[2], (RELAY_SECTIONS, MICRO, ROWS_MB, ADAPTER_RANK), 1.0, 6.0, ((0, 2), (2, 16))),
        "projection_weight": scatter_about(streams_of[3], (RELAY_SECTIONS, N_TENSOR, MODEL_WIDTH // UPPER_GROUPS, MODEL_WIDTH // LOWER_GROUPS), MODEL_WIDTH ** -0.5, 0.0625, ((0, 2), (1, 16))),
        "adapter_down_maps": scatter_about(streams_of[4], (RELAY_SECTIONS, CLASS_ADAPTERS, ADAPTER_RANK, MODEL_WIDTH), ADAPTER_RANK ** -0.5, 0.75, ((0, 2), (3, 16))),
        "adapter_up_maps": scatter_about(streams_of[5], (RELAY_SECTIONS, N_TENSOR, CLASS_ADAPTERS, ADAPTER_RANK // UPPER_GROUPS, MODEL_WIDTH // LOWER_GROUPS), MODEL_WIDTH ** -0.5, 0.0625, ((0, 2), (1, 16))),
        "segment_adapter_class": touch_ends(jax.random.randint(streams_of[6], (RELAY_SECTIONS, MICRO, SEG_MB), 0, CLASS_ADAPTERS), jax.random.fold_in(streams_of[6], 1), 0, CLASS_ADAPTERS - 1).astype(jnp.int32),
        "live_segment_table": draw_live_segment_table(jax.random.fold_in(streams_of[8], 71), 0),
    }


def untile(tiles):
    arranged = tiles.reshape((UPPER_GROUPS, LOWER_GROUPS) + tiles.shape[1:])
    arranged = jnp.moveaxis(arranged, 0, -3)
    arranged = jnp.moveaxis(arranged, 0, -2)
    lead = arranged.shape[:-4]
    return arranged.reshape(lead + (UPPER_GROUPS * tiles.shape[-2], LOWER_GROUPS * tiles.shape[-1]))


def retile(whole):
    rank_part = ADAPTER_RANK // UPPER_GROUPS
    col_part = MODEL_WIDTH // LOWER_GROUPS
    arranged = whole.reshape(CLASS_ADAPTERS, UPPER_GROUPS, rank_part, LOWER_GROUPS, col_part)
    arranged = jnp.transpose(arranged, (1, 3, 0, 2, 4))
    return arranged.reshape(N_TENSOR, CLASS_ADAPTERS, rank_part, col_part)


def relay_section_backward(items):
    grad_tiles, inputs, hidden, weight_tiles, down_matrix, up_tiles, classes, live_count = items
    grads = untile(grad_tiles)
    weight = untile(weight_tiles)
    up_matrices = untile(up_tiles)
    seg_ids = jnp.arange(ROWS_MB, dtype=jnp.int32) // SEG
    keep_rows = seg_ids[None, :] < live_count[:, None]
    masked = jnp.where(keep_rows[:, :, None], grads, jnp.zeros_like(grads))
    class_indicator = (classes[:, :, None] == jnp.arange(CLASS_ADAPTERS, dtype=jnp.int32)[None, None, :]).astype(jnp.float32)
    highest_precision = lax.Precision.HIGHEST
    selected_up_matrix = jnp.einsum('pzw,wlq->pzlq', class_indicator, up_matrices.astype(jnp.float32), precision=highest_precision)
    selected_down_matrix = jnp.einsum('pzw,wlq->pzlq', class_indicator, down_matrix.astype(jnp.float32), precision=highest_precision)
    seg_grads = masked.reshape(MICRO, SEG_MB, SEG, MODEL_WIDTH).astype(jnp.float32)
    lowrank = jnp.einsum('mskd,msrd->mskr', seg_grads, selected_up_matrix, precision=highest_precision).astype(jnp.bfloat16)
    base_term = jnp.dot(masked.reshape(ROWS, MODEL_WIDTH), weight.T, preferred_element_type=jnp.float32)
    adapter = jnp.einsum('mskr,msrd->mskd', lowrank.astype(jnp.float32), selected_down_matrix, precision=highest_precision).reshape(ROWS, MODEL_WIDTH)
    input_gradient = (base_term + adapter).astype(jnp.bfloat16).reshape(MICRO, ROWS_MB, MODEL_WIDTH)
    seg_inputs = inputs.reshape(MICRO, SEG_MB, SEG, MODEL_WIDTH).astype(jnp.float32)
    seg_hidden = hidden.reshape(MICRO, SEG_MB, SEG, ADAPTER_RANK).astype(jnp.float32)
    segment_down_matrix = jnp.einsum('mskr,mskd->msrd', lowrank.astype(jnp.float32), seg_inputs, precision=highest_precision)
    segment_up_matrix = jnp.einsum('mskr,mskd->msrd', seg_hidden, seg_grads, precision=highest_precision)
    down_map_gradient = jnp.einsum('exk,exlq->klq', class_indicator, segment_down_matrix, precision=highest_precision).astype(jnp.bfloat16)
    up_map_gradient = jnp.einsum('exk,exlq->klq', class_indicator, segment_up_matrix, precision=highest_precision).astype(jnp.bfloat16)
    return input_gradient, down_map_gradient, retile(up_map_gradient)


def reference(output_gradient, forward_input, saved_rank_outputs, projection_weight, adapter_down_maps, adapter_up_maps, segment_adapter_class, live_segment_table):
    input_gradient, down_map_gradient, up_map_gradient = lax.map(relay_section_backward, (output_gradient, forward_input, saved_rank_outputs, projection_weight, adapter_down_maps, adapter_up_maps, segment_adapter_class, live_segment_table))
    grad_prev = jnp.roll(input_gradient, -1, axis=0)
    return grad_prev, down_map_gradient, up_map_gradient
```

```python
import jax
import jax.numpy as jnp
from jax import lax
from jax.experimental import pallas as pl
from jax.experimental.pallas import tpu as pltpu
from jax.sharding import PartitionSpec as P

SEG = 128
BF16 = jnp.bfloat16
F32 = jnp.float32


def partner(value, mask):
    pairs = [(source, source ^ mask) for source in range(lax.axis_size("tensor"))]
    return lax.ppermute(value, "tensor", pairs)


def relay(value, mask):
    sections, tiles = lax.axis_size("pipe"), lax.axis_size("tensor")
    pairs = [
        (p * tiles + t, (p - 1) % sections * tiles + (t ^ mask))
        for p in range(sections)
        for t in range(tiles)
    ]
    return lax.ppermute(value, ("pipe", "tensor"), pairs)


def product_body(table_ref, limit_ref, rows_ref, weight_ref, out_ref):
    value = lax.dot_general(
        rows_ref[...], weight_ref[0], (((1,), (1,)), ((), ())), preferred_element_type=F32
    )
    row = lax.broadcasted_iota(jnp.int32, value.shape, 0)
    out_ref[0] = jnp.where(row < limit_ref[0], value, 0.0).astype(out_ref.dtype)


def product(rows, weight_blocks, table, limit, dtype):
    count, depth = rows.shape
    _, width, _ = weight_blocks.shape
    blocks = table.shape[0]
    return pl.pallas_call(
        product_body,
        grid_spec=pltpu.PrefetchScalarGridSpec(
            num_scalar_prefetch=2,
            grid=(blocks,),
            in_specs=[
                pl.BlockSpec((count, depth), lambda k, table, limit: (0, 0)),
                pl.BlockSpec((1, width, depth), lambda k, table, limit: (table[k], 0, 0)),
            ],
            out_specs=pl.BlockSpec((1, count, width), lambda k, table, limit: (k, 0, 0)),
        ),
        out_shape=jax.ShapeDtypeStruct((blocks, count, width), dtype),
        compiler_params=pltpu.CompilerParams(vmem_limit_bytes=24 * 2**20),
        cost_estimate=pl.CostEstimate(
            flops=2 * blocks * count * width * depth,
            bytes_accessed=2 * (blocks * width * depth + count * depth + blocks * count * width),
            transcendentals=0,
        ),
    )(table, limit, rows, weight_blocks)


def unrelate(parts, own):
    bits = len(parts).bit_length() - 1
    for bit in range(bits):
        swap = (own >> bit) & 1 == 1
        parts = [jnp.where(swap, parts[k ^ (1 << bit)], parts[k]) for k in range(len(parts))]
    return parts


def shards(
    output_gradient,
    forward_input,
    saved_rank_outputs,
    projection_weight,
    adapter_down_maps,
    adapter_up_maps,
    segment_adapter_class,
    live_segment_table,
):
    grad_tile = output_gradient[0, 0]
    micro_count, tile_rows, tile_cols = grad_tile.shape
    up_tile = adapter_up_maps[0, 0]
    class_count, rank_part, _ = up_tile.shape
    down = adapter_down_maps[0]
    rank = down.shape[1]
    portion = down.shape[2]
    tiles = lax.axis_size("tensor")
    low_size = min(tiles, 8)
    low_bits = low_size.bit_length() - 1
    high_size = tiles // low_size
    position = lax.axis_index("tensor")
    low = position % low_size
    high = position // low_size
    batch_rows = tile_rows * high_size
    weight_blocks = projection_weight[0, 0].reshape(low_size, portion, tile_cols)
    classes = segment_adapter_class[0]
    live_count = live_segment_table[0]

    grads = [[grad_tile[m] for m in range(micro_count)]]
    for k in range(1, high_size):
        grads.append([partner(grad_tile[m], k * low_size) for m in range(micro_count)])

    def row_classes(block):
        segs = (block * tile_rows + jnp.arange(tile_rows, dtype=jnp.int32)) // SEG
        chosen = jnp.zeros((micro_count, tile_rows), jnp.int32)
        for s in range(classes.shape[1]):
            chosen = jnp.where(segs[None, :] == s, classes[:, s : s + 1], chosen)
        alive = segs[None, :] < live_count[:, None]
        chosen = jnp.where(alive, chosen, -1).reshape(1, micro_count * tile_rows)
        return chosen == jnp.arange(class_count, dtype=jnp.int32)[:, None]

    indicator = [row_classes(high ^ k) for k in range(high_size)]

    def order_of(m):
        bits = list(range(low_bits))
        if m % 2 == 1 and low_bits > 1:
            bits[0], bits[1] = bits[1], bits[0]
        return bits

    def relative_blocks(bits, first):
        blocks = [first]
        for bit in reversed(bits):
            blocks = blocks + [b | 1 << bit for b in blocks]
        return jnp.array(blocks, jnp.int32) ^ low

    def base_sum(k, m):
        bits = order_of(m)
        limit = jnp.clip(live_count[m] * SEG - (high ^ k) * tile_rows, 0, tile_rows)[None]
        rows = grads[k][m]
        sent = product(rows, weight_blocks, relative_blocks(bits[1:], 1 << bits[0]), limit, BF16)
        got = partner(sent, 1 << bits[0])
        total = product(rows, weight_blocks, relative_blocks(bits[1:], 0), limit, F32)
        for bit in bits[1:]:
            total = total + got
            half = total.shape[0] // 2
            got = total[half:].astype(BF16)
            total = total[:half]
            if bit == bits[-1]:
                return total[0], relay(got[0], 1 << bit)
            got = partner(got, 1 << bit)

    up_flat = up_tile.reshape(class_count * rank_part, tile_cols)
    own_rank = []
    for k in range(high_size):
        rows = jnp.concatenate(grads[k], 0)
        every = lax.dot_general(
            up_flat, rows, (((1,), (1,)), ((), ())), preferred_element_type=F32
        ).reshape(class_count, rank_part, micro_count * tile_rows)
        part = jnp.sum(jnp.where(indicator[k][:, None, :], every, 0.0), 0)
        for bit in range(low_bits):
            part = part + partner(part, 1 << bit)
        own_rank.append(part.astype(BF16))

    sums = [[base_sum(k, m) for m in range(micro_count)] for k in range(high_size)]

    ranks = [own_rank]
    for j in range(1, high_size):
        got = partner(jnp.stack(own_rank), j * low_size)
        ranks.append([got[k ^ j] for k in range(high_size)])
    by_rank = [
        jnp.concatenate(unrelate([ranks[j][k] for j in range(high_size)], high), 0)
        for k in range(high_size)
    ]
    spread = [
        jnp.where(indicator[k][:, None, :], by_rank[k][None], jnp.zeros((), BF16)).reshape(
            class_count * rank, micro_count * tile_rows
        )
        for k in range(high_size)
    ]

    down_flat = down.reshape(class_count * rank, portion)
    finished = []
    for k in range(high_size):
        adapter = lax.dot_general(
            spread[k], down_flat, (((0,), (0,)), ((), ())), preferred_element_type=F32
        ).reshape(micro_count, tile_rows, portion)
        done = []
        for m in range(micro_count):
            own_sum, got = sums[k][m]
            kept = relay((own_sum + adapter[m]).astype(BF16), 0)
            done.append((kept.astype(F32) + got.astype(F32)).astype(BF16))
        finished.append(jnp.stack(done))
    grad_prev = jnp.concatenate(unrelate(finished, high), 1)

    inputs = forward_input[0].reshape(micro_count, high_size, tile_rows, portion)
    spread_rows = jnp.stack(
        unrelate(
            [s.reshape(class_count * rank, micro_count, tile_rows) for s in spread], high
        ),
        2,
    )
    down_map_gradient = lax.dot_general(
        spread_rows.reshape(class_count * rank, -1),
        inputs.reshape(-1, portion),
        (((1,), (0,)), ((), ())),
        preferred_element_type=F32,
    ).astype(BF16)

    hidden = saved_rank_outputs[0]
    for bit in range(low_bits):
        got = partner(hidden, 1 << bit)
        upper = (position >> bit) & 1 == 1
        hidden = jnp.where(
            upper, jnp.concatenate([got, hidden], 1), jnp.concatenate([hidden, got], 1)
        )
    up_total = 0.0
    for k in range(high_size):
        rank_start = (high ^ k) * rank_part
        wanted = lax.dynamic_slice_in_dim(hidden, rank_start, rank_part, 2)
        if k > 0:
            wanted = partner(wanted, k * low_size)
        wanted = wanted.reshape(micro_count * tile_rows, rank_part).T
        wide = jnp.where(indicator[k][:, None, :], wanted[None], jnp.zeros((), BF16))
        up_total = up_total + lax.dot_general(
            wide.reshape(class_count * rank_part, -1),
            jnp.concatenate(grads[k], 0),
            (((1,), (0,)), ((), ())),
            preferred_element_type=F32,
        )
    up_map_gradient = up_total.astype(BF16)
    return (
        grad_prev[None],
        down_map_gradient.reshape(1, class_count, rank, portion),
        up_map_gradient.reshape(1, 1, class_count, rank_part, tile_cols),
    )


def solution(mesh):
    in_specs = (
        P("pipe", "tensor", None, None, None),
        P("pipe", None, None, "tensor"),
        P("pipe", None, "tensor", None),
        P("pipe", "tensor", None, None),
        P("pipe", None, None, "tensor"),
        P("pipe", "tensor", None, None, None),
        P("pipe", None, None),
        P("pipe", None),
    )
    out_specs = (
        P("pipe", None, None, "tensor"),
        P("pipe", None, None, "tensor"),
        P("pipe", "tensor", None, None, None),
    )
    return jax.shard_map(shards, mesh=mesh, in_specs=in_specs, out_specs=out_specs, check_vma=False)
```

```python
import jax
import jax.numpy as jnp
from jax import lax
from jax.experimental import pallas as pl
from jax.experimental.pallas import tpu as pltpu
from jax.sharding import PartitionSpec as P

SEG = 128
BF16 = jnp.bfloat16
F32 = jnp.float32


def partner(value, mask):
    pairs = [(source, source ^ mask) for source in range(lax.axis_size("tensor"))]
    return lax.ppermute(value, "tensor", pairs)


def relay(value, mask):
    sections, tiles = lax.axis_size("pipe"), lax.axis_size("tensor")
    pairs = [
        (p * tiles + t, (p - 1) % sections * tiles + (t ^ mask))
        for p in range(sections)
        for t in range(tiles)
    ]
    return lax.ppermute(value, ("pipe", "tensor"), pairs)


def product_body(table_ref, limit_ref, rows_ref, weight_ref, out_ref, turned_ref):
    @pl.when(pl.program_id(0) == 0)
    def _():
        turned_ref[...] = rows_ref[...].reshape(turned_ref.shape[::-1]).T

    value = jnp.dot(weight_ref[0], turned_ref[...], preferred_element_type=F32)
    row = lax.broadcasted_iota(jnp.int32, value.shape, 1)
    out_ref[0] = jnp.where(row < limit_ref[0], value, 0.0).astype(out_ref.dtype)


def product(rows, micro, weight_blocks, table, limit, dtype):
    _, count, depth = rows.shape
    _, width, _ = weight_blocks.shape
    blocks = table.shape[0]
    return pl.pallas_call(
        product_body,
        grid_spec=pltpu.PrefetchScalarGridSpec(
            num_scalar_prefetch=2,
            grid=(blocks,),
            in_specs=[
                pl.BlockSpec((1, count, depth), lambda k, table, limit: (micro, 0, 0)),
                pl.BlockSpec((1, width, depth), lambda k, table, limit: (table[k], 0, 0)),
            ],
            out_specs=pl.BlockSpec((1, width, count), lambda k, table, limit: (k, 0, 0)),
            scratch_shapes=[pltpu.VMEM((depth, count), rows.dtype)],
        ),
        out_shape=jax.ShapeDtypeStruct((blocks, width, count), dtype),
        cost_estimate=pl.CostEstimate(
            flops=2 * blocks * count * width * depth,
            bytes_accessed=2 * (blocks * width * depth + count * depth + blocks * count * width),
            transcendentals=0,
        ),
    )(table, limit, rows, weight_blocks)


def finish_body(micro_count, high_size, high_ref, kept_ref, *refs):
    *got_refs, out_ref = refs
    _, _, count = kept_ref.shape
    for k in range(high_size):
        start = pl.multiple_of((high_ref[0] ^ k) * count, count)
        for m in range(micro_count):
            at = k * micro_count + m
            total = kept_ref[at].astype(F32) + got_refs[at][...].astype(F32)
            out_ref[m, pl.ds(start, count), :] = total.T.astype(out_ref.dtype)


def finish(kept, got, high, micro_count):
    _, width, count = kept.shape
    high_size = len(got) // micro_count
    return pl.pallas_call(
        lambda *refs: finish_body(micro_count, high_size, *refs),
        in_specs=[pl.BlockSpec(memory_space=pltpu.SMEM)]
        + [pl.BlockSpec(memory_space=pltpu.VMEM)] * (1 + len(got)),
        out_specs=pl.BlockSpec(memory_space=pltpu.VMEM),
        out_shape=jax.ShapeDtypeStruct((micro_count, high_size * count, width), BF16),
    )(high[None], kept, *got)


def unrelate(parts, own):
    bits = len(parts).bit_length() - 1
    for bit in range(bits):
        swap = (own >> bit) & 1 == 1
        parts = [jnp.where(swap, parts[k ^ (1 << bit)], parts[k]) for k in range(len(parts))]
    return parts


def shards(
    output_gradient,
    forward_input,
    saved_rank_outputs,
    projection_weight,
    adapter_down_maps,
    adapter_up_maps,
    segment_adapter_class,
    live_segment_table,
):
    grad_tile = output_gradient[0, 0]
    micro_count, tile_rows, tile_cols = grad_tile.shape
    up_tile = adapter_up_maps[0, 0]
    class_count, rank_part, _ = up_tile.shape
    down = adapter_down_maps[0]
    rank = down.shape[1]
    portion = down.shape[2]
    tiles = lax.axis_size("tensor")
    low_size = min(tiles, 8)
    low_bits = low_size.bit_length() - 1
    high_size = tiles // low_size
    position = lax.axis_index("tensor")
    low = position % low_size
    high = position // low_size
    batch_rows = tile_rows * high_size
    weight_blocks = projection_weight[0, 0].reshape(low_size, portion, tile_cols)
    classes = segment_adapter_class[0]
    live_count = live_segment_table[0]

    groups = [(k, m) for k in range(high_size) for m in range(micro_count)]

    grads = {(0, m): (grad_tile, m) for m in range(micro_count)}
    for k in range(1, high_size):
        for m in range(micro_count):
            grads[k, m] = (partner(grad_tile[m], k * low_size)[None], 0)

    def order_of(m):
        bits = list(range(low_bits))
        if m % 2 == 1 and low_bits > 1:
            bits[0], bits[1] = bits[1], bits[0]
        return bits

    def relative_blocks(bits, first):
        blocks = [first]
        for bit in reversed(bits):
            blocks = blocks + [b | 1 << bit for b in blocks]
        return jnp.array(blocks, jnp.int32) ^ low

    def limit_of(k, m):
        return jnp.clip(live_count[m] * SEG - (high ^ k) * tile_rows, 0, tile_rows)[None]

    def sent_product(k, m):
        bits = order_of(m)
        table = relative_blocks(bits[1:], 1 << bits[0])
        return product(*grads[k, m], weight_blocks, table, limit_of(k, m), BF16)

    def kept_product(k, m):
        table = relative_blocks(order_of(m)[1:], 0)
        return product(*grads[k, m], weight_blocks, table, limit_of(k, m), F32)

    first = {(0, m): sent_product(0, m) for m in range(micro_count)}
    held = lax.optimization_barrier(
        (*first.values(), up_tile, saved_rank_outputs[0], forward_input[0], down)
    )
    first = dict(zip(first, held))
    up_tile, hidden, inputs, down = held[-4:]

    def row_classes(k, m):
        segs = ((high ^ k) * tile_rows + jnp.arange(tile_rows, dtype=jnp.int32)) // SEG
        chosen = jnp.zeros((tile_rows,), jnp.int32)
        for s in range(classes.shape[1]):
            chosen = jnp.where(segs == s, classes[m, s], chosen)
        chosen = jnp.where(segs < live_count[m], chosen, -1)
        return (chosen[None] == jnp.arange(class_count, dtype=jnp.int32)[:, None])[:, None]

    indicator = {g: row_classes(*g) for g in groups}

    def base_sum(k, m):
        bits = order_of(m)
        sent = first[k, m] if (k, m) in first else sent_product(k, m)
        got = partner(sent, 1 << bits[0])
        total = kept_product(k, m)
        for bit in bits[1:]:
            total = total + got
            half = total.shape[0] // 2
            got = total[half:].astype(BF16)
            total = total[:half]
            if bit == bits[-1]:
                return total[0], relay(got[0], 1 << bit)
            got = partner(got, 1 << bit)

    sums = {g: base_sum(*g) for g in groups}

    up_flat = up_tile.reshape(class_count * rank_part, tile_cols)
    parts = []
    for g in groups:
        rows, at = grads[g]
        every = lax.dot_general(
            up_flat, rows[at], (((1,), (1,)), ((), ())), preferred_element_type=F32
        ).reshape(class_count, rank_part, tile_rows)
        parts.append(jnp.sum(jnp.where(indicator[g], every, 0.0), 0))
    own_rank = jnp.concatenate(parts, 1)
    for bit in range(low_bits):
        own_rank = own_rank + partner(own_rank, 1 << bit)
    own_rank = own_rank.astype(BF16)

    def by_group(whole):
        return dict(zip(groups, jnp.split(whole, len(groups), 1)))

    ranks = [by_group(own_rank)]
    for j in range(1, high_size):
        got = by_group(partner(own_rank, j * low_size))
        ranks.append({(k, m): got[k ^ j, m] for k, m in groups})
    spread = {}
    for g in groups:
        whole = jnp.concatenate(unrelate([r[g] for r in ranks], high), 0)
        spread[g] = jnp.where(indicator[g], whole[None], jnp.zeros((), BF16)).reshape(
            class_count * rank, tile_rows
        )

    down_flat = down.reshape(class_count * rank, portion)
    kept = []
    for g in groups:
        adapter = lax.dot_general(
            down_flat, spread[g], (((0,), (0,)), ((), ())), preferred_element_type=F32
        )
        kept.append((sums[g][0] + adapter).astype(BF16))
    kept = relay(jnp.stack(kept), 0)
    grad_prev = finish(kept, [sums[g][1] for g in groups], high, micro_count)

    inputs = inputs.reshape(micro_count, high_size, tile_rows, portion)
    down_total = 0.0
    for k, m in groups:
        rows = lax.dynamic_index_in_dim(inputs[m], high ^ k, 0, False)
        down_total = down_total + jnp.dot(spread[k, m], rows, preferred_element_type=F32)
    down_map_gradient = down_total.astype(BF16)

    for bit in range(low_bits):
        got = partner(hidden, 1 << bit)
        upper = (position >> bit) & 1 == 1
        hidden = jnp.where(
            upper, jnp.concatenate([got, hidden], 1), jnp.concatenate([hidden, got], 1)
        )
    up_total = 0.0
    for k in range(high_size):
        wanted = lax.dynamic_slice_in_dim(hidden, (high ^ k) * rank_part, rank_part, 2)
        if k > 0:
            wanted = partner(wanted, k * low_size)
        for m in range(micro_count):
            rows, at = grads[k, m]
            wide = jnp.where(indicator[k, m], wanted[m].T[None], jnp.zeros((), BF16))
            up_total = up_total + jnp.dot(
                wide.reshape(class_count * rank_part, tile_rows),
                rows[at],
                preferred_element_type=F32,
            )
    up_map_gradient = up_total.astype(BF16)
    return (
        grad_prev[None],
        down_map_gradient.reshape(1, class_count, rank, portion),
        up_map_gradient.reshape(1, 1, class_count, rank_part, tile_cols),
    )


def solution(mesh):
    in_specs = (
        P("pipe", "tensor", None, None, None),
        P("pipe", None, None, "tensor"),
        P("pipe", None, "tensor", None),
        P("pipe", "tensor", None, None),
        P("pipe", None, None, "tensor"),
        P("pipe", "tensor", None, None, None),
        P("pipe", None, None),
        P("pipe", None),
    )
    out_specs = (
        P("pipe", None, None, "tensor"),
        P("pipe", None, None, "tensor"),
        P("pipe", "tensor", None, None, None),
    )
    return jax.shard_map(shards, mesh=mesh, in_specs=in_specs, out_specs=out_specs, check_vma=False)
```

```python
import functools

import jax
import jax.numpy as jnp
from jax import lax
from jax.experimental import pallas as pl
from jax.experimental.pallas import tpu as pltpu
from jax.sharding import PartitionSpec as P

SEG = 128
BF16 = jnp.bfloat16
F32 = jnp.float32
SMEM = pl.BlockSpec(memory_space=pltpu.SMEM)
VMEM = pl.BlockSpec(memory_space=pltpu.VMEM)
NT = (((1,), (1,)), ((), ()))
TN = (((0,), (0,)), ((), ()))


def partner(value, mask):
    pairs = [(source, source ^ mask) for source in range(lax.axis_size("tensor"))]
    return lax.ppermute(value, "tensor", pairs)


def relay(value, mask):
    sections, tiles = lax.axis_size("pipe"), lax.axis_size("tensor")
    pairs = [
        (p * tiles + t, (p - 1) % sections * tiles + (t ^ mask))
        for p in range(sections)
        for t in range(tiles)
    ]
    return lax.ppermute(value, ("pipe", "tensor"), pairs)


def segment_of(high, piece, tile_rows):
    k, _, offset = piece
    return ((high ^ k) * tile_rows + offset) // SEG


def product_body(low_size, tile_rows, pieces, tiles, subs, *refs):
    pos_ref, classes_ref, live_ref = refs[:3]
    grad_refs = refs[3 : 3 + tiles]
    weight_refs = refs[3 + tiles : 3 + tiles + subs]
    up_ref = refs[3 + tiles + subs]
    sent_x, kept_x, sent_y, kept_y, rank_ref, rows_ref = refs[4 + tiles + subs :]
    step = pl.program_id(0)
    high = pos_ref[0] // low_size
    size = pieces[0][3]
    half = rows_ref.shape[0] // 2

    @pl.when(step == 0)
    def _():
        for at, (tile, index, piece, _) in enumerate(pieces):
            seg = segment_of(high, piece, tile_rows)
            alive = seg < live_ref[piece[1]]
            place = slice(at * size, (at + 1) * size)

            @pl.when(alive)
            def _():
                rows = grad_refs[tile][index, piece[2] : piece[2] + size, :]
                rows_ref[place, :] = rows
                up = up_ref[classes_ref[piece[1], seg]]
                rank_ref[:, place] = lax.dot_general(up, rows, NT, preferred_element_type=F32)

            @pl.when(jnp.logical_not(alive))
            def _():
                rows_ref[place, :] = jnp.zeros((size, rows_ref.shape[1]), rows_ref.dtype)
                rank_ref[:, place] = jnp.zeros((rank_ref.shape[0], size), F32)

    for sub, weight_ref in enumerate(weight_refs):
        width = weight_ref.shape[1]
        columns = slice(sub * width, (sub + 1) * width)
        value = lax.dot_general(rows_ref[...], weight_ref[0], NT, preferred_element_type=F32)

        @pl.when(step < 4)
        def _():
            sent_x[0, :, columns] = value[:half].astype(BF16)

        @pl.when(step >= 4)
        def _():
            kept_x[0, :, columns] = value[:half]

        @pl.when(step & 2 == 0)
        def _():
            sent_y[0, :, columns] = value[half:].astype(BF16)

        @pl.when(step & 2 != 0)
        def _():
            kept_y[0, :, columns] = value[half:]


def product(scalars, grads, pieces, weight_blocks, up_tile, low_size):
    blocks, width, depth = weight_blocks.shape
    tile_rows = grads[0].shape[1]
    rows = len(pieces) * pieces[0][3]
    half = rows // 2
    subs = 2 if width % 512 == 0 else 1

    def block_of(k):
        return 1 - k // 4 + (2 - (k & 2)) + 4 * (k & 1)

    def whole(array):
        return pl.BlockSpec(array.shape, lambda k, *_: (0,) * array.ndim)

    def weight_spec(sub):
        return pl.BlockSpec(
            (1, width // subs, depth), lambda k, pos, *_: (block_of(k) ^ (pos[0] % low_size), sub, 0)
        )

    def slot(place):
        return pl.BlockSpec((1, half, width), lambda k, *_: (place(k), 0, 0))

    def by_y(k):
        return 2 - (k & 2) + (k & 1)

    outs = [
        (BF16, lambda k: jnp.where(k < 4, by_y(k), 1)),
        (F32, lambda k: jnp.where(k < 4, 2, by_y(k))),
        (BF16, lambda k: 2 * (1 - k // 4) + jnp.where(k & 2 == 0, k & 1, 1)),
        (F32, lambda k: 2 * (1 - k // 4) + jnp.where(k & 2 == 0, 0, k & 1)),
    ]
    rank_part = up_tile.shape[1]
    return pl.pallas_call(
        functools.partial(product_body, low_size, tile_rows, pieces, len(grads), subs),
        grid_spec=pltpu.PrefetchScalarGridSpec(
            num_scalar_prefetch=3,
            grid=(blocks,),
            in_specs=[whole(g) for g in grads]
            + [weight_spec(sub) for sub in range(subs)]
            + [whole(up_tile)],
            out_specs=[slot(place) for _, place in outs]
            + [pl.BlockSpec((rank_part, rows), lambda k, *_: (0, 0))],
            scratch_shapes=[pltpu.VMEM((rows, depth), BF16)],
        ),
        out_shape=[jax.ShapeDtypeStruct((blocks // 2, half, width), dtype) for dtype, _ in outs]
        + [jax.ShapeDtypeStruct((rank_part, rows), F32)],
        cost_estimate=pl.CostEstimate(
            flops=2 * blocks * rows * width * depth,
            bytes_accessed=2 * blocks * width * depth + 8 * blocks * rows * width,
            transcendentals=0,
        ),
    )(*scalars, *grads, *([weight_blocks] * subs), up_tile)


def up_body(low_size, tile_rows, pieces, tiles, *refs):
    pos_ref, classes_ref, live_ref = refs[:3]
    grad_refs = refs[3 : 3 + tiles]
    hidden_refs = refs[3 + tiles : -2]
    out_ref, total_ref = refs[-2:]
    high = pos_ref[0] // low_size
    total_ref[...] = jnp.zeros_like(total_ref)
    for tile, index, piece, size in pieces:
        k, m, offset = piece
        seg = segment_of(high, piece, tile_rows)

        @pl.when(seg < live_ref[m])
        def _():
            total_ref[classes_ref[m, seg]] += lax.dot_general(
                hidden_refs[k][m, offset : offset + size, :],
                grad_refs[tile][index, offset : offset + size, :],
                TN,
                preferred_element_type=F32,
            )

    out_ref[...] = total_ref[...].astype(BF16)


def shards(
    output_gradient,
    forward_input,
    saved_rank_outputs,
    projection_weight,
    adapter_down_maps,
    adapter_up_maps,
    segment_adapter_class,
    live_segment_table,
):
    grad_tile = output_gradient[0, 0]
    micro_count, tile_rows, tile_cols = grad_tile.shape
    up_tile = adapter_up_maps[0, 0]
    class_count, rank_part, _ = up_tile.shape
    rank, portion = adapter_down_maps.shape[2:]
    tiles = lax.axis_size("tensor")
    low_size = min(tiles, 8)
    low_bits = low_size.bit_length() - 1
    high_size = tiles // low_size
    position = lax.axis_index("tensor")
    high = position // low_size
    weight_blocks = projection_weight[0, 0].reshape(low_size, portion, tile_cols)
    scalars = (position.astype(jnp.int32)[None], segment_adapter_class[0], live_segment_table[0])
    size = min(SEG, tile_rows)
    offsets = range(0, tile_rows, size)

    own_pieces = [(0, m, (0, m, o), size) for m in range(micro_count) for o in offsets]
    chunks = [([grad_tile], own_pieces)]
    for m in range(micro_count):
        got = [partner(grad_tile[m], k * low_size)[None] for k in range(1, high_size)]
        pieces = [(k - 1, 0, (k, m, o), size) for k in range(1, high_size) for o in offsets]
        chunks.append((got, pieces))
    order = [piece for _, pieces in chunks for _, _, piece, _ in pieces]

    hidden = saved_rank_outputs[0]
    sums, got_last, parts = [], [], []
    for grads, pieces in chunks:
        sent_x, kept_x, sent_y, kept_y, part = product(
            scalars, grads, pieces, weight_blocks, up_tile, low_size
        )
        parts.append(part)
        if not sums:
            sent_x, sent_y, hidden = lax.optimization_barrier((sent_x, sent_y, hidden))
        for bits, sent, kept in (((0, 1, 2), sent_x, kept_x), ((1, 0, 2), sent_y, kept_y)):
            got = partner(sent, 1 << bits[0])
            second = partner((kept[2:] + got[2:]).astype(BF16), 1 << bits[1])
            third = (kept[1] + got[1] + second[1]).astype(BF16)
            got_last.append(relay(third, 1 << bits[2]))
            sums.append((kept, got, second))

    for bit in range(low_bits):
        got = partner(hidden, 1 << bit)
        upper = (position >> bit) & 1 == 1
        hidden = jnp.where(
            upper, jnp.concatenate([got, hidden], 1), jnp.concatenate([hidden, got], 1)
        )
    hiddens = []
    for k in range(high_size):
        wanted = lax.dynamic_slice_in_dim(hidden, (high ^ k) * rank_part, rank_part, 2)
        hiddens.append(partner(wanted, k * low_size) if k > 0 else wanted)

    all_grads, all_pieces = [], []
    for grads, pieces in chunks:
        all_pieces += [(tile + len(all_grads), index, piece, size) for tile, index, piece, size in pieces]
        all_grads += grads
    up_map_gradient = pl.pallas_call(
        functools.partial(up_body, low_size, tile_rows, all_pieces, len(all_grads)),
        in_specs=[SMEM] * 3 + [VMEM] * (len(all_grads) + high_size),
        out_specs=VMEM,
        out_shape=jax.ShapeDtypeStruct(up_tile.shape, BF16),
        scratch_shapes=[pltpu.VMEM(up_tile.shape, F32)],
        cost_estimate=pl.CostEstimate(
            flops=2 * len(order) * size * rank_part * tile_cols,
            bytes_accessed=2 * len(order) * size * tile_cols,
            transcendentals=0,
        ),
    )(*scalars, *all_grads, *hiddens)

    own_rank = jnp.concatenate(parts, 1)
    for bit in range(low_bits):
        own_rank = own_rank + partner(own_rank, 1 << bit)
    own_rank = own_rank.astype(BF16)
    ranks = [own_rank] + [partner(own_rank, j * low_size) for j in range(1, high_size)]

    def columns_of(j, piece):
        k, m, offset = piece
        at = order.index((k ^ j, m, offset))
        return slice(at * size, (at + 1) * size)

    down_parts = adapter_down_maps[0].reshape(class_count, high_size, rank_part, portion)

    def adapter_kernel(pos_ref, classes_ref, live_ref, down_ref, *refs):
        rank_refs, sum_refs = refs[:high_size], refs[high_size:-2]
        out_ref, total_ref = refs[-2:]
        own = pos_ref[0] // low_size
        start = 0
        for g in range(len(sums)):
            kept_ref, got_ref, second_ref = sum_refs[3 * g : 3 * g + 3]
            count = kept_ref.shape[1]
            total_ref[start : start + count, :] = (
                kept_ref[0] + got_ref[0].astype(F32) + second_ref[0].astype(F32)
            )
            start += count
        for at, piece in enumerate(order):
            seg = segment_of(own, piece, tile_rows)
            rows = slice(at * size, (at + 1) * size)
            adapter = 0.0
            for j in range(high_size):
                adapter = adapter + lax.dot_general(
                    rank_refs[j][:, columns_of(j, piece)],
                    down_ref[classes_ref[piece[1], seg], own ^ j],
                    TN,
                    preferred_element_type=F32,
                )
            out_ref[rows, :] = (total_ref[rows, :] + adapter).astype(BF16)

    rows_total = len(order) * size
    kept = pl.pallas_call(
        adapter_kernel,
        grid=(1,),
        in_specs=[SMEM] * 3
        + [pl.BlockSpec(a.shape, lambda _, n=a.ndim: (0,) * n) for a in [down_parts, *ranks]]
        + [pl.BlockSpec((1,) + a.shape[1:], lambda _: (0, 0, 0)) for three in sums for a in three],
        out_specs=pl.BlockSpec((rows_total, portion), lambda _: (0, 0)),
        out_shape=jax.ShapeDtypeStruct((rows_total, portion), BF16),
        scratch_shapes=[pltpu.VMEM((rows_total, portion), F32)],
        compiler_params=pltpu.CompilerParams(vmem_limit_bytes=40 * 2**20),
        cost_estimate=pl.CostEstimate(
            flops=2 * rows_total * rank * portion,
            bytes_accessed=10 * rows_total * portion,
            transcendentals=0,
        ),
    )(*scalars, down_parts, *ranks, *[a for three in sums for a in three])
    kept = relay(kept, 0)

    def finish_kernel(pos_ref, kept_ref, *refs):
        got_refs, out_ref = refs[:-1], refs[-1]
        own = pos_ref[0] // low_size
        start, found = 0, []
        for got_ref in got_refs:
            for row in range(0, got_ref.shape[0], 16):
                found.append((got_ref, row))
        for at, (k, m, offset) in enumerate(order):
            base = pl.multiple_of((own ^ k) * tile_rows + offset, size)
            row = 0
            while row < size:
                got_ref, first = found[(at * size + row) // 16]
                count = min(size - row, got_ref.shape[0] - first)
                spot = at * size + row
                out_ref[m, pl.ds(base + row, count), :] = (
                    kept_ref[spot : spot + count, :].astype(F32)
                    + got_ref[first : first + count, :].astype(F32)
                ).astype(BF16)
                row += count

    grad_prev = pl.pallas_call(
        finish_kernel,
        in_specs=[SMEM] + [VMEM] * (1 + len(got_last)),
        out_specs=VMEM,
        out_shape=jax.ShapeDtypeStruct((micro_count, high_size * tile_rows, portion), BF16),
    )(scalars[0], kept, *got_last)

    def down_kernel(pos_ref, classes_ref, live_ref, inputs_ref, *refs):
        rank_refs, out_ref, total_ref = refs[:-2], refs[-2], refs[-1]
        own = pos_ref[0] // low_size
        total_ref[...] = jnp.zeros_like(total_ref)
        for piece in order:
            k, m, offset = piece
            seg = segment_of(own, piece, tile_rows)

            @pl.when(seg < live_ref[m])
            def _():
                base = pl.multiple_of((own ^ k) * tile_rows + offset, size)
                rows = inputs_ref[m, pl.ds(base, size), :]
                for j in range(high_size):
                    total_ref[classes_ref[m, seg], own ^ j] += jnp.dot(
                        rank_refs[j][:, columns_of(j, piece)], rows, preferred_element_type=F32
                    )

        out_ref[...] = total_ref[...].astype(BF16)

    down_map_gradient = pl.pallas_call(
        down_kernel,
        in_specs=[SMEM] * 3 + [VMEM] * (1 + high_size),
        out_specs=VMEM,
        out_shape=jax.ShapeDtypeStruct(down_parts.shape, BF16),
        scratch_shapes=[pltpu.VMEM(down_parts.shape, F32)],
        cost_estimate=pl.CostEstimate(
            flops=2 * rows_total * rank * portion,
            bytes_accessed=2 * rows_total * portion,
            transcendentals=0,
        ),
    )(*scalars, forward_input[0], *ranks)

    return (
        grad_prev[None],
        down_map_gradient.reshape(1, class_count, rank, portion),
        up_map_gradient[None, None],
    )


def solution(mesh):
    in_specs = (
        P("pipe", "tensor", None, None, None),
        P("pipe", None, None, "tensor"),
        P("pipe", None, "tensor", None),
        P("pipe", "tensor", None, None),
        P("pipe", None, None, "tensor"),
        P("pipe", "tensor", None, None, None),
        P("pipe", None, None),
        P("pipe", None),
    )
    out_specs = (
        P("pipe", None, None, "tensor"),
        P("pipe", None, None, "tensor"),
        P("pipe", "tensor", None, None, None),
    )
    return jax.shard_map(shards, mesh=mesh, in_specs=in_specs, out_specs=out_specs, check_vma=False)
```

```python
import functools

import jax
import jax.numpy as jnp
from jax import lax
from jax.experimental import pallas as pl
from jax.experimental.pallas import tpu as pltpu
from jax.sharding import PartitionSpec as P

SEG = 128
BF16 = jnp.bfloat16
F32 = jnp.float32
SMEM = pl.BlockSpec(memory_space=pltpu.SMEM)
VMEM = pl.BlockSpec(memory_space=pltpu.VMEM)
TN = (((0,), (0,)), ((), ()))


def partner(value, mask):
    pairs = [(source, source ^ mask) for source in range(lax.axis_size("tensor"))]
    return lax.ppermute(value, "tensor", pairs)


def relay(value, mask):
    sections, tiles = lax.axis_size("pipe"), lax.axis_size("tensor")
    pairs = [
        (p * tiles + t, (p - 1) % sections * tiles + (t ^ mask))
        for p in range(sections)
        for t in range(tiles)
    ]
    return lax.ppermute(value, ("pipe", "tensor"), pairs)


def segment_of(high, piece, tile_rows):
    k, _, offset = piece
    return ((high ^ k) * tile_rows + offset) // SEG


def product_body(low_size, tile_rows, pieces, tiles, half, *refs):
    pos_ref, classes_ref, live_ref = refs[:3]
    grad_refs = refs[3 : 3 + tiles]
    weight_hbm, up_ref, sent_x, kept_x, sent_y, kept_y, rank_ref, rows_ref, weight_ref, sems = refs[
        3 + tiles :
    ]
    step = pl.program_id(0)
    low, high = pos_ref[0] % low_size, pos_ref[0] // low_size
    size = pieces[0][3]

    def weight_copy(k):
        block = (1 - k // 4 + (2 - (k & 2)) + 4 * (k & 1)) ^ low
        return pltpu.make_async_copy(weight_hbm.at[block], weight_ref.at[k], sems.at[k])

    @pl.when(step == 0)
    def _():
        for k in range(low_size):
            weight_copy(k).start()
        for at, (tile, index, piece, _) in enumerate(pieces):
            seg = segment_of(high, piece, tile_rows)
            alive = seg < live_ref[piece[1]]
            place = slice(at * size, (at + 1) * size)

            @pl.when(alive)
            def _():
                rows = grad_refs[tile][index, piece[2] : piece[2] + size, :].T
                rows_ref[:, place] = rows
                up = up_ref[classes_ref[piece[1], seg]]
                rank_ref[:, place] = jnp.dot(up, rows, preferred_element_type=F32)

            @pl.when(jnp.logical_not(alive))
            def _():
                rows_ref[:, place] = jnp.zeros((rows_ref.shape[0], size), rows_ref.dtype)
                rank_ref[:, place] = jnp.zeros((rank_ref.shape[0], size), F32)

    weight_copy(step).wait()
    value = jnp.dot(weight_ref[step], rows_ref[...], preferred_element_type=F32)

    @pl.when(step < 4)
    def _():
        sent_x[0] = value[:, :half].astype(BF16)

    @pl.when(step >= 4)
    def _():
        kept_x[0] = value[:, :half]

    @pl.when(step & 2 == 0)
    def _():
        sent_y[0] = value[:, half:].astype(BF16)

    @pl.when(step & 2 != 0)
    def _():
        kept_y[0] = value[:, half:]


def product(scalars, grads, pieces, weight_blocks, up_tile, low_size):
    blocks, width, depth = weight_blocks.shape
    tile_rows = grads[0].shape[1]
    rows = len(pieces) * pieces[0][3]
    half = rows // 2
    if rows > 128 and half % 128:
        half = half // 128 * 128 + 128

    def whole(array):
        return pl.BlockSpec(array.shape, lambda k, *_: (0,) * array.ndim)

    def by_y(k):
        return 2 - (k & 2) + (k & 1)

    outs = [
        (half, BF16, lambda k: jnp.where(k < 4, by_y(k), 1)),
        (half, F32, lambda k: jnp.where(k < 4, 2, by_y(k))),
        (rows - half, BF16, lambda k: 2 * (1 - k // 4) + jnp.where(k & 2 == 0, k & 1, 1)),
        (rows - half, F32, lambda k: 2 * (1 - k // 4) + jnp.where(k & 2 == 0, 0, k & 1)),
    ]
    rank_part = up_tile.shape[1]
    return pl.pallas_call(
        functools.partial(product_body, low_size, tile_rows, pieces, len(grads), half),
        grid_spec=pltpu.PrefetchScalarGridSpec(
            num_scalar_prefetch=3,
            grid=(blocks,),
            in_specs=[whole(g) for g in grads]
            + [pl.BlockSpec(memory_space=pl.ANY), whole(up_tile)],
            out_specs=[
                pl.BlockSpec((1, width, count), lambda k, *_, place=place: (place(k), 0, 0))
                for count, _, place in outs
            ]
            + [pl.BlockSpec((rank_part, rows), lambda k, *_: (0, 0))],
            scratch_shapes=[
                pltpu.VMEM((depth, rows), BF16),
                pltpu.VMEM(weight_blocks.shape, BF16),
                pltpu.SemaphoreType.DMA((blocks,)),
            ],
        ),
        out_shape=[
            jax.ShapeDtypeStruct((blocks // 2, width, count), dtype) for count, dtype, _ in outs
        ]
        + [jax.ShapeDtypeStruct((rank_part, rows), F32)],
        compiler_params=pltpu.CompilerParams(vmem_limit_bytes=48 * 2**20),
        cost_estimate=pl.CostEstimate(
            flops=2 * blocks * rows * width * depth,
            bytes_accessed=2 * blocks * width * depth + 3 * blocks * rows * width,
            transcendentals=0,
        ),
    )(*scalars, *grads, weight_blocks, up_tile)


def up_body(low_size, tile_rows, pieces, tiles, *refs):
    pos_ref, classes_ref, live_ref = refs[:3]
    grad_refs = refs[3 : 3 + tiles]
    hidden_refs = refs[3 + tiles : -2]
    out_ref, total_ref = refs[-2:]
    high = pos_ref[0] // low_size
    total_ref[...] = jnp.zeros_like(total_ref)
    for tile, index, piece, size in pieces:
        k, m, offset = piece
        seg = segment_of(high, piece, tile_rows)

        @pl.when(seg < live_ref[m])
        def _():
            total_ref[classes_ref[m, seg]] += lax.dot_general(
                hidden_refs[k][m, offset : offset + size, :],
                grad_refs[tile][index, offset : offset + size, :],
                TN,
                preferred_element_type=F32,
            )

    out_ref[...] = total_ref[...].astype(BF16)


def shards(
    output_gradient,
    forward_input,
    saved_rank_outputs,
    projection_weight,
    adapter_down_maps,
    adapter_up_maps,
    segment_adapter_class,
    live_segment_table,
):
    grad_tile = output_gradient[0, 0]
    micro_count, tile_rows, tile_cols = grad_tile.shape
    up_tile = adapter_up_maps[0, 0]
    class_count, rank_part, _ = up_tile.shape
    rank, portion = adapter_down_maps.shape[2:]
    tiles = lax.axis_size("tensor")
    low_size = min(tiles, 8)
    low_bits = low_size.bit_length() - 1
    high_size = tiles // low_size
    position = lax.axis_index("tensor")
    high = position // low_size
    weight_blocks = projection_weight[0, 0].reshape(low_size, portion, tile_cols)
    scalars = (position.astype(jnp.int32)[None], segment_adapter_class[0], live_segment_table[0])
    size = min(SEG, tile_rows)
    offsets = range(0, tile_rows, size)

    own_pieces = [(0, m, (0, m, o), size) for m in range(micro_count) for o in offsets]
    chunks = [([grad_tile], own_pieces)]
    source = grad_tile
    for m in range(micro_count):
        got = [partner(source[m], k * low_size)[None] for k in range(1, high_size)]
        *got, source = lax.optimization_barrier((*got, source))
        pieces = [(k - 1, 0, (k, m, o), size) for k in range(1, high_size) for o in offsets]
        chunks.append((got, pieces))
    order = [piece for _, pieces in chunks for _, _, piece, _ in pieces]

    hidden = saved_rank_outputs[0]
    sums, got_last, parts = [], [], []
    arrived = [None, None]
    for grads, pieces in chunks:
        sent_x, kept_x, sent_y, kept_y, part = product(
            scalars, grads, pieces, weight_blocks, up_tile, low_size
        )
        parts.append(part)
        if not sums:
            sent_x, sent_y, hidden = lax.optimization_barrier((sent_x, sent_y, hidden))
        ways = (((0, 1, 2), sent_x, kept_x), ((1, 0, 2), sent_y, kept_y))
        for way, (bits, sent, kept) in enumerate(ways):
            if arrived[way] is not None:
                sent, _ = lax.optimization_barrier((sent, arrived[way]))
            got = arrived[way] = partner(sent, 1 << bits[0])
            second = partner((kept[2:] + got[2:]).astype(BF16), 1 << bits[1])
            third = (kept[1] + got[1] + second[1]).astype(BF16)
            got_last.append(relay(third, 1 << bits[2]))
            sums.append((kept, got, second))

    for bit in range(low_bits):
        got = partner(hidden, 1 << bit)
        upper = (position >> bit) & 1 == 1
        hidden = jnp.where(
            upper, jnp.concatenate([got, hidden], 1), jnp.concatenate([hidden, got], 1)
        )
    hiddens = []
    for k in range(high_size):
        wanted = lax.dynamic_slice_in_dim(hidden, (high ^ k) * rank_part, rank_part, 2)
        hiddens.append(partner(wanted, k * low_size) if k > 0 else wanted)

    all_grads, all_pieces = [], []
    for grads, pieces in chunks:
        all_pieces += [(tile + len(all_grads), index, piece, size) for tile, index, piece, size in pieces]
        all_grads += grads
    up_map_gradient = pl.pallas_call(
        functools.partial(up_body, low_size, tile_rows, all_pieces, len(all_grads)),
        in_specs=[SMEM] * 3 + [VMEM] * (len(all_grads) + high_size),
        out_specs=VMEM,
        out_shape=jax.ShapeDtypeStruct(up_tile.shape, BF16),
        scratch_shapes=[pltpu.VMEM(up_tile.shape, F32)],
        cost_estimate=pl.CostEstimate(
            flops=2 * len(order) * size * rank_part * tile_cols,
            bytes_accessed=2 * len(order) * size * tile_cols,
            transcendentals=0,
        ),
    )(*scalars, *all_grads, *hiddens)

    own_rank = jnp.concatenate(parts, 1)
    for bit in range(low_bits):
        own_rank = own_rank + partner(own_rank, 1 << bit)
    own_rank = own_rank.astype(BF16)
    ranks = [own_rank] + [partner(own_rank, j * low_size) for j in range(1, high_size)]

    def columns_of(j, piece):
        k, m, offset = piece
        at = order.index((k ^ j, m, offset))
        return slice(at * size, (at + 1) * size)

    down_parts = adapter_down_maps[0].reshape(class_count, high_size, rank_part, portion)

    def adapter_kernel(pos_ref, classes_ref, live_ref, down_ref, *refs):
        rank_refs, sum_refs = refs[:high_size], refs[high_size:-2]
        out_ref, total_ref = refs[-2:]
        own = pos_ref[0] // low_size
        start = 0
        for g in range(len(sums)):
            kept_ref, got_ref, second_ref = sum_refs[3 * g : 3 * g + 3]
            count = kept_ref.shape[2]
            total_ref[:, start : start + count] = (
                kept_ref[0] + got_ref[0].astype(F32) + second_ref[0].astype(F32)
            )
            start += count
        for at, piece in enumerate(order):
            seg = segment_of(own, piece, tile_rows)
            rows = slice(at * size, (at + 1) * size)
            adapter = total_ref[:, rows]
            for j in range(high_size):
                adapter = adapter + lax.dot_general(
                    down_ref[classes_ref[piece[1], seg], own ^ j],
                    rank_refs[j][:, columns_of(j, piece)],
                    TN,
                    preferred_element_type=F32,
                )
            out_ref[:, rows] = adapter.astype(BF16)

    rows_total = len(order) * size
    kept = pl.pallas_call(
        adapter_kernel,
        grid=(1,),
        in_specs=[SMEM] * 3
        + [pl.BlockSpec(a.shape, lambda _, n=a.ndim: (0,) * n) for a in [down_parts, *ranks]]
        + [pl.BlockSpec((1,) + a.shape[1:], lambda _: (0, 0, 0)) for three in sums for a in three],
        out_specs=pl.BlockSpec((portion, rows_total), lambda _: (0, 0)),
        out_shape=jax.ShapeDtypeStruct((portion, rows_total), BF16),
        scratch_shapes=[pltpu.VMEM((portion, rows_total), F32)],
        compiler_params=pltpu.CompilerParams(vmem_limit_bytes=40 * 2**20),
        cost_estimate=pl.CostEstimate(
            flops=2 * rows_total * rank * portion,
            bytes_accessed=10 * rows_total * portion,
            transcendentals=0,
        ),
    )(*scalars, down_parts, *ranks, *[a for three in sums for a in three])
    kept = relay(kept, 0)

    def finish_kernel(pos_ref, kept_ref, *refs):
        *got_refs, out_ref, total_ref = refs
        own = pos_ref[0] // low_size
        start = 0
        for got_ref in got_refs:
            count = got_ref.shape[1]
            total_ref[:, start : start + count] = (
                kept_ref[:, start : start + count].astype(F32) + got_ref[...].astype(F32)
            ).astype(BF16)
            start += count
        for at, (k, m, offset) in enumerate(order):
            base = pl.multiple_of((own ^ k) * tile_rows + offset, size)
            out_ref[m, pl.ds(base, size), :] = total_ref[:, at * size : (at + 1) * size].T

    grad_prev = pl.pallas_call(
        finish_kernel,
        in_specs=[SMEM] + [VMEM] * (1 + len(got_last)),
        out_specs=VMEM,
        out_shape=jax.ShapeDtypeStruct((micro_count, high_size * tile_rows, portion), BF16),
        scratch_shapes=[pltpu.VMEM((portion, rows_total), BF16)],
    )(scalars[0], kept, *got_last)

    def down_kernel(pos_ref, classes_ref, live_ref, inputs_ref, *refs):
        rank_refs, out_ref, total_ref = refs[:-2], refs[-2], refs[-1]
        own = pos_ref[0] // low_size
        total_ref[...] = jnp.zeros_like(total_ref)
        for piece in order:
            k, m, offset = piece
            seg = segment_of(own, piece, tile_rows)

            @pl.when(seg < live_ref[m])
            def _():
                base = pl.multiple_of((own ^ k) * tile_rows + offset, size)
                rows = inputs_ref[m, pl.ds(base, size), :]
                for j in range(high_size):
                    total_ref[classes_ref[m, seg], own ^ j] += jnp.dot(
                        rank_refs[j][:, columns_of(j, piece)], rows, preferred_element_type=F32
                    )

        out_ref[...] = total_ref[...].astype(BF16)

    down_map_gradient = pl.pallas_call(
        down_kernel,
        in_specs=[SMEM] * 3 + [VMEM] * (1 + high_size),
        out_specs=VMEM,
        out_shape=jax.ShapeDtypeStruct(down_parts.shape, BF16),
        scratch_shapes=[pltpu.VMEM(down_parts.shape, F32)],
        cost_estimate=pl.CostEstimate(
            flops=2 * rows_total * rank * portion,
            bytes_accessed=2 * rows_total * portion,
            transcendentals=0,
        ),
    )(*scalars, forward_input[0], *ranks)

    return (
        grad_prev[None],
        down_map_gradient.reshape(1, class_count, rank, portion),
        up_map_gradient[None, None],
    )


def solution(mesh):
    in_specs = (
        P("pipe", "tensor", None, None, None),
        P("pipe", None, None, "tensor"),
        P("pipe", None, "tensor", None),
        P("pipe", "tensor", None, None),
        P("pipe", None, None, "tensor"),
        P("pipe", "tensor", None, None, None),
        P("pipe", None, None),
        P("pipe", None),
    )
    out_specs = (
        P("pipe", None, None, "tensor"),
        P("pipe", None, None, "tensor"),
        P("pipe", "tensor", None, None, None),
    )
    return jax.shard_map(shards, mesh=mesh, in_specs=in_specs, out_specs=out_specs, check_vma=False)
```

```python
import functools

import jax
import jax.numpy as jnp
from jax import lax
from jax.experimental import pallas as pl
from jax.experimental.pallas import tpu as pltpu
from jax.sharding import PartitionSpec as P

SEG = 128
BF16 = jnp.bfloat16
F32 = jnp.float32
SMEM = pl.BlockSpec(memory_space=pltpu.SMEM)
VMEM = pl.BlockSpec(memory_space=pltpu.VMEM)
TN = (((0,), (0,)), ((), ()))


def partner(value, mask):
    pairs = [(source, source ^ mask) for source in range(lax.axis_size("tensor"))]
    return lax.ppermute(value, "tensor", pairs)


def relay(value, mask):
    sections, tiles = lax.axis_size("pipe"), lax.axis_size("tensor")
    pairs = [
        (p * tiles + t, (p - 1) % sections * tiles + (t ^ mask))
        for p in range(sections)
        for t in range(tiles)
    ]
    return lax.ppermute(value, ("pipe", "tensor"), pairs)


def segment_of(high, piece, tile_rows):
    k, _, offset = piece
    return ((high ^ k) * tile_rows + offset) // SEG


def product_body(low_size, tile_rows, pieces, tiles, half, sends, keeps, *refs):
    pos_ref, classes_ref, live_ref = refs[:3]
    grad_refs = refs[3 : 3 + tiles]
    weight_hbm = refs[3 + tiles]
    rows_ref, weight_ref, sems = refs[-3:]
    rest = list(refs[4 + tiles : -3])
    up_ref = rest.pop(0) if keeps else None
    sent_x, sent_y = (rest.pop(0), rest.pop(0)) if sends else (None, None)
    kept_x, kept_y, rank_ref = rest if keeps else (None, None, None)
    low, high = pos_ref[0] % low_size, pos_ref[0] // low_size
    size = pieces[0][3]
    total = rows_ref.shape[1]

    def weight_copy(block):
        return pltpu.make_async_copy(
            weight_hbm.at[block ^ low], weight_ref.at[block], sems.at[block]
        )

    jobs = []
    for x, y in ((1, 1), (1, 0), (0, 1), (0, 0)):
        to_x = (sent_x if x else kept_x, 2 * y)
        to_y = (sent_y if y else kept_y, 2 * x)
        start = 0 if to_x[0] is not None else half
        stop = total if to_y[0] is not None else half
        if start < stop:
            jobs.append((x + 2 * y, start, stop, to_x, to_y))
    for block, *_ in jobs:
        for z in range(2):
            weight_copy(block + 4 * z).start()

    for at, (tile, index, piece, _) in enumerate(pieces):
        seg = segment_of(high, piece, tile_rows)
        alive = seg < live_ref[piece[1]]
        place = slice(at * size, (at + 1) * size)

        @pl.when(alive)
        def _():
            rows = grad_refs[tile][index, piece[2] : piece[2] + size, :].T
            rows_ref[:, place] = rows
            if keeps:
                up = up_ref[classes_ref[piece[1], seg]]
                rank_ref[:, place] = jnp.dot(up, rows, preferred_element_type=F32)

        @pl.when(jnp.logical_not(alive))
        def _():
            rows_ref[:, place] = jnp.zeros((rows_ref.shape[0], size), rows_ref.dtype)
            if keeps:
                rank_ref[:, place] = jnp.zeros((rank_ref.shape[0], size), F32)

    for block, start, stop, to_x, to_y in jobs:

        @pl.loop(0, 2)
        def _(z):
            weight_copy(block + 4 * z).wait()
            value = jnp.dot(
                weight_ref[block + 4 * z], rows_ref[:, start:stop], preferred_element_type=F32
            )
            if to_x[0] is not None:
                to_x[0][to_x[1] + z] = value[:, : half - start].astype(to_x[0].dtype)
            if to_y[0] is not None:
                to_y[0][to_y[1] + z] = value[:, half - start :].astype(to_y[0].dtype)


def product(scalars, grads, pieces, weight_blocks, up_tile, low_size, sends, keeps):
    blocks, width, depth = weight_blocks.shape
    tile_rows = grads[0].shape[1]
    rows = len(pieces) * pieces[0][3]
    half = rows // 2
    if rows > 128 and half % 128:
        half = half // 128 * 128 + 128
    outs = []
    for wanted, dtype in ((sends, BF16), (keeps, F32)):
        if wanted:
            outs += [
                jax.ShapeDtypeStruct((blocks // 2, width, n), dtype) for n in (half, rows - half)
            ]
    if keeps:
        outs.append(jax.ShapeDtypeStruct((up_tile.shape[1], rows), F32))
    share = (sends + keeps) / 2
    return pl.pallas_call(
        functools.partial(
            product_body, low_size, tile_rows, pieces, len(grads), half, sends, keeps
        ),
        in_specs=[SMEM] * 3
        + [VMEM] * len(grads)
        + [pl.BlockSpec(memory_space=pl.ANY)]
        + [VMEM] * keeps,
        out_specs=[VMEM] * len(outs),
        out_shape=outs,
        scratch_shapes=[
            pltpu.VMEM((depth, rows), BF16),
            pltpu.VMEM(weight_blocks.shape, BF16),
            pltpu.SemaphoreType.DMA((blocks,)),
        ],
        compiler_params=pltpu.CompilerParams(vmem_limit_bytes=32 * 2**20),
        cost_estimate=pl.CostEstimate(
            flops=int(2 * share * blocks * rows * width * depth),
            bytes_accessed=int(share * (2 * blocks * width * depth + 3 * blocks * rows * width)),
            transcendentals=0,
        ),
    )(*scalars, *grads, weight_blocks, *([up_tile] * keeps))


def after(value, *others):
    return lax.optimization_barrier((value, *others))[0]


def up_body(low_size, tile_rows, pieces, tiles, *refs):
    pos_ref, classes_ref, live_ref = refs[:3]
    grad_refs = refs[3 : 3 + tiles]
    hidden_refs = refs[3 + tiles : -2]
    out_ref, total_ref = refs[-2:]
    high = pos_ref[0] // low_size
    total_ref[...] = jnp.zeros_like(total_ref)
    for tile, index, piece, size in pieces:
        k, m, offset = piece
        seg = segment_of(high, piece, tile_rows)

        @pl.when(seg < live_ref[m])
        def _():
            total_ref[classes_ref[m, seg]] += lax.dot_general(
                hidden_refs[k][m, offset : offset + size, :],
                grad_refs[tile][index, offset : offset + size, :],
                TN,
                preferred_element_type=F32,
            )

    out_ref[...] = total_ref[...].astype(BF16)


def shards(
    output_gradient,
    forward_input,
    saved_rank_outputs,
    projection_weight,
    adapter_down_maps,
    adapter_up_maps,
    segment_adapter_class,
    live_segment_table,
):
    grad_tile = output_gradient[0, 0]
    micro_count, tile_rows, tile_cols = grad_tile.shape
    up_tile = adapter_up_maps[0, 0]
    class_count, rank_part, _ = up_tile.shape
    rank, portion = adapter_down_maps.shape[2:]
    tiles = lax.axis_size("tensor")
    low_size = min(tiles, 8)
    high_size = tiles // low_size
    position = lax.axis_index("tensor")
    high = position // low_size
    weight_blocks = projection_weight[0, 0].reshape(low_size, portion, tile_cols)
    position, classes, live = lax.optimization_barrier(
        (position.astype(jnp.int32)[None], segment_adapter_class[0] + 0, live_segment_table[0] + 0)
    )
    scalars = position, classes, live
    position = position[0]
    size = min(SEG, tile_rows)
    offsets = range(0, tile_rows, size)

    def send_rows(source, m):
        return [partner(source[m], k * low_size)[None] for k in range(1, high_size)]

    def pieces_of(m):
        return [(k - 1, 0, (k, m, o), size) for k in range(1, high_size) for o in offsets]

    own_pieces = [(0, m, (0, m, o), size) for m in range(micro_count) for o in offsets]

    def produce(grads, pieces, sends, keeps):
        return product(scalars, grads, pieces, weight_blocks, up_tile, low_size, sends, keeps)

    hidden = saved_rank_outputs[0]

    def spread_hidden(hidden, bit):
        got = partner(hidden, 1 << bit)
        upper = (position >> bit) & 1 == 1
        return jnp.where(
            upper, jnp.concatenate([got, hidden], 1), jnp.concatenate([hidden, got], 1)
        )

    def second_part(kept, got):
        return (kept[2:] + got[2:]).astype(BF16)

    got0 = send_rows(grad_tile, 0)
    hidden = spread_hidden(hidden, 0)
    sent_x, sent_y = produce([grad_tile], own_pieces, True, False)
    first_x, first_y = partner(sent_x, 1), partner(sent_y, 2)
    own_kept = produce([after(grad_tile, sent_x, sent_y)], own_pieces, False, True)
    kept_x, kept_y, part = own_kept
    parts = [part]
    chunks = [([grad_tile], own_pieces), (got0, pieces_of(0))]
    rows0 = after(got0[0], part), *got0[1:]
    c_sent_x, c_sent_y, c_kept_x, c_kept_y, part = produce(list(rows0), pieces_of(0), True, True)
    parts.append(part)
    got1 = send_rows(after(grad_tile, *got0), 1)

    c_sent_x, c_sent_y = after(c_sent_x, first_x, first_y), after(c_sent_y, first_x, first_y)
    c_first_x, c_first_y = partner(c_sent_x, 1), partner(c_sent_y, 2)
    second_x = partner(second_part(kept_x, first_x), 2)
    second_y = partner(second_part(kept_y, first_y), 1)
    hidden = spread_hidden(after(hidden, first_x, first_y), 1)
    own_sums = (kept_x, first_x, second_x), (kept_y, first_y, second_y)

    chunks.append((got1, pieces_of(1)))
    order = [piece for _, pieces in chunks for _, _, piece, _ in pieces]
    rows1 = after(got1[0], part), *got1[1:]
    d_sent_x, d_sent_y, d_kept_x, d_kept_y, part = produce(list(rows1), pieces_of(1), True, True)
    parts.append(part)
    slot = c_first_x, c_first_y, second_x, second_y
    own_rank = jnp.concatenate(parts, 1)
    own_rank = after(own_rank, *slot)
    own_rank = own_rank + partner(own_rank, 1)
    d_first_x = partner(after(d_sent_x, *slot), 1)
    d_first_y = partner(after(d_sent_y, *slot), 2)
    c_second_x = partner(second_part(c_kept_x, c_first_x), 2)
    c_second_y = partner(second_part(c_kept_y, c_first_y), 1)
    c_sums = (c_kept_x, c_first_x, c_second_x), (c_kept_y, c_first_y, c_second_y)

    def third_part(sums):
        return [(kept[1] + got[1] + second[1]).astype(BF16) for kept, got, second in sums]

    own_last = [relay(third, 4) for third in third_part(own_sums)]
    hidden = spread_hidden(after(hidden, *slot), 2)
    own_rank = own_rank + partner(own_rank, 4)
    hiddens = []
    for k in range(high_size):
        wanted = lax.dynamic_slice_in_dim(hidden, (high ^ k) * rank_part, rank_part, 2)
        hiddens.append(partner(wanted, k * low_size) if k > 0 else wanted)

    slot = d_first_x, d_first_y, *own_last
    own_rank = after(own_rank, *slot)
    own_rank = (own_rank + partner(own_rank, 2)).astype(BF16)
    d_second_x = partner(second_part(d_kept_x, after(d_first_x, *slot)), 2)
    d_second_y = partner(second_part(d_kept_y, after(d_first_y, *slot)), 1)
    d_sums = (d_kept_x, d_first_x, d_second_x), (d_kept_y, d_first_y, d_second_y)
    c_last = [relay(third, 4) for third in third_part(c_sums)]
    ranks = [own_rank] + [partner(own_rank, j * low_size) for j in range(1, high_size)]

    slot = d_second_x, d_second_y, *c_last
    d_last = [relay(third, 4) for third in third_part(d_sums)]
    sums = own_sums + c_sums + d_sums
    got_last = own_last + c_last + d_last

    all_grads, all_pieces = [], []
    for grads, pieces in chunks:
        all_pieces += [(tile + len(all_grads), index, piece, size) for tile, index, piece, size in pieces]
        all_grads += grads
    up_map_gradient = pl.pallas_call(
        functools.partial(up_body, low_size, tile_rows, all_pieces, len(all_grads)),
        in_specs=[SMEM] * 3 + [VMEM] * (len(all_grads) + high_size),
        out_specs=VMEM,
        out_shape=jax.ShapeDtypeStruct(up_tile.shape, BF16),
        scratch_shapes=[pltpu.VMEM(up_tile.shape, F32)],
        cost_estimate=pl.CostEstimate(
            flops=2 * len(order) * size * rank_part * tile_cols,
            bytes_accessed=2 * len(order) * size * tile_cols,
            transcendentals=0,
        ),
    )(*scalars, *all_grads, *hiddens)

    def columns_of(j, piece):
        k, m, offset = piece
        at = order.index((k ^ j, m, offset))
        return slice(at * size, (at + 1) * size)

    down_parts = adapter_down_maps[0].reshape(class_count, high_size, rank_part, portion)

    def adapter_kernel(pos_ref, classes_ref, live_ref, down_ref, *refs):
        rank_refs, sum_refs = refs[:high_size], refs[high_size:-2]
        out_ref, total_ref = refs[-2:]
        own = pos_ref[0] // low_size
        start = 0
        for g in range(len(sums)):
            kept_ref, got_ref, second_ref = sum_refs[3 * g : 3 * g + 3]
            count = kept_ref.shape[2]
            total_ref[:, start : start + count] = (
                kept_ref[0] + got_ref[0].astype(F32) + second_ref[0].astype(F32)
            )
            start += count
        for at, piece in enumerate(order):
            seg = segment_of(own, piece, tile_rows)
            rows = slice(at * size, (at + 1) * size)
            adapter = total_ref[:, rows]
            for j in range(high_size):
                adapter = adapter + lax.dot_general(
                    down_ref[classes_ref[piece[1], seg], own ^ j],
                    rank_refs[j][:, columns_of(j, piece)],
                    TN,
                    preferred_element_type=F32,
                )
            out_ref[:, rows] = adapter.astype(BF16)

    rows_total = len(order) * size
    kept = pl.pallas_call(
        adapter_kernel,
        grid=(1,),
        in_specs=[SMEM] * 3
        + [pl.BlockSpec(a.shape, lambda _, n=a.ndim: (0,) * n) for a in [down_parts, *ranks]]
        + [pl.BlockSpec((1,) + a.shape[1:], lambda _: (0, 0, 0)) for three in sums for a in three],
        out_specs=pl.BlockSpec((portion, rows_total), lambda _: (0, 0)),
        out_shape=jax.ShapeDtypeStruct((portion, rows_total), BF16),
        scratch_shapes=[pltpu.VMEM((portion, rows_total), F32)],
        compiler_params=pltpu.CompilerParams(vmem_limit_bytes=40 * 2**20),
        cost_estimate=pl.CostEstimate(
            flops=2 * rows_total * rank * portion,
            bytes_accessed=10 * rows_total * portion,
            transcendentals=0,
        ),
    )(*scalars, down_parts, *ranks, *[a for three in sums for a in three])
    kept = relay(kept, 0)

    def finish_kernel(pos_ref, kept_ref, *refs):
        *got_refs, out_ref, total_ref = refs
        own = pos_ref[0] // low_size
        start = 0
        for got_ref in got_refs:
            count = got_ref.shape[1]
            total_ref[:, start : start + count] = (
                kept_ref[:, start : start + count].astype(F32) + got_ref[...].astype(F32)
            ).astype(BF16)
            start += count
        for at, (k, m, offset) in enumerate(order):
            base = pl.multiple_of((own ^ k) * tile_rows + offset, size)
            out_ref[m, pl.ds(base, size), :] = total_ref[:, at * size : (at + 1) * size].T

    grad_prev = pl.pallas_call(
        finish_kernel,
        in_specs=[SMEM] + [VMEM] * (1 + len(got_last)),
        out_specs=VMEM,
        out_shape=jax.ShapeDtypeStruct((micro_count, high_size * tile_rows, portion), BF16),
        scratch_shapes=[pltpu.VMEM((portion, rows_total), BF16)],
    )(scalars[0], kept, *got_last)

    def down_kernel(pos_ref, classes_ref, live_ref, inputs_ref, *refs):
        rank_refs, out_ref, total_ref = refs[:-2], refs[-2], refs[-1]
        own = pos_ref[0] // low_size
        total_ref[...] = jnp.zeros_like(total_ref)
        for piece in order:
            k, m, offset = piece
            seg = segment_of(own, piece, tile_rows)

            @pl.when(seg < live_ref[m])
            def _():
                base = pl.multiple_of((own ^ k) * tile_rows + offset, size)
                rows = inputs_ref[m, pl.ds(base, size), :]
                for j in range(high_size):
                    total_ref[classes_ref[m, seg], own ^ j] += jnp.dot(
                        rank_refs[j][:, columns_of(j, piece)], rows, preferred_element_type=F32
                    )

        out_ref[...] = total_ref[...].astype(BF16)

    down_map_gradient = pl.pallas_call(
        down_kernel,
        in_specs=[SMEM] * 3 + [VMEM] * (1 + high_size),
        out_specs=VMEM,
        out_shape=jax.ShapeDtypeStruct(down_parts.shape, BF16),
        scratch_shapes=[pltpu.VMEM(down_parts.shape, F32)],
        cost_estimate=pl.CostEstimate(
            flops=2 * rows_total * rank * portion,
            bytes_accessed=2 * rows_total * portion,
            transcendentals=0,
        ),
    )(*scalars, forward_input[0], *ranks)

    return (
        grad_prev[None],
        down_map_gradient.reshape(1, class_count, rank, portion),
        up_map_gradient[None, None],
    )


def solution(mesh):
    in_specs = (
        P("pipe", "tensor", None, None, None),
        P("pipe", None, None, "tensor"),
        P("pipe", None, "tensor", None),
        P("pipe", "tensor", None, None),
        P("pipe", None, None, "tensor"),
        P("pipe", "tensor", None, None, None),
        P("pipe", None, None),
        P("pipe", None),
    )
    out_specs = (
        P("pipe", None, None, "tensor"),
        P("pipe", None, None, "tensor"),
        P("pipe", "tensor", None, None, None),
    )
    return jax.shard_map(shards, mesh=mesh, in_specs=in_specs, out_specs=out_specs, check_vma=False)
```

```python
import functools

import jax
import jax.numpy as jnp
from jax import lax
from jax.experimental import pallas as pl
from jax.experimental.pallas import tpu as pltpu
from jax.sharding import PartitionSpec as P

SEG = 128
BF16 = jnp.bfloat16
F32 = jnp.float32
SMEM = pl.BlockSpec(memory_space=pltpu.SMEM)
VMEM = pl.BlockSpec(memory_space=pltpu.VMEM)
TN = (((0,), (0,)), ((), ()))
QUICK = pl.CostEstimate(flops=1000, bytes_accessed=1000, transcendentals=0)
LONG = pl.CostEstimate(flops=4 * 10**10, bytes_accessed=1000, transcendentals=0)


def partner(value, mask):
    pairs = [(source, source ^ mask) for source in range(lax.axis_size("tensor"))]
    return lax.ppermute(value, "tensor", pairs)


def relay(value, mask):
    sections, tiles = lax.axis_size("pipe"), lax.axis_size("tensor")
    pairs = [
        (p * tiles + t, (p - 1) % sections * tiles + (t ^ mask))
        for p in range(sections)
        for t in range(tiles)
    ]
    return lax.ppermute(value, ("pipe", "tensor"), pairs)


def segment_of(high, piece, tile_rows):
    k, _, offset = piece
    return ((high ^ k) * tile_rows + offset) // SEG


def product_body(low_size, tile_rows, pieces, tiles, half, turns, sends, keeps, *refs):
    pos_ref, classes_ref, live_ref = refs[:3]
    grad_refs = refs[3 : 3 + tiles]
    weight_hbm = refs[3 + tiles]
    rows_ref, weight_ref, sems = refs[-3:]
    rest = list(refs[4 + tiles : -3])
    up_ref = rest.pop(0) if keeps else None
    sent_x, sent_y = (rest.pop(0), rest.pop(0)) if sends else (None, None)
    kept_x, kept_y, rank_ref = rest if keeps else (None, None, None)
    low, high = pos_ref[0] % low_size, pos_ref[0] // low_size
    size = pieces[0][3]
    total = rows_ref.shape[1]

    def weight_copy(block):
        return pltpu.make_async_copy(
            weight_hbm.at[block ^ low], weight_ref.at[block], sems.at[block]
        )

    jobs = []
    for x, y in ((1, 1), (1, 0), (0, 1), (0, 0)):
        to_x = (sent_x if x else kept_x, 2 * y, 1)
        to_y = (sent_y if y else kept_y, *((x, 2) if turns else (2 * x, 1)))
        start = 0 if to_x[0] is not None else half
        stop = total if to_y[0] is not None else half
        if start < stop:
            jobs.append((x + 2 * y, start, stop, to_x, to_y))
    for block, *_ in jobs:
        for z in range(2):
            weight_copy(block + 4 * z).start()

    for at, (tile, index, piece, _) in enumerate(pieces):
        seg = segment_of(high, piece, tile_rows)
        alive = seg < live_ref[piece[1]]
        place = slice(at * size, (at + 1) * size)

        @pl.when(alive)
        def _():
            rows = grad_refs[tile][index, piece[2] : piece[2] + size, :].T
            rows_ref[:, place] = rows
            if keeps:
                up = up_ref[classes_ref[piece[1], seg]]
                rank_ref[:, place] = jnp.dot(up, rows, preferred_element_type=F32)

        @pl.when(jnp.logical_not(alive))
        def _():
            rows_ref[:, place] = jnp.zeros((rows_ref.shape[0], size), rows_ref.dtype)
            if keeps:
                rank_ref[:, place] = jnp.zeros((rank_ref.shape[0], size), F32)

    for block, start, stop, to_x, to_y in jobs:

        @pl.loop(0, 2)
        def _(z):
            weight_copy(block + 4 * z).wait()
            value = jnp.dot(
                weight_ref[block + 4 * z], rows_ref[:, start:stop], preferred_element_type=F32
            )
            if to_x[0] is not None:
                to_x[0][to_x[1] + to_x[2] * z] = value[:, : half - start].astype(to_x[0].dtype)
            if to_y[0] is not None:
                to_y[0][to_y[1] + to_y[2] * z] = value[:, half - start :].astype(to_y[0].dtype)


def product(scalars, grads, pieces, weight_blocks, up_tile, low_size, turns, sends, keeps):
    blocks, width, depth = weight_blocks.shape
    tile_rows = grads[0].shape[1]
    rows = len(pieces) * pieces[0][3]
    half = rows // 2
    if rows > 128 and half % 128:
        half = half // 128 * 128 + 128
    outs = []
    for wanted, dtype in ((sends, BF16), (keeps, F32)):
        if wanted:
            outs += [
                jax.ShapeDtypeStruct((blocks // 2, width, n), dtype) for n in (half, rows - half)
            ]
    if keeps:
        outs.append(jax.ShapeDtypeStruct((up_tile.shape[1], rows), F32))
    return pl.pallas_call(
        functools.partial(
            product_body, low_size, tile_rows, pieces, len(grads), half, turns, sends, keeps
        ),
        in_specs=[SMEM] * 3
        + [VMEM] * len(grads)
        + [pl.BlockSpec(memory_space=pl.ANY)]
        + [VMEM] * keeps,
        out_specs=[VMEM] * len(outs),
        out_shape=outs,
        scratch_shapes=[
            pltpu.VMEM((depth, rows), BF16),
            pltpu.VMEM(weight_blocks.shape, BF16),
            pltpu.SemaphoreType.DMA((blocks,)),
        ],
        compiler_params=pltpu.CompilerParams(vmem_limit_bytes=56 * 2**20),
        cost_estimate=LONG if keeps else QUICK,
    )(*scalars, *grads, weight_blocks, *([up_tile] * keeps))


def after(value, *others):
    return lax.optimization_barrier((value, *others))[0]


def up_body(low_size, tile_rows, pieces, tiles, *refs):
    pos_ref, classes_ref, live_ref = refs[:3]
    grad_refs = refs[3 : 3 + tiles]
    hidden_refs = refs[3 + tiles : -2]
    out_ref, total_ref = refs[-2:]
    high = pos_ref[0] // low_size
    total_ref[...] = jnp.zeros_like(total_ref)
    for tile, index, piece, size in pieces:
        k, m, offset = piece
        seg = segment_of(high, piece, tile_rows)

        @pl.when(seg < live_ref[m])
        def _():
            total_ref[classes_ref[m, seg]] += lax.dot_general(
                hidden_refs[k][m, offset : offset + size, :],
                grad_refs[tile][index, offset : offset + size, :],
                TN,
                preferred_element_type=F32,
            )

    out_ref[...] = total_ref[...].astype(BF16)


def shards(
    output_gradient,
    forward_input,
    saved_rank_outputs,
    projection_weight,
    adapter_down_maps,
    adapter_up_maps,
    segment_adapter_class,
    live_segment_table,
):
    grad_tile = output_gradient[0, 0]
    micro_count, tile_rows, tile_cols = grad_tile.shape
    up_tile = adapter_up_maps[0, 0]
    class_count, rank_part, _ = up_tile.shape
    rank, portion = adapter_down_maps.shape[2:]
    tiles = lax.axis_size("tensor")
    low_size = min(tiles, 8)
    high_size = tiles // low_size
    position = lax.axis_index("tensor")
    high = position // low_size
    weight_blocks = projection_weight[0, 0].reshape(low_size, portion, tile_cols)
    position, classes, live = lax.optimization_barrier(
        (position.astype(jnp.int32)[None], segment_adapter_class[0] + 0, live_segment_table[0] + 0)
    )
    scalars = position, classes, live
    position = position[0]
    size = min(SEG, tile_rows)
    offsets = range(0, tile_rows, size)

    def send_rows(source, m):
        return [partner(source[m], k * low_size)[None] for k in range(1, high_size)]

    def pieces_of(m):
        return [(k - 1, 0, (k, m, o), size) for k in range(1, high_size) for o in offsets]

    own_pieces = [(0, m, (0, m, o), size) for m in range(micro_count) for o in offsets]

    def produce(grads, pieces, turns, sends, keeps):
        return product(
            scalars, grads, pieces, weight_blocks, up_tile, low_size, turns, sends, keeps
        )

    hidden = saved_rank_outputs[0]

    def spread_hidden(hidden, bit):
        got = partner(hidden, 1 << bit)
        upper = (position >> bit) & 1 == 1
        return jnp.where(
            upper, jnp.concatenate([got, hidden], 1), jnp.concatenate([hidden, got], 1)
        )

    def second_part(kept, got):
        return (kept[2:] + got[2:]).astype(BF16)

    first_rows, hidden = lax.optimization_barrier((grad_tile[0], hidden))
    got0 = [partner(first_rows, k * low_size)[None] for k in range(1, high_size)]
    hidden = spread_hidden(hidden, 0)
    own_grads = after(grad_tile, first_rows)
    sent_x, sent_y = produce([own_grads], own_pieces, False, True, False)
    first_x, first_y = partner(sent_x, 1), partner(sent_y, 2)
    rows0 = after(got0[0], sent_x, sent_y), *got0[1:]
    c_sent_x, c_sent_y, c_kept_x, c_kept_y, part = produce(
        list(rows0), pieces_of(0), False, True, True
    )
    parts = [part]
    own_kept = produce([after(grad_tile, part)], own_pieces, False, False, True)
    kept_x, kept_y, part = own_kept
    parts.insert(0, part)
    got1 = send_rows(after(grad_tile, *got0), 1)

    slot = first_x, first_y
    c_first_x, c_first_y = partner(after(c_sent_x, *slot), 1), partner(after(c_sent_y, *slot), 2)
    second_x = partner(second_part(kept_x, first_x), 2)
    second_y = partner(second_part(kept_y, first_y), 1)
    hidden = spread_hidden(after(hidden, *slot), 1)
    own_sums = (kept_x, first_x, second_x), (kept_y, first_y, second_y)

    chunks = [([grad_tile], own_pieces), (got0, pieces_of(0)), (got1, pieces_of(1))]
    order = [piece for _, pieces in chunks for _, _, piece, _ in pieces]
    rows1 = after(got1[0], part), *got1[1:]
    d_sent_x, d_sent_y, d_kept_x, d_kept_y, part = produce(
        list(rows1), pieces_of(1), True, True, True
    )
    parts.append(part)
    slot = c_first_x, c_first_y, second_x, second_y, hidden
    own_rank = after(jnp.concatenate(parts, 1), *slot)
    own_rank = own_rank + partner(own_rank, 1)
    d_first_x = partner(after(d_sent_x, *slot), 1)
    d_first_y = partner(after(d_sent_y, *slot), 2)
    c_second_x = partner(second_part(c_kept_x, c_first_x), 2)
    c_second_y = partner(second_part(c_kept_y, c_first_y), 1)
    c_sums = (c_kept_x, c_first_x, c_second_x), (c_kept_y, c_first_y, c_second_y)

    def third_part(three):
        kept, got, second = three
        return (kept[1] + got[1] + second[1]).astype(BF16)

    own_rank = own_rank + partner(own_rank, 4)
    own_last = [relay(after(third_part(three), own_rank), 4) for three in own_sums]
    hidden = spread_hidden(hidden, 2)

    slot = d_first_x, d_first_y, c_second_x, c_second_y, *own_last, own_rank, hidden
    own_rank = after(own_rank, *slot)
    own_rank = (own_rank + partner(own_rank, 2)).astype(BF16)
    d_second_x = partner(second_part(d_kept_x, after(d_first_x, *slot)), 2)
    d_second_y = partner(second_part(d_kept_y, after(d_first_y, *slot)), 4)
    d_sums = (d_kept_x, d_first_x, d_second_x), (d_kept_y, d_first_y, d_second_y)
    c_last = [relay(after(third_part(three), *slot), 4) for three in c_sums]
    hiddens = []
    for k in range(high_size):
        wanted = lax.dynamic_slice_in_dim(hidden, (high ^ k) * rank_part, rank_part, 2)
        hiddens.append(partner(wanted, k * low_size) if k > 0 else wanted)
    ranks = [own_rank] + [partner(own_rank, j * low_size) for j in range(1, high_size)]

    d_last = [
        relay(third_part((d_kept_x, d_first_x, after(d_second_x, c_last[1]))), 4),
        relay(third_part((d_kept_y, d_first_y, after(d_second_y, c_last[1]))), 1),
    ]
    ranks[-1] = after(ranks[-1], *c_last, *hiddens)
    sums = own_sums + c_sums + d_sums
    got_last = own_last + c_last + d_last

    all_grads, all_pieces = [], []
    for grads, pieces in chunks:
        all_pieces += [(tile + len(all_grads), index, piece, size) for tile, index, piece, size in pieces]
        all_grads += grads
    up_map_gradient = pl.pallas_call(
        functools.partial(up_body, low_size, tile_rows, all_pieces, len(all_grads)),
        in_specs=[SMEM] * 3 + [VMEM] * (len(all_grads) + high_size),
        out_specs=VMEM,
        out_shape=jax.ShapeDtypeStruct(up_tile.shape, BF16),
        scratch_shapes=[pltpu.VMEM(up_tile.shape, F32)],
        cost_estimate=LONG,
    )(*scalars, *all_grads, *hiddens)

    def columns_of(j, piece):
        k, m, offset = piece
        at = order.index((k ^ j, m, offset))
        return slice(at * size, (at + 1) * size)

    down_parts = adapter_down_maps[0].reshape(class_count, high_size, rank_part, portion)

    def adapter_kernel(pos_ref, classes_ref, live_ref, down_ref, *refs):
        rank_refs, sum_refs = refs[:high_size], refs[high_size:-2]
        out_ref, total_ref = refs[-2:]
        own = pos_ref[0] // low_size
        start = 0
        for g in range(len(sums)):
            kept_ref, got_ref, second_ref = sum_refs[3 * g : 3 * g + 3]
            count = kept_ref.shape[2]
            total_ref[:, start : start + count] = (
                kept_ref[0] + got_ref[0].astype(F32) + second_ref[0].astype(F32)
            )
            start += count
        for at, piece in enumerate(order):
            seg = segment_of(own, piece, tile_rows)
            rows = slice(at * size, (at + 1) * size)
            adapter = total_ref[:, rows]
            for j in range(high_size):
                adapter = adapter + lax.dot_general(
                    down_ref[classes_ref[piece[1], seg], own ^ j],
                    rank_refs[j][:, columns_of(j, piece)],
                    TN,
                    preferred_element_type=F32,
                )
            out_ref[:, rows] = adapter.astype(BF16)

    rows_total = len(order) * size
    kept = pl.pallas_call(
        adapter_kernel,
        grid=(1,),
        in_specs=[SMEM] * 3
        + [pl.BlockSpec(a.shape, lambda _, n=a.ndim: (0,) * n) for a in [down_parts, *ranks]]
        + [pl.BlockSpec((1,) + a.shape[1:], lambda _: (0, 0, 0)) for three in sums for a in three],
        out_specs=pl.BlockSpec((portion, rows_total), lambda _: (0, 0)),
        out_shape=jax.ShapeDtypeStruct((portion, rows_total), BF16),
        scratch_shapes=[pltpu.VMEM((portion, rows_total), F32)],
        compiler_params=pltpu.CompilerParams(vmem_limit_bytes=40 * 2**20),
        cost_estimate=QUICK,
    )(*scalars, down_parts, *ranks, *[a for three in sums for a in three])
    kept = relay(kept, 0)

    def finish_kernel(pos_ref, kept_ref, *refs):
        *got_refs, out_ref, total_ref = refs
        own = pos_ref[0] // low_size
        start = 0
        for got_ref in got_refs:
            count = got_ref.shape[1]
            total_ref[:, start : start + count] = (
                kept_ref[:, start : start + count].astype(F32) + got_ref[...].astype(F32)
            ).astype(BF16)
            start += count
        for at, (k, m, offset) in enumerate(order):
            base = pl.multiple_of((own ^ k) * tile_rows + offset, size)
            out_ref[m, pl.ds(base, size), :] = total_ref[:, at * size : (at + 1) * size].T

    grad_prev = pl.pallas_call(
        finish_kernel,
        in_specs=[SMEM] + [VMEM] * (1 + len(got_last)),
        out_specs=VMEM,
        out_shape=jax.ShapeDtypeStruct((micro_count, high_size * tile_rows, portion), BF16),
        scratch_shapes=[pltpu.VMEM((portion, rows_total), BF16)],
    )(scalars[0], kept, *got_last)

    def down_kernel(pos_ref, classes_ref, live_ref, inputs_ref, *refs):
        rank_refs, out_ref, total_ref = refs[:-2], refs[-2], refs[-1]
        own = pos_ref[0] // low_size
        total_ref[...] = jnp.zeros_like(total_ref)
        for piece in order:
            k, m, offset = piece
            seg = segment_of(own, piece, tile_rows)

            @pl.when(seg < live_ref[m])
            def _():
                base = pl.multiple_of((own ^ k) * tile_rows + offset, size)
                rows = inputs_ref[m, pl.ds(base, size), :]
                for j in range(high_size):
                    total_ref[classes_ref[m, seg], own ^ j] += jnp.dot(
                        rank_refs[j][:, columns_of(j, piece)], rows, preferred_element_type=F32
                    )

        out_ref[...] = total_ref[...].astype(BF16)

    down_map_gradient = pl.pallas_call(
        down_kernel,
        in_specs=[SMEM] * 3 + [VMEM] * (1 + high_size),
        out_specs=VMEM,
        out_shape=jax.ShapeDtypeStruct(down_parts.shape, BF16),
        scratch_shapes=[pltpu.VMEM(down_parts.shape, F32)],
        cost_estimate=LONG,
    )(*scalars, forward_input[0], *ranks)

    return (
        grad_prev[None],
        down_map_gradient.reshape(1, class_count, rank, portion),
        up_map_gradient[None, None],
    )


def solution(mesh):
    in_specs = (
        P("pipe", "tensor", None, None, None),
        P("pipe", None, None, "tensor"),
        P("pipe", None, "tensor", None),
        P("pipe", "tensor", None, None),
        P("pipe", None, None, "tensor"),
        P("pipe", "tensor", None, None, None),
        P("pipe", None, None),
        P("pipe", None),
    )
    out_specs = (
        P("pipe", None, None, "tensor"),
        P("pipe", None, None, "tensor"),
        P("pipe", "tensor", None, None, None),
    )
    return jax.shard_map(shards, mesh=mesh, in_specs=in_specs, out_specs=out_specs, check_vma=False)
```

```python
import functools

import jax
import jax.numpy as jnp
from jax import lax
from jax.experimental import pallas as pl
from jax.experimental.pallas import tpu as pltpu
from jax.sharding import PartitionSpec as P

SEG = 128
BF16 = jnp.bfloat16
F32 = jnp.float32
SMEM = pl.BlockSpec(memory_space=pltpu.SMEM)
VMEM = pl.BlockSpec(memory_space=pltpu.VMEM)
TN = (((0,), (0,)), ((), ()))
QUICK = pl.CostEstimate(flops=1000, bytes_accessed=1000, transcendentals=0)
LONG = pl.CostEstimate(flops=4 * 10**10, bytes_accessed=1000, transcendentals=0)


def partner(value, mask):
    pairs = [(source, source ^ mask) for source in range(lax.axis_size("tensor"))]
    return lax.ppermute(value, "tensor", pairs)


def relay(value, mask):
    sections, tiles = lax.axis_size("pipe"), lax.axis_size("tensor")
    pairs = [
        (p * tiles + t, (p - 1) % sections * tiles + (t ^ mask))
        for p in range(sections)
        for t in range(tiles)
    ]
    return lax.ppermute(value, ("pipe", "tensor"), pairs)


def segment_of(high, piece, tile_rows):
    k, _, offset = piece
    return ((high ^ k) * tile_rows + offset) // SEG


def product_body(low_size, tile_rows, pieces, tiles, half, turns, sends, keeps, *refs):
    pos_ref, classes_ref, live_ref = refs[:3]
    grad_refs = refs[3 : 3 + tiles]
    weight_hbm = refs[3 + tiles]
    rows_ref, weight_ref, sems = refs[-3:]
    rest = list(refs[4 + tiles : -3])
    up_ref = rest.pop(0) if keeps else None
    sent_x, sent_y = (rest.pop(0), rest.pop(0)) if sends else (None, None)
    kept_x, kept_y, rank_ref = rest if keeps else (None, None, None)
    low, high = pos_ref[0] % low_size, pos_ref[0] // low_size
    size = pieces[0][3]
    total = rows_ref.shape[1]

    def weight_copy(block):
        return pltpu.make_async_copy(
            weight_hbm.at[block ^ low], weight_ref.at[block], sems.at[block]
        )

    jobs = []
    for x, y in ((1, 1), (1, 0), (0, 1), (0, 0)):
        to_x = (sent_x if x else kept_x, 2 * y, 1)
        to_y = (sent_y if y else kept_y, *((x, 2) if turns else (2 * x, 1)))
        start = 0 if to_x[0] is not None else half
        stop = total if to_y[0] is not None else half
        if start < stop:
            jobs.append((x + 2 * y, start, stop, to_x, to_y))
    for block, *_ in jobs:
        for z in range(2):
            weight_copy(block + 4 * z).start()

    for at, (tile, index, piece, _) in enumerate(pieces):
        seg = segment_of(high, piece, tile_rows)
        alive = seg < live_ref[piece[1]]
        place = slice(at * size, (at + 1) * size)

        @pl.when(alive)
        def _():
            rows = grad_refs[tile][index, piece[2] : piece[2] + size, :].T
            rows_ref[:, place] = rows
            if keeps:
                up = up_ref[classes_ref[piece[1], seg]]
                rank_ref[:, place] = jnp.dot(up, rows, preferred_element_type=F32)

        @pl.when(jnp.logical_not(alive))
        def _():
            rows_ref[:, place] = jnp.zeros((rows_ref.shape[0], size), rows_ref.dtype)
            if keeps:
                rank_ref[:, place] = jnp.zeros((rank_ref.shape[0], size), F32)

    for block, start, stop, to_x, to_y in jobs:

        @pl.loop(0, 2)
        def _(z):
            weight_copy(block + 4 * z).wait()
            value = jnp.dot(
                weight_ref[block + 4 * z], rows_ref[:, start:stop], preferred_element_type=F32
            )
            if to_x[0] is not None:
                to_x[0][to_x[1] + to_x[2] * z] = value[:, : half - start].astype(to_x[0].dtype)
            if to_y[0] is not None:
                to_y[0][to_y[1] + to_y[2] * z] = value[:, half - start :].astype(to_y[0].dtype)


def product(scalars, grads, pieces, weight_blocks, up_tile, low_size, turns, sends, keeps, cost):
    blocks, width, depth = weight_blocks.shape
    tile_rows = grads[0].shape[1]
    rows = len(pieces) * pieces[0][3]
    half = rows // 2
    if rows > 128 and half % 128:
        half = half // 128 * 128 + 128
    outs = []
    for wanted, dtype in ((sends, BF16), (keeps, F32)):
        if wanted:
            outs += [
                jax.ShapeDtypeStruct((blocks // 2, width, n), dtype) for n in (half, rows - half)
            ]
    if keeps:
        outs.append(jax.ShapeDtypeStruct((up_tile.shape[1], rows), F32))
    return pl.pallas_call(
        functools.partial(
            product_body, low_size, tile_rows, pieces, len(grads), half, turns, sends, keeps
        ),
        in_specs=[SMEM] * 3
        + [VMEM] * len(grads)
        + [pl.BlockSpec(memory_space=pltpu.HBM)]
        + [VMEM] * keeps,
        out_specs=[VMEM] * len(outs),
        out_shape=outs,
        scratch_shapes=[
            pltpu.VMEM((depth, rows), BF16),
            pltpu.VMEM(weight_blocks.shape, BF16),
            pltpu.SemaphoreType.DMA((blocks,)),
        ],
        compiler_params=pltpu.CompilerParams(vmem_limit_bytes=24 * 2**20),
        cost_estimate=cost,
    )(*in_hbm(*scalars), *grads, *in_hbm(weight_blocks), *in_hbm(*[up_tile] * keeps))


def in_hbm(*arrays):
    return [pltpu.with_memory_space_constraint(array, pltpu.HBM) for array in arrays]


def after(value, *others):
    return lax.optimization_barrier((value, *others))[0]


def halve_kernel(*refs):
    ways = len(refs) // 4
    for way in range(ways):
        kept_ref, got_ref, sent_ref, rest_ref = refs[way::ways]
        half = kept_ref.shape[0] // 2
        sent_ref[...] = (kept_ref[half:] + got_ref[half:].astype(F32)).astype(BF16)
        rest_ref[...] = kept_ref[:half] + got_ref[:half].astype(F32)


def halve(kept, got):
    shapes = [(k.shape[0] // 2,) + k.shape[1:] for k in kept]
    outs = pl.pallas_call(
        halve_kernel,
        in_specs=[VMEM] * (2 * len(kept)),
        out_specs=[VMEM] * (2 * len(kept)),
        out_shape=[jax.ShapeDtypeStruct(s, dtype) for dtype in (BF16, F32) for s in shapes],
        compiler_params=pltpu.CompilerParams(vmem_limit_bytes=24 * 2**20),
        cost_estimate=QUICK,
    )(*kept, *got)
    return outs[: len(kept)], outs[len(kept) :]


def up_body(low_size, tile_rows, pieces, tiles, *refs):
    pos_ref, classes_ref, live_ref = refs[:3]
    grad_refs = refs[3 : 3 + tiles]
    hidden_refs = refs[3 + tiles : -2]
    out_ref, total_ref = refs[-2:]
    high = pos_ref[0] // low_size
    total_ref[...] = jnp.zeros_like(total_ref)
    for tile, index, piece, size in pieces:
        k, m, offset = piece
        seg = segment_of(high, piece, tile_rows)

        @pl.when(seg < live_ref[m])
        def _():
            total_ref[classes_ref[m, seg]] += lax.dot_general(
                hidden_refs[k][m, offset : offset + size, :],
                grad_refs[tile][index, offset : offset + size, :],
                TN,
                preferred_element_type=F32,
            )

    out_ref[...] = total_ref[...].astype(BF16)


def shards(
    output_gradient,
    forward_input,
    saved_rank_outputs,
    projection_weight,
    adapter_down_maps,
    adapter_up_maps,
    segment_adapter_class,
    live_segment_table,
):
    grad_tile = output_gradient[0, 0]
    micro_count, tile_rows, tile_cols = grad_tile.shape
    up_tile = adapter_up_maps[0, 0]
    class_count, rank_part, _ = up_tile.shape
    rank, portion = adapter_down_maps.shape[2:]
    tiles = lax.axis_size("tensor")
    low_size = min(tiles, 8)
    high_size = tiles // low_size
    position = lax.axis_index("tensor")
    high = position // low_size
    weight_blocks = projection_weight[0, 0].reshape(low_size, portion, tile_cols)
    position, classes, live = lax.optimization_barrier(
        (position.astype(jnp.int32)[None], segment_adapter_class[0] + 0, live_segment_table[0] + 0)
    )
    scalars = position, classes, live
    position = position[0]
    size = min(SEG, tile_rows)
    offsets = range(0, tile_rows, size)

    def send_rows(source, m):
        return [partner(source[m], k * low_size)[None] for k in range(1, high_size)]

    def pieces_of(m):
        return [(k - 1, 0, (k, m, o), size) for k in range(1, high_size) for o in offsets]

    own_pieces = [(0, m, (0, m, o), size) for m in range(micro_count) for o in offsets]

    def produce(grads, pieces, turns, sends, keeps, cost):
        return product(
            scalars, grads, pieces, weight_blocks, up_tile, low_size, turns, sends, keeps, cost
        )

    hidden = saved_rank_outputs[0]

    def spread_hidden(hidden, bit):
        got = partner(hidden, 1 << bit)
        upper = (position >> bit) & 1 == 1
        return jnp.where(
            upper, jnp.concatenate([got, hidden], 1), jnp.concatenate([hidden, got], 1)
        )

    first_rows = lax.optimization_barrier(grad_tile[0])
    got0 = [partner(first_rows, k * low_size)[None] for k in range(1, high_size)]
    (own_grads,) = in_hbm(after(grad_tile, first_rows))
    sent_x, sent_y = produce([own_grads], own_pieces, False, True, False, QUICK)
    first_x, first_y = partner(sent_x, 1), partner(sent_y, 2)
    hidden = spread_hidden(after(hidden, sent_x, sent_y), 0)
    rows0 = after(got0[0], sent_x, sent_y), *got0[1:]
    c_sent_x, c_sent_y, c_kept_x, c_kept_y, part = produce(
        list(rows0), pieces_of(0), False, True, True, LONG
    )
    parts = [part]
    (own_grads,) = in_hbm(after(grad_tile, part))
    kept_x, kept_y, part = produce([own_grads], own_pieces, False, False, True, LONG)
    parts.insert(0, part)
    got1 = send_rows(after(grad_tile, *got0), 1)

    (sent_x, sent_y), (kept_x, kept_y) = halve((kept_x, kept_y), (first_x, first_y))
    second_x, second_y = partner(sent_x, 2), partner(sent_y, 1)
    c_first_x = partner(after(c_sent_x, sent_x, sent_y), 1)
    c_first_y = partner(after(c_sent_y, sent_x, sent_y), 2)
    hidden = spread_hidden(after(hidden, sent_x, sent_y), 1)
    own_sums = (kept_x, second_x), (kept_y, second_y)

    def third_part(two):
        kept, second = two
        return (kept[1] + second[1]).astype(BF16)

    chunks = [([grad_tile], own_pieces), (got0, pieces_of(0)), (got1, pieces_of(1))]
    order = [piece for _, pieces in chunks for _, _, piece, _ in pieces]
    rows1 = after(got1[0], part), *got1[1:]
    d_sent_x, d_sent_y, d_kept_x, d_kept_y, part = produce(
        list(rows1), pieces_of(1), True, True, True, LONG
    )
    parts.append(part)
    own_last = [relay(third_part(two), 4) for two in own_sums]
    slot = c_first_x, c_first_y, second_x, second_y
    own_rank = after(jnp.concatenate(parts, 1), *slot)
    own_rank = own_rank + partner(own_rank, 1)
    d_first_x = partner(after(d_sent_x, *slot), 1)
    d_first_y = partner(after(d_sent_y, *slot), 2)
    (c_sent_x, c_sent_y), c_kept = halve((c_kept_x, c_kept_y), (c_first_x, c_first_y))
    c_second_x, c_second_y = partner(c_sent_x, 2), partner(c_sent_y, 1)
    c_sums = (c_kept[0], c_second_x), (c_kept[1], c_second_y)
    own_rank = own_rank + partner(after(own_rank, *own_last), 4)
    hidden = spread_hidden(after(hidden, own_rank), 2)

    slot = d_first_x, d_first_y, c_second_x, c_second_y, own_rank
    own_rank = after(own_rank, *slot)
    own_rank = (own_rank + partner(own_rank, 2)).astype(BF16)
    (d_sent_x, d_sent_y), d_kept = halve(
        (d_kept_x, d_kept_y), (after(d_first_x, *slot), after(d_first_y, *slot))
    )
    d_second_x, d_second_y = partner(d_sent_x, 2), partner(d_sent_y, 4)
    d_sums = (d_kept[0], d_second_x), (d_kept[1], d_second_y)
    c_last = [relay(after(third_part(two), *slot), 4) for two in c_sums]
    ranks = [own_rank] + [partner(own_rank, j * low_size) for j in range(1, high_size)]
    hiddens = []
    for k in range(high_size):
        wanted = lax.dynamic_slice_in_dim(hidden, (high ^ k) * rank_part, rank_part, 2)
        wanted = after(wanted, ranks[-1])
        hiddens.append(partner(wanted, k * low_size) if k > 0 else wanted)

    all_grads, all_pieces = [], []
    for grads, pieces in chunks:
        all_pieces += [(tile + len(all_grads), index, piece, size) for tile, index, piece, size in pieces]
        all_grads += grads
    up_map_gradient = pl.pallas_call(
        functools.partial(up_body, low_size, tile_rows, all_pieces, len(all_grads)),
        in_specs=[SMEM] * 3 + [VMEM] * (len(all_grads) + high_size),
        out_specs=VMEM,
        out_shape=jax.ShapeDtypeStruct(up_tile.shape, BF16),
        scratch_shapes=[pltpu.VMEM(up_tile.shape, F32)],
        cost_estimate=LONG,
    )(*in_hbm(*scalars), *all_grads, *hiddens)

    def columns_of(j, piece):
        k, m, offset = piece
        at = order.index((k ^ j, m, offset))
        return slice(at * size, (at + 1) * size)

    down_parts = adapter_down_maps[0].reshape(class_count, high_size, rank_part, portion)

    def adapter_kernel(first, with_last, groups, *refs):
        pos_ref, classes_ref, _, down_ref = refs[:4]
        rank_refs = refs[4 : 4 + high_size]
        sum_refs = refs[4 + high_size : 4 + high_size + 2 * groups]
        *last_refs, out_ref, total_ref = refs[4 + high_size + 2 * groups :]
        own = pos_ref[0] // low_size
        start = 0
        for g in range(groups):
            kept_ref, second_ref = sum_refs[2 * g : 2 * g + 2]
            count = kept_ref.shape[2]
            total_ref[:, start : start + count] = kept_ref[0] + second_ref[0].astype(F32)
            if with_last:
                last_refs[g][...] = (kept_ref[1] + second_ref[1].astype(F32)).astype(BF16)
            start += count
        for at in range(start // size):
            piece = order[first + at]
            seg = segment_of(own, piece, tile_rows)
            rows = slice(at * size, (at + 1) * size)
            adapter = total_ref[:, rows]
            for j in range(high_size):
                adapter = adapter + lax.dot_general(
                    down_ref[classes_ref[piece[1], seg], own ^ j],
                    rank_refs[j][:, columns_of(j, piece)],
                    TN,
                    preferred_element_type=F32,
                )
            out_ref[:, rows] = adapter.astype(BF16)

    def with_adapter(sums, first, with_last):
        counts = [kept.shape[2] for kept, _ in sums]
        shapes = [(portion, n) for n in counts] * with_last + [(portion, sum(counts))]
        outs = pl.pallas_call(
            functools.partial(adapter_kernel, first, with_last, len(sums)),
            in_specs=[SMEM] * 3 + [VMEM] * (1 + high_size + 2 * len(sums)),
            out_specs=[VMEM] * len(shapes),
            out_shape=[jax.ShapeDtypeStruct(shape, BF16) for shape in shapes],
            scratch_shapes=[pltpu.VMEM(shapes[-1], F32)],
            compiler_params=pltpu.CompilerParams(vmem_limit_bytes=24 * 2**20),
            cost_estimate=QUICK,
        )(*in_hbm(*scalars), *in_hbm(down_parts), *ranks, *[a for two in sums for a in two])
        return outs[:-1], outs[-1]

    def finish_kernel(first, groups, *refs):
        pos_ref, kept_ref = refs[:2]
        got_refs = refs[2 : 2 + groups]
        out_ref, total_ref, turned_ref, sem = refs[-4:]
        own = pos_ref[0] // low_size
        start = 0
        for got_ref in got_refs:
            count = got_ref.shape[1]
            total_ref[:, start : start + count] = (
                kept_ref[:, start : start + count].astype(F32) + got_ref[...].astype(F32)
            ).astype(BF16)
            start += count
        copies = []
        for at in range(start // size):
            k, m, offset = order[first + at]
            base = pl.multiple_of((own ^ k) * tile_rows + offset, size)
            rows = slice(at * size, (at + 1) * size)
            turned_ref[rows, :] = total_ref[:, rows].T
            copies.append(
                pltpu.make_async_copy(
                    turned_ref.at[rows, :], out_ref.at[m, pl.ds(base, size), :], sem.at[at]
                )
            )
            copies[-1].start()
        for copy in copies:
            copy.wait()

    def finish(kept, got, first, result):
        rows = kept.shape[1]
        shape = jax.ShapeDtypeStruct((micro_count, high_size * tile_rows, portion), BF16)
        hbm = pl.BlockSpec(memory_space=pltpu.HBM)
        before = [] if result is None else [result]
        return pl.pallas_call(
            functools.partial(finish_kernel, first, len(got)),
            in_specs=[SMEM] + [VMEM] * (1 + len(got)) + [hbm] * len(before),
            out_specs=hbm,
            out_shape=shape,
            input_output_aliases={2 + len(got): 0} if before else {},
            scratch_shapes=[
                pltpu.VMEM((portion, rows), BF16),
                pltpu.VMEM((rows, portion), BF16),
                pltpu.SemaphoreType.DMA((rows // size,)),
            ],
            cost_estimate=QUICK,
        )(*in_hbm(scalars[0]), kept, *got, *before)

    _, kept = with_adapter(own_sums + c_sums, 0, False)
    early = relay(kept, 0)
    d_lasts, d_kept = with_adapter(d_sums, kept.shape[1] // size, True)
    d_last = [relay(d_lasts[0], 4), relay(d_lasts[1], 1)]
    d_kept = relay(d_kept, 0)
    grad_prev = finish(early, own_last + c_last, 0, None)
    grad_prev = finish(d_kept, d_last, kept.shape[1] // size, grad_prev)

    def down_kernel(pos_ref, classes_ref, live_ref, inputs_ref, *refs):
        rank_refs, out_ref, total_ref = refs[:-2], refs[-2], refs[-1]
        own = pos_ref[0] // low_size
        total_ref[...] = jnp.zeros_like(total_ref)
        for piece in order:
            k, m, offset = piece
            seg = segment_of(own, piece, tile_rows)

            @pl.when(seg < live_ref[m])
            def _():
                base = pl.multiple_of((own ^ k) * tile_rows + offset, size)
                rows = inputs_ref[m, pl.ds(base, size), :]
                for j in range(high_size):
                    total_ref[classes_ref[m, seg], own ^ j] += jnp.dot(
                        rank_refs[j][:, columns_of(j, piece)], rows, preferred_element_type=F32
                    )

        out_ref[...] = total_ref[...].astype(BF16)

    down_map_gradient = pl.pallas_call(
        down_kernel,
        in_specs=[SMEM] * 3 + [VMEM] * (1 + high_size),
        out_specs=VMEM,
        out_shape=jax.ShapeDtypeStruct(down_parts.shape, BF16),
        scratch_shapes=[pltpu.VMEM(down_parts.shape, F32)],
        cost_estimate=LONG,
    )(*in_hbm(*scalars, forward_input[0]), *ranks)

    return (
        grad_prev[None],
        down_map_gradient.reshape(1, class_count, rank, portion),
        up_map_gradient[None, None],
    )


def solution(mesh):
    in_specs = (
        P("pipe", "tensor", None, None, None),
        P("pipe", None, None, "tensor"),
        P("pipe", None, "tensor", None),
        P("pipe", "tensor", None, None),
        P("pipe", None, None, "tensor"),
        P("pipe", "tensor", None, None, None),
        P("pipe", None, None),
        P("pipe", None),
    )
    out_specs = (
        P("pipe", None, None, "tensor"),
        P("pipe", None, None, "tensor"),
        P("pipe", "tensor", None, None, None),
    )
    return jax.shard_map(shards, mesh=mesh, in_specs=in_specs, out_specs=out_specs, check_vma=False)
```

```python
import functools

import jax
import jax.numpy as jnp
from jax import lax
from jax.experimental import pallas as pl
from jax.experimental.pallas import tpu as pltpu
from jax.sharding import PartitionSpec as P

SEG = 128
BF16 = jnp.bfloat16
F32 = jnp.float32
SMEM = pl.BlockSpec(memory_space=pltpu.SMEM)
VMEM = pl.BlockSpec(memory_space=pltpu.VMEM)
TN = (((0,), (0,)), ((), ()))
PARAMS = pltpu.CompilerParams(vmem_limit_bytes=24 * 2**20)
QUICK = pl.CostEstimate(flops=1000, bytes_accessed=1000, transcendentals=0)
LONG = pl.CostEstimate(flops=4 * 10**10, bytes_accessed=1000, transcendentals=0)


def partner(value, mask):
    pairs = [(source, source ^ mask) for source in range(lax.axis_size("tensor"))]
    return lax.ppermute(value, "tensor", pairs)


def relay(value, mask):
    sections, tiles = lax.axis_size("pipe"), lax.axis_size("tensor")
    pairs = [
        (p * tiles + t, (p - 1) % sections * tiles + (t ^ mask))
        for p in range(sections)
        for t in range(tiles)
    ]
    return lax.ppermute(value, ("pipe", "tensor"), pairs)


def segment_of(high, piece, tile_rows):
    k, _, offset = piece
    return ((high ^ k) * tile_rows + offset) // SEG


def product_body(low_size, tile_rows, pieces, tiles, half, turns, sends, keeps, with_hidden, *refs):
    pos_ref, classes_ref, live_ref = refs[:3]
    grad_refs = refs[3 : 3 + tiles]
    weight_hbm = refs[3 + tiles]
    rows_ref, weight_ref, sems = refs[-3:]
    rest = list(refs[4 + tiles : -3])
    up_ref = rest.pop(0) if keeps else None
    hidden_ref = rest.pop(0) if with_hidden else None
    sent_x, sent_y = (rest.pop(0), rest.pop(0)) if sends else (None, None)
    placed_ref = rest.pop(0) if with_hidden else None
    kept_x, kept_y, rank_ref = rest if keeps else (None, None, None)
    low, high = pos_ref[0] % low_size, pos_ref[0] // low_size
    total = rows_ref.shape[1]
    size = total // len(pieces)

    def weight_copy(block):
        return pltpu.make_async_copy(
            weight_hbm.at[block ^ low], weight_ref.at[block], sems.at[block]
        )

    jobs = []
    for x, y in ((1, 1), (1, 0), (0, 1), (0, 0)):
        to_x = (sent_x if x else kept_x, 2 * y, 1)
        to_y = (sent_y if y else kept_y, *((x, 2) if turns else (2 * x, 1)))
        start = 0 if to_x[0] is not None else half
        stop = total if to_y[0] is not None else half
        if start < stop:
            jobs.append((x + 2 * y, start, stop, to_x, to_y))
    for block, *_ in jobs:
        for z in range(2):
            weight_copy(block + 4 * z).start()

    if with_hidden:
        micro_count, count, rank = hidden_ref.shape
        spot = lax.broadcasted_iota(jnp.int32, (count, half), 1)
        row = lax.broadcasted_iota(jnp.int32, (count, half), 0)
        chosen = (spot == low * count + row).astype(F32).astype(BF16)
        for m in range(micro_count):
            placed = lax.dot_general(
                hidden_ref[m], chosen, TN, preferred_element_type=F32
            ).astype(BF16)
            placed_ref[m * rank : (m + 1) * rank, :] = placed
            start = sent_x.shape[0] - (micro_count - m) * rank
            sent_x[start : start + rank, :] = placed

    for at, (tile, index, piece, first) in enumerate(pieces):
        seg = segment_of(high, piece, tile_rows)
        alive = seg < live_ref[piece[1]]
        place = slice(at * size, (at + 1) * size)

        @pl.when(alive)
        def _():
            rows = grad_refs[tile][index, first : first + size, :].T
            rows_ref[:, place] = rows
            if keeps:
                up = up_ref[classes_ref[piece[1], seg]]
                rank_ref[:, place] = jnp.dot(up, rows, preferred_element_type=F32)

        @pl.when(jnp.logical_not(alive))
        def _():
            rows_ref[:, place] = jnp.zeros((rows_ref.shape[0], size), rows_ref.dtype)
            if keeps:
                rank_ref[:, place] = jnp.zeros((rank_ref.shape[0], size), F32)

    for block, start, stop, to_x, to_y in jobs:

        @pl.loop(0, 2)
        def _(z):
            weight_copy(block + 4 * z).wait()
            value = jnp.dot(
                weight_ref[block + 4 * z], rows_ref[:, start:stop], preferred_element_type=F32
            )
            for (ref, slot, step), part in (
                (to_x, value[:, : half - start]),
                (to_y, value[:, half - start :]),
            ):
                if ref is not None:
                    width = part.shape[0]
                    place = pl.ds(pl.multiple_of((slot + step * z) * width, width), width)
                    ref[place, :] = part.astype(ref.dtype)


def product(scalars, grads, pieces, tile_rows, weight_blocks, up_tile, low_size, turns, sends, keeps, cost, size, hidden=None):
    blocks, width, depth = weight_blocks.shape
    rows = len(pieces) * size
    half = rows // 2
    if rows > 128 and half % 128:
        half = half // 128 * 128 + 128
    outs = []
    extra = 0 if hidden is None else hidden.shape[0] * hidden.shape[2]
    for wanted, dtype in ((sends, BF16), (keeps, F32)):
        if wanted:
            for more, n in ((extra, half), (0, rows - half)):
                outs.append(jax.ShapeDtypeStruct((blocks // 2 * width + more, n), dtype))
    if extra:
        outs.append(jax.ShapeDtypeStruct((extra, half), BF16))
    if keeps:
        outs.append(jax.ShapeDtypeStruct((up_tile.shape[1], rows), F32))
    more = ([up_tile] if keeps else []) + ([] if hidden is None else [hidden])
    return pl.pallas_call(
        functools.partial(
            product_body, low_size, tile_rows, pieces, len(grads), half, turns, sends, keeps, extra > 0
        ),
        in_specs=[SMEM] * 3
        + [VMEM] * len(grads)
        + [pl.BlockSpec(memory_space=pltpu.HBM)]
        + [VMEM] * len(more),
        out_specs=[VMEM] * len(outs),
        out_shape=outs,
        scratch_shapes=[
            pltpu.VMEM((depth, rows), BF16),
            pltpu.VMEM(weight_blocks.shape, BF16),
            pltpu.SemaphoreType.DMA((blocks,)),
        ],
        compiler_params=PARAMS,
        cost_estimate=cost,
    )(*in_hbm(*scalars), *grads, *in_hbm(weight_blocks, *more))


def in_hbm(*arrays):
    return [pltpu.with_memory_space_constraint(array, pltpu.HBM) for array in arrays]


def after(value, *others):
    return lax.optimization_barrier((value, *others))[0]


def halve_kernel(ways, *refs):
    kept_refs, got_refs = refs[:ways], refs[ways : 2 * ways]
    placed_ref = refs[2 * ways] if len(refs) > 4 * ways else None
    outs = refs[-2 * ways - (placed_ref is not None) :]
    for way in range(ways):
        kept_ref, got_ref, sent_ref, rest_ref = kept_refs[way], got_refs[way], outs[way], outs[ways + way]
        half = kept_ref.shape[0] // 2
        sent_ref[:half, :] = (kept_ref[half:, :] + got_ref[half : 2 * half, :].astype(F32)).astype(BF16)
        rest_ref[...] = kept_ref[:half, :] + got_ref[:half, :].astype(F32)
        if way == 0 and placed_ref is not None:
            placed = placed_ref[...] + got_ref[2 * half :, :]
            sent_ref[half:, :] = placed
            outs[-1][...] = placed


def halve(kept, got, placed=None):
    placed = [] if placed is None else [placed]
    extra = [placed[0].shape[0] if placed and not way else 0 for way in range(len(kept))]
    shapes = [(k.shape[0] // 2, k.shape[1]) for k in kept]
    outs = pl.pallas_call(
        functools.partial(halve_kernel, len(kept)),
        in_specs=[VMEM] * (2 * len(kept) + len(placed)),
        out_specs=[VMEM] * (2 * len(kept) + len(placed)),
        out_shape=[jax.ShapeDtypeStruct((n + e, r), BF16) for (n, r), e in zip(shapes, extra)]
        + [jax.ShapeDtypeStruct(shape, F32) for shape in shapes]
        + [jax.ShapeDtypeStruct(p.shape, BF16) for p in placed],
        compiler_params=PARAMS,
        cost_estimate=QUICK,
    )(*kept, *got, *placed)
    ways = len(kept)
    return outs[:ways], outs[ways : 2 * ways], *outs[2 * ways :]


def last_kernel(ways, *refs):
    kept_refs, got_refs = refs[:ways], refs[ways : 2 * ways]
    placed_ref = refs[2 * ways] if len(refs) > 3 * ways else None
    outs = refs[-ways - (placed_ref is not None) :]
    for way in range(ways):
        kept_ref, got_ref = kept_refs[way], got_refs[way]
        half = kept_ref.shape[0] // 2
        outs[way][...] = (
            kept_ref[half:, :] + got_ref[half : 2 * half, :].astype(F32)
        ).astype(BF16)
        if way == 0 and placed_ref is not None:
            outs[-1][...] = placed_ref[...] + got_ref[2 * half :, :]


def last_parts(kept, got, placed=None):
    placed = [] if placed is None else [placed]
    return pl.pallas_call(
        functools.partial(last_kernel, len(kept)),
        in_specs=[VMEM] * (2 * len(kept) + len(placed)),
        out_specs=[VMEM] * (len(kept) + len(placed)),
        out_shape=[jax.ShapeDtypeStruct((k.shape[0] // 2, k.shape[1]), BF16) for k in kept]
        + [jax.ShapeDtypeStruct(p.shape, BF16) for p in placed],
        compiler_params=PARAMS,
        cost_estimate=QUICK,
    )(*kept, *got, *placed)


def up_body(low_size, tile_rows, pieces, tiles, micro_count, *refs):
    pos_ref, classes_ref, live_ref = refs[:3]
    grad_refs = refs[3 : 3 + tiles]
    hidden_refs = refs[3 + tiles : -2]
    out_ref, total_ref = refs[-2:]
    high = pos_ref[0] // low_size
    total_ref[...] = jnp.zeros_like(total_ref)
    rank_part = total_ref.shape[1]
    for tile, index, piece, first in pieces:
        k, m, offset = piece
        size = min(SEG, tile_rows)
        seg = segment_of(high, piece, tile_rows)
        near_ref, far_ref = hidden_refs[2 * k : 2 * k + 2]
        start = m * (near_ref.shape[0] // micro_count)
        if k == 0:
            start = pl.multiple_of(start + high * rank_part, rank_part)

        @pl.when(seg < live_ref[m])
        def _():
            place = pl.ds(start, rank_part), slice(offset, offset + size)
            total_ref[classes_ref[m, seg]] += jnp.dot(
                near_ref[place] + far_ref[place],
                grad_refs[tile][index, first : first + size, :],
                preferred_element_type=F32,
            )

    out_ref[...] = total_ref[...].astype(BF16)


def shards(
    output_gradient,
    forward_input,
    saved_rank_outputs,
    projection_weight,
    adapter_down_maps,
    adapter_up_maps,
    segment_adapter_class,
    live_segment_table,
):
    grad_tile = output_gradient[0, 0]
    micro_count, tile_rows, tile_cols = grad_tile.shape
    up_tile = adapter_up_maps[0, 0]
    class_count, rank_part, _ = up_tile.shape
    rank, portion = adapter_down_maps.shape[2:]
    tiles = lax.axis_size("tensor")
    low_size = min(tiles, 8)
    high_size = tiles // low_size
    position = lax.axis_index("tensor")
    high = position // low_size
    weight_blocks = projection_weight[0, 0].reshape(low_size, portion, tile_cols)
    position, classes, live = lax.optimization_barrier(
        (position.astype(jnp.int32)[None], segment_adapter_class[0] + 0, live_segment_table[0] + 0)
    )
    scalars = position, classes, live
    position = position[0]
    size = min(SEG, tile_rows)
    offsets = range(0, tile_rows, size)

    own_pieces = [(0, m, (0, m, o), o) for m in range(micro_count) for o in offsets]

    def pieces_of(m, count=1):
        span = tile_rows // count
        return [
            ((k - 1) * count + o // span, 0, (k, m, o), o % span)
            for k in range(1, high_size)
            for o in offsets
        ]

    def produce(grads, pieces, turns, sends, keeps, cost, hidden=None):
        return product(
            scalars, grads, pieces, tile_rows, weight_blocks, up_tile, low_size, turns, sends, keeps,
            cost, size, hidden,
        )

    hidden = saved_rank_outputs[0]

    first_rows = lax.optimization_barrier(grad_tile[0])
    got0 = [partner(first_rows, k * low_size)[None] for k in range(1, high_size)]
    (own_grads,) = in_hbm(after(grad_tile, first_rows))
    sent_x, sent_y, placed = produce([own_grads], own_pieces, False, True, False, QUICK, hidden)
    first_x, first_y = partner(sent_x, 1), partner(sent_y, 2)
    (own_grads,) = in_hbm(after(grad_tile, sent_x, sent_y))
    kept_x, kept_y, part = produce([own_grads], own_pieces, False, False, True, QUICK)
    parts = [part]
    rows0 = after(got0[0], part), *got0[1:]
    c_sent_x, c_sent_y, c_kept_x, c_kept_y, part = produce(
        list(rows0), pieces_of(0), False, True, True, LONG
    )
    parts.append(part)
    count = 2 if size == SEG and tile_rows >= 2 * SEG else 1
    source, got1 = after(grad_tile[1], *got0), [[] for _ in range(1, high_size)]
    for at in range(count):
        span = tile_rows // count
        rows = source[at * span : (at + 1) * span]
        for k in range(1, high_size):
            got1[k - 1].append(partner(rows, k * low_size)[None])
        source = after(source, *[got[-1] for got in got1])
    early, got1 = got1[0][0], [part for got in got1 for part in got]

    (sent_x, sent_y), (kept_x, kept_y), placed = halve(
        (after(kept_x, part, early), kept_y), (first_x, first_y), placed
    )
    second_x, second_y = partner(sent_x, 2), partner(sent_y, 1)
    c_first_x = partner(after(c_sent_x, sent_x, sent_y), 1)
    c_first_y = partner(after(c_sent_y, sent_x, sent_y), 2)

    chunks = [([grad_tile], own_pieces), (got0, pieces_of(0)), (got1, pieces_of(1, count))]
    order = [piece for _, pieces in chunks for _, _, piece, _ in pieces]
    *own_third, placed = last_parts((kept_x, kept_y), (second_x, second_y), placed)
    own_last = [relay(third, 4) for third in own_third]
    own_sums = (kept_x, second_x), (kept_y, second_y)
    rows1 = after(got1[0], part, *own_third), *got1[1:]
    d_sent_x, d_sent_y, d_kept_x, d_kept_y, part = produce(
        list(rows1), pieces_of(1, count), True, True, True, LONG
    )
    parts.append(part)
    hiddens = [placed, partner(placed, 4)]
    for k in range(1, high_size):
        wanted = placed.reshape(micro_count, rank, tile_rows)
        wanted = lax.dynamic_slice_in_dim(wanted, (high ^ k) * rank_part, rank_part, 1)
        wanted = wanted.reshape(micro_count * rank_part, tile_rows)
        hiddens += [partner(wanted, k * low_size), partner(wanted, k * low_size + 4)]
    own_rank = jnp.concatenate(parts, 1)
    shared = after(own_rank.astype(BF16), *own_last, *hiddens)
    for mask in (1, 2, 3):
        own_rank = own_rank + partner(shared, mask)
    (c_sent_x, c_sent_y), c_kept = halve((c_kept_x, c_kept_y), (c_first_x, c_first_y))
    slot = own_rank, c_sent_x, c_sent_y
    d_first_x, d_first_y = partner(after(d_sent_x, *slot), 1), partner(after(d_sent_y, *slot), 2)
    c_second_x, c_second_y = partner(c_sent_x, 2), partner(c_sent_y, 1)
    shared = own_rank.astype(BF16)
    ranks = [(own_rank + partner(shared, 4)).astype(BF16)]
    for j in range(1, high_size):
        one, other = partner(shared, j * low_size), partner(shared, j * low_size + 4)
        ranks.append((one.astype(F32) + other.astype(F32)).astype(BF16))

    all_grads, all_pieces = [], []
    for grads, pieces in chunks:
        all_pieces += [(tile + len(all_grads), *rest) for tile, *rest in pieces]
        all_grads += grads
    up_map_gradient = pl.pallas_call(
        functools.partial(
            up_body, low_size, tile_rows, all_pieces, len(all_grads), micro_count
        ),
        in_specs=[SMEM] * 3 + [VMEM] * (len(all_grads) + 2 * high_size),
        out_specs=VMEM,
        out_shape=jax.ShapeDtypeStruct(up_tile.shape, BF16),
        scratch_shapes=[pltpu.VMEM(up_tile.shape, F32)],
        compiler_params=PARAMS,
        cost_estimate=QUICK,
    )(*in_hbm(*scalars), *all_grads, *hiddens)

    (d_sent_x, d_sent_y), d_kept = halve(
        (after(d_kept_x, up_map_gradient), d_kept_y), (d_first_x, d_first_y)
    )
    d_second_x, d_second_y = partner(d_sent_x, 2), partner(d_sent_y, 4)
    c_third = last_parts(c_kept, (c_second_x, c_second_y))
    c_last = [relay(third, 4) for third in c_third]
    c_sums = (c_kept[0], c_second_x), (c_kept[1], c_second_y)
    d_sums = (d_kept[0], d_second_x), (d_kept[1], d_second_y)

    def columns_of(j, piece):
        k, m, offset = piece
        at = order.index((k ^ j, m, offset))
        return slice(at * size, (at + 1) * size)

    down_parts = adapter_down_maps[0].reshape(class_count, high_size, rank_part, portion)

    def adapter_kernel(first, with_last, groups, *refs):
        pos_ref, classes_ref, _, down_ref = refs[:4]
        rank_refs = refs[4 : 4 + high_size]
        sum_refs = refs[4 + high_size : 4 + high_size + 2 * groups]
        *last_refs, out_ref, total_ref = refs[4 + high_size + 2 * groups :]
        own = pos_ref[0] // low_size
        start = 0
        for g in range(groups):
            kept_ref, second_ref = sum_refs[2 * g : 2 * g + 2]
            half, count = kept_ref.shape[0] // 2, kept_ref.shape[1]
            total_ref[:, start : start + count] = (
                kept_ref[:half, :] + second_ref[:half, :].astype(F32)
            )
            if with_last:
                last_refs[g][...] = (
                    kept_ref[half:, :] + second_ref[half : 2 * half, :].astype(F32)
                ).astype(BF16)
            start += count
        for at in range(start // size):
            piece = order[first + at]
            seg = segment_of(own, piece, tile_rows)
            rows = slice(at * size, (at + 1) * size)
            adapter = total_ref[:, rows]
            for j in range(high_size):
                adapter = adapter + lax.dot_general(
                    down_ref[classes_ref[piece[1], seg], own ^ j],
                    rank_refs[j][:, columns_of(j, piece)],
                    TN,
                    preferred_element_type=F32,
                )
            out_ref[:, rows] = adapter.astype(BF16)

    def with_adapter(sums, first, with_last):
        counts = [kept.shape[1] for kept, _ in sums]
        shapes = [(portion, n) for n in counts] * with_last + [(portion, sum(counts))]
        outs = pl.pallas_call(
            functools.partial(adapter_kernel, first, with_last, len(sums)),
            in_specs=[SMEM] * 3 + [VMEM] * (1 + high_size + 2 * len(sums)),
            out_specs=[VMEM] * len(shapes),
            out_shape=[jax.ShapeDtypeStruct(shape, BF16) for shape in shapes],
            scratch_shapes=[pltpu.VMEM(shapes[-1], F32)],
            compiler_params=PARAMS,
            cost_estimate=QUICK,
        )(*in_hbm(*scalars), *in_hbm(down_parts), *ranks, *[a for two in sums for a in two])
        return outs[:-1], outs[-1]

    def finish_kernel(first, groups, *refs):
        pos_ref, kept_ref = refs[:2]
        got_refs = refs[2 : 2 + groups]
        out_ref, total_ref, turned_ref, sem = refs[-4:]
        own = pos_ref[0] // low_size
        start = 0
        for got_ref in got_refs:
            count = got_ref.shape[1]
            total_ref[:, start : start + count] = (
                kept_ref[:, start : start + count].astype(F32) + got_ref[...].astype(F32)
            ).astype(BF16)
            start += count
        copies = []
        for at in range(start // size):
            k, m, offset = order[first + at]
            base = pl.multiple_of((own ^ k) * tile_rows + offset, size)
            rows = slice(at * size, (at + 1) * size)
            turned_ref[rows, :] = total_ref[:, rows].T
            copies.append(
                pltpu.make_async_copy(
                    turned_ref.at[rows, :], out_ref.at[m, pl.ds(base, size), :], sem.at[at]
                )
            )
            copies[-1].start()
        for copy in copies:
            copy.wait()

    def finish(kept, got, first, result):
        rows = kept.shape[1]
        shape = jax.ShapeDtypeStruct((micro_count, high_size * tile_rows, portion), BF16)
        hbm = pl.BlockSpec(memory_space=pltpu.HBM)
        before = [] if result is None else [result]
        return pl.pallas_call(
            functools.partial(finish_kernel, first, len(got)),
            in_specs=[SMEM] + [VMEM] * (1 + len(got)) + [hbm] * len(before),
            out_specs=hbm,
            out_shape=shape,
            input_output_aliases={2 + len(got): 0} if before else {},
            scratch_shapes=[
                pltpu.VMEM((portion, rows), BF16),
                pltpu.VMEM((rows, portion), BF16),
                pltpu.SemaphoreType.DMA((rows // size,)),
            ],
            compiler_params=PARAMS,
            cost_estimate=QUICK,
        )(*in_hbm(scalars[0]), kept, *got, *before)

    _, kept = with_adapter(own_sums + c_sums, 0, False)
    early = relay(kept, 0)
    d_lasts, d_kept = with_adapter(d_sums, kept.shape[1] // size, True)
    d_last = [relay(d_lasts[0], 4), relay(d_lasts[1], 1)]
    d_kept = relay(d_kept, 0)
    grad_prev = finish(early, own_last + c_last, 0, None)
    grad_prev = finish(d_kept, d_last, kept.shape[1] // size, grad_prev)

    def down_kernel(pos_ref, classes_ref, live_ref, inputs_ref, *refs):
        rank_refs, out_ref, total_ref = refs[:-2], refs[-2], refs[-1]
        own = pos_ref[0] // low_size
        total_ref[...] = jnp.zeros_like(total_ref)
        for piece in order:
            k, m, offset = piece
            seg = segment_of(own, piece, tile_rows)

            @pl.when(seg < live_ref[m])
            def _():
                base = pl.multiple_of((own ^ k) * tile_rows + offset, size)
                rows = inputs_ref[m, pl.ds(base, size), :]
                for j in range(high_size):
                    total_ref[classes_ref[m, seg], own ^ j] += jnp.dot(
                        rank_refs[j][:, columns_of(j, piece)], rows, preferred_element_type=F32
                    )

        out_ref[...] = total_ref[...].astype(BF16)

    down_map_gradient = pl.pallas_call(
        down_kernel,
        in_specs=[SMEM] * 3 + [VMEM] * (1 + high_size),
        out_specs=VMEM,
        out_shape=jax.ShapeDtypeStruct(down_parts.shape, BF16),
        scratch_shapes=[pltpu.VMEM(down_parts.shape, F32)],
        compiler_params=PARAMS,
        cost_estimate=LONG,
    )(*in_hbm(*scalars, forward_input[0]), *ranks)

    return (
        grad_prev[None],
        down_map_gradient.reshape(1, class_count, rank, portion),
        up_map_gradient[None, None],
    )


def solution(mesh):
    in_specs = (
        P("pipe", "tensor", None, None, None),
        P("pipe", None, None, "tensor"),
        P("pipe", None, "tensor", None),
        P("pipe", "tensor", None, None),
        P("pipe", None, None, "tensor"),
        P("pipe", "tensor", None, None, None),
        P("pipe", None, None),
        P("pipe", None),
    )
    out_specs = (
        P("pipe", None, None, "tensor"),
        P("pipe", None, None, "tensor"),
        P("pipe", "tensor", None, None, None),
    )
    return jax.shard_map(shards, mesh=mesh, in_specs=in_specs, out_specs=out_specs, check_vma=False)
```

```python
import functools

import jax
import jax.numpy as jnp
from jax import lax
from jax.experimental import pallas as pl
from jax.experimental.pallas import tpu as pltpu
from jax.sharding import PartitionSpec as P

SEG = 128
BF16 = jnp.bfloat16
F32 = jnp.float32
SMEM = pl.BlockSpec(memory_space=pltpu.SMEM)
VMEM = pl.BlockSpec(memory_space=pltpu.VMEM)
TN = (((0,), (0,)), ((), ()))
PARAMS = pltpu.CompilerParams(vmem_limit_bytes=24 * 2**20)
QUICK = pl.CostEstimate(flops=1000, bytes_accessed=1000, transcendentals=0)
LONG = pl.CostEstimate(flops=4 * 10**10, bytes_accessed=1000, transcendentals=0)


def partner(value, mask):
    pairs = [(source, source ^ mask) for source in range(lax.axis_size("tensor"))]
    return lax.ppermute(value, "tensor", pairs)


def relay(value, mask):
    sections, tiles = lax.axis_size("pipe"), lax.axis_size("tensor")
    pairs = [
        (p * tiles + t, (p - 1) % sections * tiles + (t ^ mask))
        for p in range(sections)
        for t in range(tiles)
    ]
    return lax.ppermute(value, ("pipe", "tensor"), pairs)


def segment_of(high, piece, tile_rows):
    k, _, offset = piece
    return ((high ^ k) * tile_rows + offset) // SEG


def product_body(low_size, tile_rows, pieces, tiles, half, turns, sends, keeps, with_hidden, *refs):
    pos_ref, classes_ref, live_ref = refs[:3]
    grad_refs = refs[3 : 3 + tiles]
    weight_hbm = refs[3 + tiles]
    rows_ref, weight_ref, sems = refs[-3:]
    rest = list(refs[4 + tiles : -3])
    up_ref = rest.pop(0) if keeps else None
    hidden_ref = rest.pop(0) if with_hidden else None
    sent_x, sent_y = (rest.pop(0), rest.pop(0)) if sends else (None, None)
    placed_ref = rest.pop(0) if with_hidden else None
    kept_x, kept_y, rank_ref = rest if keeps else (None, None, None)
    low, high = pos_ref[0] % low_size, pos_ref[0] // low_size
    total = rows_ref.shape[1]
    size = total // len(pieces)

    def weight_copy(block):
        return pltpu.make_async_copy(
            weight_hbm.at[block ^ low], weight_ref.at[block], sems.at[block]
        )

    jobs = []
    for x, y in ((1, 1), (1, 0), (0, 1), (0, 0)):
        to_x = (sent_x if x else kept_x, 2 * y, 1)
        to_y = (sent_y if y else kept_y, *((x, 2) if turns else (2 * x, 1)))
        start = 0 if to_x[0] is not None else half
        stop = total if to_y[0] is not None else half
        if start < stop:
            jobs.append((x + 2 * y, start, stop, to_x, to_y))
    for block, *_ in jobs:
        for z in range(2):
            weight_copy(block + 4 * z).start()

    if with_hidden:
        micro_count, count, rank = hidden_ref.shape
        spot = lax.broadcasted_iota(jnp.int32, (count, half), 1)
        row = lax.broadcasted_iota(jnp.int32, (count, half), 0)
        chosen = (spot == low * count + row).astype(F32).astype(BF16)
        for m in range(micro_count):
            placed = lax.dot_general(
                hidden_ref[m], chosen, TN, preferred_element_type=F32
            ).astype(BF16)
            placed_ref[m * rank : (m + 1) * rank, :] = placed
            start = sent_x.shape[0] - (micro_count - m) * rank
            sent_x[start : start + rank, :] = placed

    for at, (tile, index, piece, first) in enumerate(pieces):
        seg = segment_of(high, piece, tile_rows)
        alive = seg < live_ref[piece[1]]
        place = slice(at * size, (at + 1) * size)

        @pl.when(alive)
        def _():
            rows = grad_refs[tile][index, first : first + size, :].T
            rows_ref[:, place] = rows
            if keeps:
                up = up_ref[classes_ref[piece[1], seg]]
                rank_ref[:, place] = jnp.dot(up, rows, preferred_element_type=F32)

        @pl.when(jnp.logical_not(alive))
        def _():
            rows_ref[:, place] = jnp.zeros((rows_ref.shape[0], size), rows_ref.dtype)
            if keeps:
                rank_ref[:, place] = jnp.zeros((rank_ref.shape[0], size), F32)

    for block, start, stop, to_x, to_y in jobs:

        @pl.loop(0, 2)
        def _(z):
            weight_copy(block + 4 * z).wait()
            value = jnp.dot(
                weight_ref[block + 4 * z], rows_ref[:, start:stop], preferred_element_type=F32
            )
            for (ref, slot, step), part in (
                (to_x, value[:, : half - start]),
                (to_y, value[:, half - start :]),
            ):
                if ref is not None:
                    width = part.shape[0]
                    place = pl.ds(pl.multiple_of((slot + step * z) * width, width), width)
                    ref[place, :] = part.astype(ref.dtype)


def product(scalars, grads, pieces, tile_rows, weight_blocks, up_tile, low_size, turns, sends, keeps, cost, size, hidden=None):
    blocks, width, depth = weight_blocks.shape
    rows = len(pieces) * size
    half = rows // 2
    if rows > 128 and half % 128:
        half = half // 128 * 128 + 128
    outs = []
    extra = 0 if hidden is None else hidden.shape[0] * hidden.shape[2]
    for wanted, dtype in ((sends, BF16), (keeps, F32)):
        if wanted:
            for more, n in ((extra, half), (0, rows - half)):
                outs.append(jax.ShapeDtypeStruct((blocks // 2 * width + more, n), dtype))
    if extra:
        outs.append(jax.ShapeDtypeStruct((extra, half), BF16))
    if keeps:
        outs.append(jax.ShapeDtypeStruct((up_tile.shape[1], rows), F32))
    more = ([up_tile] if keeps else []) + ([] if hidden is None else [hidden])
    return pl.pallas_call(
        functools.partial(
            product_body, low_size, tile_rows, pieces, len(grads), half, turns, sends, keeps, extra > 0
        ),
        in_specs=[SMEM] * 3
        + [VMEM] * len(grads)
        + [pl.BlockSpec(memory_space=pltpu.HBM)]
        + [VMEM] * len(more),
        out_specs=[VMEM] * len(outs),
        out_shape=outs,
        scratch_shapes=[
            pltpu.VMEM((depth, rows), BF16),
            pltpu.VMEM(weight_blocks.shape, BF16),
            pltpu.SemaphoreType.DMA((blocks,)),
        ],
        compiler_params=PARAMS,
        cost_estimate=cost,
    )(*in_hbm(*scalars), *grads, *in_hbm(weight_blocks, *more))


def in_hbm(*arrays):
    return [pltpu.with_memory_space_constraint(array, pltpu.HBM) for array in arrays]


def after(value, *others):
    return lax.optimization_barrier((value, *others))[0]


def halve_kernel(ways, *refs):
    kept_refs, got_refs = refs[:ways], refs[ways : 2 * ways]
    placed_ref = refs[2 * ways] if len(refs) > 4 * ways else None
    outs = refs[-2 * ways - (placed_ref is not None) :]
    for way in range(ways):
        kept_ref, got_ref, sent_ref, rest_ref = kept_refs[way], got_refs[way], outs[way], outs[ways + way]
        half = kept_ref.shape[0] // 2
        sent_ref[:half, :] = (kept_ref[half:, :] + got_ref[half : 2 * half, :].astype(F32)).astype(BF16)
        rest_ref[...] = kept_ref[:half, :] + got_ref[:half, :].astype(F32)
        if way == 0 and placed_ref is not None:
            placed = placed_ref[...] + got_ref[2 * half :, :]
            sent_ref[half:, :] = placed
            outs[-1][...] = placed


def halve(kept, got, placed=None):
    placed = [] if placed is None else [placed]
    extra = [placed[0].shape[0] if placed and not way else 0 for way in range(len(kept))]
    shapes = [(k.shape[0] // 2, k.shape[1]) for k in kept]
    outs = pl.pallas_call(
        functools.partial(halve_kernel, len(kept)),
        in_specs=[VMEM] * (2 * len(kept) + len(placed)),
        out_specs=[VMEM] * (2 * len(kept) + len(placed)),
        out_shape=[jax.ShapeDtypeStruct((n + e, r), BF16) for (n, r), e in zip(shapes, extra)]
        + [jax.ShapeDtypeStruct(shape, F32) for shape in shapes]
        + [jax.ShapeDtypeStruct(p.shape, BF16) for p in placed],
        compiler_params=PARAMS,
        cost_estimate=QUICK,
    )(*kept, *got, *placed)
    ways = len(kept)
    return outs[:ways], outs[ways : 2 * ways], *outs[2 * ways :]


def last_kernel(ways, *refs):
    kept_refs, got_refs = refs[:ways], refs[ways : 2 * ways]
    placed_ref = refs[2 * ways] if len(refs) > 2 * ways + 1 else None
    out_ref = refs[2 * ways + (placed_ref is not None)]
    start = 0
    for kept_ref, got_ref in zip(kept_refs, got_refs):
        half, count = kept_ref.shape[0] // 2, kept_ref.shape[1]
        out_ref[:, start : start + count] = (
            kept_ref[half:, :] + got_ref[half : 2 * half, :].astype(F32)
        ).astype(BF16)
        start += count
    if placed_ref is not None:
        refs[-1][...] = placed_ref[...] + got_refs[0][2 * kept_refs[0].shape[0] // 2 :, :]


def last_parts(kept, got, placed=None):
    placed = [] if placed is None else [placed]
    shape = kept[0].shape[0] // 2, sum(k.shape[1] for k in kept)
    return pl.pallas_call(
        functools.partial(last_kernel, len(kept)),
        in_specs=[VMEM] * (2 * len(kept) + len(placed)),
        out_specs=[VMEM] * (1 + len(placed)),
        out_shape=[jax.ShapeDtypeStruct(shape, BF16)]
        + [jax.ShapeDtypeStruct(p.shape, BF16) for p in placed],
        compiler_params=PARAMS,
        cost_estimate=QUICK,
    )(*kept, *got, *placed)


def up_body(low_size, tile_rows, pieces, tiles, micro_count, *refs):
    pos_ref, classes_ref, live_ref = refs[:3]
    grad_refs = refs[3 : 3 + tiles]
    hidden_refs = refs[3 + tiles : -2]
    out_ref, total_ref = refs[-2:]
    high = pos_ref[0] // low_size
    total_ref[...] = jnp.zeros_like(total_ref)
    rank_part = total_ref.shape[1]
    for tile, index, piece, first in pieces:
        k, m, offset = piece
        size = min(SEG, tile_rows)
        seg = segment_of(high, piece, tile_rows)
        near_ref, far_ref = hidden_refs[2 * k : 2 * k + 2]
        start = m * (near_ref.shape[0] // micro_count)
        if k == 0:
            start = pl.multiple_of(start + high * rank_part, rank_part)

        @pl.when(seg < live_ref[m])
        def _():
            place = pl.ds(start, rank_part), slice(offset, offset + size)
            total_ref[classes_ref[m, seg]] += jnp.dot(
                near_ref[place] + far_ref[place],
                grad_refs[tile][index, first : first + size, :],
                preferred_element_type=F32,
            )

    out_ref[...] = total_ref[...].astype(BF16)


def shards(
    output_gradient,
    forward_input,
    saved_rank_outputs,
    projection_weight,
    adapter_down_maps,
    adapter_up_maps,
    segment_adapter_class,
    live_segment_table,
):
    grad_tile = output_gradient[0, 0]
    micro_count, tile_rows, tile_cols = grad_tile.shape
    up_tile = adapter_up_maps[0, 0]
    class_count, rank_part, _ = up_tile.shape
    rank, portion = adapter_down_maps.shape[2:]
    tiles = lax.axis_size("tensor")
    low_size = min(tiles, 8)
    high_size = tiles // low_size
    position = lax.axis_index("tensor")
    high = position // low_size
    weight_blocks = projection_weight[0, 0].reshape(low_size, portion, tile_cols)
    position, classes, live = lax.optimization_barrier(
        (position.astype(jnp.int32)[None], segment_adapter_class[0] + 0, live_segment_table[0] + 0)
    )
    scalars = position, classes, live
    position = position[0]
    size = min(SEG, tile_rows)
    offsets = range(0, tile_rows, size)

    own_pieces = [(0, m, (0, m, o), o) for m in range(micro_count) for o in offsets]

    def pieces_of(m, count=1):
        span = tile_rows // count
        return [
            ((k - 1) * count + o // span, 0, (k, m, o), o % span)
            for k in range(1, high_size)
            for o in offsets
        ]

    def produce(grads, pieces, turns, sends, keeps, cost, hidden=None):
        return product(
            scalars, grads, pieces, tile_rows, weight_blocks, up_tile, low_size, turns, sends, keeps,
            cost, size, hidden,
        )

    hidden = saved_rank_outputs[0]

    first_rows = lax.optimization_barrier(grad_tile[0])
    got0 = [partner(first_rows, k * low_size)[None] for k in range(1, high_size)]
    (own_grads,) = in_hbm(after(grad_tile, first_rows))
    sent_x, sent_y, placed = produce([own_grads], own_pieces, False, True, False, QUICK, hidden)
    first_x, first_y = partner(sent_x, 1), partner(sent_y, 2)
    (own_grads,) = in_hbm(after(grad_tile, sent_x, sent_y))
    kept_x, kept_y, part = produce([own_grads], own_pieces, False, False, True, QUICK)
    parts = [part]
    rows0 = after(got0[0], part), *got0[1:]
    c_sent_x, c_sent_y, c_kept_x, c_kept_y, part = produce(
        list(rows0), pieces_of(0), False, True, True, LONG
    )
    parts.append(part)
    second_rows = after(grad_tile[1], *got0)
    got1 = [partner(second_rows, k * low_size)[None] for k in range(1, high_size)]

    (sent_x, sent_y), (kept_x, kept_y), placed = halve(
        (after(kept_x, part), kept_y), (first_x, first_y), placed
    )
    second_x, second_y = partner(sent_x, 2), partner(sent_y, 1)
    c_first_x = partner(after(c_sent_x, sent_x, sent_y), 1)
    c_first_y = partner(after(c_sent_y, sent_x, sent_y), 2)

    chunks = [([grad_tile], own_pieces), (got0, pieces_of(0)), (got1, pieces_of(1))]
    order = [piece for _, pieces in chunks for _, _, piece, _ in pieces]
    own_third, placed = last_parts((kept_x, kept_y), (second_x, second_y), placed)
    own_last = relay(own_third, 4)
    own_sums = (kept_x, second_x), (kept_y, second_y)
    d_sent_x, d_sent_y, d_kept_x, d_kept_y, part = produce(
        [after(got1[0], own_third), *got1[1:]], pieces_of(1), True, True, True, LONG
    )
    parts.append(part)
    own_rank = jnp.concatenate(parts, 1)
    shared = after(own_rank.astype(BF16), own_last)
    for mask in (1, 2, 3):
        own_rank = own_rank + partner(shared, mask)
    (c_sent_x, c_sent_y), c_kept = halve((c_kept_x, c_kept_y), (c_first_x, c_first_y))
    c_second_x, c_second_y = partner(c_sent_x, 2), partner(c_sent_y, 1)
    slot = own_rank, c_second_x, c_second_y
    d_first_x, d_first_y = partner(after(d_sent_x, *slot), 1), partner(after(d_sent_y, *slot), 2)
    shared = own_rank.astype(BF16)
    ranks = [(own_rank + partner(shared, 4)).astype(BF16)]
    for j in range(1, high_size):
        one, other = partner(shared, j * low_size), partner(shared, j * low_size + 4)
        ranks.append((one.astype(F32) + other.astype(F32)).astype(BF16))
    hiddens = [placed, partner(placed, 4)]
    for k in range(1, high_size):
        wanted = placed.reshape(micro_count, rank, tile_rows)
        wanted = lax.dynamic_slice_in_dim(wanted, (high ^ k) * rank_part, rank_part, 1)
        wanted = wanted.reshape(micro_count * rank_part, tile_rows)
        hiddens += [partner(wanted, k * low_size), partner(wanted, k * low_size + 4)]

    all_grads, all_pieces = [], []
    for grads, pieces in chunks:
        all_pieces += [(tile + len(all_grads), *rest) for tile, *rest in pieces]
        all_grads += grads
    up_map_gradient = pl.pallas_call(
        functools.partial(
            up_body, low_size, tile_rows, all_pieces, len(all_grads), micro_count
        ),
        in_specs=[SMEM] * 3 + [VMEM] * (len(all_grads) + 2 * high_size),
        out_specs=VMEM,
        out_shape=jax.ShapeDtypeStruct(up_tile.shape, BF16),
        scratch_shapes=[pltpu.VMEM(up_tile.shape, F32)],
        compiler_params=PARAMS,
        cost_estimate=LONG,
    )(*in_hbm(*scalars), *all_grads, *hiddens)

    def columns_of(j, piece):
        k, m, offset = piece
        at = order.index((k ^ j, m, offset))
        return slice(at * size, (at + 1) * size)

    down_parts = adapter_down_maps[0].reshape(class_count, high_size, rank_part, portion)

    def adapter_kernel(first, with_last, groups, *refs):
        pos_ref, classes_ref, _, down_ref = refs[:4]
        rank_refs = refs[4 : 4 + high_size]
        sum_refs = refs[4 + high_size : 4 + high_size + 2 * groups]
        *last_refs, out_ref, total_ref = refs[4 + high_size + 2 * groups :]
        own = pos_ref[0] // low_size
        start = 0
        for g in range(groups):
            kept_ref, second_ref = sum_refs[2 * g : 2 * g + 2]
            half, count = kept_ref.shape[0] // 2, kept_ref.shape[1]
            total_ref[:, start : start + count] = (
                kept_ref[:half, :] + second_ref[:half, :].astype(F32)
            )
            if with_last:
                last_refs[g][...] = (
                    kept_ref[half:, :] + second_ref[half : 2 * half, :].astype(F32)
                ).astype(BF16)
            start += count
        for at in range(start // size):
            piece = order[first + at]
            seg = segment_of(own, piece, tile_rows)
            rows = slice(at * size, (at + 1) * size)
            adapter = total_ref[:, rows]
            for j in range(high_size):
                adapter = adapter + lax.dot_general(
                    down_ref[classes_ref[piece[1], seg], own ^ j],
                    rank_refs[j][:, columns_of(j, piece)],
                    TN,
                    preferred_element_type=F32,
                )
            out_ref[:, rows] = adapter.astype(BF16)

    def with_adapter(sums, first, with_last):
        counts = [kept.shape[1] for kept, _ in sums]
        shapes = [(portion, n) for n in counts] * with_last + [(portion, sum(counts))]
        outs = pl.pallas_call(
            functools.partial(adapter_kernel, first, with_last, len(sums)),
            in_specs=[SMEM] * 3 + [VMEM] * (1 + high_size + 2 * len(sums)),
            out_specs=[VMEM] * len(shapes),
            out_shape=[jax.ShapeDtypeStruct(shape, BF16) for shape in shapes],
            scratch_shapes=[pltpu.VMEM(shapes[-1], F32)],
            compiler_params=PARAMS,
            cost_estimate=QUICK,
        )(*in_hbm(*scalars), *in_hbm(down_parts), *ranks, *[a for two in sums for a in two])
        return outs[:-1], outs[-1]

    def finish_kernel(first, groups, *refs):
        pos_ref, kept_ref = refs[:2]
        got_refs = refs[2 : 2 + groups]
        out_ref, total_ref, turned_ref, sem = refs[-4:]
        own = pos_ref[0] // low_size
        start = 0
        for got_ref in got_refs:
            count = got_ref.shape[1]
            total_ref[:, start : start + count] = (
                kept_ref[:, start : start + count].astype(F32) + got_ref[...].astype(F32)
            ).astype(BF16)
            start += count
        copies = []
        for at in range(start // size):
            k, m, offset = order[first + at]
            base = pl.multiple_of((own ^ k) * tile_rows + offset, size)
            rows = slice(at * size, (at + 1) * size)
            turned_ref[rows, :] = total_ref[:, rows].T
            copies.append(
                pltpu.make_async_copy(
                    turned_ref.at[rows, :], out_ref.at[m, pl.ds(base, size), :], sem.at[at]
                )
            )
            copies[-1].start()
        for copy in copies:
            copy.wait()

    def finish(kept, got, first, result):
        rows = kept.shape[1]
        shape = jax.ShapeDtypeStruct((micro_count, high_size * tile_rows, portion), BF16)
        hbm = pl.BlockSpec(memory_space=pltpu.HBM)
        before = [] if result is None else [result]
        return pl.pallas_call(
            functools.partial(finish_kernel, first, len(got)),
            in_specs=[SMEM] + [VMEM] * (1 + len(got)) + [hbm] * len(before),
            out_specs=hbm,
            out_shape=shape,
            input_output_aliases={2 + len(got): 0} if before else {},
            scratch_shapes=[
                pltpu.VMEM((portion, rows), BF16),
                pltpu.VMEM((rows, portion), BF16),
                pltpu.SemaphoreType.DMA((rows // size,)),
            ],
            compiler_params=PARAMS,
            cost_estimate=QUICK,
        )(*in_hbm(scalars[0]), kept, *got, *before)

    def down_kernel(pos_ref, classes_ref, live_ref, inputs_ref, *refs):
        rank_refs, out_ref, total_ref = refs[:-2], refs[-2], refs[-1]
        own = pos_ref[0] // low_size
        total_ref[...] = jnp.zeros_like(total_ref)
        for piece in order:
            k, m, offset = piece
            seg = segment_of(own, piece, tile_rows)

            @pl.when(seg < live_ref[m])
            def _():
                base = pl.multiple_of((own ^ k) * tile_rows + offset, size)
                rows = inputs_ref[m, pl.ds(base, size), :]
                for j in range(high_size):
                    total_ref[classes_ref[m, seg], own ^ j] += jnp.dot(
                        rank_refs[j][:, columns_of(j, piece)], rows, preferred_element_type=F32
                    )

        out_ref[...] = total_ref[...].astype(BF16)

    down_map_gradient = pl.pallas_call(
        down_kernel,
        in_specs=[SMEM] * 3 + [VMEM] * (1 + high_size),
        out_specs=VMEM,
        out_shape=jax.ShapeDtypeStruct(down_parts.shape, BF16),
        scratch_shapes=[pltpu.VMEM(down_parts.shape, F32)],
        compiler_params=PARAMS,
        cost_estimate=QUICK,
    )(*in_hbm(*scalars, forward_input[0]), *ranks)

    (c_third,) = last_parts(c_kept, (c_second_x, c_second_y))
    c_last = relay(c_third, 4)
    c_sums = (c_kept[0], c_second_x), (c_kept[1], c_second_y)
    _, kept = with_adapter(own_sums + c_sums, 0, False)
    early = relay(kept, 0)
    (d_sent_x, d_sent_y), d_kept = halve(
        (after(d_kept_x, c_last, *ranks), d_kept_y), (d_first_x, d_first_y)
    )
    d_second_x, d_second_y = partner(d_sent_x, 2), partner(d_sent_y, 4)

    d_kept_x = after(d_kept[0], down_map_gradient, kept)
    d_sums = (d_kept_x, d_second_x), (d_kept[1], d_second_y)
    d_lasts, d_kept = with_adapter(d_sums, kept.shape[1] // size, True)
    d_last = [relay(d_lasts[0], 4), relay(d_lasts[1], 1)]
    d_kept = relay(d_kept, 0)
    grad_prev = finish(early, [own_last, c_last], 0, None)
    grad_prev = finish(d_kept, d_last, kept.shape[1] // size, grad_prev)

    return (
        grad_prev[None],
        down_map_gradient.reshape(1, class_count, rank, portion),
        up_map_gradient[None, None],
    )


def solution(mesh):
    in_specs = (
        P("pipe", "tensor", None, None, None),
        P("pipe", None, None, "tensor"),
        P("pipe", None, "tensor", None),
        P("pipe", "tensor", None, None),
        P("pipe", None, None, "tensor"),
        P("pipe", "tensor", None, None, None),
        P("pipe", None, None),
        P("pipe", None),
    )
    out_specs = (
        P("pipe", None, None, "tensor"),
        P("pipe", None, None, "tensor"),
        P("pipe", "tensor", None, None, None),
    )
    return jax.shard_map(shards, mesh=mesh, in_specs=in_specs, out_specs=out_specs, check_vma=False)
```

```python
import functools

import jax
import jax.numpy as jnp
from jax import lax
from jax.experimental import pallas as pl
from jax.experimental.pallas import tpu as pltpu
from jax.sharding import PartitionSpec as P

SEG = 128
BF16 = jnp.bfloat16
F32 = jnp.float32
SMEM = pl.BlockSpec(memory_space=pltpu.SMEM)
VMEM = pl.BlockSpec(memory_space=pltpu.VMEM)
TN = (((0,), (0,)), ((), ()))
PARAMS = pltpu.CompilerParams(vmem_limit_bytes=24 * 2**20)
QUICK = pl.CostEstimate(flops=1000, bytes_accessed=1000, transcendentals=0)
LONG = pl.CostEstimate(flops=4 * 10**10, bytes_accessed=1000, transcendentals=0)


def partner(value, mask):
    pairs = [(source, source ^ mask) for source in range(lax.axis_size("tensor"))]
    return lax.ppermute(value, "tensor", pairs)


def relay(value, mask):
    sections, tiles = lax.axis_size("pipe"), lax.axis_size("tensor")
    pairs = [
        (p * tiles + t, (p - 1) % sections * tiles + (t ^ mask))
        for p in range(sections)
        for t in range(tiles)
    ]
    return lax.ppermute(value, ("pipe", "tensor"), pairs)


def segment_of(high, piece, tile_rows):
    k, _, offset = piece
    return ((high ^ k) * tile_rows + offset) // SEG


def product_body(low_size, tile_rows, pieces, tiles, half, turns, sends, keeps, with_hidden, *refs):
    pos_ref, classes_ref, live_ref = refs[:3]
    grad_refs = refs[3 : 3 + tiles]
    weight_hbm = refs[3 + tiles]
    rows_ref, weight_ref, sems = refs[-3:]
    rest = list(refs[4 + tiles : -3])
    up_ref = rest.pop(0) if keeps else None
    hidden_ref = rest.pop(0) if with_hidden else None
    sent_x, sent_y = (rest.pop(0), rest.pop(0)) if sends else (None, None)
    placed_ref = rest.pop(0) if with_hidden else None
    kept_x, kept_y, rank_ref = rest if keeps else (None, None, None)
    low, high = pos_ref[0] % low_size, pos_ref[0] // low_size
    total = rows_ref.shape[1]
    size = total // len(pieces)

    def weight_copy(block):
        return pltpu.make_async_copy(
            weight_hbm.at[block ^ low], weight_ref.at[block], sems.at[block]
        )

    jobs = []
    for x, y in ((1, 1), (1, 0), (0, 1), (0, 0)):
        to_x = (sent_x if x else kept_x, 2 * y, 1)
        to_y = (sent_y if y else kept_y, *((x, 2) if turns else (2 * x, 1)))
        start = 0 if to_x[0] is not None else half
        stop = total if to_y[0] is not None else half
        if start < stop:
            jobs.append((x + 2 * y, start, stop, to_x, to_y))
    for block, *_ in jobs:
        for z in range(2):
            weight_copy(block + 4 * z).start()

    if with_hidden:
        micro_count, count, rank = hidden_ref.shape
        spot = lax.broadcasted_iota(jnp.int32, (count, half), 1)
        row = lax.broadcasted_iota(jnp.int32, (count, half), 0)
        chosen = (spot == low * count + row).astype(F32).astype(BF16)
        for m in range(micro_count):
            placed = lax.dot_general(
                hidden_ref[m], chosen, TN, preferred_element_type=F32
            ).astype(BF16)
            placed_ref[m * rank : (m + 1) * rank, :] = placed
            start = sent_x.shape[0] - (micro_count - m) * rank
            sent_x[start : start + rank, :] = placed

    for at, (tile, index, piece, first) in enumerate(pieces):
        seg = segment_of(high, piece, tile_rows)
        alive = seg < live_ref[piece[1]]
        place = slice(at * size, (at + 1) * size)

        @pl.when(alive)
        def _():
            rows = grad_refs[tile][index, first : first + size, :].T
            rows_ref[:, place] = rows
            if keeps:
                up = up_ref[classes_ref[piece[1], seg]]
                rank_ref[:, place] = jnp.dot(up, rows, preferred_element_type=F32)

        @pl.when(jnp.logical_not(alive))
        def _():
            rows_ref[:, place] = jnp.zeros((rows_ref.shape[0], size), rows_ref.dtype)
            if keeps:
                rank_ref[:, place] = jnp.zeros((rank_ref.shape[0], size), F32)

    for block, start, stop, to_x, to_y in jobs:

        @pl.loop(0, 2)
        def _(z):
            weight_copy(block + 4 * z).wait()
            value = jnp.dot(
                weight_ref[block + 4 * z], rows_ref[:, start:stop], preferred_element_type=F32
            )
            for (ref, slot, step), part in (
                (to_x, value[:, : half - start]),
                (to_y, value[:, half - start :]),
            ):
                if ref is not None:
                    width = part.shape[0]
                    place = pl.ds(pl.multiple_of((slot + step * z) * width, width), width)
                    ref[place, :] = part.astype(ref.dtype)


def product(scalars, grads, pieces, tile_rows, weight_blocks, up_tile, low_size, turns, sends, keeps, cost, size, hidden=None):
    blocks, width, depth = weight_blocks.shape
    rows = len(pieces) * size
    half = rows // 2
    if rows > 128 and half % 128:
        half = half // 128 * 128 + 128
    outs = []
    extra = 0 if hidden is None else hidden.shape[0] * hidden.shape[2]
    for wanted, dtype in ((sends, BF16), (keeps, F32)):
        if wanted:
            for more, n in ((extra, half), (0, rows - half)):
                outs.append(jax.ShapeDtypeStruct((blocks // 2 * width + more, n), dtype))
    if extra:
        outs.append(jax.ShapeDtypeStruct((extra, half), BF16))
    if keeps:
        outs.append(jax.ShapeDtypeStruct((up_tile.shape[1], rows), F32))
    more = ([up_tile] if keeps else []) + ([] if hidden is None else [hidden])
    return pl.pallas_call(
        functools.partial(
            product_body, low_size, tile_rows, pieces, len(grads), half, turns, sends, keeps, extra > 0
        ),
        in_specs=[SMEM] * 3
        + [VMEM] * len(grads)
        + [pl.BlockSpec(memory_space=pltpu.HBM)]
        + [VMEM] * len(more),
        out_specs=[VMEM] * len(outs),
        out_shape=outs,
        scratch_shapes=[
            pltpu.VMEM((depth, rows), BF16),
            pltpu.VMEM(weight_blocks.shape, BF16),
            pltpu.SemaphoreType.DMA((blocks,)),
        ],
        compiler_params=PARAMS,
        cost_estimate=cost,
    )(*in_hbm(*scalars), *grads, *in_hbm(weight_blocks, *more))


def in_hbm(*arrays):
    return [pltpu.with_memory_space_constraint(array, pltpu.HBM) for array in arrays]


def after(value, *others):
    return lax.optimization_barrier((value, *others))[0]


def halve_kernel(ways, *refs):
    kept_refs, got_refs = refs[:ways], refs[ways : 2 * ways]
    placed_ref = refs[2 * ways] if len(refs) > 4 * ways else None
    outs = refs[-2 * ways - (placed_ref is not None) :]
    for way in range(ways):
        kept_ref, got_ref, sent_ref, rest_ref = kept_refs[way], got_refs[way], outs[way], outs[ways + way]
        half = kept_ref.shape[0] // 2
        sent_ref[:half, :] = (kept_ref[half:, :] + got_ref[half : 2 * half, :].astype(F32)).astype(BF16)
        rest_ref[...] = kept_ref[:half, :] + got_ref[:half, :].astype(F32)
        if way == 0 and placed_ref is not None:
            placed = placed_ref[...] + got_ref[2 * half :, :]
            sent_ref[half:, :] = placed
            outs[-1][...] = placed


def halve(kept, got, placed=None):
    placed = [] if placed is None else [placed]
    extra = [placed[0].shape[0] if placed and not way else 0 for way in range(len(kept))]
    shapes = [(k.shape[0] // 2, k.shape[1]) for k in kept]
    outs = pl.pallas_call(
        functools.partial(halve_kernel, len(kept)),
        in_specs=[VMEM] * (2 * len(kept) + len(placed)),
        out_specs=[VMEM] * (2 * len(kept) + len(placed)),
        out_shape=[jax.ShapeDtypeStruct((n + e, r), BF16) for (n, r), e in zip(shapes, extra)]
        + [jax.ShapeDtypeStruct(shape, F32) for shape in shapes]
        + [jax.ShapeDtypeStruct(p.shape, BF16) for p in placed],
        compiler_params=PARAMS,
        cost_estimate=QUICK,
    )(*kept, *got, *placed)
    ways = len(kept)
    return outs[:ways], outs[ways : 2 * ways], *outs[2 * ways :]


def last_kernel(ways, *refs):
    kept_refs, got_refs = refs[:ways], refs[ways : 2 * ways]
    placed_ref = refs[2 * ways] if len(refs) > 2 * ways + 1 else None
    out_ref = refs[2 * ways + (placed_ref is not None)]
    start = 0
    for kept_ref, got_ref in zip(kept_refs, got_refs):
        half, count = kept_ref.shape[0] // 2, kept_ref.shape[1]
        out_ref[:, start : start + count] = (
            kept_ref[half:, :] + got_ref[half : 2 * half, :].astype(F32)
        ).astype(BF16)
        start += count
    if placed_ref is not None:
        refs[-1][...] = placed_ref[...] + got_refs[0][2 * kept_refs[0].shape[0] // 2 :, :]


def last_parts(kept, got, placed=None):
    placed = [] if placed is None else [placed]
    shape = kept[0].shape[0] // 2, sum(k.shape[1] for k in kept)
    return pl.pallas_call(
        functools.partial(last_kernel, len(kept)),
        in_specs=[VMEM] * (2 * len(kept) + len(placed)),
        out_specs=[VMEM] * (1 + len(placed)),
        out_shape=[jax.ShapeDtypeStruct(shape, BF16)]
        + [jax.ShapeDtypeStruct(p.shape, BF16) for p in placed],
        compiler_params=PARAMS,
        cost_estimate=QUICK,
    )(*kept, *got, *placed)


def up_body(low_size, tile_rows, pieces, tiles, micro_count, *refs):
    pos_ref, classes_ref, live_ref = refs[:3]
    grad_refs = refs[3 : 3 + tiles]
    hidden_refs = refs[3 + tiles : -2]
    out_ref, total_ref = refs[-2:]
    high = pos_ref[0] // low_size
    total_ref[...] = jnp.zeros_like(total_ref)
    rank_part = total_ref.shape[1]
    for tile, index, piece, first in pieces:
        k, m, offset = piece
        size = min(SEG, tile_rows)
        seg = segment_of(high, piece, tile_rows)
        near_ref, far_ref = hidden_refs[2 * k : 2 * k + 2]
        start = m * (near_ref.shape[0] // micro_count)
        if k == 0:
            start = pl.multiple_of(start + high * rank_part, rank_part)

        @pl.when(seg < live_ref[m])
        def _():
            place = pl.ds(start, rank_part), slice(offset, offset + size)
            total_ref[classes_ref[m, seg]] += jnp.dot(
                near_ref[place] + far_ref[place],
                grad_refs[tile][index, first : first + size, :],
                preferred_element_type=F32,
            )

    out_ref[...] = total_ref[...].astype(BF16)


def shards(
    output_gradient,
    forward_input,
    saved_rank_outputs,
    projection_weight,
    adapter_down_maps,
    adapter_up_maps,
    segment_adapter_class,
    live_segment_table,
):
    grad_tile = output_gradient[0, 0]
    micro_count, tile_rows, tile_cols = grad_tile.shape
    up_tile = adapter_up_maps[0, 0]
    class_count, rank_part, _ = up_tile.shape
    rank, portion = adapter_down_maps.shape[2:]
    tiles = lax.axis_size("tensor")
    low_size = min(tiles, 8)
    high_size = tiles // low_size
    position = lax.axis_index("tensor")
    high = position // low_size
    weight_blocks = projection_weight[0, 0].reshape(low_size, portion, tile_cols)
    position, classes, live = lax.optimization_barrier(
        (position.astype(jnp.int32)[None], segment_adapter_class[0] + 0, live_segment_table[0] + 0)
    )
    scalars = position, classes, live
    position = position[0]
    size = min(SEG, tile_rows)
    offsets = range(0, tile_rows, size)

    own_pieces = [(0, m, (0, m, o), o) for m in range(micro_count) for o in offsets]

    def pieces_of(m, count=1):
        span = tile_rows // count
        return [
            ((k - 1) * count + o // span, 0, (k, m, o), o % span)
            for k in range(1, high_size)
            for o in offsets
        ]

    def produce(grads, pieces, turns, sends, keeps, cost, hidden=None):
        return product(
            scalars, grads, pieces, tile_rows, weight_blocks, up_tile, low_size, turns, sends, keeps,
            cost, size, hidden,
        )

    hidden = saved_rank_outputs[0]

    first_rows = lax.optimization_barrier(grad_tile[0])
    got0 = [partner(first_rows, k * low_size)[None] for k in range(1, high_size)]
    (own_grads,) = in_hbm(after(grad_tile, first_rows))
    sent_x, sent_y, placed = produce([own_grads], own_pieces, False, True, False, QUICK, hidden)
    first_x, first_y = partner(sent_x, 1), partner(sent_y, 2)
    (own_grads,) = in_hbm(after(grad_tile, sent_x, sent_y))
    kept_x, kept_y, part = produce([own_grads], own_pieces, False, False, True, QUICK)
    parts = [part]
    rows0 = after(got0[0], part), *got0[1:]
    c_sent_x, c_sent_y, c_kept_x, c_kept_y, part = produce(
        list(rows0), pieces_of(0), False, True, True, LONG
    )
    parts.append(part)
    second_rows = after(grad_tile[1], *got0)
    got1 = [partner(second_rows, k * low_size)[None] for k in range(1, high_size)]

    (sent_x, sent_y), (kept_x, kept_y), placed = halve(
        (after(kept_x, part), kept_y), (first_x, first_y), placed
    )
    second_x, second_y = partner(sent_x, 2), partner(sent_y, 1)
    c_first_x = partner(after(c_sent_x, sent_x, sent_y), 1)
    c_first_y = partner(after(c_sent_y, sent_x, sent_y), 2)

    chunks = [([grad_tile], own_pieces), (got0, pieces_of(0)), (got1, pieces_of(1))]
    order = [piece for _, pieces in chunks for _, _, piece, _ in pieces]
    d_sent_x, d_sent_y, d_kept_x, d_kept_y, part = produce(
        got1, pieces_of(1), True, True, True, LONG
    )
    parts.append(part)
    own_third, placed = last_parts((after(kept_x, part), kept_y), (second_x, second_y), placed)
    own_last = relay(own_third, 4)
    own_sums = (kept_x, second_x), (kept_y, second_y)
    own_rank = jnp.concatenate(parts, 1)
    shared = own_rank.astype(BF16)
    for mask in (1, 2, 3):
        own_rank = own_rank + partner(shared, mask)
    (c_sent_x, c_sent_y), c_kept = halve((c_kept_x, c_kept_y), (c_first_x, c_first_y))
    c_second_x, c_second_y = partner(c_sent_x, 2), partner(c_sent_y, 1)
    slot = own_rank, c_second_x, c_second_y
    d_sent_x, d_sent_y = lax.optimization_barrier((d_sent_x, d_sent_y, *slot))[:2]
    d_first_x, d_first_y = partner(d_sent_x, 1), partner(d_sent_y, 2)
    shared = after(own_rank.astype(BF16), own_last, d_sent_x)
    ranks = [(own_rank + partner(shared, 4)).astype(BF16)]
    for j in range(1, high_size):
        one, other = partner(shared, j * low_size), partner(shared, j * low_size + 4)
        ranks.append((one.astype(F32) + other.astype(F32)).astype(BF16))
    hiddens = [placed, partner(placed, 4)]
    for k in range(1, high_size):
        wanted = placed.reshape(micro_count, rank, tile_rows)
        wanted = lax.dynamic_slice_in_dim(wanted, (high ^ k) * rank_part, rank_part, 1)
        wanted = wanted.reshape(micro_count * rank_part, tile_rows)
        hiddens += [partner(wanted, k * low_size), partner(wanted, k * low_size + 4)]

    all_grads, all_pieces = [], []
    for grads, pieces in chunks:
        all_pieces += [(tile + len(all_grads), *rest) for tile, *rest in pieces]
        all_grads += grads
    up_map_gradient = pl.pallas_call(
        functools.partial(
            up_body, low_size, tile_rows, all_pieces, len(all_grads), micro_count
        ),
        in_specs=[SMEM] * 3 + [VMEM] * (len(all_grads) + 2 * high_size),
        out_specs=VMEM,
        out_shape=jax.ShapeDtypeStruct(up_tile.shape, BF16),
        scratch_shapes=[pltpu.VMEM(up_tile.shape, F32)],
        compiler_params=PARAMS,
        cost_estimate=LONG,
    )(*in_hbm(*scalars), *all_grads, *hiddens)

    def columns_of(j, piece):
        k, m, offset = piece
        at = order.index((k ^ j, m, offset))
        return slice(at * size, (at + 1) * size)

    down_parts = adapter_down_maps[0].reshape(class_count, high_size, rank_part, portion)

    def adapter_kernel(first, with_last, groups, *refs):
        pos_ref, classes_ref, _, down_ref = refs[:4]
        rank_refs = refs[4 : 4 + high_size]
        sum_refs = refs[4 + high_size : 4 + high_size + 2 * groups]
        *last_refs, out_ref, total_ref = refs[4 + high_size + 2 * groups :]
        own = pos_ref[0] // low_size
        start = 0
        for g in range(groups):
            kept_ref, second_ref = sum_refs[2 * g : 2 * g + 2]
            half, count = kept_ref.shape[0] // 2, kept_ref.shape[1]
            total_ref[:, start : start + count] = (
                kept_ref[:half, :] + second_ref[:half, :].astype(F32)
            )
            if with_last:
                last_refs[g][...] = (
                    kept_ref[half:, :] + second_ref[half : 2 * half, :].astype(F32)
                ).astype(BF16)
            start += count
        for at in range(start // size):
            piece = order[first + at]
            seg = segment_of(own, piece, tile_rows)
            rows = slice(at * size, (at + 1) * size)
            adapter = total_ref[:, rows]
            for j in range(high_size):
                adapter = adapter + lax.dot_general(
                    down_ref[classes_ref[piece[1], seg], own ^ j],
                    rank_refs[j][:, columns_of(j, piece)],
                    TN,
                    preferred_element_type=F32,
                )
            out_ref[:, rows] = adapter.astype(BF16)

    def with_adapter(sums, first, with_last):
        counts = [kept.shape[1] for kept, _ in sums]
        shapes = [(portion, n) for n in counts] * with_last + [(portion, sum(counts))]
        outs = pl.pallas_call(
            functools.partial(adapter_kernel, first, with_last, len(sums)),
            in_specs=[SMEM] * 3 + [VMEM] * (1 + high_size + 2 * len(sums)),
            out_specs=[VMEM] * len(shapes),
            out_shape=[jax.ShapeDtypeStruct(shape, BF16) for shape in shapes],
            scratch_shapes=[pltpu.VMEM(shapes[-1], F32)],
            compiler_params=PARAMS,
            cost_estimate=QUICK,
        )(*in_hbm(*scalars), *in_hbm(down_parts), *ranks, *[a for two in sums for a in two])
        return outs[:-1], outs[-1]

    def finish_kernel(first, groups, *refs):
        pos_ref, kept_ref = refs[:2]
        got_refs = refs[2 : 2 + groups]
        out_ref, total_ref, turned_ref, sem = refs[-4:]
        own = pos_ref[0] // low_size
        start = 0
        for got_ref in got_refs:
            count = got_ref.shape[1]
            total_ref[:, start : start + count] = (
                kept_ref[:, start : start + count].astype(F32) + got_ref[...].astype(F32)
            ).astype(BF16)
            start += count
        copies = []
        for at in range(start // size):
            k, m, offset = order[first + at]
            base = pl.multiple_of((own ^ k) * tile_rows + offset, size)
            rows = slice(at * size, (at + 1) * size)
            turned_ref[rows, :] = total_ref[:, rows].T
            copies.append(
                pltpu.make_async_copy(
                    turned_ref.at[rows, :], out_ref.at[m, pl.ds(base, size), :], sem.at[at]
                )
            )
            copies[-1].start()
        for copy in copies:
            copy.wait()

    def finish(kept, got, first, result):
        rows = kept.shape[1]
        shape = jax.ShapeDtypeStruct((micro_count, high_size * tile_rows, portion), BF16)
        hbm = pl.BlockSpec(memory_space=pltpu.HBM)
        before = [] if result is None else [result]
        return pl.pallas_call(
            functools.partial(finish_kernel, first, len(got)),
            in_specs=[SMEM] + [VMEM] * (1 + len(got)) + [hbm] * len(before),
            out_specs=hbm,
            out_shape=shape,
            input_output_aliases={2 + len(got): 0} if before else {},
            scratch_shapes=[
                pltpu.VMEM((portion, rows), BF16),
                pltpu.VMEM((rows, portion), BF16),
                pltpu.SemaphoreType.DMA((rows // size,)),
            ],
            compiler_params=PARAMS,
            cost_estimate=QUICK,
        )(*in_hbm(scalars[0]), kept, *got, *before)

    def down_kernel(pos_ref, classes_ref, live_ref, inputs_ref, *refs):
        rank_refs, out_ref, total_ref = refs[:-2], refs[-2], refs[-1]
        own = pos_ref[0] // low_size
        total_ref[...] = jnp.zeros_like(total_ref)
        for piece in order:
            k, m, offset = piece
            seg = segment_of(own, piece, tile_rows)

            @pl.when(seg < live_ref[m])
            def _():
                base = pl.multiple_of((own ^ k) * tile_rows + offset, size)
                rows = inputs_ref[m, pl.ds(base, size), :]
                for j in range(high_size):
                    total_ref[classes_ref[m, seg], own ^ j] += jnp.dot(
                        rank_refs[j][:, columns_of(j, piece)], rows, preferred_element_type=F32
                    )

        out_ref[...] = total_ref[...].astype(BF16)

    down_map_gradient = pl.pallas_call(
        down_kernel,
        in_specs=[SMEM] * 3 + [VMEM] * (1 + high_size),
        out_specs=VMEM,
        out_shape=jax.ShapeDtypeStruct(down_parts.shape, BF16),
        scratch_shapes=[pltpu.VMEM(down_parts.shape, F32)],
        compiler_params=PARAMS,
        cost_estimate=QUICK,
    )(*in_hbm(*scalars, forward_input[0]), *ranks)

    (c_third,) = last_parts(c_kept, (c_second_x, c_second_y))
    c_last = relay(c_third, 4)
    c_sums = (c_kept[0], c_second_x), (c_kept[1], c_second_y)
    _, kept = with_adapter(own_sums + c_sums, 0, False)
    early = relay(kept, 0)
    (d_sent_x, d_sent_y), d_kept = halve(
        (after(d_kept_x, c_last, *ranks), d_kept_y), (d_first_x, d_first_y)
    )
    d_second_x, d_second_y = partner(d_sent_x, 2), partner(d_sent_y, 4)

    d_kept_x = after(d_kept[0], down_map_gradient, kept)
    d_sums = (d_kept_x, d_second_x), (d_kept[1], d_second_y)
    d_lasts, d_kept = with_adapter(d_sums, kept.shape[1] // size, True)
    d_last = [relay(d_lasts[0], 4), relay(d_lasts[1], 1)]
    d_kept = relay(d_kept, 0)
    grad_prev = finish(early, [own_last, c_last], 0, None)
    grad_prev = finish(d_kept, d_last, kept.shape[1] // size, grad_prev)

    return (
        grad_prev[None],
        down_map_gradient.reshape(1, class_count, rank, portion),
        up_map_gradient[None, None],
    )


def solution(mesh):
    in_specs = (
        P("pipe", "tensor", None, None, None),
        P("pipe", None, None, "tensor"),
        P("pipe", None, "tensor", None),
        P("pipe", "tensor", None, None),
        P("pipe", None, None, "tensor"),
        P("pipe", "tensor", None, None, None),
        P("pipe", None, None),
        P("pipe", None),
    )
    out_specs = (
        P("pipe", None, None, "tensor"),
        P("pipe", None, None, "tensor"),
        P("pipe", "tensor", None, None, None),
    )
    return jax.shard_map(shards, mesh=mesh, in_specs=in_specs, out_specs=out_specs, check_vma=False)
```

```python
import functools

import jax
import jax.numpy as jnp
from jax import lax
from jax.experimental import pallas as pl
from jax.experimental.pallas import tpu as pltpu
from jax.sharding import PartitionSpec as P

SEG = 128
BF16 = jnp.bfloat16
F32 = jnp.float32
SMEM = pl.BlockSpec(memory_space=pltpu.SMEM)
VMEM = pl.BlockSpec(memory_space=pltpu.VMEM)
TN = (((0,), (0,)), ((), ()))
PARAMS = pltpu.CompilerParams(vmem_limit_bytes=12 * 2**20)
PRODUCT_PARAMS = pltpu.CompilerParams(vmem_limit_bytes=20 * 2**20)
QUICK = pl.CostEstimate(flops=1000, bytes_accessed=1000, transcendentals=0)
LONG = pl.CostEstimate(flops=4 * 10**10, bytes_accessed=1000, transcendentals=0)


def partner(value, mask):
    pairs = [(source, source ^ mask) for source in range(lax.axis_size("tensor"))]
    return lax.ppermute(value, "tensor", pairs)


def relay(value, mask):
    sections, tiles = lax.axis_size("pipe"), lax.axis_size("tensor")
    pairs = [
        (p * tiles + t, (p - 1) % sections * tiles + (t ^ mask))
        for p in range(sections)
        for t in range(tiles)
    ]
    return lax.ppermute(value, ("pipe", "tensor"), pairs)


def segment_of(high, piece, tile_rows):
    k, _, offset = piece
    return ((high ^ k) * tile_rows + offset) // SEG


def product_body(low_size, tile_rows, pieces, tiles, half, turns, sends, keeps, with_hidden, *refs):
    pos_ref, classes_ref, live_ref = refs[:3]
    grad_refs = refs[3 : 3 + tiles]
    weight_hbm = refs[3 + tiles]
    rows_ref, weight_ref, sems = refs[-3:]
    rest = list(refs[4 + tiles : -3])
    up_ref = rest.pop(0) if keeps else None
    hidden_ref = rest.pop(0) if with_hidden else None
    sent_x, sent_y = (rest.pop(0), rest.pop(0)) if sends else (None, None)
    placed_ref = rest.pop(0) if with_hidden else None
    kept_x, kept_y, rank_ref = rest if keeps else (None, None, None)
    low, high = pos_ref[0] % low_size, pos_ref[0] // low_size
    total = rows_ref.shape[1]
    size = total // len(pieces)

    def weight_copy(block):
        return pltpu.make_async_copy(
            weight_hbm.at[block ^ low], weight_ref.at[block], sems.at[block]
        )

    jobs = []
    for x, y in ((1, 1), (1, 0), (0, 1), (0, 0)):
        to_x = (sent_x if x else kept_x, 2 * y, 1)
        to_y = (sent_y if y else kept_y, *((x, 2) if turns else (2 * x, 1)))
        start = 0 if to_x[0] is not None else half
        stop = total if to_y[0] is not None else half
        if start < stop:
            jobs.append((x + 2 * y, start, stop, to_x, to_y))
    for block, *_ in jobs:
        for z in range(2):
            weight_copy(block + 4 * z).start()

    if with_hidden:
        micro_count, count, rank = hidden_ref.shape
        spot = lax.broadcasted_iota(jnp.int32, (count, half), 1)
        row = lax.broadcasted_iota(jnp.int32, (count, half), 0)
        chosen = (spot == low * count + row).astype(F32).astype(BF16)
        for m in range(micro_count):
            placed = lax.dot_general(
                hidden_ref[m], chosen, TN, preferred_element_type=F32
            ).astype(BF16)
            placed_ref[m * rank : (m + 1) * rank, :] = placed
            start = sent_x.shape[0] - (micro_count - m) * rank
            sent_x[start : start + rank, :] = placed

    for at, (tile, index, piece, first) in enumerate(pieces):
        seg = segment_of(high, piece, tile_rows)
        alive = seg < live_ref[piece[1]]
        place = slice(at * size, (at + 1) * size)

        @pl.when(alive)
        def _():
            rows = grad_refs[tile][index, first : first + size, :].T
            rows_ref[:, place] = rows
            if keeps:
                up = up_ref[classes_ref[piece[1], seg]]
                rank_ref[:, place] = jnp.dot(up, rows, preferred_element_type=F32)

        @pl.when(jnp.logical_not(alive))
        def _():
            rows_ref[:, place] = jnp.zeros((rows_ref.shape[0], size), rows_ref.dtype)
            if keeps:
                rank_ref[:, place] = jnp.zeros((rank_ref.shape[0], size), F32)

    for block, start, stop, to_x, to_y in jobs:

        @pl.loop(0, 2)
        def _(z):
            weight_copy(block + 4 * z).wait()
            value = jnp.dot(
                weight_ref[block + 4 * z], rows_ref[:, start:stop], preferred_element_type=F32
            )
            for (ref, slot, step), part in (
                (to_x, value[:, : half - start]),
                (to_y, value[:, half - start :]),
            ):
                if ref is not None:
                    width = part.shape[0]
                    place = pl.ds(pl.multiple_of((slot + step * z) * width, width), width)
                    ref[place, :] = part.astype(ref.dtype)


def product(scalars, grads, pieces, tile_rows, weight_blocks, up_tile, low_size, turns, sends, keeps, cost, size, hidden=None):
    blocks, width, depth = weight_blocks.shape
    rows = len(pieces) * size
    half = rows // 2
    if rows > 128 and half % 128:
        half = half // 128 * 128 + 128
    outs = []
    extra = 0 if hidden is None else hidden.shape[0] * hidden.shape[2]
    for wanted, dtype in ((sends, BF16), (keeps, F32)):
        if wanted:
            for more, n in ((extra, half), (0, rows - half)):
                outs.append(jax.ShapeDtypeStruct((blocks // 2 * width + more, n), dtype))
    if extra:
        outs.append(jax.ShapeDtypeStruct((extra, half), BF16))
    if keeps:
        outs.append(jax.ShapeDtypeStruct((up_tile.shape[1], rows), F32))
    more = ([up_tile] if keeps else []) + ([] if hidden is None else [hidden])
    return pl.pallas_call(
        functools.partial(
            product_body, low_size, tile_rows, pieces, len(grads), half, turns, sends, keeps, extra > 0
        ),
        in_specs=[SMEM] * 3
        + [VMEM] * len(grads)
        + [pl.BlockSpec(memory_space=pltpu.HBM)]
        + [VMEM] * len(more),
        out_specs=[VMEM] * len(outs),
        out_shape=outs,
        scratch_shapes=[
            pltpu.VMEM((depth, rows), BF16),
            pltpu.VMEM(weight_blocks.shape, BF16),
            pltpu.SemaphoreType.DMA((blocks,)),
        ],
        compiler_params=PRODUCT_PARAMS,
        cost_estimate=cost,
    )(*in_hbm(*scalars), *grads, *in_hbm(weight_blocks, *more))


def in_hbm(*arrays):
    return [pltpu.with_memory_space_constraint(array, pltpu.HBM) for array in arrays]


def after(value, *others):
    return lax.optimization_barrier((value, *others))[0]


def halve_kernel(ways, *refs):
    kept_refs, got_refs = refs[:ways], refs[ways : 2 * ways]
    placed_ref = refs[2 * ways] if len(refs) > 4 * ways else None
    outs = refs[-2 * ways - (placed_ref is not None) :]
    for way in range(ways):
        kept_ref, got_ref, sent_ref, rest_ref = kept_refs[way], got_refs[way], outs[way], outs[ways + way]
        half = kept_ref.shape[0] // 2
        sent_ref[:half, :] = (kept_ref[half:, :] + got_ref[half : 2 * half, :].astype(F32)).astype(BF16)
        rest_ref[...] = kept_ref[:half, :] + got_ref[:half, :].astype(F32)
        if way == 0 and placed_ref is not None:
            placed = placed_ref[...] + got_ref[2 * half :, :]
            sent_ref[half:, :] = placed
            outs[-1][...] = placed


def halve(kept, got, placed=None, cost=QUICK):
    placed = [] if placed is None else [placed]
    extra = [placed[0].shape[0] if placed and not way else 0 for way in range(len(kept))]
    shapes = [(k.shape[0] // 2, k.shape[1]) for k in kept]
    outs = pl.pallas_call(
        functools.partial(halve_kernel, len(kept)),
        in_specs=[VMEM] * (2 * len(kept) + len(placed)),
        out_specs=[VMEM] * (2 * len(kept) + len(placed)),
        out_shape=[jax.ShapeDtypeStruct((n + e, r), BF16) for (n, r), e in zip(shapes, extra)]
        + [jax.ShapeDtypeStruct(shape, F32) for shape in shapes]
        + [jax.ShapeDtypeStruct(p.shape, BF16) for p in placed],
        compiler_params=PARAMS,
        cost_estimate=cost,
    )(*kept, *got, *placed)
    ways = len(kept)
    return outs[:ways], outs[ways : 2 * ways], *outs[2 * ways :]


def last_kernel(ways, *refs):
    kept_refs, got_refs = refs[:ways], refs[ways : 2 * ways]
    placed_ref = refs[2 * ways] if len(refs) > 2 * ways + 1 else None
    out_ref = refs[2 * ways + (placed_ref is not None)]
    start = 0
    for kept_ref, got_ref in zip(kept_refs, got_refs):
        half, count = kept_ref.shape[0] // 2, kept_ref.shape[1]
        out_ref[:, start : start + count] = (
            kept_ref[half:, :] + got_ref[half : 2 * half, :].astype(F32)
        ).astype(BF16)
        start += count
    if placed_ref is not None:
        refs[-1][...] = placed_ref[...] + got_refs[0][2 * kept_refs[0].shape[0] // 2 :, :]


def last_parts(kept, got, placed=None, cost=QUICK):
    placed = [] if placed is None else [placed]
    shape = kept[0].shape[0] // 2, sum(k.shape[1] for k in kept)
    return pl.pallas_call(
        functools.partial(last_kernel, len(kept)),
        in_specs=[VMEM] * (2 * len(kept) + len(placed)),
        out_specs=[VMEM] * (1 + len(placed)),
        out_shape=[jax.ShapeDtypeStruct(shape, BF16)]
        + [jax.ShapeDtypeStruct(p.shape, BF16) for p in placed],
        compiler_params=PARAMS,
        cost_estimate=cost,
    )(*kept, *got, *placed)


def up_body(low_size, tile_rows, pieces, tiles, micro_count, *refs):
    pos_ref, classes_ref, live_ref = refs[:3]
    grad_refs = refs[3 : 3 + tiles]
    placed_ref, near_ref, *far_refs = refs[3 + tiles : -2]
    out_ref, total_ref = refs[-2:]
    high = pos_ref[0] // low_size
    total_ref[...] = jnp.zeros_like(total_ref)
    rank_part = total_ref.shape[1]
    skip = near_ref.shape[0] - placed_ref.shape[0]
    for tile, index, piece, first in pieces:
        k, m, offset = piece
        size = min(SEG, tile_rows)
        seg = segment_of(high, piece, tile_rows)
        lanes = slice(offset, offset + size)

        @pl.when(seg < live_ref[m])
        def _():
            if k == 0:
                start = pl.multiple_of(
                    m * (placed_ref.shape[0] // micro_count) + high * rank_part, rank_part
                )
                other = pl.multiple_of(skip + start, rank_part)
                hidden = (
                    placed_ref[pl.ds(start, rank_part), lanes]
                    + near_ref[pl.ds(other, rank_part), lanes]
                )
            else:
                rows = slice(skip + m * rank_part, skip + (m + 1) * rank_part)
                one_ref, other_ref = far_refs[2 * k - 2 : 2 * k]
                hidden = one_ref[rows, lanes] + other_ref[rows, lanes]
            total_ref[classes_ref[m, seg]] += jnp.dot(
                hidden,
                grad_refs[tile][index, first : first + size, :],
                preferred_element_type=F32,
            )

    out_ref[...] = total_ref[...].astype(BF16)


def shards(
    output_gradient,
    forward_input,
    saved_rank_outputs,
    projection_weight,
    adapter_down_maps,
    adapter_up_maps,
    segment_adapter_class,
    live_segment_table,
):
    grad_tile = output_gradient[0, 0]
    micro_count, tile_rows, tile_cols = grad_tile.shape
    up_tile = adapter_up_maps[0, 0]
    class_count, rank_part, _ = up_tile.shape
    rank, portion = adapter_down_maps.shape[2:]
    tiles = lax.axis_size("tensor")
    low_size = min(tiles, 8)
    high_size = tiles // low_size
    position = lax.axis_index("tensor")
    high = position // low_size
    weight_blocks = projection_weight[0, 0].reshape(low_size, portion, tile_cols)
    position, classes, live = lax.optimization_barrier(
        (position.astype(jnp.int32)[None], segment_adapter_class[0] + 0, live_segment_table[0] + 0)
    )
    scalars = position, classes, live
    position = position[0]
    size = min(SEG, tile_rows)
    offsets = range(0, tile_rows, size)

    own_pieces = [(0, m, (0, m, o), o) for m in range(micro_count) for o in offsets]

    def pieces_of(m, count=1):
        span = tile_rows // count
        return [
            ((k - 1) * count + o // span, 0, (k, m, o), o % span)
            for k in range(1, high_size)
            for o in offsets
        ]

    def produce(grads, pieces, turns, sends, keeps, cost, hidden=None):
        return product(
            scalars, grads, pieces, tile_rows, weight_blocks, up_tile, low_size, turns, sends, keeps,
            cost, size, hidden,
        )

    hidden = saved_rank_outputs[0]

    first_rows = lax.optimization_barrier(grad_tile[0])
    got0 = [partner(first_rows, k * low_size)[None] for k in range(1, high_size)]
    (own_grads,) = in_hbm(after(grad_tile, first_rows))
    sent_x, sent_y, placed = produce([own_grads], own_pieces, False, True, False, QUICK, hidden)
    first_x, first_y = partner(sent_x, 1), partner(sent_y, 2)
    (own_grads,) = in_hbm(after(grad_tile, sent_x, sent_y))
    kept_x, kept_y, part = produce([own_grads], own_pieces, False, False, True, QUICK)
    parts = [part]
    rows0 = after(got0[0], part), *got0[1:]
    c_sent_x, c_sent_y, c_kept_x, c_kept_y, part = produce(
        list(rows0), pieces_of(0), False, True, True, LONG
    )
    parts.append(part)
    second_rows = after(grad_tile[1], *got0)
    got1 = [partner(second_rows, k * low_size)[None] for k in range(1, high_size)]

    (sent_x, sent_y), (kept_x, kept_y), placed = halve(
        (after(kept_x, part), kept_y), (first_x, first_y), placed
    )
    second_x, second_y = partner(sent_x, 2), partner(sent_y, 1)
    c_first_x = partner(after(c_sent_x, sent_x, sent_y), 1)
    c_first_y = partner(after(c_sent_y, sent_x, sent_y), 2)

    chunks = [([grad_tile], own_pieces), (got0, pieces_of(0)), (got1, pieces_of(1))]
    order = [piece for _, pieces in chunks for _, _, piece, _ in pieces]
    d_sent_x, d_sent_y, d_kept_x, d_kept_y, part = produce(
        got1, pieces_of(1), True, True, True, LONG
    )
    parts.append(part)
    d_first_x, d_first_y = partner(d_sent_x, 1), partner(d_sent_y, 2)
    own_third, placed = last_parts(
        (after(kept_x, part, c_first_x, c_first_y), kept_y), (second_x, second_y), placed, LONG
    )
    own_last = relay(own_third, 4)
    own_sums = (kept_x, second_x), (kept_y, second_y)

    rows_total = len(order) * size
    blocks = rows_total // tile_rows

    def small(kernel, shapes, *operands, cost=QUICK):
        return pl.pallas_call(
            kernel,
            in_specs=[VMEM] * len(operands),
            out_specs=[VMEM] * len(shapes),
            out_shape=[jax.ShapeDtypeStruct(*shape) for shape in shapes],
            compiler_params=PARAMS,
            cost_estimate=cost,
        )(*operands)

    def collect_kernel(*refs):
        start = 0
        for ref in refs[:-1]:
            refs[-1][:, start : start + ref.shape[1]] = ref[...].astype(BF16)
            start += ref.shape[1]

    parts[-1] = after(parts[-1], own_third)
    (shared,) = small(collect_kernel, [((rank_part, rows_total), BF16)], *parts)
    flat = [partner(shared, mask) for mask in (1, 2, 3)]

    (c_sent_x, c_sent_y), c_kept = halve(
        (after(c_kept_x, shared), c_kept_y), (c_first_x, c_first_y), None, LONG
    )
    c_second_x, c_second_y = partner(c_sent_x, 2), partner(c_sent_y, 1)
    (d_sent_x, d_sent_y), d_kept = halve(
        (after(d_kept_x, c_sent_x), d_kept_y), (d_first_x, d_first_y)
    )
    d_second_x, d_second_y = partner(d_sent_x, 2), partner(d_sent_y, 4)

    wanted = placed.reshape(micro_count, rank, tile_rows)
    wanted = [
        lax.dynamic_slice_in_dim(wanted, (high ^ k) * rank_part, rank_part, 1).reshape(
            micro_count * rank_part, tile_rows
        )
        for k in range(1, high_size)
    ]

    def spread_kernel(*refs):
        count = len(parts)
        part_refs, flat_refs, hidden_refs = refs[:count], refs[count : count + 3], refs[count + 3 : -1 - high_size]
        *message_refs, total_ref = refs[-1 - high_size :]
        start = 0
        for part_ref in part_refs:
            columns = slice(start, start + part_ref.shape[1])
            total = part_ref[...]
            for flat_ref in flat_refs:
                total = total + flat_ref[:, columns].astype(F32)
            total_ref[:, columns] = total
            start += part_ref.shape[1]
        for message_ref, hidden_ref in zip(message_refs, hidden_refs):
            for block in range(blocks):
                message_ref[block * rank_part : (block + 1) * rank_part, :] = total_ref[
                    :, block * tile_rows : (block + 1) * tile_rows
                ].astype(BF16)
            message_ref[blocks * rank_part :, :] = hidden_ref[...]

    *messages, total = small(
        spread_kernel,
        [
            ((blocks * rank_part + hidden.shape[0], tile_rows), BF16)
            for hidden in [placed, *wanted]
        ]
        + [((rank_part, rows_total), F32)],
        *parts,
        *flat,
        after(placed, d_sent_x, own_last),
        *wanted,
        cost=LONG,
    )
    near = partner(messages[0], 4)
    far = []
    for k in range(1, high_size):
        far += [partner(messages[k], k * low_size), partner(messages[k], k * low_size + 4)]

    def columns_of(j, piece):
        k, m, offset = piece
        at = order.index((k ^ j, m, offset))
        return slice(at * size, (at + 1) * size)

    def block_of(message_ref, columns):
        block, start = columns.start // tile_rows, columns.start % tile_rows
        rows = slice(block * rank_part, (block + 1) * rank_part)
        return message_ref[rows, start : start + size].astype(F32)

    def lowrank_kernel(high_ref, total_ref, near_ref, *refs):
        *far_refs, out_ref, whole_ref = refs
        for at, piece in enumerate(order):
            columns = slice(at * size, (at + 1) * size)
            for j in range(high_size):
                if j == 0:
                    value = total_ref[:, columns] + block_of(near_ref, columns)
                else:
                    other = columns_of(j, piece)
                    value = block_of(far_refs[2 * j - 2], other) + block_of(far_refs[2 * j - 1], other)
                start = pl.multiple_of(((high_ref[0] // low_size) ^ j) * rank_part, rank_part)
                whole_ref[pl.ds(start, rank_part), columns] = value
        out_ref[...] = whole_ref[...].astype(BF16)

    lowrank = pl.pallas_call(
        lowrank_kernel,
        in_specs=[SMEM] + [VMEM] * (2 + len(far)),
        out_specs=VMEM,
        out_shape=jax.ShapeDtypeStruct((rank, rows_total), BF16),
        scratch_shapes=[pltpu.VMEM((rank, rows_total), F32)],
        compiler_params=PARAMS,
        cost_estimate=QUICK,
    )(*in_hbm(scalars[0]), total, near, *far)

    (c_third,) = last_parts((after(c_kept[0], lowrank), c_kept[1]), (c_second_x, c_second_y))
    c_last = relay(c_third, 4)

    all_grads, all_pieces = [], []
    for grads, pieces in chunks:
        all_pieces += [(tile + len(all_grads), *rest) for tile, *rest in pieces]
        all_grads += grads
    up_map_gradient = pl.pallas_call(
        functools.partial(
            up_body, low_size, tile_rows, all_pieces, len(all_grads), micro_count
        ),
        in_specs=[SMEM] * 3 + [VMEM] * (len(all_grads) + 2 * high_size),
        out_specs=VMEM,
        out_shape=jax.ShapeDtypeStruct(up_tile.shape, BF16),
        scratch_shapes=[pltpu.VMEM(up_tile.shape, F32)],
        compiler_params=PARAMS,
        cost_estimate=LONG,
    )(*in_hbm(*scalars), *all_grads, placed, near, *far)

    down = adapter_down_maps[0]

    def adapter_kernel(first, with_last, groups, *refs):
        pos_ref, classes_ref, _, down_ref, lowrank_ref = refs[:5]
        sum_refs = refs[5 : 5 + 2 * groups]
        *last_refs, out_ref, total_ref = refs[5 + 2 * groups :]
        own = pos_ref[0] // low_size
        start = 0
        for g in range(groups):
            kept_ref, second_ref = sum_refs[2 * g : 2 * g + 2]
            half, count = kept_ref.shape[0] // 2, kept_ref.shape[1]
            total_ref[:, start : start + count] = (
                kept_ref[:half, :] + second_ref[:half, :].astype(F32)
            )
            if with_last:
                last_refs[g][...] = (
                    kept_ref[half:, :] + second_ref[half : 2 * half, :].astype(F32)
                ).astype(BF16)
            start += count
        for at in range(start // size):
            piece = order[first + at]
            seg = segment_of(own, piece, tile_rows)
            rows = slice(at * size, (at + 1) * size)
            columns = slice((first + at) * size, (first + at + 1) * size)
            adapter = lax.dot_general(
                down_ref[classes_ref[piece[1], seg]],
                lowrank_ref[:, columns],
                TN,
                preferred_element_type=F32,
            )
            out_ref[:, rows] = (total_ref[:, rows] + adapter).astype(BF16)

    def with_adapter(sums, first, with_last):
        counts = [kept.shape[1] for kept, _ in sums]
        shapes = [(portion, n) for n in counts] * with_last + [(portion, sum(counts))]
        outs = pl.pallas_call(
            functools.partial(adapter_kernel, first, with_last, len(sums)),
            in_specs=[SMEM] * 3 + [VMEM] * (2 + 2 * len(sums)),
            out_specs=[VMEM] * len(shapes),
            out_shape=[jax.ShapeDtypeStruct(shape, BF16) for shape in shapes],
            scratch_shapes=[pltpu.VMEM(shapes[-1], F32)],
            compiler_params=PARAMS,
            cost_estimate=QUICK,
        )(*in_hbm(*scalars, down), lowrank, *[a for two in sums for a in two])
        return outs[:-1], outs[-1]

    def finish_kernel(first, groups, *refs):
        pos_ref, kept_ref = refs[:2]
        got_refs = refs[2 : 2 + groups]
        out_ref, total_ref, turned_ref, sem = refs[-4:]
        own = pos_ref[0] // low_size
        start = 0
        for got_ref in got_refs:
            count = got_ref.shape[1]
            total_ref[:, start : start + count] = (
                kept_ref[:, start : start + count].astype(F32) + got_ref[...].astype(F32)
            ).astype(BF16)
            start += count
        copies = []
        for at in range(start // size):
            k, m, offset = order[first + at]
            base = pl.multiple_of((own ^ k) * tile_rows + offset, size)
            rows = slice(at * size, (at + 1) * size)
            turned_ref[rows, :] = total_ref[:, rows].T
            copies.append(
                pltpu.make_async_copy(
                    turned_ref.at[rows, :], out_ref.at[m, pl.ds(base, size), :], sem.at[at]
                )
            )
            copies[-1].start()
        for copy in copies:
            copy.wait()

    def finish(kept, got, first, result):
        rows = kept.shape[1]
        shape = jax.ShapeDtypeStruct((micro_count, high_size * tile_rows, portion), BF16)
        hbm = pl.BlockSpec(memory_space=pltpu.HBM)
        before = [] if result is None else [result]
        return pl.pallas_call(
            functools.partial(finish_kernel, first, len(got)),
            in_specs=[SMEM] + [VMEM] * (1 + len(got)) + [hbm] * len(before),
            out_specs=hbm,
            out_shape=shape,
            input_output_aliases={2 + len(got): 0} if before else {},
            scratch_shapes=[
                pltpu.VMEM((portion, rows), BF16),
                pltpu.VMEM((rows, portion), BF16),
                pltpu.SemaphoreType.DMA((rows // size,)),
            ],
            compiler_params=PARAMS,
            cost_estimate=QUICK,
        )(*in_hbm(scalars[0]), kept, *got, *before)

    def down_kernel(pos_ref, classes_ref, live_ref, inputs_ref, lowrank_ref, out_ref, total_ref):
        own = pos_ref[0] // low_size
        total_ref[...] = jnp.zeros_like(total_ref)
        for at, piece in enumerate(order):
            k, m, offset = piece
            seg = segment_of(own, piece, tile_rows)

            @pl.when(seg < live_ref[m])
            def _():
                base = pl.multiple_of((own ^ k) * tile_rows + offset, size)
                total_ref[classes_ref[m, seg]] += jnp.dot(
                    lowrank_ref[:, at * size : (at + 1) * size],
                    inputs_ref[m, pl.ds(base, size), :],
                    preferred_element_type=F32,
                )

        out_ref[...] = total_ref[...].astype(BF16)

    down_map_gradient = pl.pallas_call(
        down_kernel,
        in_specs=[SMEM] * 3 + [VMEM] * 2,
        out_specs=VMEM,
        out_shape=jax.ShapeDtypeStruct(down.shape, BF16),
        scratch_shapes=[pltpu.VMEM(down.shape, F32)],
        compiler_params=PARAMS,
        cost_estimate=QUICK,
    )(*in_hbm(*scalars, forward_input[0]), lowrank)

    c_sums = (c_kept[0], c_second_x), (c_kept[1], c_second_y)
    _, kept = with_adapter(own_sums + c_sums, 0, False)
    early = relay(kept, 0)
    d_sums = (d_kept[0], d_second_x), (d_kept[1], d_second_y)
    d_lasts, d_kept = with_adapter(d_sums, kept.shape[1] // size, True)
    d_last = [relay(d_lasts[0], 4), relay(d_lasts[1], 1)]
    d_kept = relay(d_kept, 0)
    grad_prev = finish(early, [own_last, c_last], 0, None)
    grad_prev = finish(d_kept, d_last, kept.shape[1] // size, grad_prev)

    return (
        grad_prev[None],
        down_map_gradient[None],
        up_map_gradient[None, None],
    )


def solution(mesh):
    in_specs = (
        P("pipe", "tensor", None, None, None),
        P("pipe", None, None, "tensor"),
        P("pipe", None, "tensor", None),
        P("pipe", "tensor", None, None),
        P("pipe", None, None, "tensor"),
        P("pipe", "tensor", None, None, None),
        P("pipe", None, None),
        P("pipe", None),
    )
    out_specs = (
        P("pipe", None, None, "tensor"),
        P("pipe", None, None, "tensor"),
        P("pipe", "tensor", None, None, None),
    )
    return jax.shard_map(shards, mesh=mesh, in_specs=in_specs, out_specs=out_specs, check_vma=False)
```

```python
import functools

import jax
import jax.numpy as jnp
from jax import lax
from jax.experimental import pallas as pl
from jax.experimental.pallas import tpu as pltpu
from jax.sharding import PartitionSpec as P

SEG = 128
BF16 = jnp.bfloat16
F32 = jnp.float32
SMEM = pl.BlockSpec(memory_space=pltpu.SMEM)
VMEM = pl.BlockSpec(memory_space=pltpu.VMEM)
TN = (((0,), (0,)), ((), ()))
PARAMS = pltpu.CompilerParams(vmem_limit_bytes=16 * 2**20)
PRODUCT_PARAMS = pltpu.CompilerParams(vmem_limit_bytes=24 * 2**20)
QUICK = pl.CostEstimate(flops=1000, bytes_accessed=1000, transcendentals=0)
LONG = pl.CostEstimate(flops=4 * 10**10, bytes_accessed=1000, transcendentals=0)


def partner(value, mask):
    pairs = [(source, source ^ mask) for source in range(lax.axis_size("tensor"))]
    return lax.ppermute(value, "tensor", pairs)


def relay(value, mask):
    sections, tiles = lax.axis_size("pipe"), lax.axis_size("tensor")
    pairs = [
        (p * tiles + t, (p - 1) % sections * tiles + (t ^ mask))
        for p in range(sections)
        for t in range(tiles)
    ]
    return lax.ppermute(value, ("pipe", "tensor"), pairs)


def segment_of(high, piece, tile_rows):
    k, _, offset = piece
    return ((high ^ k) * tile_rows + offset) // SEG


def product_body(low_size, tile_rows, pieces, tiles, half, turns, sends, keeps, with_hidden, *refs):
    pos_ref, classes_ref, live_ref = refs[:3]
    grad_refs = refs[3 : 3 + tiles]
    weight_hbm = refs[3 + tiles]
    rows_ref, weight_ref, sems = refs[-3:]
    rest = list(refs[4 + tiles : -3])
    up_ref = rest.pop(0) if keeps else None
    hidden_ref = rest.pop(0) if with_hidden else None
    sent_x, sent_y = (rest.pop(0), rest.pop(0)) if sends else (None, None)
    placed_ref = rest.pop(0) if with_hidden else None
    kept_x, kept_y, rank_ref = rest if keeps else (None, None, None)
    low, high = pos_ref[0] % low_size, pos_ref[0] // low_size
    total = rows_ref.shape[1]
    size = total // len(pieces)

    def weight_copy(block):
        return pltpu.make_async_copy(
            weight_hbm.at[block ^ low], weight_ref.at[block], sems.at[block]
        )

    jobs = []
    for x, y in ((1, 1), (1, 0), (0, 1), (0, 0)):
        to_x = (sent_x if x else kept_x, 2 * y, 1)
        to_y = (sent_y if y else kept_y, *((x, 2) if turns else (2 * x, 1)))
        start = 0 if to_x[0] is not None else half
        stop = total if to_y[0] is not None else half
        if start < stop:
            jobs.append((x + 2 * y, start, stop, to_x, to_y))
    for block, *_ in jobs:
        for z in range(2):
            weight_copy(block + 4 * z).start()

    if with_hidden:
        micro_count, count, rank = hidden_ref.shape
        spot = lax.broadcasted_iota(jnp.int32, (count, half), 1)
        row = lax.broadcasted_iota(jnp.int32, (count, half), 0)
        chosen = (spot == low * count + row).astype(F32).astype(BF16)
        for m in range(micro_count):
            placed = lax.dot_general(
                hidden_ref[m], chosen, TN, preferred_element_type=F32
            ).astype(BF16)
            placed_ref[m * rank : (m + 1) * rank, :] = placed
            start = sent_x.shape[0] - (micro_count - m) * rank
            sent_x[start : start + rank, :] = placed

    for at, (tile, index, piece, first) in enumerate(pieces):
        seg = segment_of(high, piece, tile_rows)
        alive = seg < live_ref[piece[1]]
        place = slice(at * size, (at + 1) * size)

        @pl.when(alive)
        def _():
            rows = grad_refs[tile][index, first : first + size, :].T
            rows_ref[:, place] = rows
            if keeps:
                up = up_ref[classes_ref[piece[1], seg]]
                rank_ref[:, place] = jnp.dot(up, rows, preferred_element_type=F32)

        @pl.when(jnp.logical_not(alive))
        def _():
            rows_ref[:, place] = jnp.zeros((rows_ref.shape[0], size), rows_ref.dtype)
            if keeps:
                rank_ref[:, place] = jnp.zeros((rank_ref.shape[0], size), F32)

    for block, start, stop, to_x, to_y in jobs:

        @pl.loop(0, 2)
        def _(z):
            weight_copy(block + 4 * z).wait()
            value = jnp.dot(
                weight_ref[block + 4 * z], rows_ref[:, start:stop], preferred_element_type=F32
            )
            for (ref, slot, step), part in (
                (to_x, value[:, : half - start]),
                (to_y, value[:, half - start :]),
            ):
                if ref is not None:
                    width = part.shape[0]
                    place = pl.ds(pl.multiple_of((slot + step * z) * width, width), width)
                    ref[place, :] = part.astype(ref.dtype)


def product(scalars, grads, pieces, tile_rows, weight_blocks, up_tile, low_size, turns, sends, keeps, cost, size, hidden=None):
    blocks, width, depth = weight_blocks.shape
    rows = len(pieces) * size
    half = rows // 2
    if rows > 128 and half % 128:
        half = half // 128 * 128 + 128
    outs = []
    extra = 0 if hidden is None else hidden.shape[0] * hidden.shape[2]
    for wanted, dtype in ((sends, BF16), (keeps, F32)):
        if wanted:
            for more, n in ((extra, half), (0, rows - half)):
                outs.append(jax.ShapeDtypeStruct((blocks // 2 * width + more, n), dtype))
    if extra:
        outs.append(jax.ShapeDtypeStruct((extra, half), BF16))
    if keeps:
        outs.append(jax.ShapeDtypeStruct((up_tile.shape[1], rows), F32))
    more = ([up_tile] if keeps else []) + ([] if hidden is None else [hidden])
    return pl.pallas_call(
        functools.partial(
            product_body, low_size, tile_rows, pieces, len(grads), half, turns, sends, keeps, extra > 0
        ),
        in_specs=[SMEM] * 3
        + [VMEM] * len(grads)
        + [pl.BlockSpec(memory_space=pltpu.HBM)]
        + [VMEM] * len(more),
        out_specs=[VMEM] * len(outs),
        out_shape=outs,
        scratch_shapes=[
            pltpu.VMEM((depth, rows), BF16),
            pltpu.VMEM(weight_blocks.shape, BF16),
            pltpu.SemaphoreType.DMA((blocks,)),
        ],
        compiler_params=PRODUCT_PARAMS,
        cost_estimate=cost,
    )(*in_hbm(*scalars), *grads, *in_hbm(weight_blocks, *more))


def in_hbm(*arrays):
    return [pltpu.with_memory_space_constraint(array, pltpu.HBM) for array in arrays]


def after(value, *others):
    return lax.optimization_barrier((value, *others))[0]


def halve_kernel(ways, *refs):
    kept_refs, got_refs = refs[:ways], refs[ways : 2 * ways]
    placed_ref = refs[2 * ways] if len(refs) > 4 * ways else None
    outs = refs[-2 * ways - (placed_ref is not None) :]
    for way in range(ways):
        kept_ref, got_ref, sent_ref, rest_ref = kept_refs[way], got_refs[way], outs[way], outs[ways + way]
        half = kept_ref.shape[0] // 2
        sent_ref[:half, :] = (kept_ref[half:, :] + got_ref[half : 2 * half, :].astype(F32)).astype(BF16)
        rest_ref[...] = kept_ref[:half, :] + got_ref[:half, :].astype(F32)
        if way == 0 and placed_ref is not None:
            placed = placed_ref[...] + got_ref[2 * half :, :]
            sent_ref[half:, :] = placed
            outs[-1][...] = placed


def halve(kept, got, placed=None, cost=QUICK):
    placed = [] if placed is None else [placed]
    extra = [placed[0].shape[0] if placed and not way else 0 for way in range(len(kept))]
    shapes = [(k.shape[0] // 2, k.shape[1]) for k in kept]
    outs = pl.pallas_call(
        functools.partial(halve_kernel, len(kept)),
        in_specs=[VMEM] * (2 * len(kept) + len(placed)),
        out_specs=[VMEM] * (2 * len(kept) + len(placed)),
        out_shape=[jax.ShapeDtypeStruct((n + e, r), BF16) for (n, r), e in zip(shapes, extra)]
        + [jax.ShapeDtypeStruct(shape, F32) for shape in shapes]
        + [jax.ShapeDtypeStruct(p.shape, BF16) for p in placed],
        compiler_params=PARAMS,
        cost_estimate=cost,
    )(*kept, *got, *placed)
    ways = len(kept)
    return outs[:ways], outs[ways : 2 * ways], *outs[2 * ways :]


def last_kernel(ways, *refs):
    kept_refs, got_refs = refs[:ways], refs[ways : 2 * ways]
    placed_ref = refs[2 * ways] if len(refs) > 2 * ways + 1 else None
    out_ref = refs[2 * ways + (placed_ref is not None)]
    start = 0
    for kept_ref, got_ref in zip(kept_refs, got_refs):
        half, count = kept_ref.shape[0] // 2, kept_ref.shape[1]
        out_ref[:, start : start + count] = (
            kept_ref[half:, :] + got_ref[half : 2 * half, :].astype(F32)
        ).astype(BF16)
        start += count
    if placed_ref is not None:
        refs[-1][...] = placed_ref[...] + got_refs[0][2 * kept_refs[0].shape[0] // 2 :, :]


def last_parts(kept, got, placed=None, cost=QUICK):
    placed = [] if placed is None else [placed]
    shape = kept[0].shape[0] // 2, sum(k.shape[1] for k in kept)
    return pl.pallas_call(
        functools.partial(last_kernel, len(kept)),
        in_specs=[VMEM] * (2 * len(kept) + len(placed)),
        out_specs=[VMEM] * (1 + len(placed)),
        out_shape=[jax.ShapeDtypeStruct(shape, BF16)]
        + [jax.ShapeDtypeStruct(p.shape, BF16) for p in placed],
        compiler_params=PARAMS,
        cost_estimate=cost,
    )(*kept, *got, *placed)


def up_body(low_size, tile_rows, pieces, tiles, micro_count, *refs):
    pos_ref, classes_ref, live_ref = refs[:3]
    grad_refs = refs[3 : 3 + tiles]
    placed_ref, near_ref, *far_refs = refs[3 + tiles : -2]
    out_ref, total_ref = refs[-2:]
    high = pos_ref[0] // low_size
    total_ref[...] = jnp.zeros_like(total_ref)
    rank_part = total_ref.shape[1]
    skip = near_ref.shape[0] - placed_ref.shape[0]
    for tile, index, piece, first in pieces:
        k, m, offset = piece
        size = min(SEG, tile_rows)
        seg = segment_of(high, piece, tile_rows)
        lanes = slice(offset, offset + size)

        @pl.when(seg < live_ref[m])
        def _():
            if k == 0:
                start = pl.multiple_of(
                    m * (placed_ref.shape[0] // micro_count) + high * rank_part, rank_part
                )
                other = pl.multiple_of(skip + start, rank_part)
                hidden = (
                    placed_ref[pl.ds(start, rank_part), lanes]
                    + near_ref[pl.ds(other, rank_part), lanes]
                )
            else:
                rows = slice(skip + m * rank_part, skip + (m + 1) * rank_part)
                one_ref, other_ref = far_refs[2 * k - 2 : 2 * k]
                hidden = one_ref[rows, lanes] + other_ref[rows, lanes]
            total_ref[classes_ref[m, seg]] += jnp.dot(
                hidden,
                grad_refs[tile][index, first : first + size, :],
                preferred_element_type=F32,
            )

    out_ref[...] = total_ref[...].astype(BF16)


def shards(
    output_gradient,
    forward_input,
    saved_rank_outputs,
    projection_weight,
    adapter_down_maps,
    adapter_up_maps,
    segment_adapter_class,
    live_segment_table,
):
    grad_tile = output_gradient[0, 0]
    micro_count, tile_rows, tile_cols = grad_tile.shape
    up_tile = adapter_up_maps[0, 0]
    class_count, rank_part, _ = up_tile.shape
    rank, portion = adapter_down_maps.shape[2:]
    tiles = lax.axis_size("tensor")
    low_size = min(tiles, 8)
    high_size = tiles // low_size
    position = lax.axis_index("tensor")
    high = position // low_size
    weight_blocks = projection_weight[0, 0].reshape(low_size, portion, tile_cols)
    position, classes, live = lax.optimization_barrier(
        (position.astype(jnp.int32)[None], segment_adapter_class[0] + 0, live_segment_table[0] + 0)
    )
    scalars = position, classes, live
    position = position[0]
    size = min(SEG, tile_rows)
    offsets = range(0, tile_rows, size)

    own_pieces = [(0, m, (0, m, o), o) for m in range(micro_count) for o in offsets]

    def pieces_of(m, count=1):
        span = tile_rows // count
        return [
            ((k - 1) * count + o // span, 0, (k, m, o), o % span)
            for k in range(1, high_size)
            for o in offsets
        ]

    def produce(grads, pieces, turns, sends, keeps, cost, hidden=None):
        return product(
            scalars, grads, pieces, tile_rows, weight_blocks, up_tile, low_size, turns, sends, keeps,
            cost, size, hidden,
        )

    hidden = saved_rank_outputs[0]

    first_rows = lax.optimization_barrier(grad_tile[0])
    got0 = [partner(first_rows, k * low_size)[None] for k in range(1, high_size)]
    (own_grads,) = in_hbm(after(grad_tile, first_rows))
    sent_x, sent_y, placed = produce([own_grads], own_pieces, False, True, False, QUICK, hidden)
    first_x, first_y = partner(sent_x, 1), partner(sent_y, 2)
    (own_grads,) = in_hbm(after(grad_tile, sent_x, sent_y))
    kept_x, kept_y, part = produce([own_grads], own_pieces, False, False, True, QUICK)
    parts = [part]
    rows0 = after(got0[0], part), *got0[1:]
    c_sent_x, c_sent_y, c_kept_x, c_kept_y, part = produce(
        list(rows0), pieces_of(0), False, True, True, LONG
    )
    parts.append(part)
    second_rows = after(grad_tile[1], *got0)
    got1 = [partner(second_rows, k * low_size)[None] for k in range(1, high_size)]

    (sent_x, sent_y), (kept_x, kept_y), placed = halve(
        (after(kept_x, part), kept_y), (first_x, first_y), placed
    )
    second_x, second_y = partner(sent_x, 2), partner(sent_y, 1)
    c_first_x = partner(after(c_sent_x, sent_x, sent_y), 1)
    c_first_y = partner(after(c_sent_y, sent_x, sent_y), 2)

    chunks = [([grad_tile], own_pieces), (got0, pieces_of(0)), (got1, pieces_of(1))]
    order = [piece for _, pieces in chunks for _, _, piece, _ in pieces]
    d_sent_x, d_sent_y, d_kept_x, d_kept_y, part = produce(
        got1, pieces_of(1), True, True, True, LONG
    )
    parts.append(part)
    own_third, placed = last_parts((after(kept_x, part), kept_y), (second_x, second_y), placed)
    own_last = relay(own_third, 4)
    own_sums = (kept_x, second_x), (kept_y, second_y)

    rows_total = len(order) * size
    blocks = rows_total // tile_rows

    def small(kernel, shapes, *operands, cost=QUICK):
        return pl.pallas_call(
            kernel,
            in_specs=[VMEM] * len(operands),
            out_specs=[VMEM] * len(shapes),
            out_shape=[jax.ShapeDtypeStruct(*shape) for shape in shapes],
            compiler_params=PARAMS,
            cost_estimate=cost,
        )(*operands)

    def collect_kernel(*refs):
        start = 0
        for ref in refs[:-1]:
            refs[-1][:, start : start + ref.shape[1]] = ref[...].astype(BF16)
            start += ref.shape[1]

    (shared,) = small(collect_kernel, [((rank_part, rows_total), BF16)], *parts)
    flat = [partner(shared, mask) for mask in (1, 2, 3)]

    (c_sent_x, c_sent_y), c_kept = halve(
        (after(c_kept_x, shared), c_kept_y), (c_first_x, c_first_y)
    )
    c_second_x, c_second_y = partner(c_sent_x, 2), partner(c_sent_y, 1)

    wanted = placed.reshape(micro_count, rank, tile_rows)
    wanted = [
        lax.dynamic_slice_in_dim(wanted, (high ^ k) * rank_part, rank_part, 1).reshape(
            micro_count * rank_part, tile_rows
        )
        for k in range(1, high_size)
    ]

    def spread_kernel(*refs):
        count = len(parts)
        part_refs, flat_refs, hidden_refs = refs[:count], refs[count : count + 3], refs[count + 3 : -1 - high_size]
        *message_refs, total_ref = refs[-1 - high_size :]
        start = 0
        for part_ref in part_refs:
            columns = slice(start, start + part_ref.shape[1])
            total = part_ref[...]
            for flat_ref in flat_refs:
                total = total + flat_ref[:, columns].astype(F32)
            total_ref[:, columns] = total
            start += part_ref.shape[1]
        for message_ref, hidden_ref in zip(message_refs, hidden_refs):
            for block in range(blocks):
                message_ref[block * rank_part : (block + 1) * rank_part, :] = total_ref[
                    :, block * tile_rows : (block + 1) * tile_rows
                ].astype(BF16)
            message_ref[blocks * rank_part :, :] = hidden_ref[...]

    *messages, total = small(
        spread_kernel,
        [
            ((blocks * rank_part + hidden.shape[0], tile_rows), BF16)
            for hidden in [placed, *wanted]
        ]
        + [((rank_part, rows_total), F32)],
        *parts,
        *flat,
        placed,
        *wanted,
    )
    d_sent_x, d_sent_y, _ = lax.optimization_barrier(
        (d_sent_x, d_sent_y, total, c_second_x, c_second_y)
    )[:3]
    d_first_x, d_first_y = partner(d_sent_x, 1), partner(d_sent_y, 2)
    messages = lax.optimization_barrier((*messages, d_sent_x, own_last))[:high_size]
    near = partner(messages[0], 4)
    far = []
    for k in range(1, high_size):
        far += [partner(messages[k], k * low_size), partner(messages[k], k * low_size + 4)]

    def columns_of(j, piece):
        k, m, offset = piece
        at = order.index((k ^ j, m, offset))
        return slice(at * size, (at + 1) * size)

    def block_of(message_ref, columns):
        block, start = columns.start // tile_rows, columns.start % tile_rows
        rows = slice(block * rank_part, (block + 1) * rank_part)
        return message_ref[rows, start : start + size].astype(F32)

    def lowrank_kernel(high_ref, total_ref, near_ref, *refs):
        *far_refs, out_ref, whole_ref = refs
        for at, piece in enumerate(order):
            columns = slice(at * size, (at + 1) * size)
            for j in range(high_size):
                if j == 0:
                    value = total_ref[:, columns] + block_of(near_ref, columns)
                else:
                    other = columns_of(j, piece)
                    value = block_of(far_refs[2 * j - 2], other) + block_of(far_refs[2 * j - 1], other)
                start = pl.multiple_of(((high_ref[0] // low_size) ^ j) * rank_part, rank_part)
                whole_ref[pl.ds(start, rank_part), columns] = value
        out_ref[...] = whole_ref[...].astype(BF16)

    lowrank = pl.pallas_call(
        lowrank_kernel,
        in_specs=[SMEM] + [VMEM] * (2 + len(far)),
        out_specs=VMEM,
        out_shape=jax.ShapeDtypeStruct((rank, rows_total), BF16),
        scratch_shapes=[pltpu.VMEM((rank, rows_total), F32)],
        compiler_params=PARAMS,
        cost_estimate=QUICK,
    )(*in_hbm(scalars[0]), total, near, *far)

    (c_third,) = last_parts((after(c_kept[0], messages[0]), c_kept[1]), (c_second_x, c_second_y))
    c_last = relay(c_third, 4)

    all_grads, all_pieces = [], []
    for grads, pieces in chunks:
        all_pieces += [(tile + len(all_grads), *rest) for tile, *rest in pieces]
        all_grads += grads
    up_map_gradient = pl.pallas_call(
        functools.partial(
            up_body, low_size, tile_rows, all_pieces, len(all_grads), micro_count
        ),
        in_specs=[SMEM] * 3 + [VMEM] * (len(all_grads) + 2 * high_size),
        out_specs=VMEM,
        out_shape=jax.ShapeDtypeStruct(up_tile.shape, BF16),
        scratch_shapes=[pltpu.VMEM(up_tile.shape, F32)],
        compiler_params=PARAMS,
        cost_estimate=QUICK,
    )(*in_hbm(*scalars), *all_grads, placed, near, *far)

    down = adapter_down_maps[0]

    def adapter_kernel(first, with_last, groups, *refs):
        pos_ref, classes_ref, _, down_ref, lowrank_ref = refs[:5]
        sum_refs = refs[5 : 5 + 2 * groups]
        *last_refs, out_ref, total_ref = refs[5 + 2 * groups :]
        own = pos_ref[0] // low_size
        start = 0
        for g in range(groups):
            kept_ref, second_ref = sum_refs[2 * g : 2 * g + 2]
            half, count = kept_ref.shape[0] // 2, kept_ref.shape[1]
            total_ref[:, start : start + count] = (
                kept_ref[:half, :] + second_ref[:half, :].astype(F32)
            )
            if with_last:
                last_refs[g][...] = (
                    kept_ref[half:, :] + second_ref[half : 2 * half, :].astype(F32)
                ).astype(BF16)
            start += count
        for at in range(start // size):
            piece = order[first + at]
            seg = segment_of(own, piece, tile_rows)
            rows = slice(at * size, (at + 1) * size)
            columns = slice((first + at) * size, (first + at + 1) * size)
            adapter = lax.dot_general(
                down_ref[classes_ref[piece[1], seg]],
                lowrank_ref[:, columns],
                TN,
                preferred_element_type=F32,
            )
            out_ref[:, rows] = (total_ref[:, rows] + adapter).astype(BF16)

    def with_adapter(sums, first, with_last, cost):
        counts = [kept.shape[1] for kept, _ in sums]
        shapes = [(portion, n) for n in counts] * with_last + [(portion, sum(counts))]
        outs = pl.pallas_call(
            functools.partial(adapter_kernel, first, with_last, len(sums)),
            in_specs=[SMEM] * 3 + [VMEM] * (2 + 2 * len(sums)),
            out_specs=[VMEM] * len(shapes),
            out_shape=[jax.ShapeDtypeStruct(shape, BF16) for shape in shapes],
            scratch_shapes=[pltpu.VMEM(shapes[-1], F32)],
            compiler_params=PARAMS,
            cost_estimate=cost,
        )(*in_hbm(*scalars, down), lowrank, *[a for two in sums for a in two])
        return outs[:-1], outs[-1]

    def finish_kernel(first, groups, *refs):
        pos_ref, kept_ref = refs[:2]
        got_refs = refs[2 : 2 + groups]
        out_ref, total_ref, turned_ref, sem = refs[-4:]
        own = pos_ref[0] // low_size
        start = 0
        for got_ref in got_refs:
            count = got_ref.shape[1]
            total_ref[:, start : start + count] = (
                kept_ref[:, start : start + count].astype(F32) + got_ref[...].astype(F32)
            ).astype(BF16)
            start += count
        copies = []
        for at in range(start // size):
            k, m, offset = order[first + at]
            base = pl.multiple_of((own ^ k) * tile_rows + offset, size)
            rows = slice(at * size, (at + 1) * size)
            turned_ref[rows, :] = total_ref[:, rows].T
            copies.append(
                pltpu.make_async_copy(
                    turned_ref.at[rows, :], out_ref.at[m, pl.ds(base, size), :], sem.at[at]
                )
            )
            copies[-1].start()
        for copy in copies:
            copy.wait()

    def finish(kept, got, first, result):
        rows = kept.shape[1]
        shape = jax.ShapeDtypeStruct((micro_count, high_size * tile_rows, portion), BF16)
        hbm = pl.BlockSpec(memory_space=pltpu.HBM)
        before = [] if result is None else [result]
        return pl.pallas_call(
            functools.partial(finish_kernel, first, len(got)),
            in_specs=[SMEM] + [VMEM] * (1 + len(got)) + [hbm] * len(before),
            out_specs=hbm,
            out_shape=shape,
            input_output_aliases={2 + len(got): 0} if before else {},
            scratch_shapes=[
                pltpu.VMEM((portion, rows), BF16),
                pltpu.VMEM((rows, portion), BF16),
                pltpu.SemaphoreType.DMA((rows // size,)),
            ],
            compiler_params=PARAMS,
            cost_estimate=QUICK,
        )(*in_hbm(scalars[0]), kept, *got, *before)

    def down_kernel(pos_ref, classes_ref, live_ref, inputs_ref, lowrank_ref, out_ref, total_ref):
        own = pos_ref[0] // low_size
        total_ref[...] = jnp.zeros_like(total_ref)
        for at, piece in enumerate(order):
            k, m, offset = piece
            seg = segment_of(own, piece, tile_rows)

            @pl.when(seg < live_ref[m])
            def _():
                base = pl.multiple_of((own ^ k) * tile_rows + offset, size)
                total_ref[classes_ref[m, seg]] += jnp.dot(
                    lowrank_ref[:, at * size : (at + 1) * size],
                    inputs_ref[m, pl.ds(base, size), :],
                    preferred_element_type=F32,
                )

        out_ref[...] = total_ref[...].astype(BF16)

    down_map_gradient = pl.pallas_call(
        down_kernel,
        in_specs=[SMEM] * 3 + [VMEM] * 2,
        out_specs=VMEM,
        out_shape=jax.ShapeDtypeStruct(down.shape, BF16),
        scratch_shapes=[pltpu.VMEM(down.shape, F32)],
        compiler_params=PARAMS,
        cost_estimate=QUICK,
    )(*in_hbm(*scalars, forward_input[0]), lowrank)

    c_sums = (after(c_kept[0], c_third), c_second_x), (c_kept[1], c_second_y)
    _, kept = with_adapter(own_sums + c_sums, 0, False, QUICK)
    (d_sent_x, d_sent_y), d_kept = halve(
        (after(d_kept_x, up_map_gradient, kept), d_kept_y), (d_first_x, d_first_y)
    )
    d_second_x, d_second_y = partner(d_sent_x, 2), partner(d_sent_y, 4)

    early = relay(kept, 0)
    d_sums = (after(d_kept[0], down_map_gradient, c_last, early), d_second_x), (d_kept[1], d_second_y)
    d_lasts, d_kept = with_adapter(d_sums, kept.shape[1] // size, True, QUICK)
    d_last = [relay(d_lasts[0], 4), relay(d_lasts[1], 1)]
    d_kept = relay(d_kept, 0)
    grad_prev = finish(early, [own_last, c_last], 0, None)
    grad_prev = finish(d_kept, d_last, kept.shape[1] // size, grad_prev)

    return (
        grad_prev[None],
        down_map_gradient[None],
        up_map_gradient[None, None],
    )


def solution(mesh):
    in_specs = (
        P("pipe", "tensor", None, None, None),
        P("pipe", None, None, "tensor"),
        P("pipe", None, "tensor", None),
        P("pipe", "tensor", None, None),
        P("pipe", None, None, "tensor"),
        P("pipe", "tensor", None, None, None),
        P("pipe", None, None),
        P("pipe", None),
    )
    out_specs = (
        P("pipe", None, None, "tensor"),
        P("pipe", None, None, "tensor"),
        P("pipe", "tensor", None, None, None),
    )
    return jax.shard_map(shards, mesh=mesh, in_specs=in_specs, out_specs=out_specs, check_vma=False)
```

```python
import functools

import jax
import jax.numpy as jnp
from jax import lax
from jax.experimental import pallas as pl
from jax.experimental.pallas import tpu as pltpu
from jax.sharding import PartitionSpec as P

SEG = 128
BF16 = jnp.bfloat16
F32 = jnp.float32
SMEM = pl.BlockSpec(memory_space=pltpu.SMEM)
VMEM = pl.BlockSpec(memory_space=pltpu.VMEM)
TN = (((0,), (0,)), ((), ()))
PARAMS = pltpu.CompilerParams(vmem_limit_bytes=16 * 2**20)
PRODUCT_PARAMS = pltpu.CompilerParams(vmem_limit_bytes=24 * 2**20)
QUICK = pl.CostEstimate(flops=1000, bytes_accessed=1000, transcendentals=0)
LONG = pl.CostEstimate(flops=4 * 10**10, bytes_accessed=1000, transcendentals=0)


def partner(value, mask):
    pairs = [(source, source ^ mask) for source in range(lax.axis_size("tensor"))]
    return lax.ppermute(value, "tensor", pairs)


def relay(value, mask):
    sections, tiles = lax.axis_size("pipe"), lax.axis_size("tensor")
    pairs = [
        (p * tiles + t, (p - 1) % sections * tiles + (t ^ mask))
        for p in range(sections)
        for t in range(tiles)
    ]
    return lax.ppermute(value, ("pipe", "tensor"), pairs)


def segment_of(high, piece, tile_rows):
    k, _, offset = piece
    return ((high ^ k) * tile_rows + offset) // SEG


def product_body(low_size, tile_rows, pieces, tiles, half, turns, sends, keeps, with_hidden, *refs):
    pos_ref, classes_ref, live_ref = refs[:3]
    grad_refs = refs[3 : 3 + tiles]
    weight_hbm = refs[3 + tiles]
    rows_ref, weight_ref, sems = refs[-3:]
    rest = list(refs[4 + tiles : -3])
    up_ref = rest.pop(0) if keeps else None
    hidden_ref = rest.pop(0) if with_hidden else None
    sent_x, sent_y = (rest.pop(0), rest.pop(0)) if sends else (None, None)
    placed_ref = rest.pop(0) if with_hidden else None
    kept_x, kept_y, rank_ref = rest if keeps else (None, None, None)
    low, high = pos_ref[0] % low_size, pos_ref[0] // low_size
    total = rows_ref.shape[1]
    size = total // len(pieces)

    def weight_copy(block):
        return pltpu.make_async_copy(
            weight_hbm.at[block ^ low], weight_ref.at[block], sems.at[block]
        )

    jobs = []
    for x, y in ((1, 1), (1, 0), (0, 1), (0, 0)):
        to_x = (sent_x if x else kept_x, 2 * y, 1)
        to_y = (sent_y if y else kept_y, *((x, 2) if turns else (2 * x, 1)))
        start = 0 if to_x[0] is not None else half
        stop = total if to_y[0] is not None else half
        if start < stop:
            jobs.append((x + 2 * y, start, stop, to_x, to_y))
    for block, *_ in jobs:
        for z in range(2):
            weight_copy(block + 4 * z).start()

    if with_hidden:
        micro_count, count, rank = hidden_ref.shape
        spot = lax.broadcasted_iota(jnp.int32, (count, half), 1)
        row = lax.broadcasted_iota(jnp.int32, (count, half), 0)
        chosen = (spot == low * count + row).astype(F32).astype(BF16)
        for m in range(micro_count):
            placed = lax.dot_general(
                hidden_ref[m], chosen, TN, preferred_element_type=F32
            ).astype(BF16)
            placed_ref[m * rank : (m + 1) * rank, :] = placed
            start = sent_x.shape[0] - (micro_count - m) * rank
            sent_x[start : start + rank, :] = placed

    for at, (tile, index, piece, first) in enumerate(pieces):
        seg = segment_of(high, piece, tile_rows)
        alive = seg < live_ref[piece[1]]
        place = slice(at * size, (at + 1) * size)

        @pl.when(alive)
        def _():
            rows = grad_refs[tile][index, first : first + size, :].T
            rows_ref[:, place] = rows
            if keeps:
                up = up_ref[classes_ref[piece[1], seg]]
                rank_ref[:, place] = jnp.dot(up, rows, preferred_element_type=F32)

        @pl.when(jnp.logical_not(alive))
        def _():
            rows_ref[:, place] = jnp.zeros((rows_ref.shape[0], size), rows_ref.dtype)
            if keeps:
                rank_ref[:, place] = jnp.zeros((rank_ref.shape[0], size), F32)

    for block, start, stop, to_x, to_y in jobs:

        @pl.loop(0, 2)
        def _(z):
            weight_copy(block + 4 * z).wait()
            value = jnp.dot(
                weight_ref[block + 4 * z], rows_ref[:, start:stop], preferred_element_type=F32
            )
            for (ref, slot, step), part in (
                (to_x, value[:, : half - start]),
                (to_y, value[:, half - start :]),
            ):
                if ref is not None:
                    width = part.shape[0]
                    place = pl.ds(pl.multiple_of((slot + step * z) * width, width), width)
                    ref[place, :] = part.astype(ref.dtype)


def product(scalars, grads, pieces, tile_rows, weight_blocks, up_tile, low_size, turns, sends, keeps, cost, size, hidden=None):
    blocks, width, depth = weight_blocks.shape
    rows = len(pieces) * size
    half = rows // 2
    if rows > 128 and half % 128:
        half = half // 128 * 128 + 128
    outs = []
    extra = 0 if hidden is None else hidden.shape[0] * hidden.shape[2]
    for wanted, dtype in ((sends, BF16), (keeps, F32)):
        if wanted:
            for more, n in ((extra, half), (0, rows - half)):
                outs.append(jax.ShapeDtypeStruct((blocks // 2 * width + more, n), dtype))
    if extra:
        outs.append(jax.ShapeDtypeStruct((extra, half), BF16))
    if keeps:
        outs.append(jax.ShapeDtypeStruct((up_tile.shape[1], rows), F32))
    more = ([up_tile] if keeps else []) + ([] if hidden is None else [hidden])
    return pl.pallas_call(
        functools.partial(
            product_body, low_size, tile_rows, pieces, len(grads), half, turns, sends, keeps, extra > 0
        ),
        in_specs=[SMEM] * 3
        + [VMEM] * len(grads)
        + [pl.BlockSpec(memory_space=pltpu.HBM)]
        + [VMEM] * len(more),
        out_specs=[VMEM] * len(outs),
        out_shape=outs,
        scratch_shapes=[
            pltpu.VMEM((depth, rows), BF16),
            pltpu.VMEM(weight_blocks.shape, BF16),
            pltpu.SemaphoreType.DMA((blocks,)),
        ],
        compiler_params=PRODUCT_PARAMS,
        cost_estimate=cost,
    )(*in_hbm(*scalars), *grads, *in_hbm(weight_blocks, *more))


def in_hbm(*arrays):
    return [pltpu.with_memory_space_constraint(array, pltpu.HBM) for array in arrays]


def after(value, *others):
    return lax.optimization_barrier((value, *others))[0]


def halve_kernel(ways, *refs):
    kept_refs, got_refs = refs[:ways], refs[ways : 2 * ways]
    placed_ref = refs[2 * ways] if len(refs) > 4 * ways else None
    outs = refs[-2 * ways - (placed_ref is not None) :]
    for way in range(ways):
        kept_ref, got_ref, sent_ref, rest_ref = kept_refs[way], got_refs[way], outs[way], outs[ways + way]
        half = kept_ref.shape[0] // 2
        sent_ref[:half, :] = (kept_ref[half:, :] + got_ref[half : 2 * half, :].astype(F32)).astype(BF16)
        rest_ref[...] = kept_ref[:half, :] + got_ref[:half, :].astype(F32)
        if way == 0 and placed_ref is not None:
            placed = placed_ref[...] + got_ref[2 * half :, :]
            sent_ref[half:, :] = placed
            outs[-1][...] = placed


def halve(kept, got, placed=None, cost=QUICK):
    placed = [] if placed is None else [placed]
    extra = [placed[0].shape[0] if placed and not way else 0 for way in range(len(kept))]
    shapes = [(k.shape[0] // 2, k.shape[1]) for k in kept]
    outs = pl.pallas_call(
        functools.partial(halve_kernel, len(kept)),
        in_specs=[VMEM] * (2 * len(kept) + len(placed)),
        out_specs=[VMEM] * (2 * len(kept) + len(placed)),
        out_shape=[jax.ShapeDtypeStruct((n + e, r), BF16) for (n, r), e in zip(shapes, extra)]
        + [jax.ShapeDtypeStruct(shape, F32) for shape in shapes]
        + [jax.ShapeDtypeStruct(p.shape, BF16) for p in placed],
        compiler_params=PARAMS,
        cost_estimate=cost,
    )(*kept, *got, *placed)
    ways = len(kept)
    return outs[:ways], outs[ways : 2 * ways], *outs[2 * ways :]


def last_kernel(ways, *refs):
    kept_refs, got_refs = refs[:ways], refs[ways : 2 * ways]
    placed_ref = refs[2 * ways] if len(refs) > 2 * ways + 1 else None
    out_ref = refs[2 * ways + (placed_ref is not None)]
    start = 0
    for kept_ref, got_ref in zip(kept_refs, got_refs):
        half, count = kept_ref.shape[0] // 2, kept_ref.shape[1]
        out_ref[:, start : start + count] = (
            kept_ref[half:, :] + got_ref[half : 2 * half, :].astype(F32)
        ).astype(BF16)
        start += count
    if placed_ref is not None:
        refs[-1][...] = placed_ref[...] + got_refs[0][2 * kept_refs[0].shape[0] // 2 :, :]


def last_parts(kept, got, placed=None, cost=QUICK):
    placed = [] if placed is None else [placed]
    shape = kept[0].shape[0] // 2, sum(k.shape[1] for k in kept)
    return pl.pallas_call(
        functools.partial(last_kernel, len(kept)),
        in_specs=[VMEM] * (2 * len(kept) + len(placed)),
        out_specs=[VMEM] * (1 + len(placed)),
        out_shape=[jax.ShapeDtypeStruct(shape, BF16)]
        + [jax.ShapeDtypeStruct(p.shape, BF16) for p in placed],
        compiler_params=PARAMS,
        cost_estimate=cost,
    )(*kept, *got, *placed)


def up_body(low_size, tile_rows, pieces, tiles, micro_count, *refs):
    pos_ref, classes_ref, live_ref = refs[:3]
    grad_refs = refs[3 : 3 + tiles]
    placed_ref, near_ref, *far_refs = refs[3 + tiles : -2]
    out_ref, total_ref = refs[-2:]
    high = pos_ref[0] // low_size
    total_ref[...] = jnp.zeros_like(total_ref)
    rank_part = total_ref.shape[1]
    skip = near_ref.shape[0] - placed_ref.shape[0]
    for tile, index, piece, first in pieces:
        k, m, offset = piece
        size = min(SEG, tile_rows)
        seg = segment_of(high, piece, tile_rows)
        lanes = slice(offset, offset + size)

        @pl.when(seg < live_ref[m])
        def _():
            if k == 0:
                start = pl.multiple_of(
                    m * (placed_ref.shape[0] // micro_count) + high * rank_part, rank_part
                )
                other = pl.multiple_of(skip + start, rank_part)
                hidden = (
                    placed_ref[pl.ds(start, rank_part), lanes]
                    + near_ref[pl.ds(other, rank_part), lanes]
                )
            else:
                rows = slice(skip + m * rank_part, skip + (m + 1) * rank_part)
                one_ref, other_ref = far_refs[2 * k - 2 : 2 * k]
                hidden = one_ref[rows, lanes] + other_ref[rows, lanes]
            total_ref[classes_ref[m, seg]] += jnp.dot(
                hidden,
                grad_refs[tile][index, first : first + size, :],
                preferred_element_type=F32,
            )

    out_ref[...] = total_ref[...].astype(BF16)


def shards(
    output_gradient,
    forward_input,
    saved_rank_outputs,
    projection_weight,
    adapter_down_maps,
    adapter_up_maps,
    segment_adapter_class,
    live_segment_table,
):
    grad_tile = output_gradient[0, 0]
    micro_count, tile_rows, tile_cols = grad_tile.shape
    up_tile = adapter_up_maps[0, 0]
    class_count, rank_part, _ = up_tile.shape
    rank, portion = adapter_down_maps.shape[2:]
    tiles = lax.axis_size("tensor")
    low_size = min(tiles, 8)
    high_size = tiles // low_size
    position = lax.axis_index("tensor")
    high = position // low_size
    weight_blocks = projection_weight[0, 0].reshape(low_size, portion, tile_cols)
    position, classes, live = lax.optimization_barrier(
        (position.astype(jnp.int32)[None], segment_adapter_class[0] + 0, live_segment_table[0] + 0)
    )
    scalars = position, classes, live
    position = position[0]
    size = min(SEG, tile_rows)
    offsets = range(0, tile_rows, size)

    own_pieces = [(0, m, (0, m, o), o) for m in range(micro_count) for o in offsets]

    def pieces_of(m, count=1):
        span = tile_rows // count
        return [
            ((k - 1) * count + o // span, 0, (k, m, o), o % span)
            for k in range(1, high_size)
            for o in offsets
        ]

    def produce(grads, pieces, turns, sends, keeps, cost, hidden=None):
        return product(
            scalars, grads, pieces, tile_rows, weight_blocks, up_tile, low_size, turns, sends, keeps,
            cost, size, hidden,
        )

    hidden = saved_rank_outputs[0]

    first_rows = lax.optimization_barrier(grad_tile[0])
    got0 = [partner(first_rows, k * low_size)[None] for k in range(1, high_size)]
    (own_grads,) = in_hbm(after(grad_tile, first_rows))
    sent_x, sent_y, placed = produce([own_grads], own_pieces, False, True, False, QUICK, hidden)
    first_x, first_y = partner(sent_x, 1), partner(sent_y, 2)
    (own_grads,) = in_hbm(after(grad_tile, sent_x, sent_y))
    kept_x, kept_y, part = produce([own_grads], own_pieces, False, False, True, QUICK)
    parts = [part]
    rows0 = after(got0[0], part), *got0[1:]
    c_sent_x, c_sent_y, c_kept_x, c_kept_y, part = produce(
        list(rows0), pieces_of(0), False, True, True, LONG
    )
    parts.append(part)
    second_rows = after(grad_tile[1], *got0)
    got1 = [partner(second_rows, k * low_size)[None] for k in range(1, high_size)]

    (sent_x, sent_y), (kept_x, kept_y), placed = halve(
        (after(kept_x, part), kept_y), (first_x, first_y), placed
    )
    second_x, second_y = partner(sent_x, 2), partner(sent_y, 1)
    c_first_x = partner(after(c_sent_x, sent_x, sent_y), 1)
    c_first_y = partner(after(c_sent_y, sent_x, sent_y), 2)

    chunks = [([grad_tile], own_pieces), (got0, pieces_of(0)), (got1, pieces_of(1))]
    order = [piece for _, pieces in chunks for _, _, piece, _ in pieces]
    d_sent_x, d_sent_y, d_kept_x, d_kept_y, part = produce(
        got1, pieces_of(1), True, True, True, LONG
    )
    parts.append(part)
    own_third, placed = last_parts((after(kept_x, part), kept_y), (second_x, second_y), placed)
    own_last = relay(own_third, 4)
    own_sums = (kept_x, second_x), (kept_y, second_y)

    rows_total = len(order) * size
    blocks = rows_total // tile_rows

    def small(kernel, shapes, *operands, scratch=(), cost=QUICK):
        return pl.pallas_call(
            kernel,
            in_specs=[SMEM] + [VMEM] * len(operands),
            out_specs=[VMEM] * len(shapes),
            out_shape=[jax.ShapeDtypeStruct(*shape) for shape in shapes],
            scratch_shapes=list(scratch),
            compiler_params=PARAMS,
            cost_estimate=cost,
        )(*in_hbm(scalars[0]), *operands)

    def collect_kernel(pos_ref, *refs):
        part_refs, placed_ref = refs[: len(parts)], refs[len(parts)]
        *message_refs, wide_ref = refs[len(parts) + 1 :]
        own = pos_ref[0] // low_size
        block = 0
        for part_ref in part_refs:
            for start in range(0, part_ref.shape[1], tile_rows):
                value = part_ref[:, start : start + tile_rows].astype(BF16)
                for message_ref in message_refs:
                    message_ref[block * rank_part : (block + 1) * rank_part, :] = value
                block += 1
        wide_ref[...] = placed_ref[...].astype(F32)
        message_refs[0][block * rank_part :, :] = placed_ref[...]
        for k in range(1, high_size):
            for m in range(micro_count):
                start = pl.multiple_of(m * rank + (own ^ k) * rank_part, rank_part)
                first = (block + m) * rank_part
                message_refs[k][first : first + rank_part, :] = wide_ref[
                    pl.ds(start, rank_part), :
                ].astype(BF16)

    counts = [placed.shape[0]] + [micro_count * rank_part] * (high_size - 1)
    messages = small(
        collect_kernel,
        [((blocks * rank_part + n, tile_rows), BF16) for n in counts],
        *parts,
        placed,
        scratch=[pltpu.VMEM(placed.shape, F32)],
    )
    near = partner(messages[0], 4)
    far = []
    for k in range(1, high_size):
        far += [partner(messages[k], k * low_size), partner(messages[k], k * low_size + 4)]

    def columns_of(j, piece):
        k, m, offset = piece
        at = order.index((k ^ j, m, offset))
        return slice(at * size, (at + 1) * size)

    def block_of(message_ref, columns):
        block, start = columns.start // tile_rows, columns.start % tile_rows
        rows = slice(block * rank_part, (block + 1) * rank_part)
        return message_ref[rows, start : start + size].astype(F32)

    def lowrank_kernel(pos_ref, *refs):
        part_refs = refs[: len(parts)]
        near_ref, *far_refs = refs[len(parts) : -1]
        out_ref = refs[-1]
        whole = [(ref, start) for ref in part_refs for start in range(0, ref.shape[1], size)]
        for at, piece in enumerate(order):
            columns = slice(at * size, (at + 1) * size)
            for j in range(high_size):
                if j == 0:
                    part_ref, start = whole[at]
                    value = part_ref[:, start : start + size] + block_of(near_ref, columns)
                else:
                    other = columns_of(j, piece)
                    value = block_of(far_refs[2 * j - 2], other) + block_of(far_refs[2 * j - 1], other)
                start = pl.multiple_of(((pos_ref[0] // low_size) ^ j) * rank_part, rank_part)
                out_ref[pl.ds(start, rank_part), columns] = value

    (lowrank,) = small(lowrank_kernel, [((rank, rows_total), F32)], *parts, near, *far)

    halves = [range(0, len(order) // 2), range(len(order) // 2, len(order))]

    def riders(way, count):
        fit = count // size
        for i, at in enumerate(halves[way]):
            rows = slice(i // fit * rank, (i // fit + 1) * rank)
            yield rows, slice(i % fit * size, (i % fit + 1) * size), slice(at * size, (at + 1) * size)

    def riding(way, count):
        return -(-len(halves[way]) // (count // size)) * rank

    def ride(ref, first, way, lowrank_ref):
        for rows, there, whole in riders(way, ref.shape[1]):
            ref[first + rows.start : first + rows.stop, there] = lowrank_ref[:, whole].astype(BF16)

    def arrive(ref, first, way, lowrank_ref, out_ref):
        for rows, there, whole in riders(way, ref.shape[1]):
            got = ref[first + rows.start : first + rows.stop, there].astype(F32)
            out_ref[:, whole] = (lowrank_ref[:, whole] + got).astype(out_ref.dtype)

    def second_kernel(_, *refs):
        lowrank_ref = refs[4]
        for way in range(2):
            kept_ref, got_ref, sent_ref, rest_ref = refs[way], refs[2 + way], refs[5 + way], refs[7 + way]
            half = kept_ref.shape[0] // 2
            sent_ref[:half, :] = (kept_ref[half:, :] + got_ref[half:, :].astype(F32)).astype(BF16)
            rest_ref[...] = kept_ref[:half, :] + got_ref[:half, :].astype(F32)
            ride(sent_ref, half, way, lowrank_ref)

    c_counts = [c_kept_x.shape[1], c_kept_y.shape[1]]
    half_rows = c_kept_x.shape[0] // 2
    c_sent_x, c_sent_y, *c_kept = small(
        second_kernel,
        [((half_rows + riding(way, n), n), BF16) for way, n in enumerate(c_counts)]
        + [((half_rows, n), F32) for n in c_counts],
        c_kept_x,
        c_kept_y,
        c_first_x,
        c_first_y,
        lowrank,
    )
    c_second_x, c_second_y = partner(c_sent_x, 2), partner(c_sent_y, 1)

    def append_kernel(_, *refs):
        lowrank_ref = refs[4]
        next_ref = refs[7]
        for way in range(2):
            sent_ref, got_ref, out_ref = refs[way], refs[2 + way], refs[5 + way]
            out_ref[: 2 * half_rows, :] = sent_ref[...]
            arrive(got_ref, half_rows, way, lowrank_ref, next_ref)
            ride(out_ref, 2 * half_rows, way, next_ref)

    d_sent_x, d_sent_y, lowrank = small(
        append_kernel,
        [((2 * half_rows + riding(way, n), n), BF16) for way, n in enumerate(c_counts)]
        + [((rank, rows_total), F32)],
        d_sent_x,
        d_sent_y,
        c_second_x,
        c_second_y,
        lowrank,
    )
    d_first_x, d_first_y = partner(d_sent_x, 1), partner(d_sent_y, 2)

    all_grads, all_pieces = [], []
    for grads, pieces in chunks:
        all_pieces += [(tile + len(all_grads), *rest) for tile, *rest in pieces]
        all_grads += grads
    up_map_gradient = pl.pallas_call(
        functools.partial(
            up_body, low_size, tile_rows, all_pieces, len(all_grads), micro_count
        ),
        in_specs=[SMEM] * 3 + [VMEM] * (len(all_grads) + 2 * high_size),
        out_specs=VMEM,
        out_shape=jax.ShapeDtypeStruct(up_tile.shape, BF16),
        scratch_shapes=[pltpu.VMEM(up_tile.shape, F32)],
        compiler_params=PARAMS,
        cost_estimate=LONG,
    )(*in_hbm(*scalars), *all_grads, placed, near, *far)

    def third_kernel(_, *refs):
        lowrank_ref, whole_ref = refs[4], refs[9]
        for way in range(2):
            kept_ref, got_ref, sent_ref, rest_ref = refs[way], refs[2 + way], refs[5 + way], refs[7 + way]
            half = kept_ref.shape[0] // 2
            sent_ref[...] = (kept_ref[half:, :] + got_ref[half : 2 * half, :].astype(F32)).astype(BF16)
            rest_ref[...] = kept_ref[:half, :] + got_ref[:half, :].astype(F32)
            arrive(got_ref, 2 * half, way, lowrank_ref, whole_ref)

    d_sent_x, d_sent_y, *d_kept, lowrank = small(
        third_kernel,
        [((half_rows, n), dtype) for dtype in (BF16, F32) for n in c_counts]
        + [((rank, rows_total), BF16)],
        d_kept_x,
        after(d_kept_y, up_map_gradient, own_last),
        d_first_x,
        d_first_y,
        lowrank,
    )
    d_second_x, d_second_y = partner(d_sent_x, 2), partner(d_sent_y, 4)
    (c_third,) = last_parts((after(c_kept[0], d_sent_x), c_kept[1]), (c_second_x, c_second_y))
    c_last = relay(c_third, 4)

    down = adapter_down_maps[0]

    def adapter_kernel(first, with_last, groups, *refs):
        pos_ref, classes_ref, _, down_ref, lowrank_ref = refs[:5]
        sum_refs = refs[5 : 5 + 2 * groups]
        *last_refs, out_ref, total_ref = refs[5 + 2 * groups :]
        own = pos_ref[0] // low_size
        start = 0
        for g in range(groups):
            kept_ref, second_ref = sum_refs[2 * g : 2 * g + 2]
            half, count = kept_ref.shape[0] // 2, kept_ref.shape[1]
            total_ref[:, start : start + count] = (
                kept_ref[:half, :] + second_ref[:half, :].astype(F32)
            )
            if with_last:
                last_refs[g][...] = (
                    kept_ref[half:, :] + second_ref[half : 2 * half, :].astype(F32)
                ).astype(BF16)
            start += count
        for at in range(start // size):
            piece = order[first + at]
            seg = segment_of(own, piece, tile_rows)
            rows = slice(at * size, (at + 1) * size)
            columns = slice((first + at) * size, (first + at + 1) * size)
            adapter = lax.dot_general(
                down_ref[classes_ref[piece[1], seg]],
                lowrank_ref[:, columns],
                TN,
                preferred_element_type=F32,
            )
            out_ref[:, rows] = (total_ref[:, rows] + adapter).astype(BF16)

    def with_adapter(sums, first, with_last, cost):
        counts = [kept.shape[1] for kept, _ in sums]
        shapes = [(portion, n) for n in counts] * with_last + [(portion, sum(counts))]
        outs = pl.pallas_call(
            functools.partial(adapter_kernel, first, with_last, len(sums)),
            in_specs=[SMEM] * 3 + [VMEM] * (2 + 2 * len(sums)),
            out_specs=[VMEM] * len(shapes),
            out_shape=[jax.ShapeDtypeStruct(shape, BF16) for shape in shapes],
            scratch_shapes=[pltpu.VMEM(shapes[-1], F32)],
            compiler_params=PARAMS,
            cost_estimate=cost,
        )(*in_hbm(*scalars, down), lowrank, *[a for two in sums for a in two])
        return outs[:-1], outs[-1]

    def finish_kernel(first, groups, *refs):
        pos_ref, kept_ref = refs[:2]
        got_refs = refs[2 : 2 + groups]
        out_ref, total_ref, turned_ref, sem = refs[-4:]
        own = pos_ref[0] // low_size
        start = 0
        for got_ref in got_refs:
            count = got_ref.shape[1]
            total_ref[:, start : start + count] = (
                kept_ref[:, start : start + count].astype(F32) + got_ref[...].astype(F32)
            ).astype(BF16)
            start += count
        copies = []
        for at in range(start // size):
            k, m, offset = order[first + at]
            base = pl.multiple_of((own ^ k) * tile_rows + offset, size)
            rows = slice(at * size, (at + 1) * size)
            turned_ref[rows, :] = total_ref[:, rows].T
            copies.append(
                pltpu.make_async_copy(
                    turned_ref.at[rows, :], out_ref.at[m, pl.ds(base, size), :], sem.at[at]
                )
            )
            copies[-1].start()
        for copy in copies:
            copy.wait()

    def finish(kept, got, first, result):
        rows = kept.shape[1]
        shape = jax.ShapeDtypeStruct((micro_count, high_size * tile_rows, portion), BF16)
        hbm = pl.BlockSpec(memory_space=pltpu.HBM)
        before = [] if result is None else [result]
        return pl.pallas_call(
            functools.partial(finish_kernel, first, len(got)),
            in_specs=[SMEM] + [VMEM] * (1 + len(got)) + [hbm] * len(before),
            out_specs=hbm,
            out_shape=shape,
            input_output_aliases={2 + len(got): 0} if before else {},
            scratch_shapes=[
                pltpu.VMEM((portion, rows), BF16),
                pltpu.VMEM((rows, portion), BF16),
                pltpu.SemaphoreType.DMA((rows // size,)),
            ],
            compiler_params=PARAMS,
            cost_estimate=QUICK,
        )(*in_hbm(scalars[0]), kept, *got, *before)

    def down_kernel(pos_ref, classes_ref, live_ref, inputs_ref, lowrank_ref, out_ref, total_ref):
        own = pos_ref[0] // low_size
        total_ref[...] = jnp.zeros_like(total_ref)
        for at, piece in enumerate(order):
            k, m, offset = piece
            seg = segment_of(own, piece, tile_rows)

            @pl.when(seg < live_ref[m])
            def _():
                base = pl.multiple_of((own ^ k) * tile_rows + offset, size)
                total_ref[classes_ref[m, seg]] += jnp.dot(
                    lowrank_ref[:, at * size : (at + 1) * size],
                    inputs_ref[m, pl.ds(base, size), :],
                    preferred_element_type=F32,
                )

        out_ref[...] = total_ref[...].astype(BF16)

    down_map_gradient = pl.pallas_call(
        down_kernel,
        in_specs=[SMEM] * 3 + [VMEM] * 2,
        out_specs=VMEM,
        out_shape=jax.ShapeDtypeStruct(down.shape, BF16),
        scratch_shapes=[pltpu.VMEM(down.shape, F32)],
        compiler_params=PARAMS,
        cost_estimate=LONG,
    )(*in_hbm(*scalars, forward_input[0]), lowrank)

    c_sums = (after(c_kept[0], c_third, down_map_gradient), c_second_x), (c_kept[1], c_second_y)
    _, kept = with_adapter(own_sums + c_sums, 0, False, QUICK)
    early = relay(kept, 0)
    d_sums = (after(d_kept[0], kept), d_second_x), (d_kept[1], d_second_y)
    d_lasts, d_kept = with_adapter(d_sums, kept.shape[1] // size, True, QUICK)
    d_last = [relay(d_lasts[0], 4), relay(d_lasts[1], 1)]
    d_kept = relay(d_kept, 0)
    grad_prev = finish(early, [own_last, c_last], 0, None)
    grad_prev = finish(d_kept, d_last, kept.shape[1] // size, grad_prev)

    return (
        grad_prev[None],
        down_map_gradient[None],
        up_map_gradient[None, None],
    )


def solution(mesh):
    in_specs = (
        P("pipe", "tensor", None, None, None),
        P("pipe", None, None, "tensor"),
        P("pipe", None, "tensor", None),
        P("pipe", "tensor", None, None),
        P("pipe", None, None, "tensor"),
        P("pipe", "tensor", None, None, None),
        P("pipe", None, None),
        P("pipe", None),
    )
    out_specs = (
        P("pipe", None, None, "tensor"),
        P("pipe", None, None, "tensor"),
        P("pipe", "tensor", None, None, None),
    )
    return jax.shard_map(shards, mesh=mesh, in_specs=in_specs, out_specs=out_specs, check_vma=False)
```

```python
import functools

import jax
import jax.numpy as jnp
from jax import lax
from jax.experimental import pallas as pl
from jax.experimental.pallas import tpu as pltpu
from jax.sharding import PartitionSpec as P

SEG = 128
BF16 = jnp.bfloat16
F32 = jnp.float32
SMEM = pl.BlockSpec(memory_space=pltpu.SMEM)
VMEM = pl.BlockSpec(memory_space=pltpu.VMEM)
TN = (((0,), (0,)), ((), ()))
PARAMS = pltpu.CompilerParams(vmem_limit_bytes=16 * 2**20)
PRODUCT_PARAMS = pltpu.CompilerParams(vmem_limit_bytes=24 * 2**20)
QUICK = pl.CostEstimate(flops=1000, bytes_accessed=1000, transcendentals=0)
LONG = pl.CostEstimate(flops=4 * 10**10, bytes_accessed=1000, transcendentals=0)


def partner(value, mask):
    pairs = [(source, source ^ mask) for source in range(lax.axis_size("tensor"))]
    return lax.ppermute(value, "tensor", pairs)


def relay(value, mask):
    sections, tiles = lax.axis_size("pipe"), lax.axis_size("tensor")
    pairs = [
        (p * tiles + t, (p - 1) % sections * tiles + (t ^ mask))
        for p in range(sections)
        for t in range(tiles)
    ]
    return lax.ppermute(value, ("pipe", "tensor"), pairs)


def segment_of(high, piece, tile_rows):
    k, _, offset = piece
    return ((high ^ k) * tile_rows + offset) // SEG


def product_body(low_size, tile_rows, pieces, tiles, half, turns, sends, keeps, with_hidden, *refs):
    pos_ref, classes_ref, live_ref = refs[:3]
    grad_refs = refs[3 : 3 + tiles]
    weight_hbm = refs[3 + tiles]
    rows_ref, weight_ref, sems = refs[-3:]
    rest = list(refs[4 + tiles : -3])
    up_ref = rest.pop(0) if keeps else None
    hidden_ref = rest.pop(0) if with_hidden else None
    sent_x, sent_y = (rest.pop(0), rest.pop(0)) if sends else (None, None)
    placed_ref = rest.pop(0) if with_hidden else None
    kept_x, kept_y, rank_ref = rest if keeps else (None, None, None)
    low, high = pos_ref[0] % low_size, pos_ref[0] // low_size
    total = rows_ref.shape[1]
    size = total // len(pieces)

    def weight_copy(block):
        return pltpu.make_async_copy(
            weight_hbm.at[block ^ low], weight_ref.at[block], sems.at[block]
        )

    jobs = []
    for x, y in ((1, 1), (1, 0), (0, 1), (0, 0)):
        to_x = (sent_x if x else kept_x, 2 * y, 1)
        to_y = (sent_y if y else kept_y, *((x, 2) if turns else (2 * x, 1)))
        start = 0 if to_x[0] is not None else half
        stop = total if to_y[0] is not None else half
        if start < stop:
            jobs.append((x + 2 * y, start, stop, to_x, to_y))
    for block, *_ in jobs:
        for z in range(2):
            weight_copy(block + 4 * z).start()

    if with_hidden:
        micro_count, count, rank = hidden_ref.shape
        spot = lax.broadcasted_iota(jnp.int32, (count, half), 1)
        row = lax.broadcasted_iota(jnp.int32, (count, half), 0)
        chosen = (spot == low * count + row).astype(F32).astype(BF16)
        for m in range(micro_count):
            placed = lax.dot_general(
                hidden_ref[m], chosen, TN, preferred_element_type=F32
            ).astype(BF16)
            placed_ref[m * rank : (m + 1) * rank, :] = placed
            start = sent_x.shape[0] - (micro_count - m) * rank
            sent_x[start : start + rank, :] = placed

    for at, (tile, index, piece, first) in enumerate(pieces):
        seg = segment_of(high, piece, tile_rows)
        alive = seg < live_ref[piece[1]]
        place = slice(at * size, (at + 1) * size)

        @pl.when(alive)
        def _():
            rows = grad_refs[tile][index, first : first + size, :].T
            rows_ref[:, place] = rows
            if keeps:
                up = up_ref[classes_ref[piece[1], seg]]
                rank_ref[:, place] = jnp.dot(up, rows, preferred_element_type=F32)

        @pl.when(jnp.logical_not(alive))
        def _():
            rows_ref[:, place] = jnp.zeros((rows_ref.shape[0], size), rows_ref.dtype)
            if keeps:
                rank_ref[:, place] = jnp.zeros((rank_ref.shape[0], size), F32)

    for block, start, stop, to_x, to_y in jobs:

        @pl.loop(0, 2)
        def _(z):
            weight_copy(block + 4 * z).wait()
            value = jnp.dot(
                weight_ref[block + 4 * z], rows_ref[:, start:stop], preferred_element_type=F32
            )
            for (ref, slot, step), part in (
                (to_x, value[:, : half - start]),
                (to_y, value[:, half - start :]),
            ):
                if ref is not None:
                    width = part.shape[0]
                    place = pl.ds(pl.multiple_of((slot + step * z) * width, width), width)
                    ref[place, :] = part.astype(ref.dtype)


def product(scalars, grads, pieces, tile_rows, weight_blocks, up_tile, low_size, turns, sends, keeps, cost, size, hidden=None):
    blocks, width, depth = weight_blocks.shape
    rows = len(pieces) * size
    half = rows // 2
    if rows > 128 and half % 128:
        half = half // 128 * 128 + 128
    outs = []
    extra = 0 if hidden is None else hidden.shape[0] * hidden.shape[2]
    for wanted, dtype in ((sends, BF16), (keeps, F32)):
        if wanted:
            for more, n in ((extra, half), (0, rows - half)):
                outs.append(jax.ShapeDtypeStruct((blocks // 2 * width + more, n), dtype))
    if extra:
        outs.append(jax.ShapeDtypeStruct((extra, half), BF16))
    if keeps:
        outs.append(jax.ShapeDtypeStruct((up_tile.shape[1], rows), F32))
    more = ([up_tile] if keeps else []) + ([] if hidden is None else [hidden])
    return pl.pallas_call(
        functools.partial(
            product_body, low_size, tile_rows, pieces, len(grads), half, turns, sends, keeps, extra > 0
        ),
        in_specs=[SMEM] * 3
        + [VMEM] * len(grads)
        + [pl.BlockSpec(memory_space=pltpu.HBM)]
        + [VMEM] * len(more),
        out_specs=[VMEM] * len(outs),
        out_shape=outs,
        scratch_shapes=[
            pltpu.VMEM((depth, rows), BF16),
            pltpu.VMEM(weight_blocks.shape, BF16),
            pltpu.SemaphoreType.DMA((blocks,)),
        ],
        compiler_params=PRODUCT_PARAMS,
        cost_estimate=cost,
    )(*in_hbm(*scalars), *grads, *in_hbm(weight_blocks, *more))


def in_hbm(*arrays):
    return [pltpu.with_memory_space_constraint(array, pltpu.HBM) for array in arrays]


def after(value, *others):
    return lax.optimization_barrier((value, *others))[0]


def halve_kernel(ways, *refs):
    kept_refs, got_refs = refs[:ways], refs[ways : 2 * ways]
    placed_ref = refs[2 * ways] if len(refs) > 4 * ways else None
    outs = refs[-2 * ways - (placed_ref is not None) :]
    for way in range(ways):
        kept_ref, got_ref, sent_ref, rest_ref = kept_refs[way], got_refs[way], outs[way], outs[ways + way]
        half = kept_ref.shape[0] // 2
        sent_ref[:half, :] = (kept_ref[half:, :] + got_ref[half : 2 * half, :].astype(F32)).astype(BF16)
        rest_ref[...] = kept_ref[:half, :] + got_ref[:half, :].astype(F32)
        if way == 0 and placed_ref is not None:
            placed = placed_ref[...] + got_ref[2 * half :, :]
            sent_ref[half:, :] = placed
            outs[-1][...] = placed


def halve(kept, got, placed=None, cost=QUICK):
    placed = [] if placed is None else [placed]
    extra = [placed[0].shape[0] if placed and not way else 0 for way in range(len(kept))]
    shapes = [(k.shape[0] // 2, k.shape[1]) for k in kept]
    outs = pl.pallas_call(
        functools.partial(halve_kernel, len(kept)),
        in_specs=[VMEM] * (2 * len(kept) + len(placed)),
        out_specs=[VMEM] * (2 * len(kept) + len(placed)),
        out_shape=[jax.ShapeDtypeStruct((n + e, r), BF16) for (n, r), e in zip(shapes, extra)]
        + [jax.ShapeDtypeStruct(shape, F32) for shape in shapes]
        + [jax.ShapeDtypeStruct(p.shape, BF16) for p in placed],
        compiler_params=PARAMS,
        cost_estimate=cost,
    )(*kept, *got, *placed)
    ways = len(kept)
    return outs[:ways], outs[ways : 2 * ways], *outs[2 * ways :]


def last_kernel(ways, *refs):
    kept_refs, got_refs = refs[:ways], refs[ways : 2 * ways]
    placed_ref = refs[2 * ways] if len(refs) > 2 * ways + 1 else None
    out_ref = refs[2 * ways + (placed_ref is not None)]
    start = 0
    for kept_ref, got_ref in zip(kept_refs, got_refs):
        half, count = kept_ref.shape[0] // 2, kept_ref.shape[1]
        out_ref[:, start : start + count] = (
            kept_ref[half:, :] + got_ref[half : 2 * half, :].astype(F32)
        ).astype(BF16)
        start += count
    if placed_ref is not None:
        refs[-1][...] = placed_ref[...] + got_refs[0][2 * kept_refs[0].shape[0] // 2 :, :]


def last_parts(kept, got, placed=None, cost=QUICK):
    placed = [] if placed is None else [placed]
    shape = kept[0].shape[0] // 2, sum(k.shape[1] for k in kept)
    return pl.pallas_call(
        functools.partial(last_kernel, len(kept)),
        in_specs=[VMEM] * (2 * len(kept) + len(placed)),
        out_specs=[VMEM] * (1 + len(placed)),
        out_shape=[jax.ShapeDtypeStruct(shape, BF16)]
        + [jax.ShapeDtypeStruct(p.shape, BF16) for p in placed],
        compiler_params=PARAMS,
        cost_estimate=cost,
    )(*kept, *got, *placed)


def up_body(low_size, tile_rows, pieces, tiles, micro_count, *refs):
    pos_ref, classes_ref, live_ref = refs[:3]
    grad_refs = refs[3 : 3 + tiles]
    placed_ref, near_ref, *far_refs = refs[3 + tiles : -2]
    out_ref, total_ref = refs[-2:]
    high = pos_ref[0] // low_size
    total_ref[...] = jnp.zeros_like(total_ref)
    rank_part = total_ref.shape[1]
    skip = near_ref.shape[0] - placed_ref.shape[0]
    for tile, index, piece, first in pieces:
        k, m, offset = piece
        size = min(SEG, tile_rows)
        seg = segment_of(high, piece, tile_rows)
        lanes = slice(offset, offset + size)

        @pl.when(seg < live_ref[m])
        def _():
            if k == 0:
                start = pl.multiple_of(
                    m * (placed_ref.shape[0] // micro_count) + high * rank_part, rank_part
                )
                other = pl.multiple_of(skip + start, rank_part)
                hidden = (
                    placed_ref[pl.ds(start, rank_part), lanes]
                    + near_ref[pl.ds(other, rank_part), lanes]
                )
            else:
                rows = slice(skip + m * rank_part, skip + (m + 1) * rank_part)
                one_ref, other_ref = far_refs[2 * k - 2 : 2 * k]
                hidden = one_ref[rows, lanes] + other_ref[rows, lanes]
            total_ref[classes_ref[m, seg]] += jnp.dot(
                hidden,
                grad_refs[tile][index, first : first + size, :],
                preferred_element_type=F32,
            )

    out_ref[...] = total_ref[...].astype(BF16)


def shards(
    output_gradient,
    forward_input,
    saved_rank_outputs,
    projection_weight,
    adapter_down_maps,
    adapter_up_maps,
    segment_adapter_class,
    live_segment_table,
):
    grad_tile = output_gradient[0, 0]
    micro_count, tile_rows, tile_cols = grad_tile.shape
    up_tile = adapter_up_maps[0, 0]
    class_count, rank_part, _ = up_tile.shape
    rank, portion = adapter_down_maps.shape[2:]
    tiles = lax.axis_size("tensor")
    low_size = min(tiles, 8)
    high_size = tiles // low_size
    position = lax.axis_index("tensor")
    high = position // low_size
    weight_blocks = projection_weight[0, 0].reshape(low_size, portion, tile_cols)
    position, classes, live = lax.optimization_barrier(
        (position.astype(jnp.int32)[None], segment_adapter_class[0] + 0, live_segment_table[0] + 0)
    )
    scalars = position, classes, live
    position = position[0]
    size = min(SEG, tile_rows)
    offsets = range(0, tile_rows, size)

    own_pieces = [(0, m, (0, m, o), o) for m in range(micro_count) for o in offsets]

    def pieces_of(m, count=1):
        span = tile_rows // count
        return [
            ((k - 1) * count + o // span, 0, (k, m, o), o % span)
            for k in range(1, high_size)
            for o in offsets
        ]

    def produce(grads, pieces, turns, sends, keeps, cost, hidden=None):
        return product(
            scalars, grads, pieces, tile_rows, weight_blocks, up_tile, low_size, turns, sends, keeps,
            cost, size, hidden,
        )

    hidden = saved_rank_outputs[0]

    first_rows = lax.optimization_barrier(grad_tile[0])
    got0 = [partner(first_rows, k * low_size)[None] for k in range(1, high_size)]
    (own_grads,) = in_hbm(after(grad_tile, first_rows))
    sent_x, sent_y, placed = produce([own_grads], own_pieces, False, True, False, QUICK, hidden)
    first_x, first_y = partner(sent_x, 1), partner(sent_y, 2)
    (own_grads,) = in_hbm(after(grad_tile, sent_x, sent_y))
    kept_x, kept_y, part = produce([own_grads], own_pieces, False, False, True, QUICK)
    parts = [part]
    rows0 = after(got0[0], part), *got0[1:]
    c_sent_x, c_sent_y, c_kept_x, c_kept_y, part = produce(
        list(rows0), pieces_of(0), False, True, True, LONG
    )
    parts.append(part)
    second_rows = after(grad_tile[1], *got0)
    got1 = [partner(second_rows, k * low_size)[None] for k in range(1, high_size)]

    (sent_x, sent_y), (kept_x, kept_y), placed = halve(
        (after(kept_x, part), kept_y), (first_x, first_y), placed
    )
    second_x, second_y = partner(sent_x, 2), partner(sent_y, 1)
    c_first_x = partner(after(c_sent_x, sent_x, sent_y), 1)
    c_first_y = partner(after(c_sent_y, sent_x, sent_y), 2)

    chunks = [([grad_tile], own_pieces), (got0, pieces_of(0)), (got1, pieces_of(1))]
    order = [piece for _, pieces in chunks for _, _, piece, _ in pieces]
    d_sent_x, d_sent_y, d_kept_x, d_kept_y, part = produce(
        got1, pieces_of(1), False, True, True, LONG
    )
    parts.append(part)
    own_third, placed = last_parts((after(kept_x, part), kept_y), (second_x, second_y), placed)
    own_last = relay(own_third, 4)
    own_sums = (kept_x, second_x), (kept_y, second_y)

    rows_total = len(order) * size
    blocks = rows_total // tile_rows

    def small(kernel, shapes, *operands, scratch=(), cost=QUICK):
        return pl.pallas_call(
            kernel,
            in_specs=[SMEM] + [VMEM] * len(operands),
            out_specs=[VMEM] * len(shapes),
            out_shape=[jax.ShapeDtypeStruct(*shape) for shape in shapes],
            scratch_shapes=list(scratch),
            compiler_params=PARAMS,
            cost_estimate=cost,
        )(*in_hbm(scalars[0]), *operands)

    def collect_kernel(pos_ref, *refs):
        part_refs, placed_ref = refs[: len(parts)], refs[len(parts)]
        *message_refs, wide_ref = refs[len(parts) + 1 :]
        own = pos_ref[0] // low_size
        block = 0
        for part_ref in part_refs:
            for start in range(0, part_ref.shape[1], tile_rows):
                value = part_ref[:, start : start + tile_rows].astype(BF16)
                for message_ref in message_refs:
                    message_ref[block * rank_part : (block + 1) * rank_part, :] = value
                block += 1
        wide_ref[...] = placed_ref[...].astype(F32)
        message_refs[0][block * rank_part :, :] = placed_ref[...]
        for k in range(1, high_size):
            for m in range(micro_count):
                start = pl.multiple_of(m * rank + (own ^ k) * rank_part, rank_part)
                first = (block + m) * rank_part
                message_refs[k][first : first + rank_part, :] = wide_ref[
                    pl.ds(start, rank_part), :
                ].astype(BF16)

    counts = [placed.shape[0]] + [micro_count * rank_part] * (high_size - 1)
    messages = small(
        collect_kernel,
        [((blocks * rank_part + n, tile_rows), BF16) for n in counts],
        *parts,
        placed,
        scratch=[pltpu.VMEM(placed.shape, F32)],
    )
    (c_sent_x, c_sent_y), c_kept = halve(
        (after(c_kept_x, messages[0]), c_kept_y), (c_first_x, c_first_y)
    )
    c_second_x, c_second_y = partner(c_sent_x, 2), partner(c_sent_y, 1)
    near = partner(messages[0], 4)
    far = []
    for k in range(1, high_size):
        far += [partner(messages[k], k * low_size), partner(messages[k], k * low_size + 4)]

    def columns_of(j, piece):
        k, m, offset = piece
        at = order.index((k ^ j, m, offset))
        return slice(at * size, (at + 1) * size)

    def block_of(message_ref, columns):
        block, start = columns.start // tile_rows, columns.start % tile_rows
        rows = slice(block * rank_part, (block + 1) * rank_part)
        return message_ref[rows, start : start + size].astype(F32)

    def lowrank_kernel(pos_ref, *refs):
        part_refs = refs[: len(parts)]
        near_ref, *far_refs = refs[len(parts) : -1]
        out_ref = refs[-1]
        whole = [(ref, start) for ref in part_refs for start in range(0, ref.shape[1], size)]
        for at, piece in enumerate(order):
            columns = slice(at * size, (at + 1) * size)
            for j in range(high_size):
                if j == 0:
                    part_ref, start = whole[at]
                    value = part_ref[:, start : start + size] + block_of(near_ref, columns)
                else:
                    other = columns_of(j, piece)
                    value = block_of(far_refs[2 * j - 2], other) + block_of(far_refs[2 * j - 1], other)
                start = pl.multiple_of(((pos_ref[0] // low_size) ^ j) * rank_part, rank_part)
                out_ref[pl.ds(start, rank_part), columns] = value

    (lowrank,) = small(lowrank_kernel, [((rank, rows_total), F32)], *parts, near, *far)

    halves = [range(0, len(order) // 2), range(len(order) // 2, len(order))]

    def riders(way, count):
        fit = count // size
        for i, at in enumerate(halves[way]):
            rows = slice(i // fit * rank, (i // fit + 1) * rank)
            yield rows, slice(i % fit * size, (i % fit + 1) * size), slice(at * size, (at + 1) * size)

    def riding(way, count):
        return -(-len(halves[way]) // (count // size)) * rank

    def ride(ref, first, way, lowrank_ref):
        for rows, there, whole in riders(way, ref.shape[1]):
            ref[first + rows.start : first + rows.stop, there] = lowrank_ref[:, whole].astype(BF16)

    def arrive(ref, first, way, lowrank_ref, out_ref):
        for rows, there, whole in riders(way, ref.shape[1]):
            got = ref[first + rows.start : first + rows.stop, there].astype(F32)
            out_ref[:, whole] = (lowrank_ref[:, whole] + got).astype(out_ref.dtype)

    half_rows = d_sent_x.shape[0] // 2
    d_counts = [d_sent_x.shape[1], d_sent_y.shape[1]]

    def append_kernel(_, *refs):
        for way in range(2):
            refs[3 + way][: 2 * half_rows, :] = refs[way][...]
            ride(refs[3 + way], 2 * half_rows, way, refs[2])

    d_sent_x, d_sent_y = small(
        append_kernel,
        [((2 * half_rows + riding(way, n), n), BF16) for way, n in enumerate(d_counts)],
        d_sent_x,
        d_sent_y,
        after(lowrank, *c_kept),
    )
    d_first_x, d_first_y = partner(d_sent_x, 1), partner(d_sent_y, 2)

    all_grads, all_pieces = [], []
    for grads, pieces in chunks:
        all_pieces += [(tile + len(all_grads), *rest) for tile, *rest in pieces]
        all_grads += grads
    up_map_gradient = pl.pallas_call(
        functools.partial(
            up_body, low_size, tile_rows, all_pieces, len(all_grads), micro_count
        ),
        in_specs=[SMEM] * 3 + [VMEM] * (len(all_grads) + 2 * high_size),
        out_specs=VMEM,
        out_shape=jax.ShapeDtypeStruct(up_tile.shape, BF16),
        scratch_shapes=[pltpu.VMEM(up_tile.shape, F32)],
        compiler_params=PARAMS,
        cost_estimate=LONG,
    )(*in_hbm(*scalars), *all_grads, placed, near, *far)

    (c_third,) = last_parts((after(c_kept[0], d_sent_x), c_kept[1]), (c_second_x, c_second_y))
    c_last = relay(c_third, 4)

    def third_kernel(_, *refs):
        lowrank_ref, next_ref = refs[4], refs[9]
        for way in range(2):
            kept_ref, got_ref, sent_ref, rest_ref = refs[way], refs[2 + way], refs[5 + way], refs[7 + way]
            half = kept_ref.shape[0] // 2
            sent_ref[:half, :] = (
                kept_ref[half:, :] + got_ref[half : 2 * half, :].astype(F32)
            ).astype(BF16)
            rest_ref[...] = kept_ref[:half, :] + got_ref[:half, :].astype(F32)
            arrive(got_ref, 2 * half, way, lowrank_ref, next_ref)
            ride(sent_ref, half, way, next_ref)

    d_sent_x, d_sent_y, *d_kept, lowrank = small(
        third_kernel,
        [((half_rows + riding(way, n), n), BF16) for way, n in enumerate(d_counts)]
        + [((half_rows, n), F32) for n in d_counts]
        + [((rank, rows_total), F32)],
        d_kept_x,
        after(d_kept_y, up_map_gradient, own_last, c_third),
        d_first_x,
        d_first_y,
        lowrank,
    )
    d_second_x, d_second_y = partner(d_sent_x, 2), partner(d_sent_y, 1)
    (d_third,) = last_parts(d_kept, (d_second_x, d_second_y))
    d_last = relay(d_third, 4)

    def whole_kernel(_, lowrank_ref, got_x_ref, got_y_ref, out_ref):
        for way, got_ref in enumerate((got_x_ref, got_y_ref)):
            arrive(got_ref, half_rows, way, lowrank_ref, out_ref)

    (lowrank,) = small(
        whole_kernel,
        [((rank, rows_total), BF16)],
        after(lowrank, d_third),
        d_second_x,
        d_second_y,
    )

    down = adapter_down_maps[0]

    def adapter_kernel(groups, *refs):
        pos_ref, classes_ref, _, down_ref, lowrank_ref = refs[:5]
        sum_refs = refs[5 : 5 + 2 * groups]
        out_ref, total_ref = refs[5 + 2 * groups :]
        own = pos_ref[0] // low_size
        start = 0
        for g in range(groups):
            kept_ref, second_ref = sum_refs[2 * g : 2 * g + 2]
            half, count = kept_ref.shape[0] // 2, kept_ref.shape[1]
            total_ref[:, start : start + count] = (
                kept_ref[:half, :] + second_ref[:half, :].astype(F32)
            )
            start += count
        for at in range(start // size):
            piece = order[at]
            seg = segment_of(own, piece, tile_rows)
            rows = slice(at * size, (at + 1) * size)
            adapter = lax.dot_general(
                down_ref[classes_ref[piece[1], seg]],
                lowrank_ref[:, rows],
                TN,
                preferred_element_type=F32,
            )
            out_ref[:, rows] = (total_ref[:, rows] + adapter).astype(BF16)

    sums = own_sums + (
        (c_kept[0], c_second_x),
        (c_kept[1], c_second_y),
        (d_kept[0], d_second_x),
        (d_kept[1], d_second_y),
    )
    kept = pl.pallas_call(
        functools.partial(adapter_kernel, len(sums)),
        in_specs=[SMEM] * 3 + [VMEM] * (2 + 2 * len(sums)),
        out_specs=VMEM,
        out_shape=jax.ShapeDtypeStruct((portion, rows_total), BF16),
        scratch_shapes=[pltpu.VMEM((portion, rows_total), F32)],
        compiler_params=PARAMS,
        cost_estimate=QUICK,
    )(*in_hbm(*scalars, down), lowrank, *[a for two in sums for a in two])
    kept = relay(kept, 0)

    def finish_kernel(pos_ref, kept_ref, *refs):
        *got_refs, out_ref, total_ref, turned_ref, sem = refs
        own = pos_ref[0] // low_size
        start = 0
        for got_ref in got_refs:
            count = got_ref.shape[1]
            total_ref[:, start : start + count] = (
                kept_ref[:, start : start + count].astype(F32) + got_ref[...].astype(F32)
            ).astype(BF16)
            start += count
        copies = []
        for at in range(start // size):
            k, m, offset = order[at]
            base = pl.multiple_of((own ^ k) * tile_rows + offset, size)
            rows = slice(at * size, (at + 1) * size)
            turned_ref[rows, :] = total_ref[:, rows].T
            copies.append(
                pltpu.make_async_copy(
                    turned_ref.at[rows, :], out_ref.at[m, pl.ds(base, size), :], sem.at[at]
                )
            )
            copies[-1].start()
        for copy in copies:
            copy.wait()

    got = [own_last, c_last, d_last]
    grad_prev = pl.pallas_call(
        finish_kernel,
        in_specs=[SMEM] + [VMEM] * (1 + len(got)),
        out_specs=pl.BlockSpec(memory_space=pltpu.HBM),
        out_shape=jax.ShapeDtypeStruct((micro_count, high_size * tile_rows, portion), BF16),
        scratch_shapes=[
            pltpu.VMEM((portion, rows_total), BF16),
            pltpu.VMEM((rows_total, portion), BF16),
            pltpu.SemaphoreType.DMA((rows_total // size,)),
        ],
        compiler_params=PARAMS,
        cost_estimate=QUICK,
    )(*in_hbm(scalars[0]), kept, *got)

    def down_kernel(pos_ref, classes_ref, live_ref, inputs_ref, lowrank_ref, out_ref, total_ref):
        own = pos_ref[0] // low_size
        total_ref[...] = jnp.zeros_like(total_ref)
        for at, piece in enumerate(order):
            k, m, offset = piece
            seg = segment_of(own, piece, tile_rows)

            @pl.when(seg < live_ref[m])
            def _():
                base = pl.multiple_of((own ^ k) * tile_rows + offset, size)
                total_ref[classes_ref[m, seg]] += jnp.dot(
                    lowrank_ref[:, at * size : (at + 1) * size],
                    inputs_ref[m, pl.ds(base, size), :],
                    preferred_element_type=F32,
                )

        out_ref[...] = total_ref[...].astype(BF16)

    down_map_gradient = pl.pallas_call(
        down_kernel,
        in_specs=[SMEM] * 3 + [VMEM] * 2,
        out_specs=VMEM,
        out_shape=jax.ShapeDtypeStruct(down.shape, BF16),
        scratch_shapes=[pltpu.VMEM(down.shape, F32)],
        compiler_params=PARAMS,
        cost_estimate=LONG,
    )(*in_hbm(*scalars, forward_input[0]), lowrank)

    return (
        grad_prev[None],
        down_map_gradient[None],
        up_map_gradient[None, None],
    )


def solution(mesh):
    in_specs = (
        P("pipe", "tensor", None, None, None),
        P("pipe", None, None, "tensor"),
        P("pipe", None, "tensor", None),
        P("pipe", "tensor", None, None),
        P("pipe", None, None, "tensor"),
        P("pipe", "tensor", None, None, None),
        P("pipe", None, None),
        P("pipe", None),
    )
    out_specs = (
        P("pipe", None, None, "tensor"),
        P("pipe", None, None, "tensor"),
        P("pipe", "tensor", None, None, None),
    )
    return jax.shard_map(shards, mesh=mesh, in_specs=in_specs, out_specs=out_specs, check_vma=False)
```

```python
import functools

import jax
import jax.numpy as jnp
from jax import lax
from jax.experimental import pallas as pl
from jax.experimental.pallas import tpu as pltpu
from jax.sharding import PartitionSpec as P

SEG = 128
BF16 = jnp.bfloat16
F32 = jnp.float32
SMEM = pl.BlockSpec(memory_space=pltpu.SMEM)
VMEM = pl.BlockSpec(memory_space=pltpu.VMEM)
TN = (((0,), (0,)), ((), ()))
PARAMS = pltpu.CompilerParams(vmem_limit_bytes=16 * 2**20)
PRODUCT_PARAMS = pltpu.CompilerParams(vmem_limit_bytes=24 * 2**20)
QUICK = pl.CostEstimate(flops=1000, bytes_accessed=1000, transcendentals=0)
LONG = pl.CostEstimate(flops=4 * 10**10, bytes_accessed=1000, transcendentals=0)


def partner(value, mask):
    pairs = [(source, source ^ mask) for source in range(lax.axis_size("tensor"))]
    return lax.ppermute(value, "tensor", pairs)


def relay(value, mask):
    sections, tiles = lax.axis_size("pipe"), lax.axis_size("tensor")
    pairs = [
        (p * tiles + t, (p - 1) % sections * tiles + (t ^ mask))
        for p in range(sections)
        for t in range(tiles)
    ]
    return lax.ppermute(value, ("pipe", "tensor"), pairs)


def segment_of(high, piece, tile_rows):
    k, _, offset = piece
    return ((high ^ k) * tile_rows + offset) // SEG


def product_body(low_size, tile_rows, pieces, tiles, half, turns, sends, keeps, with_hidden, fetches, *refs):
    pos_ref, classes_ref, live_ref = refs[:3]
    grad_refs = refs[3 : 3 + tiles]
    weight_hbm = refs[3 + tiles]
    rows_ref, *scratch = refs[-3:] if fetches else refs[-1:]
    rest = list(refs[4 + tiles : -1 - len(scratch)])
    weight_ref, sems = scratch if fetches else (weight_hbm, None)
    up_ref = rest.pop(0) if keeps else None
    hidden_ref = rest.pop(0) if with_hidden else None
    sent_x, sent_y = (rest.pop(0), rest.pop(0)) if sends else (None, None)
    placed_ref = rest.pop(0) if with_hidden else None
    kept_x, kept_y, rank_ref = rest if keeps else (None, None, None)
    low, high = pos_ref[0] % low_size, pos_ref[0] // low_size
    total = rows_ref.shape[1]
    size = total // len(pieces)

    def weight_copy(block):
        return pltpu.make_async_copy(
            weight_hbm.at[block ^ low], weight_ref.at[block], sems.at[block]
        )

    jobs = []
    for x, y in ((1, 1), (1, 0), (0, 1), (0, 0)):
        to_x = (sent_x if x else kept_x, *((y, 2) if turns else (2 * y, 1)))
        to_y = (sent_y if y else kept_y, *((x, 2) if turns else (2 * x, 1)))
        start = 0 if to_x[0] is not None else half
        stop = total if to_y[0] is not None else half
        if start < stop:
            jobs.append((x + 2 * y, start, stop, to_x, to_y))
    if fetches:
        for block, *_ in jobs:
            for z in range(2):
                weight_copy(block + 4 * z).start()

    if with_hidden:
        micro_count, count, rank = hidden_ref.shape
        spot = lax.broadcasted_iota(jnp.int32, (count, half), 1)
        row = lax.broadcasted_iota(jnp.int32, (count, half), 0)
        chosen = (spot == low * count + row).astype(F32).astype(BF16)
        for m in range(micro_count):
            placed = lax.dot_general(
                hidden_ref[m], chosen, TN, preferred_element_type=F32
            ).astype(BF16)
            placed_ref[m * rank : (m + 1) * rank, :] = placed
            start = sent_x.shape[0] - (micro_count - m) * rank
            sent_x[start : start + rank, :] = placed

    for at, (tile, index, piece, first) in enumerate(pieces):
        seg = segment_of(high, piece, tile_rows)
        alive = seg < live_ref[piece[1]]
        place = slice(at * size, (at + 1) * size)

        @pl.when(alive)
        def _():
            rows = grad_refs[tile][index, first : first + size, :].T
            rows_ref[:, place] = rows
            if keeps:
                up = up_ref[classes_ref[piece[1], seg]]
                rank_ref[:, place] = jnp.dot(up, rows, preferred_element_type=F32)

        @pl.when(jnp.logical_not(alive))
        def _():
            rows_ref[:, place] = jnp.zeros((rows_ref.shape[0], size), rows_ref.dtype)
            if keeps:
                rank_ref[:, place] = jnp.zeros((rank_ref.shape[0], size), F32)

    for block, start, stop, to_x, to_y in jobs:

        @pl.loop(0, 2)
        def _(z):
            if fetches:
                weight_copy(block + 4 * z).wait()
            value = jnp.dot(
                weight_ref[block + 4 * z], rows_ref[:, start:stop], preferred_element_type=F32
            )
            for (ref, slot, step), part in (
                (to_x, value[:, : half - start]),
                (to_y, value[:, half - start :]),
            ):
                if ref is not None:
                    width = part.shape[0]
                    place = pl.ds(pl.multiple_of((slot + step * z) * width, width), width)
                    ref[place, :] = part.astype(ref.dtype)


def product(scalars, grads, pieces, tile_rows, weight_blocks, up_tile, low_size, turns, sends, keeps, cost, size, hidden=None, fetched=None):
    blocks, width, depth = weight_blocks.shape
    rows = len(pieces) * size
    half = rows // 2
    if rows > 128 and half % 128:
        half = half // 128 * 128 + 128
    outs = []
    extra = 0 if hidden is None else hidden.shape[0] * hidden.shape[2]
    for wanted, dtype in ((sends, BF16), (keeps, F32)):
        if wanted:
            for more, n in ((extra, half), (0, rows - half)):
                outs.append(jax.ShapeDtypeStruct((blocks // 2 * width + more, n), dtype))
    if extra:
        outs.append(jax.ShapeDtypeStruct((extra, half), BF16))
    if keeps:
        outs.append(jax.ShapeDtypeStruct((up_tile.shape[1], rows), F32))
    more = ([up_tile] if keeps else []) + ([] if hidden is None else [hidden])
    return pl.pallas_call(
        functools.partial(
            product_body, low_size, tile_rows, pieces, len(grads), half, turns, sends, keeps, extra > 0,
            fetched is None,
        ),
        in_specs=[SMEM] * 3
        + [VMEM] * len(grads)
        + [pl.BlockSpec(memory_space=pltpu.HBM) if fetched is None else VMEM]
        + [VMEM] * len(more),
        out_specs=[VMEM] * len(outs),
        out_shape=outs,
        scratch_shapes=[pltpu.VMEM((depth, rows), BF16)]
        + [pltpu.VMEM(weight_blocks.shape, BF16), pltpu.SemaphoreType.DMA((blocks,))]
        * (fetched is None),
        compiler_params=PRODUCT_PARAMS,
        cost_estimate=cost,
    )(
        *in_hbm(*scalars),
        *grads,
        *(in_hbm(weight_blocks) if fetched is None else [fetched]),
        *in_hbm(*more),
    )


def fetch_kernel(low_size, pos_ref, weight_ref, out_ref, sems):
    copies = [
        pltpu.make_async_copy(
            weight_ref.at[block ^ (pos_ref[0] % low_size)], out_ref.at[block], sems.at[block]
        )
        for block in range(low_size)
    ]
    for copy in copies:
        copy.start()
    for copy in copies:
        copy.wait()


def fetch(position, weight_blocks, low_size):
    return pl.pallas_call(
        functools.partial(fetch_kernel, low_size),
        in_specs=[SMEM, pl.BlockSpec(memory_space=pltpu.HBM)],
        out_specs=VMEM,
        out_shape=pltpu.VMEM(weight_blocks.shape, BF16),
        scratch_shapes=[pltpu.SemaphoreType.DMA((low_size,))],
        compiler_params=PARAMS,
        cost_estimate=QUICK,
    )(*in_hbm(position, weight_blocks))


def in_hbm(*arrays):
    return [pltpu.with_memory_space_constraint(array, pltpu.HBM) for array in arrays]


def after(value, *others):
    return lax.optimization_barrier((value, *others))[0]


def halve_kernel(ways, *refs):
    kept_refs, got_refs = refs[:ways], refs[ways : 2 * ways]
    placed_ref = refs[2 * ways] if len(refs) > 4 * ways else None
    outs = refs[-2 * ways - (placed_ref is not None) :]
    for way in range(ways):
        kept_ref, got_ref, sent_ref, rest_ref = kept_refs[way], got_refs[way], outs[way], outs[ways + way]
        half = kept_ref.shape[0] // 2
        sent_ref[:half, :] = (kept_ref[half:, :] + got_ref[half : 2 * half, :].astype(F32)).astype(BF16)
        rest_ref[...] = kept_ref[:half, :] + got_ref[:half, :].astype(F32)
        if way == 0 and placed_ref is not None:
            placed = placed_ref[...] + got_ref[2 * half :, :]
            sent_ref[half:, :] = placed
            outs[-1][...] = placed


def halve(kept, got, placed=None, cost=QUICK):
    placed = [] if placed is None else [placed]
    extra = [placed[0].shape[0] if placed and not way else 0 for way in range(len(kept))]
    shapes = [(k.shape[0] // 2, k.shape[1]) for k in kept]
    outs = pl.pallas_call(
        functools.partial(halve_kernel, len(kept)),
        in_specs=[VMEM] * (2 * len(kept) + len(placed)),
        out_specs=[VMEM] * (2 * len(kept) + len(placed)),
        out_shape=[jax.ShapeDtypeStruct((n + e, r), BF16) for (n, r), e in zip(shapes, extra)]
        + [jax.ShapeDtypeStruct(shape, F32) for shape in shapes]
        + [jax.ShapeDtypeStruct(p.shape, BF16) for p in placed],
        compiler_params=PARAMS,
        cost_estimate=cost,
    )(*kept, *got, *placed)
    ways = len(kept)
    return outs[:ways], outs[ways : 2 * ways], *outs[2 * ways :]


def last_kernel(ways, *refs):
    kept_refs, got_refs = refs[:ways], refs[ways : 2 * ways]
    placed_ref = refs[2 * ways] if len(refs) > 2 * ways + 1 else None
    out_ref = refs[2 * ways + (placed_ref is not None)]
    start = 0
    for kept_ref, got_ref in zip(kept_refs, got_refs):
        half, count = kept_ref.shape[0] // 2, kept_ref.shape[1]
        out_ref[:, start : start + count] = (
            kept_ref[half:, :] + got_ref[half : 2 * half, :].astype(F32)
        ).astype(BF16)
        start += count
    if placed_ref is not None:
        refs[-1][...] = placed_ref[...] + got_refs[0][2 * kept_refs[0].shape[0] // 2 :, :]


def last_parts(kept, got, placed=None, cost=QUICK):
    placed = [] if placed is None else [placed]
    shape = kept[0].shape[0] // 2, sum(k.shape[1] for k in kept)
    return pl.pallas_call(
        functools.partial(last_kernel, len(kept)),
        in_specs=[VMEM] * (2 * len(kept) + len(placed)),
        out_specs=[VMEM] * (1 + len(placed)),
        out_shape=[jax.ShapeDtypeStruct(shape, BF16)]
        + [jax.ShapeDtypeStruct(p.shape, BF16) for p in placed],
        compiler_params=PARAMS,
        cost_estimate=cost,
    )(*kept, *got, *placed)


def up_body(low_size, tile_rows, pieces, tiles, micro_count, *refs):
    pos_ref, classes_ref, live_ref = refs[:3]
    grad_refs = refs[3 : 3 + tiles]
    placed_ref, near_ref, *far_refs = refs[3 + tiles : -2]
    out_ref, total_ref = refs[-2:]
    high = pos_ref[0] // low_size
    total_ref[...] = jnp.zeros_like(total_ref)
    rank_part = total_ref.shape[1]
    skip = near_ref.shape[0] - placed_ref.shape[0]
    for tile, index, piece, first in pieces:
        k, m, offset = piece
        size = min(SEG, tile_rows)
        seg = segment_of(high, piece, tile_rows)
        lanes = slice(offset, offset + size)

        @pl.when(seg < live_ref[m])
        def _():
            if k == 0:
                start = pl.multiple_of(
                    m * (placed_ref.shape[0] // micro_count) + high * rank_part, rank_part
                )
                other = pl.multiple_of(skip + start, rank_part)
                hidden = (
                    placed_ref[pl.ds(start, rank_part), lanes]
                    + near_ref[pl.ds(other, rank_part), lanes]
                )
            else:
                rows = slice(skip + m * rank_part, skip + (m + 1) * rank_part)
                one_ref, other_ref = far_refs[2 * k - 2 : 2 * k]
                hidden = one_ref[rows, lanes] + other_ref[rows, lanes]
            total_ref[classes_ref[m, seg]] += jnp.dot(
                hidden,
                grad_refs[tile][index, first : first + size, :],
                preferred_element_type=F32,
            )

    out_ref[...] = total_ref[...].astype(BF16)


def shards(
    output_gradient,
    forward_input,
    saved_rank_outputs,
    projection_weight,
    adapter_down_maps,
    adapter_up_maps,
    segment_adapter_class,
    live_segment_table,
):
    grad_tile = output_gradient[0, 0]
    micro_count, tile_rows, tile_cols = grad_tile.shape
    up_tile = adapter_up_maps[0, 0]
    class_count, rank_part, _ = up_tile.shape
    rank, portion = adapter_down_maps.shape[2:]
    tiles = lax.axis_size("tensor")
    low_size = min(tiles, 8)
    high_size = tiles // low_size
    position = lax.axis_index("tensor")
    high = position // low_size
    weight_blocks = projection_weight[0, 0].reshape(low_size, portion, tile_cols)
    position, classes, live = lax.optimization_barrier(
        (position.astype(jnp.int32)[None], segment_adapter_class[0] + 0, live_segment_table[0] + 0)
    )
    scalars = position, classes, live
    position = position[0]
    size = min(SEG, tile_rows)
    offsets = range(0, tile_rows, size)

    own_pieces = [(0, m, (0, m, o), o) for m in range(micro_count) for o in offsets]

    def pieces_of(m, count=1):
        span = tile_rows // count
        return [
            ((k - 1) * count + o // span, 0, (k, m, o), o % span)
            for k in range(1, high_size)
            for o in offsets
        ]

    def produce(grads, pieces, turns, sends, keeps, cost, hidden=None, fetched=None):
        return product(
            scalars, grads, pieces, tile_rows, weight_blocks, up_tile, low_size, turns, sends, keeps,
            cost, size, hidden, fetched,
        )

    hidden = saved_rank_outputs[0]

    first_rows = lax.optimization_barrier(grad_tile[0])
    got0 = [partner(first_rows, k * low_size)[None] for k in range(1, high_size)]
    (own_grads,) = in_hbm(after(grad_tile, first_rows))
    sent_x, sent_y, placed = produce([own_grads], own_pieces, False, True, False, QUICK, hidden)
    first_x, first_y = partner(sent_x, 1), partner(sent_y, 2)
    (own_grads,) = in_hbm(after(grad_tile, sent_x, sent_y))
    kept_x, kept_y, part = produce([own_grads], own_pieces, False, False, True, QUICK)
    parts = [part]
    rows0 = after(got0[0], part), *got0[1:]
    c_sent_x, c_sent_y, c_kept_x, c_kept_y, part = produce(
        list(rows0), pieces_of(0), False, True, True, LONG
    )
    parts.append(part)
    second_rows = after(grad_tile[1], *got0)
    got1 = [partner(second_rows, k * low_size)[None] for k in range(1, high_size)]

    (sent_x, sent_y), (kept_x, kept_y), placed = halve(
        (after(kept_x, part), kept_y), (first_x, first_y), placed
    )
    second_x, second_y = partner(sent_x, 2), partner(sent_y, 1)
    c_first_x = partner(after(c_sent_x, sent_x, sent_y), 1)
    c_first_y = partner(after(c_sent_y, sent_x, sent_y), 2)

    fetched = fetch(after(scalars[0], sent_x, sent_y), weight_blocks, low_size)

    chunks = [([grad_tile], own_pieces), (got0, pieces_of(0)), (got1, pieces_of(1))]
    order = [piece for _, pieces in chunks for _, _, piece, _ in pieces]
    d_sent_x, d_sent_y, d_kept_x, d_kept_y, part = produce(
        got1, pieces_of(1), False, True, True, LONG, None, fetched
    )
    parts.append(part)
    own_third, placed = last_parts((after(kept_x, part), kept_y), (second_x, second_y), placed)
    own_last = relay(own_third, 4)
    own_sums = (kept_x, second_x), (kept_y, second_y)

    rows_total = len(order) * size
    blocks = rows_total // tile_rows

    def small(kernel, shapes, *operands, scratch=(), cost=QUICK):
        return pl.pallas_call(
            kernel,
            in_specs=[SMEM] + [VMEM] * len(operands),
            out_specs=[VMEM] * len(shapes),
            out_shape=[jax.ShapeDtypeStruct(*shape) for shape in shapes],
            scratch_shapes=list(scratch),
            compiler_params=PARAMS,
            cost_estimate=cost,
        )(*in_hbm(scalars[0]), *operands)

    def collect_kernel(pos_ref, *refs):
        part_refs, placed_ref = refs[: len(parts)], refs[len(parts)]
        *message_refs, wide_ref = refs[len(parts) + 1 :]
        own = pos_ref[0] // low_size
        block = 0
        for part_ref in part_refs:
            for start in range(0, part_ref.shape[1], tile_rows):
                value = part_ref[:, start : start + tile_rows].astype(BF16)
                for message_ref in message_refs:
                    message_ref[block * rank_part : (block + 1) * rank_part, :] = value
                block += 1
        wide_ref[...] = placed_ref[...].astype(F32)
        message_refs[0][block * rank_part :, :] = placed_ref[...]
        for k in range(1, high_size):
            for m in range(micro_count):
                start = pl.multiple_of(m * rank + (own ^ k) * rank_part, rank_part)
                first = (block + m) * rank_part
                message_refs[k][first : first + rank_part, :] = wide_ref[
                    pl.ds(start, rank_part), :
                ].astype(BF16)

    counts = [placed.shape[0]] + [micro_count * rank_part] * (high_size - 1)
    messages = small(
        collect_kernel,
        [((blocks * rank_part + n, tile_rows), BF16) for n in counts],
        *parts,
        placed,
        scratch=[pltpu.VMEM(placed.shape, F32)],
    )
    (c_sent_x, c_sent_y), c_kept = halve(
        (after(c_kept_x, messages[0]), c_kept_y), (c_first_x, c_first_y)
    )
    c_second_x, c_second_y = partner(c_sent_x, 2), partner(c_sent_y, 1)
    near = partner(messages[0], 4)
    far = []
    for k in range(1, high_size):
        far += [partner(messages[k], k * low_size), partner(messages[k], k * low_size + 4)]

    def columns_of(j, piece):
        k, m, offset = piece
        at = order.index((k ^ j, m, offset))
        return slice(at * size, (at + 1) * size)

    def block_of(message_ref, columns):
        block, start = columns.start // tile_rows, columns.start % tile_rows
        rows = slice(block * rank_part, (block + 1) * rank_part)
        return message_ref[rows, start : start + size].astype(F32)

    def lowrank_kernel(pos_ref, *refs):
        part_refs = refs[: len(parts)]
        near_ref, *far_refs = refs[len(parts) : -1]
        out_ref = refs[-1]
        whole = [(ref, start) for ref in part_refs for start in range(0, ref.shape[1], size)]
        for at, piece in enumerate(order):
            columns = slice(at * size, (at + 1) * size)
            for j in range(high_size):
                if j == 0:
                    part_ref, start = whole[at]
                    value = part_ref[:, start : start + size] + block_of(near_ref, columns)
                else:
                    other = columns_of(j, piece)
                    value = block_of(far_refs[2 * j - 2], other) + block_of(far_refs[2 * j - 1], other)
                start = pl.multiple_of(((pos_ref[0] // low_size) ^ j) * rank_part, rank_part)
                out_ref[pl.ds(start, rank_part), columns] = value

    (lowrank,) = small(lowrank_kernel, [((rank, rows_total), F32)], *parts, near, *far)

    halves = [range(0, len(order) // 2), range(len(order) // 2, len(order))]

    def riders(way, count):
        fit = count // size
        for i, at in enumerate(halves[way]):
            rows = slice(i // fit * rank, (i // fit + 1) * rank)
            yield rows, slice(i % fit * size, (i % fit + 1) * size), slice(at * size, (at + 1) * size)

    def riding(way, count):
        return -(-len(halves[way]) // (count // size)) * rank

    def ride(ref, first, way, lowrank_ref):
        for rows, there, whole in riders(way, ref.shape[1]):
            ref[first + rows.start : first + rows.stop, there] = lowrank_ref[:, whole].astype(BF16)

    def arrive(ref, first, way, lowrank_ref, out_ref):
        for rows, there, whole in riders(way, ref.shape[1]):
            got = ref[first + rows.start : first + rows.stop, there].astype(F32)
            out_ref[:, whole] = (lowrank_ref[:, whole] + got).astype(out_ref.dtype)

    half_rows = d_sent_x.shape[0] // 2
    d_counts = [d_sent_x.shape[1], d_sent_y.shape[1]]

    def append_kernel(_, *refs):
        for way in range(2):
            refs[3 + way][: 2 * half_rows, :] = refs[way][...]
            ride(refs[3 + way], 2 * half_rows, way, refs[2])

    d_sent_x, d_sent_y = small(
        append_kernel,
        [((2 * half_rows + riding(way, n), n), BF16) for way, n in enumerate(d_counts)],
        d_sent_x,
        d_sent_y,
        after(lowrank, *c_kept),
    )
    d_first_x, d_first_y = partner(d_sent_x, 1), partner(d_sent_y, 2)

    all_grads, all_pieces = [], []
    for grads, pieces in chunks:
        all_pieces += [(tile + len(all_grads), *rest) for tile, *rest in pieces]
        all_grads += grads
    up_map_gradient = pl.pallas_call(
        functools.partial(
            up_body, low_size, tile_rows, all_pieces, len(all_grads), micro_count
        ),
        in_specs=[SMEM] * 3 + [VMEM] * (len(all_grads) + 2 * high_size),
        out_specs=VMEM,
        out_shape=jax.ShapeDtypeStruct(up_tile.shape, BF16),
        scratch_shapes=[pltpu.VMEM(up_tile.shape, F32)],
        compiler_params=PARAMS,
        cost_estimate=LONG,
    )(*in_hbm(*scalars), *all_grads, placed, near, *far)

    (c_third,) = last_parts((after(c_kept[0], d_sent_x), c_kept[1]), (c_second_x, c_second_y))
    c_last = relay(c_third, 4)

    def third_kernel(_, *refs):
        lowrank_ref, next_ref = refs[4], refs[9]
        for way in range(2):
            kept_ref, got_ref, sent_ref, rest_ref = refs[way], refs[2 + way], refs[5 + way], refs[7 + way]
            half = kept_ref.shape[0] // 2
            sent_ref[:half, :] = (
                kept_ref[half:, :] + got_ref[half : 2 * half, :].astype(F32)
            ).astype(BF16)
            rest_ref[...] = kept_ref[:half, :] + got_ref[:half, :].astype(F32)
            arrive(got_ref, 2 * half, way, lowrank_ref, next_ref)
            ride(sent_ref, half, way, next_ref)

    d_sent_x, d_sent_y, *d_kept, lowrank = small(
        third_kernel,
        [((half_rows + riding(way, n), n), BF16) for way, n in enumerate(d_counts)]
        + [((half_rows, n), F32) for n in d_counts]
        + [((rank, rows_total), F32)],
        d_kept_x,
        after(d_kept_y, up_map_gradient, own_last, c_third),
        d_first_x,
        d_first_y,
        lowrank,
    )
    d_second_x, d_second_y = partner(d_sent_x, 2), partner(d_sent_y, 1)
    (d_third,) = last_parts(d_kept, (d_second_x, d_second_y))
    d_last = relay(d_third, 4)

    def whole_kernel(_, lowrank_ref, got_x_ref, got_y_ref, out_ref):
        for way, got_ref in enumerate((got_x_ref, got_y_ref)):
            arrive(got_ref, half_rows, way, lowrank_ref, out_ref)

    (lowrank,) = small(
        whole_kernel,
        [((rank, rows_total), BF16)],
        after(lowrank, d_third),
        d_second_x,
        d_second_y,
    )

    down = adapter_down_maps[0]

    def adapter_kernel(groups, *refs):
        pos_ref, classes_ref, _, down_ref, lowrank_ref = refs[:5]
        sum_refs = refs[5 : 5 + 2 * groups]
        out_ref, total_ref = refs[5 + 2 * groups :]
        own = pos_ref[0] // low_size
        start = 0
        for g in range(groups):
            kept_ref, second_ref = sum_refs[2 * g : 2 * g + 2]
            half, count = kept_ref.shape[0] // 2, kept_ref.shape[1]
            total_ref[:, start : start + count] = (
                kept_ref[:half, :] + second_ref[:half, :].astype(F32)
            )
            start += count
        for at in range(start // size):
            piece = order[at]
            seg = segment_of(own, piece, tile_rows)
            rows = slice(at * size, (at + 1) * size)
            adapter = lax.dot_general(
                down_ref[classes_ref[piece[1], seg]],
                lowrank_ref[:, rows],
                TN,
                preferred_element_type=F32,
            )
            out_ref[:, rows] = (total_ref[:, rows] + adapter).astype(BF16)

    sums = own_sums + (
        (c_kept[0], c_second_x),
        (c_kept[1], c_second_y),
        (d_kept[0], d_second_x),
        (d_kept[1], d_second_y),
    )
    kept = pl.pallas_call(
        functools.partial(adapter_kernel, len(sums)),
        in_specs=[SMEM] * 3 + [VMEM] * (2 + 2 * len(sums)),
        out_specs=VMEM,
        out_shape=jax.ShapeDtypeStruct((portion, rows_total), BF16),
        scratch_shapes=[pltpu.VMEM((portion, rows_total), F32)],
        compiler_params=PARAMS,
        cost_estimate=QUICK,
    )(*in_hbm(*scalars, down), lowrank, *[a for two in sums for a in two])
    kept = relay(kept, 0)

    def finish_kernel(pos_ref, kept_ref, *refs):
        *got_refs, out_ref, total_ref, turned_ref, sem = refs
        own = pos_ref[0] // low_size
        start = 0
        for got_ref in got_refs:
            count = got_ref.shape[1]
            total_ref[:, start : start + count] = (
                kept_ref[:, start : start + count].astype(F32) + got_ref[...].astype(F32)
            ).astype(BF16)
            start += count
        copies = []
        for at in range(start // size):
            k, m, offset = order[at]
            base = pl.multiple_of((own ^ k) * tile_rows + offset, size)
            rows = slice(at * size, (at + 1) * size)
            turned_ref[rows, :] = total_ref[:, rows].T
            copies.append(
                pltpu.make_async_copy(
                    turned_ref.at[rows, :], out_ref.at[m, pl.ds(base, size), :], sem.at[at]
                )
            )
            copies[-1].start()
        for copy in copies:
            copy.wait()

    got = [own_last, c_last, d_last]
    grad_prev = pl.pallas_call(
        finish_kernel,
        in_specs=[SMEM] + [VMEM] * (1 + len(got)),
        out_specs=pl.BlockSpec(memory_space=pltpu.HBM),
        out_shape=jax.ShapeDtypeStruct((micro_count, high_size * tile_rows, portion), BF16),
        scratch_shapes=[
            pltpu.VMEM((portion, rows_total), BF16),
            pltpu.VMEM((rows_total, portion), BF16),
            pltpu.SemaphoreType.DMA((rows_total // size,)),
        ],
        compiler_params=PARAMS,
        cost_estimate=QUICK,
    )(*in_hbm(scalars[0]), kept, *got)

    def down_kernel(pos_ref, classes_ref, live_ref, inputs_ref, lowrank_ref, out_ref, total_ref):
        own = pos_ref[0] // low_size
        total_ref[...] = jnp.zeros_like(total_ref)
        for at, piece in enumerate(order):
            k, m, offset = piece
            seg = segment_of(own, piece, tile_rows)

            @pl.when(seg < live_ref[m])
            def _():
                base = pl.multiple_of((own ^ k) * tile_rows + offset, size)
                total_ref[classes_ref[m, seg]] += jnp.dot(
                    lowrank_ref[:, at * size : (at + 1) * size],
                    inputs_ref[m, pl.ds(base, size), :],
                    preferred_element_type=F32,
                )

        out_ref[...] = total_ref[...].astype(BF16)

    down_map_gradient = pl.pallas_call(
        down_kernel,
        in_specs=[SMEM] * 3 + [VMEM] * 2,
        out_specs=VMEM,
        out_shape=jax.ShapeDtypeStruct(down.shape, BF16),
        scratch_shapes=[pltpu.VMEM(down.shape, F32)],
        compiler_params=PARAMS,
        cost_estimate=LONG,
    )(*in_hbm(*scalars, forward_input[0]), lowrank)

    return (
        grad_prev[None],
        down_map_gradient[None],
        up_map_gradient[None, None],
    )


def solution(mesh):
    in_specs = (
        P("pipe", "tensor", None, None, None),
        P("pipe", None, None, "tensor"),
        P("pipe", None, "tensor", None),
        P("pipe", "tensor", None, None),
        P("pipe", None, None, "tensor"),
        P("pipe", "tensor", None, None, None),
        P("pipe", None, None),
        P("pipe", None),
    )
    out_specs = (
        P("pipe", None, None, "tensor"),
        P("pipe", None, None, "tensor"),
        P("pipe", "tensor", None, None, None),
    )
    return jax.shard_map(shards, mesh=mesh, in_specs=in_specs, out_specs=out_specs, check_vma=False)
```

```python
import functools

import jax
import jax.numpy as jnp
from jax import lax
from jax.experimental import pallas as pl
from jax.experimental.pallas import tpu as pltpu
from jax.sharding import PartitionSpec as P

SEG = 128
BF16 = jnp.bfloat16
F32 = jnp.float32
SMEM = pl.BlockSpec(memory_space=pltpu.SMEM)
VMEM = pl.BlockSpec(memory_space=pltpu.VMEM)
TN = (((0,), (0,)), ((), ()))
PARAMS = pltpu.CompilerParams(vmem_limit_bytes=16 * 2**20)
PRODUCT_PARAMS = pltpu.CompilerParams(vmem_limit_bytes=24 * 2**20)
QUICK = pl.CostEstimate(flops=1000, bytes_accessed=1000, transcendentals=0)
LONG = pl.CostEstimate(flops=4 * 10**10, bytes_accessed=1000, transcendentals=0)


def partner(value, mask):
    pairs = [(source, source ^ mask) for source in range(lax.axis_size("tensor"))]
    return lax.ppermute(value, "tensor", pairs)


def relay(value, mask):
    sections, tiles = lax.axis_size("pipe"), lax.axis_size("tensor")
    pairs = [
        (p * tiles + t, (p - 1) % sections * tiles + (t ^ mask))
        for p in range(sections)
        for t in range(tiles)
    ]
    return lax.ppermute(value, ("pipe", "tensor"), pairs)


def segment_of(high, piece, tile_rows):
    k, _, offset = piece
    return ((high ^ k) * tile_rows + offset) // SEG


def product_body(low_size, tile_rows, pieces, tiles, half, turns, sends, keeps, with_hidden, fetches, *refs):
    pos_ref, classes_ref, live_ref = refs[:3]
    grad_refs = refs[3 : 3 + tiles]
    weight_hbm = refs[3 + tiles]
    rows_ref, *scratch = refs[-3:] if fetches else refs[-1:]
    rest = list(refs[4 + tiles : -1 - len(scratch)])
    weight_ref, sems = scratch if fetches else (weight_hbm, None)
    up_ref = rest.pop(0) if keeps else None
    hidden_ref = rest.pop(0) if with_hidden else None
    sent_x, sent_y = (rest.pop(0), rest.pop(0)) if sends else (None, None)
    placed_ref = rest.pop(0) if with_hidden else None
    kept_x, kept_y, rank_ref = rest if keeps else (None, None, None)
    low, high = pos_ref[0] % low_size, pos_ref[0] // low_size
    total = rows_ref.shape[1]
    size = total // len(pieces)

    def weight_copy(block):
        return pltpu.make_async_copy(
            weight_hbm.at[block ^ low], weight_ref.at[block], sems.at[block]
        )

    jobs = []
    for x, y in ((1, 1), (1, 0), (0, 1), (0, 0)):
        to_x = (sent_x if x else kept_x, *((y, 2) if turns else (2 * y, 1)))
        to_y = (sent_y if y else kept_y, *((x, 2) if turns else (2 * x, 1)))
        start = 0 if to_x[0] is not None else half
        stop = total if to_y[0] is not None else half
        if start < stop:
            jobs.append((x + 2 * y, start, stop, to_x, to_y))
    if fetches:
        for block, *_ in jobs:
            for z in range(2):
                weight_copy(block + 4 * z).start()

    if with_hidden:
        micro_count, count, rank = hidden_ref.shape
        spot = lax.broadcasted_iota(jnp.int32, (count, half), 1)
        row = lax.broadcasted_iota(jnp.int32, (count, half), 0)
        chosen = (spot == low * count + row).astype(F32).astype(BF16)
        for m in range(micro_count):
            placed = lax.dot_general(
                hidden_ref[m], chosen, TN, preferred_element_type=F32
            ).astype(BF16)
            placed_ref[m * rank : (m + 1) * rank, :] = placed
            start = sent_x.shape[0] - (micro_count - m) * rank
            sent_x[start : start + rank, :] = placed

    for at, (tile, index, piece, first) in enumerate(pieces):
        seg = segment_of(high, piece, tile_rows)
        alive = seg < live_ref[piece[1]]
        place = slice(at * size, (at + 1) * size)

        @pl.when(alive)
        def _():
            rows = grad_refs[tile][index, first : first + size, :].T
            rows_ref[:, place] = rows
            if keeps:
                up = up_ref[classes_ref[piece[1], seg]]
                rank_ref[:, place] = jnp.dot(up, rows, preferred_element_type=F32)

        @pl.when(jnp.logical_not(alive))
        def _():
            rows_ref[:, place] = jnp.zeros((rows_ref.shape[0], size), rows_ref.dtype)
            if keeps:
                rank_ref[:, place] = jnp.zeros((rank_ref.shape[0], size), F32)

    for block, start, stop, to_x, to_y in jobs:

        @pl.loop(0, 2)
        def _(z):
            if fetches:
                weight_copy(block + 4 * z).wait()
            value = jnp.dot(
                weight_ref[block + 4 * z], rows_ref[:, start:stop], preferred_element_type=F32
            )
            for (ref, slot, step), part in (
                (to_x, value[:, : half - start]),
                (to_y, value[:, half - start :]),
            ):
                if ref is not None:
                    width = part.shape[0]
                    place = pl.ds(pl.multiple_of((slot + step * z) * width, width), width)
                    ref[place, :] = part.astype(ref.dtype)


def product(scalars, grads, pieces, tile_rows, weight_blocks, up_tile, low_size, turns, sends, keeps, cost, size, hidden=None, fetched=None):
    blocks, width, depth = weight_blocks.shape
    rows = len(pieces) * size
    half = rows // 2
    if rows > 128 and half % 128:
        half = half // 128 * 128 + 128
    outs = []
    extra = 0 if hidden is None else hidden.shape[0] * hidden.shape[2]
    for wanted, dtype in ((sends, BF16), (keeps, F32)):
        if wanted:
            for more, n in ((extra, half), (0, rows - half)):
                outs.append(jax.ShapeDtypeStruct((blocks // 2 * width + more, n), dtype))
    if extra:
        outs.append(jax.ShapeDtypeStruct((extra, half), BF16))
    if keeps:
        outs.append(jax.ShapeDtypeStruct((up_tile.shape[1], rows), F32))
    more = ([up_tile] if keeps else []) + ([] if hidden is None else [hidden])
    return pl.pallas_call(
        functools.partial(
            product_body, low_size, tile_rows, pieces, len(grads), half, turns, sends, keeps, extra > 0,
            fetched is None,
        ),
        in_specs=[SMEM] * 3
        + [VMEM] * len(grads)
        + [pl.BlockSpec(memory_space=pltpu.HBM) if fetched is None else VMEM]
        + [VMEM] * len(more),
        out_specs=[VMEM] * len(outs),
        out_shape=outs,
        scratch_shapes=[pltpu.VMEM((depth, rows), BF16)]
        + [pltpu.VMEM(weight_blocks.shape, BF16), pltpu.SemaphoreType.DMA((blocks,))]
        * (fetched is None),
        compiler_params=PRODUCT_PARAMS,
        cost_estimate=cost,
    )(
        *in_hbm(*scalars),
        *grads,
        *(in_hbm(weight_blocks) if fetched is None else [fetched]),
        *in_hbm(*more),
    )


def fetch_kernel(low_size, pos_ref, weight_ref, out_ref, sems):
    copies = [
        pltpu.make_async_copy(
            weight_ref.at[block ^ (pos_ref[0] % low_size)], out_ref.at[block], sems.at[block]
        )
        for block in range(low_size)
    ]
    for copy in copies:
        copy.start()
    for copy in copies:
        copy.wait()


def fetch(position, weight_blocks, low_size):
    return pl.pallas_call(
        functools.partial(fetch_kernel, low_size),
        in_specs=[SMEM, pl.BlockSpec(memory_space=pltpu.HBM)],
        out_specs=VMEM,
        out_shape=pltpu.VMEM(weight_blocks.shape, BF16),
        scratch_shapes=[pltpu.SemaphoreType.DMA((low_size,))],
        compiler_params=PARAMS,
        cost_estimate=QUICK,
    )(*in_hbm(position, weight_blocks))


def in_hbm(*arrays):
    return [pltpu.with_memory_space_constraint(array, pltpu.HBM) for array in arrays]


def after(value, *others):
    return lax.optimization_barrier((value, *others))[0]


def halve_kernel(ways, *refs):
    kept_refs, got_refs = refs[:ways], refs[ways : 2 * ways]
    placed_ref = refs[2 * ways] if len(refs) > 4 * ways else None
    outs = refs[-2 * ways - (placed_ref is not None) :]
    for way in range(ways):
        kept_ref, got_ref, sent_ref, rest_ref = kept_refs[way], got_refs[way], outs[way], outs[ways + way]
        half = kept_ref.shape[0] // 2
        sent_ref[:half, :] = (kept_ref[half:, :] + got_ref[half : 2 * half, :].astype(F32)).astype(BF16)
        rest_ref[...] = kept_ref[:half, :] + got_ref[:half, :].astype(F32)
        if way == 0 and placed_ref is not None:
            placed = placed_ref[...] + got_ref[2 * half :, :]
            sent_ref[half:, :] = placed
            outs[-1][...] = placed


def halve(kept, got, placed=None, cost=QUICK):
    placed = [] if placed is None else [placed]
    extra = [placed[0].shape[0] if placed and not way else 0 for way in range(len(kept))]
    shapes = [(k.shape[0] // 2, k.shape[1]) for k in kept]
    outs = pl.pallas_call(
        functools.partial(halve_kernel, len(kept)),
        in_specs=[VMEM] * (2 * len(kept) + len(placed)),
        out_specs=[VMEM] * (2 * len(kept) + len(placed)),
        out_shape=[jax.ShapeDtypeStruct((n + e, r), BF16) for (n, r), e in zip(shapes, extra)]
        + [jax.ShapeDtypeStruct(shape, F32) for shape in shapes]
        + [jax.ShapeDtypeStruct(p.shape, BF16) for p in placed],
        compiler_params=PARAMS,
        cost_estimate=cost,
    )(*kept, *got, *placed)
    ways = len(kept)
    return outs[:ways], outs[ways : 2 * ways], *outs[2 * ways :]


def last_kernel(ways, *refs):
    kept_refs, got_refs = refs[:ways], refs[ways : 2 * ways]
    placed_ref = refs[2 * ways] if len(refs) > 2 * ways + 1 else None
    out_ref = refs[2 * ways + (placed_ref is not None)]
    start = 0
    for kept_ref, got_ref in zip(kept_refs, got_refs):
        half, count = kept_ref.shape[0] // 2, kept_ref.shape[1]
        out_ref[:, start : start + count] = (
            kept_ref[half:, :] + got_ref[half : 2 * half, :].astype(F32)
        ).astype(BF16)
        start += count
    if placed_ref is not None:
        refs[-1][...] = placed_ref[...] + got_refs[0][2 * kept_refs[0].shape[0] // 2 :, :]


def last_parts(kept, got, placed=None, cost=QUICK):
    placed = [] if placed is None else [placed]
    shape = kept[0].shape[0] // 2, sum(k.shape[1] for k in kept)
    return pl.pallas_call(
        functools.partial(last_kernel, len(kept)),
        in_specs=[VMEM] * (2 * len(kept) + len(placed)),
        out_specs=[VMEM] * (1 + len(placed)),
        out_shape=[jax.ShapeDtypeStruct(shape, BF16)]
        + [jax.ShapeDtypeStruct(p.shape, BF16) for p in placed],
        compiler_params=PARAMS,
        cost_estimate=cost,
    )(*kept, *got, *placed)


def up_body(low_size, tile_rows, pieces, tiles, micro_count, *refs):
    pos_ref, classes_ref, live_ref = refs[:3]
    grad_refs = refs[3 : 3 + tiles]
    hidden_refs = refs[3 + tiles : -2]
    out_ref, total_ref = refs[-2:]
    high = pos_ref[0] // low_size
    total_ref[...] = jnp.zeros_like(total_ref)
    rank_part = total_ref.shape[1]
    for tile, index, piece, first in pieces:
        k, m, offset = piece
        size = min(SEG, tile_rows)
        seg = segment_of(high, piece, tile_rows)
        lanes = slice(offset, offset + size)

        @pl.when(seg < live_ref[m])
        def _():
            if k == 0:
                start = m * (hidden_refs[0].shape[0] // micro_count) + high * rank_part
                rows = pl.ds(pl.multiple_of(start, rank_part), rank_part)
            else:
                rows = slice(m * rank_part, (m + 1) * rank_part)
            hidden = hidden_refs[k][rows, lanes]
            total_ref[classes_ref[m, seg]] += jnp.dot(
                hidden,
                grad_refs[tile][index, first : first + size, :],
                preferred_element_type=F32,
            )

    out_ref[...] = total_ref[...].astype(BF16)


def shards(
    output_gradient,
    forward_input,
    saved_rank_outputs,
    projection_weight,
    adapter_down_maps,
    adapter_up_maps,
    segment_adapter_class,
    live_segment_table,
):
    grad_tile = output_gradient[0, 0]
    micro_count, tile_rows, tile_cols = grad_tile.shape
    up_tile = adapter_up_maps[0, 0]
    class_count, rank_part, _ = up_tile.shape
    rank, portion = adapter_down_maps.shape[2:]
    tiles = lax.axis_size("tensor")
    low_size = min(tiles, 8)
    high_size = tiles // low_size
    position = lax.axis_index("tensor")
    high = position // low_size
    weight_blocks = projection_weight[0, 0].reshape(low_size, portion, tile_cols)
    position, classes, live = lax.optimization_barrier(
        (position.astype(jnp.int32)[None], segment_adapter_class[0] + 0, live_segment_table[0] + 0)
    )
    scalars = position, classes, live
    position = position[0]
    size = min(SEG, tile_rows)
    offsets = range(0, tile_rows, size)

    own_pieces = [(0, m, (0, m, o), o) for m in range(micro_count) for o in offsets]

    def pieces_of(m, count=1):
        span = tile_rows // count
        return [
            ((k - 1) * count + o // span, 0, (k, m, o), o % span)
            for k in range(1, high_size)
            for o in offsets
        ]

    def produce(grads, pieces, turns, sends, keeps, cost, hidden=None, fetched=None):
        return product(
            scalars, grads, pieces, tile_rows, weight_blocks, up_tile, low_size, turns, sends, keeps,
            cost, size, hidden, fetched,
        )

    hidden = saved_rank_outputs[0]

    first_rows = lax.optimization_barrier(grad_tile[0])
    got0 = [partner(first_rows, k * low_size)[None] for k in range(1, high_size)]
    (own_grads,) = in_hbm(after(grad_tile, first_rows))
    sent_x, sent_y, placed = produce([own_grads], own_pieces, False, True, False, QUICK, hidden)
    first_x, first_y = partner(sent_x, 1), partner(sent_y, 2)
    (own_grads,) = in_hbm(after(grad_tile, sent_x, sent_y))
    kept_x, kept_y, part = produce([own_grads], own_pieces, False, False, True, QUICK)
    parts = [part]
    rows0 = after(got0[0], part), *got0[1:]
    c_sent_x, c_sent_y, c_kept_x, c_kept_y, part = produce(
        list(rows0), pieces_of(0), False, True, True, LONG
    )
    parts.append(part)
    second_rows = after(grad_tile[1], *got0)
    got1 = [partner(second_rows, k * low_size)[None] for k in range(1, high_size)]

    (sent_x, sent_y), (kept_x, kept_y), placed = halve(
        (after(kept_x, part), kept_y), (first_x, first_y), placed
    )
    second_x, second_y = partner(sent_x, 2), partner(sent_y, 1)
    c_first_x = partner(after(c_sent_x, sent_x, sent_y), 1)
    c_first_y = partner(after(c_sent_y, sent_x, sent_y), 2)

    fetched = fetch(after(scalars[0], sent_x, sent_y), weight_blocks, low_size)

    chunks = [([grad_tile], own_pieces), (got0, pieces_of(0)), (got1, pieces_of(1))]
    order = [piece for _, pieces in chunks for _, _, piece, _ in pieces]
    d_sent_x, d_sent_y, d_kept_x, d_kept_y, part = produce(
        got1, pieces_of(1), False, True, True, LONG, None, fetched
    )
    parts.append(part)
    own_third, placed = last_parts((after(kept_x, part), kept_y), (second_x, second_y), placed)
    own_last = relay(own_third, 4)
    own_sums = (kept_x, second_x), (kept_y, second_y)

    rows_total = len(order) * size
    blocks = rows_total // tile_rows

    def small(kernel, shapes, *operands, scratch=(), cost=QUICK):
        return pl.pallas_call(
            kernel,
            in_specs=[SMEM] + [VMEM] * len(operands),
            out_specs=[VMEM] * len(shapes),
            out_shape=[jax.ShapeDtypeStruct(*shape) for shape in shapes],
            scratch_shapes=list(scratch),
            compiler_params=PARAMS,
            cost_estimate=cost,
        )(*in_hbm(scalars[0]), *operands)

    whole_parts = [(at, start) for at, part in enumerate(parts) for start in range(0, part.shape[1], tile_rows)]

    def collect_kernel(_, *refs):
        *part_refs, placed_ref, out_ref = refs
        for block, (at, start) in enumerate(whole_parts):
            out_ref[block * rank_part : (block + 1) * rank_part, :] = part_refs[at][
                :, start : start + tile_rows
            ].astype(BF16)
        out_ref[blocks * rank_part :, :] = placed_ref[...]

    message = blocks * rank_part, tile_rows
    (shared,) = small(
        collect_kernel, [((message[0] + placed.shape[0], tile_rows), BF16)], *parts, placed
    )
    near = partner(shared, 4)

    (c_sent_x, c_sent_y), c_kept = halve(
        (after(c_kept_x, shared), c_kept_y), (c_first_x, c_first_y)
    )
    c_second_x, c_second_y = partner(c_sent_x, 2), partner(c_sent_y, 1)

    def near_kernel(pos_ref, *refs):
        count = len(parts)
        part_refs, placed_ref, near_ref = refs[:count], refs[count], refs[count + 1]
        shared_ref, total_ref, out_ref, *far_refs, wide_ref = refs[count + 2 :]
        for block, (at, start) in enumerate(whole_parts):
            rows = slice(block * rank_part, (block + 1) * rank_part)
            total = part_refs[at][:, start : start + tile_rows] + near_ref[rows, :].astype(F32)
            total_ref[rows, :] = total
            shared_ref[rows, :] = total.astype(BF16)
        out_ref[...] = placed_ref[...] + near_ref[blocks * rank_part :, :]
        wide_ref[...] = out_ref[...].astype(F32)
        for k, far_ref in enumerate(far_refs, 1):
            for m in range(micro_count):
                start = m * rank + ((pos_ref[0] // low_size) ^ k) * rank_part
                far_ref[m * rank_part : (m + 1) * rank_part, :] = wide_ref[
                    pl.ds(pl.multiple_of(start, rank_part), rank_part), :
                ].astype(BF16)

    shared, total, placed, *wanted = small(
        near_kernel,
        [(message, BF16), (message, F32), (placed.shape, BF16)]
        + [((micro_count * rank_part, tile_rows), BF16)] * (high_size - 1),
        *parts,
        placed,
        near,
        scratch=[pltpu.VMEM(placed.shape, F32)],
    )
    far = [partner(shared, k * low_size) for k in range(1, high_size)]

    def columns_of(j, piece):
        k, m, offset = piece
        at = order.index((k ^ j, m, offset))
        return slice(at * size, (at + 1) * size)

    def lowrank_kernel(pos_ref, *refs):
        out_ref = refs[-1]
        for at, piece in enumerate(order):
            for j in range(high_size):
                block, start = divmod(columns_of(j, piece).start, tile_rows)
                value = refs[j][
                    block * rank_part : (block + 1) * rank_part, start : start + size
                ].astype(F32)
                start = pl.multiple_of(((pos_ref[0] // low_size) ^ j) * rank_part, rank_part)
                out_ref[pl.ds(start, rank_part), at * size : (at + 1) * size] = value

    (lowrank,) = small(lowrank_kernel, [((rank, rows_total), F32)], total, *far)

    hiddens = [placed] + [
        partner(after(w, shared), k * low_size) for k, w in enumerate(wanted, 1)
    ]

    halves = [range(0, len(order) // 2), range(len(order) // 2, len(order))]

    def riders(way, count):
        fit = count // size
        for i, at in enumerate(halves[way]):
            rows = slice(i // fit * rank, (i // fit + 1) * rank)
            yield rows, slice(i % fit * size, (i % fit + 1) * size), slice(at * size, (at + 1) * size)

    def riding(way, count):
        return -(-len(halves[way]) // (count // size)) * rank

    def ride(ref, first, way, lowrank_ref):
        for rows, there, whole in riders(way, ref.shape[1]):
            ref[first + rows.start : first + rows.stop, there] = lowrank_ref[:, whole].astype(BF16)

    def arrive(ref, first, way, lowrank_ref, out_ref):
        for rows, there, whole in riders(way, ref.shape[1]):
            got = ref[first + rows.start : first + rows.stop, there].astype(F32)
            out_ref[:, whole] = (lowrank_ref[:, whole] + got).astype(out_ref.dtype)

    half_rows = d_sent_x.shape[0] // 2
    d_counts = [d_sent_x.shape[1], d_sent_y.shape[1]]

    def append_kernel(_, *refs):
        for way in range(2):
            refs[3 + way][: 2 * half_rows, :] = refs[way][...]
            ride(refs[3 + way], 2 * half_rows, way, refs[2])

    d_sent_x, d_sent_y = small(
        append_kernel,
        [((2 * half_rows + riding(way, n), n), BF16) for way, n in enumerate(d_counts)],
        d_sent_x,
        d_sent_y,
        after(lowrank, *c_kept),
    )
    d_first_x, d_first_y = partner(d_sent_x, 1), partner(d_sent_y, 2)

    all_grads, all_pieces = [], []
    for grads, pieces in chunks:
        all_pieces += [(tile + len(all_grads), *rest) for tile, *rest in pieces]
        all_grads += grads
    up_map_gradient = pl.pallas_call(
        functools.partial(
            up_body, low_size, tile_rows, all_pieces, len(all_grads), micro_count
        ),
        in_specs=[SMEM] * 3 + [VMEM] * (len(all_grads) + high_size),
        out_specs=VMEM,
        out_shape=jax.ShapeDtypeStruct(up_tile.shape, BF16),
        scratch_shapes=[pltpu.VMEM(up_tile.shape, F32)],
        compiler_params=PARAMS,
        cost_estimate=LONG,
    )(*in_hbm(*scalars), *all_grads, *hiddens)

    (c_third,) = last_parts((after(c_kept[0], d_sent_x), c_kept[1]), (c_second_x, c_second_y))
    c_last = relay(c_third, 4)

    def third_kernel(_, *refs):
        lowrank_ref, next_ref = refs[4], refs[9]
        for way in range(2):
            kept_ref, got_ref, sent_ref, rest_ref = refs[way], refs[2 + way], refs[5 + way], refs[7 + way]
            half = kept_ref.shape[0] // 2
            sent_ref[:half, :] = (
                kept_ref[half:, :] + got_ref[half : 2 * half, :].astype(F32)
            ).astype(BF16)
            rest_ref[...] = kept_ref[:half, :] + got_ref[:half, :].astype(F32)
            arrive(got_ref, 2 * half, way, lowrank_ref, next_ref)
            ride(sent_ref, half, way, next_ref)

    d_sent_x, d_sent_y, *d_kept, lowrank = small(
        third_kernel,
        [((half_rows + riding(way, n), n), BF16) for way, n in enumerate(d_counts)]
        + [((half_rows, n), F32) for n in d_counts]
        + [((rank, rows_total), F32)],
        d_kept_x,
        after(d_kept_y, up_map_gradient, own_last, c_third),
        d_first_x,
        d_first_y,
        lowrank,
    )
    d_second_x, d_second_y = partner(d_sent_x, 2), partner(d_sent_y, 1)
    (d_third,) = last_parts(d_kept, (d_second_x, d_second_y))
    d_last = relay(d_third, 4)

    def whole_kernel(_, lowrank_ref, got_x_ref, got_y_ref, out_ref):
        for way, got_ref in enumerate((got_x_ref, got_y_ref)):
            arrive(got_ref, half_rows, way, lowrank_ref, out_ref)

    (lowrank,) = small(
        whole_kernel,
        [((rank, rows_total), BF16)],
        after(lowrank, d_third),
        d_second_x,
        d_second_y,
    )

    down = adapter_down_maps[0]

    def adapter_kernel(groups, *refs):
        pos_ref, classes_ref, _, down_ref, lowrank_ref = refs[:5]
        sum_refs = refs[5 : 5 + 2 * groups]
        out_ref, total_ref = refs[5 + 2 * groups :]
        own = pos_ref[0] // low_size
        start = 0
        for g in range(groups):
            kept_ref, second_ref = sum_refs[2 * g : 2 * g + 2]
            half, count = kept_ref.shape[0] // 2, kept_ref.shape[1]
            total_ref[:, start : start + count] = (
                kept_ref[:half, :] + second_ref[:half, :].astype(F32)
            )
            start += count
        for at in range(start // size):
            piece = order[at]
            seg = segment_of(own, piece, tile_rows)
            rows = slice(at * size, (at + 1) * size)
            adapter = lax.dot_general(
                down_ref[classes_ref[piece[1], seg]],
                lowrank_ref[:, rows],
                TN,
                preferred_element_type=F32,
            )
            out_ref[:, rows] = (total_ref[:, rows] + adapter).astype(BF16)

    sums = own_sums + (
        (c_kept[0], c_second_x),
        (c_kept[1], c_second_y),
        (d_kept[0], d_second_x),
        (d_kept[1], d_second_y),
    )
    kept = pl.pallas_call(
        functools.partial(adapter_kernel, len(sums)),
        in_specs=[SMEM] * 3 + [VMEM] * (2 + 2 * len(sums)),
        out_specs=VMEM,
        out_shape=jax.ShapeDtypeStruct((portion, rows_total), BF16),
        scratch_shapes=[pltpu.VMEM((portion, rows_total), F32)],
        compiler_params=PARAMS,
        cost_estimate=QUICK,
    )(*in_hbm(*scalars, down), lowrank, *[a for two in sums for a in two])
    kept = relay(kept, 0)

    def finish_kernel(pos_ref, kept_ref, *refs):
        *got_refs, out_ref, total_ref, turned_ref, sem = refs
        own = pos_ref[0] // low_size
        start = 0
        for got_ref in got_refs:
            count = got_ref.shape[1]
            total_ref[:, start : start + count] = (
                kept_ref[:, start : start + count].astype(F32) + got_ref[...].astype(F32)
            ).astype(BF16)
            start += count
        copies = []
        for at in range(start // size):
            k, m, offset = order[at]
            base = pl.multiple_of((own ^ k) * tile_rows + offset, size)
            rows = slice(at * size, (at + 1) * size)
            turned_ref[rows, :] = total_ref[:, rows].T
            copies.append(
                pltpu.make_async_copy(
                    turned_ref.at[rows, :], out_ref.at[m, pl.ds(base, size), :], sem.at[at]
                )
            )
            copies[-1].start()
        for copy in copies:
            copy.wait()

    got = [own_last, c_last, d_last]
    grad_prev = pl.pallas_call(
        finish_kernel,
        in_specs=[SMEM] + [VMEM] * (1 + len(got)),
        out_specs=pl.BlockSpec(memory_space=pltpu.HBM),
        out_shape=jax.ShapeDtypeStruct((micro_count, high_size * tile_rows, portion), BF16),
        scratch_shapes=[
            pltpu.VMEM((portion, rows_total), BF16),
            pltpu.VMEM((rows_total, portion), BF16),
            pltpu.SemaphoreType.DMA((rows_total // size,)),
        ],
        compiler_params=PARAMS,
        cost_estimate=QUICK,
    )(*in_hbm(scalars[0]), kept, *got)

    def down_kernel(pos_ref, classes_ref, live_ref, inputs_ref, lowrank_ref, out_ref, total_ref):
        own = pos_ref[0] // low_size
        total_ref[...] = jnp.zeros_like(total_ref)
        for at, piece in enumerate(order):
            k, m, offset = piece
            seg = segment_of(own, piece, tile_rows)

            @pl.when(seg < live_ref[m])
            def _():
                base = pl.multiple_of((own ^ k) * tile_rows + offset, size)
                total_ref[classes_ref[m, seg]] += jnp.dot(
                    lowrank_ref[:, at * size : (at + 1) * size],
                    inputs_ref[m, pl.ds(base, size), :],
                    preferred_element_type=F32,
                )

        out_ref[...] = total_ref[...].astype(BF16)

    down_map_gradient = pl.pallas_call(
        down_kernel,
        in_specs=[SMEM] * 3 + [VMEM] * 2,
        out_specs=VMEM,
        out_shape=jax.ShapeDtypeStruct(down.shape, BF16),
        scratch_shapes=[pltpu.VMEM(down.shape, F32)],
        compiler_params=PARAMS,
        cost_estimate=LONG,
    )(*in_hbm(*scalars, forward_input[0]), lowrank)

    return (
        grad_prev[None],
        down_map_gradient[None],
        up_map_gradient[None, None],
    )


def solution(mesh):
    in_specs = (
        P("pipe", "tensor", None, None, None),
        P("pipe", None, None, "tensor"),
        P("pipe", None, "tensor", None),
        P("pipe", "tensor", None, None),
        P("pipe", None, None, "tensor"),
        P("pipe", "tensor", None, None, None),
        P("pipe", None, None),
        P("pipe", None),
    )
    out_specs = (
        P("pipe", None, None, "tensor"),
        P("pipe", None, None, "tensor"),
        P("pipe", "tensor", None, None, None),
    )
    return jax.shard_map(shards, mesh=mesh, in_specs=in_specs, out_specs=out_specs, check_vma=False)
```

```python
import functools

import jax
import jax.numpy as jnp
from jax import lax
from jax.experimental import pallas as pl
from jax.experimental.pallas import tpu as pltpu
from jax.sharding import PartitionSpec as P

SEG = 128
BF16 = jnp.bfloat16
F32 = jnp.float32
SMEM = pl.BlockSpec(memory_space=pltpu.SMEM)
VMEM = pl.BlockSpec(memory_space=pltpu.VMEM)
TN = (((0,), (0,)), ((), ()))
PARAMS = pltpu.CompilerParams(vmem_limit_bytes=16 * 2**20)
PRODUCT_PARAMS = pltpu.CompilerParams(vmem_limit_bytes=24 * 2**20)
QUICK = pl.CostEstimate(flops=1000, bytes_accessed=1000, transcendentals=0)
LONG = pl.CostEstimate(flops=4 * 10**10, bytes_accessed=1000, transcendentals=0)


def partner(value, mask):
    pairs = [(source, source ^ mask) for source in range(lax.axis_size("tensor"))]
    return lax.ppermute(value, "tensor", pairs)


def relay(value, mask):
    sections, tiles = lax.axis_size("pipe"), lax.axis_size("tensor")
    pairs = [
        (p * tiles + t, (p - 1) % sections * tiles + (t ^ mask))
        for p in range(sections)
        for t in range(tiles)
    ]
    return lax.ppermute(value, ("pipe", "tensor"), pairs)


def segment_of(high, piece, tile_rows):
    k, _, offset = piece
    return ((high ^ k) * tile_rows + offset) // SEG


def product_body(low_size, tile_rows, pieces, tiles, half, turns, sends, keeps, with_hidden, fetches, *refs):
    pos_ref, classes_ref, live_ref = refs[:3]
    grad_refs = refs[3 : 3 + tiles]
    weight_hbm = refs[3 + tiles]
    rows_ref, *scratch = refs[-3:] if fetches else refs[-1:]
    rest = list(refs[4 + tiles : -1 - len(scratch)])
    weight_ref, sems = scratch if fetches else (weight_hbm, None)
    up_ref = rest.pop(0) if keeps else None
    hidden_ref = rest.pop(0) if with_hidden else None
    sent_x, sent_y = (rest.pop(0), rest.pop(0)) if sends else (None, None)
    placed_ref = rest.pop(0) if with_hidden else None
    kept_x, kept_y, rank_ref = rest if keeps else (None, None, None)
    low, high = pos_ref[0] % low_size, pos_ref[0] // low_size
    total = rows_ref.shape[1]
    size = total // len(pieces)

    def weight_copy(block):
        return pltpu.make_async_copy(
            weight_hbm.at[block ^ low], weight_ref.at[block], sems.at[block]
        )

    jobs = []
    for x, y in ((1, 1), (1, 0), (0, 1), (0, 0)):
        to_x = (sent_x if x else kept_x, *((y, 2) if turns else (2 * y, 1)))
        to_y = (sent_y if y else kept_y, *((x, 2) if turns else (2 * x, 1)))
        start = 0 if to_x[0] is not None else half
        stop = total if to_y[0] is not None else half
        if start < stop:
            jobs.append((x + 2 * y, start, stop, to_x, to_y))
    if fetches:
        for block, *_ in jobs:
            for z in range(2):
                weight_copy(block + 4 * z).start()

    if with_hidden:
        micro_count, count, rank = hidden_ref.shape
        spot = lax.broadcasted_iota(jnp.int32, (count, half), 1)
        row = lax.broadcasted_iota(jnp.int32, (count, half), 0)
        chosen = (spot == low * count + row).astype(F32).astype(BF16)
        for m in range(micro_count):
            placed = lax.dot_general(
                hidden_ref[m], chosen, TN, preferred_element_type=F32
            ).astype(BF16)
            placed_ref[m * rank : (m + 1) * rank, :] = placed
            start = sent_x.shape[0] - (micro_count - m) * rank
            sent_x[start : start + rank, :] = placed

    for at, (tile, index, piece, first) in enumerate(pieces):
        seg = segment_of(high, piece, tile_rows)
        alive = seg < live_ref[piece[1]]
        place = slice(at * size, (at + 1) * size)

        @pl.when(alive)
        def _():
            rows = grad_refs[tile][index, first : first + size, :].T
            rows_ref[:, place] = rows
            if keeps:
                up = up_ref[classes_ref[piece[1], seg]]
                rank_ref[:, place] = jnp.dot(up, rows, preferred_element_type=F32)

        @pl.when(jnp.logical_not(alive))
        def _():
            rows_ref[:, place] = jnp.zeros((rows_ref.shape[0], size), rows_ref.dtype)
            if keeps:
                rank_ref[:, place] = jnp.zeros((rank_ref.shape[0], size), F32)

    for block, start, stop, to_x, to_y in jobs:

        @pl.loop(0, 2)
        def _(z):
            if fetches:
                weight_copy(block + 4 * z).wait()
            value = jnp.dot(
                weight_ref[block + 4 * z], rows_ref[:, start:stop], preferred_element_type=F32
            )
            for (ref, slot, step), part in (
                (to_x, value[:, : half - start]),
                (to_y, value[:, half - start :]),
            ):
                if ref is not None:
                    width = part.shape[0]
                    place = pl.ds(pl.multiple_of((slot + step * z) * width, width), width)
                    ref[place, :] = part.astype(ref.dtype)


def product(scalars, grads, pieces, tile_rows, weight_blocks, up_tile, low_size, turns, sends, keeps, cost, size, hidden=None, fetched=None):
    blocks, width, depth = weight_blocks.shape
    rows = len(pieces) * size
    half = rows // 2
    if rows > 128 and half % 128:
        half = half // 128 * 128 + 128
    outs = []
    extra = 0 if hidden is None else hidden.shape[0] * hidden.shape[2]
    for wanted, dtype in ((sends, BF16), (keeps, F32)):
        if wanted:
            for more, n in ((extra, half), (0, rows - half)):
                outs.append(jax.ShapeDtypeStruct((blocks // 2 * width + more, n), dtype))
    if extra:
        outs.append(jax.ShapeDtypeStruct((extra, half), BF16))
    if keeps:
        outs.append(jax.ShapeDtypeStruct((up_tile.shape[1], rows), F32))
    more = ([up_tile] if keeps else []) + ([] if hidden is None else [hidden])
    return pl.pallas_call(
        functools.partial(
            product_body, low_size, tile_rows, pieces, len(grads), half, turns, sends, keeps, extra > 0,
            fetched is None,
        ),
        in_specs=[SMEM] * 3
        + [VMEM] * len(grads)
        + [pl.BlockSpec(memory_space=pltpu.HBM) if fetched is None else VMEM]
        + [VMEM] * len(more),
        out_specs=[VMEM] * len(outs),
        out_shape=outs,
        scratch_shapes=[pltpu.VMEM((depth, rows), BF16)]
        + [pltpu.VMEM(weight_blocks.shape, BF16), pltpu.SemaphoreType.DMA((blocks,))]
        * (fetched is None),
        compiler_params=PRODUCT_PARAMS,
        cost_estimate=cost,
    )(
        *in_hbm(*scalars),
        *grads,
        *(in_hbm(weight_blocks) if fetched is None else [fetched]),
        *in_hbm(*more),
    )


def fetch_kernel(low_size, pos_ref, weight_ref, out_ref, sems):
    copies = [
        pltpu.make_async_copy(
            weight_ref.at[block ^ (pos_ref[0] % low_size)], out_ref.at[block], sems.at[block]
        )
        for block in range(low_size)
    ]
    for copy in copies:
        copy.start()
    for copy in copies:
        copy.wait()


def fetch(position, weight_blocks, low_size):
    return pl.pallas_call(
        functools.partial(fetch_kernel, low_size),
        in_specs=[SMEM, pl.BlockSpec(memory_space=pltpu.HBM)],
        out_specs=VMEM,
        out_shape=pltpu.VMEM(weight_blocks.shape, BF16),
        scratch_shapes=[pltpu.SemaphoreType.DMA((low_size,))],
        compiler_params=PARAMS,
        cost_estimate=QUICK,
    )(*in_hbm(position, weight_blocks))


def in_hbm(*arrays):
    return [pltpu.with_memory_space_constraint(array, pltpu.HBM) for array in arrays]


def after(value, *others):
    return lax.optimization_barrier((value, *others))[0]


def halve_kernel(ways, *refs):
    kept_refs, got_refs = refs[:ways], refs[ways : 2 * ways]
    placed_ref = refs[2 * ways] if len(refs) > 4 * ways else None
    outs = refs[-2 * ways - (placed_ref is not None) :]
    for way in range(ways):
        kept_ref, got_ref, sent_ref, rest_ref = kept_refs[way], got_refs[way], outs[way], outs[ways + way]
        half = kept_ref.shape[0] // 2
        sent_ref[:half, :] = (kept_ref[half:, :] + got_ref[half : 2 * half, :].astype(F32)).astype(BF16)
        rest_ref[...] = kept_ref[:half, :] + got_ref[:half, :].astype(F32)
        if way == 0 and placed_ref is not None:
            placed = placed_ref[...] + got_ref[2 * half :, :]
            sent_ref[half:, :] = placed
            outs[-1][...] = placed


def halve(kept, got, placed=None, cost=QUICK):
    placed = [] if placed is None else [placed]
    extra = [placed[0].shape[0] if placed and not way else 0 for way in range(len(kept))]
    shapes = [(k.shape[0] // 2, k.shape[1]) for k in kept]
    outs = pl.pallas_call(
        functools.partial(halve_kernel, len(kept)),
        in_specs=[VMEM] * (2 * len(kept) + len(placed)),
        out_specs=[VMEM] * (2 * len(kept) + len(placed)),
        out_shape=[jax.ShapeDtypeStruct((n + e, r), BF16) for (n, r), e in zip(shapes, extra)]
        + [jax.ShapeDtypeStruct(shape, F32) for shape in shapes]
        + [jax.ShapeDtypeStruct(p.shape, BF16) for p in placed],
        compiler_params=PARAMS,
        cost_estimate=cost,
    )(*kept, *got, *placed)
    ways = len(kept)
    return outs[:ways], outs[ways : 2 * ways], *outs[2 * ways :]


def last_kernel(ways, *refs):
    kept_refs, got_refs = refs[:ways], refs[ways : 2 * ways]
    placed_ref = refs[2 * ways] if len(refs) > 2 * ways + 1 else None
    out_ref = refs[2 * ways + (placed_ref is not None)]
    start = 0
    for kept_ref, got_ref in zip(kept_refs, got_refs):
        half, count = kept_ref.shape[0] // 2, kept_ref.shape[1]
        out_ref[:, start : start + count] = (
            kept_ref[half:, :] + got_ref[half : 2 * half, :].astype(F32)
        ).astype(BF16)
        start += count
    if placed_ref is not None:
        refs[-1][...] = placed_ref[...] + got_refs[0][2 * kept_refs[0].shape[0] // 2 :, :]


def last_parts(kept, got, placed=None, cost=QUICK):
    placed = [] if placed is None else [placed]
    shape = kept[0].shape[0] // 2, sum(k.shape[1] for k in kept)
    return pl.pallas_call(
        functools.partial(last_kernel, len(kept)),
        in_specs=[VMEM] * (2 * len(kept) + len(placed)),
        out_specs=[VMEM] * (1 + len(placed)),
        out_shape=[jax.ShapeDtypeStruct(shape, BF16)]
        + [jax.ShapeDtypeStruct(p.shape, BF16) for p in placed],
        compiler_params=PARAMS,
        cost_estimate=cost,
    )(*kept, *got, *placed)


def up_body(low_size, tile_rows, pieces, tiles, micro_count, *refs):
    pos_ref, classes_ref, live_ref = refs[:3]
    grad_refs = refs[3 : 3 + tiles]
    hidden_refs = refs[3 + tiles : -2]
    out_ref, total_ref = refs[-2:]
    high = pos_ref[0] // low_size
    total_ref[...] = jnp.zeros_like(total_ref)
    rank_part = total_ref.shape[1]
    for tile, index, piece, first in pieces:
        k, m, offset = piece
        size = min(SEG, tile_rows)
        seg = segment_of(high, piece, tile_rows)
        lanes = slice(offset, offset + size)

        @pl.when(seg < live_ref[m])
        def _():
            if k == 0:
                start = m * (hidden_refs[0].shape[0] // micro_count) + high * rank_part
                rows = pl.ds(pl.multiple_of(start, rank_part), rank_part)
            else:
                rows = slice(m * rank_part, (m + 1) * rank_part)
            hidden = hidden_refs[k][rows, lanes]
            total_ref[classes_ref[m, seg]] += jnp.dot(
                hidden,
                grad_refs[tile][index, first : first + size, :],
                preferred_element_type=F32,
            )

    out_ref[...] = total_ref[...].astype(BF16)


def shards(
    output_gradient,
    forward_input,
    saved_rank_outputs,
    projection_weight,
    adapter_down_maps,
    adapter_up_maps,
    segment_adapter_class,
    live_segment_table,
):
    grad_tile = output_gradient[0, 0]
    micro_count, tile_rows, tile_cols = grad_tile.shape
    up_tile = adapter_up_maps[0, 0]
    class_count, rank_part, _ = up_tile.shape
    rank, portion = adapter_down_maps.shape[2:]
    tiles = lax.axis_size("tensor")
    low_size = min(tiles, 8)
    high_size = tiles // low_size
    position = lax.axis_index("tensor")
    high = position // low_size
    weight_blocks = projection_weight[0, 0].reshape(low_size, portion, tile_cols)
    position, classes, live = lax.optimization_barrier(
        (position.astype(jnp.int32)[None], segment_adapter_class[0] + 0, live_segment_table[0] + 0)
    )
    scalars = position, classes, live
    position = position[0]
    size = min(SEG, tile_rows)
    offsets = range(0, tile_rows, size)

    own_pieces = [(0, m, (0, m, o), o) for m in range(micro_count) for o in offsets]

    def pieces_of(m, count=1):
        span = tile_rows // count
        return [
            ((k - 1) * count + o // span, 0, (k, m, o), o % span)
            for k in range(1, high_size)
            for o in offsets
        ]

    def produce(grads, pieces, turns, sends, keeps, cost, hidden=None, fetched=None):
        return product(
            scalars, grads, pieces, tile_rows, weight_blocks, up_tile, low_size, turns, sends, keeps,
            cost, size, hidden, fetched,
        )

    hidden = saved_rank_outputs[0]

    first_rows = lax.optimization_barrier(grad_tile[0])
    got0 = [partner(first_rows, k * low_size)[None] for k in range(1, high_size)]
    (own_grads,) = in_hbm(after(grad_tile, first_rows))
    sent_x, sent_y, placed = produce([own_grads], own_pieces, False, True, False, QUICK, hidden)
    first_x, first_y = partner(sent_x, 1), partner(sent_y, 2)
    (own_grads,) = in_hbm(after(grad_tile, sent_x, sent_y))
    kept_x, kept_y, part = produce([own_grads], own_pieces, False, False, True, QUICK)
    parts = [part]
    rows0 = after(got0[0], part), *got0[1:]
    c_sent_x, c_sent_y, c_kept_x, c_kept_y, part = produce(
        list(rows0), pieces_of(0), False, True, True, LONG
    )
    parts.append(part)
    second_rows = after(grad_tile[1], *got0)
    got1 = [partner(second_rows, k * low_size)[None] for k in range(1, high_size)]

    (sent_x, sent_y), (kept_x, kept_y), placed = halve(
        (after(kept_x, part), kept_y), (first_x, first_y), placed
    )
    second_x, second_y = partner(sent_x, 2), partner(sent_y, 1)
    c_first_x, c_first_y = partner(c_sent_x, 1), partner(c_sent_y, 2)

    fetched = fetch(after(scalars[0], sent_x, sent_y), weight_blocks, low_size)

    chunks = [([grad_tile], own_pieces), (got0, pieces_of(0)), (got1, pieces_of(1))]
    order = [piece for _, pieces in chunks for _, _, piece, _ in pieces]
    d_sent_x, d_sent_y, d_kept_x, d_kept_y, part = produce(
        got1, pieces_of(1), False, True, True, LONG, None, fetched
    )
    parts.append(part)
    rows_total = len(order) * size
    blocks = rows_total // tile_rows

    def small(kernel, shapes, *operands, scratch=(), cost=QUICK):
        return pl.pallas_call(
            kernel,
            in_specs=[SMEM] + [VMEM] * len(operands),
            out_specs=[VMEM] * len(shapes),
            out_shape=[jax.ShapeDtypeStruct(*shape) for shape in shapes],
            scratch_shapes=list(scratch),
            compiler_params=PARAMS,
            cost_estimate=cost,
        )(*in_hbm(scalars[0]), *operands)

    whole_parts = [(at, start) for at, part in enumerate(parts) for start in range(0, part.shape[1], tile_rows)]

    def collect_kernel(_, *refs):
        for block, (at, start) in enumerate(whole_parts):
            refs[-1][block * rank_part : (block + 1) * rank_part, :] = refs[at][
                :, start : start + tile_rows
            ].astype(BF16)

    message = blocks * rank_part, tile_rows
    (shared,) = small(collect_kernel, [(message, BF16)], *parts)
    (c_sent_x, c_sent_y), c_kept = halve(
        (after(c_kept_x, part), c_kept_y), (c_first_x, c_first_y)
    )
    c_second_x, c_second_y = partner(c_sent_x, 2), partner(c_sent_y, 1)

    near = partner(shared, 4)


    def near_kernel(_, *refs):
        near_ref, shared_ref, total_ref = refs[-3:]
        for block, (at, start) in enumerate(whole_parts):
            rows = slice(block * rank_part, (block + 1) * rank_part)
            total = refs[at][:, start : start + tile_rows] + near_ref[rows, :].astype(F32)
            total_ref[rows, :] = total
            shared_ref[rows, :] = total.astype(BF16)

    shared, total = small(
        near_kernel, [(message, BF16), (message, F32)], *parts[:-1], after(parts[-1], c_sent_x), near
    )
    far = [partner(shared, k * low_size) for k in range(1, high_size)]

    def columns_of(j, piece):
        k, m, offset = piece
        at = order.index((k ^ j, m, offset))
        return slice(at * size, (at + 1) * size)

    def lowrank_kernel(pos_ref, *refs):
        out_ref = refs[-1]
        for at, piece in enumerate(order):
            for j in range(high_size):
                block, start = divmod(columns_of(j, piece).start, tile_rows)
                value = refs[j][
                    block * rank_part : (block + 1) * rank_part, start : start + size
                ].astype(F32)
                start = pl.multiple_of(((pos_ref[0] // low_size) ^ j) * rank_part, rank_part)
                out_ref[pl.ds(start, rank_part), at * size : (at + 1) * size] = value

    (lowrank,) = small(lowrank_kernel, [((rank, rows_total), F32)], total, *far)

    halves = [range(0, len(order) // 2), range(len(order) // 2, len(order))]

    def riders(way, count):
        fit = count // size
        for i, at in enumerate(halves[way]):
            rows = slice(i // fit * rank, (i // fit + 1) * rank)
            yield rows, slice(i % fit * size, (i % fit + 1) * size), slice(at * size, (at + 1) * size)

    def riding(way, count):
        return -(-len(halves[way]) // (count // size)) * rank

    def ride(ref, first, way, lowrank_ref):
        for rows, there, whole in riders(way, ref.shape[1]):
            ref[first + rows.start : first + rows.stop, there] = lowrank_ref[:, whole].astype(BF16)

    def arrive(ref, first, way, lowrank_ref, out_ref):
        for rows, there, whole in riders(way, ref.shape[1]):
            got = ref[first + rows.start : first + rows.stop, there].astype(F32)
            out_ref[:, whole] = (lowrank_ref[:, whole] + got).astype(out_ref.dtype)

    half_rows = d_sent_x.shape[0] // 2
    d_counts = [d_sent_x.shape[1], d_sent_y.shape[1]]

    def append_kernel(_, *refs):
        for way in range(2):
            refs[3 + way][: 2 * half_rows, :] = refs[way][...]
            ride(refs[3 + way], 2 * half_rows, way, refs[2])

    d_sent_x, d_sent_y = small(
        append_kernel,
        [((2 * half_rows + riding(way, n), n), BF16) for way, n in enumerate(d_counts)],
        d_sent_x,
        d_sent_y,
        after(lowrank, c_second_x, c_second_y),
    )
    d_first_x, d_first_y = partner(d_sent_x, 1), partner(d_sent_y, 2)

    own_third, placed = last_parts(
        (after(kept_x, d_sent_x), kept_y), (second_x, second_y), placed, LONG
    )
    own_last = relay(own_third, 4)
    own_sums = (kept_x, second_x), (kept_y, second_y)

    def hidden_kernel(pos_ref, placed_ref, near_ref, out_ref, *refs):
        *far_refs, wide_ref = refs
        out_ref[...] = placed_ref[...] + near_ref[...]
        wide_ref[...] = out_ref[...].astype(F32)
        for k, far_ref in enumerate(far_refs, 1):
            for m in range(micro_count):
                start = m * rank + ((pos_ref[0] // low_size) ^ k) * rank_part
                far_ref[m * rank_part : (m + 1) * rank_part, :] = wide_ref[
                    pl.ds(pl.multiple_of(start, rank_part), rank_part), :
                ].astype(BF16)

    placed, *wanted = small(
        hidden_kernel,
        [(placed.shape, BF16)]
        + [((micro_count * rank_part, tile_rows), BF16)] * (high_size - 1),
        placed,
        partner(placed, 4),
        scratch=[pltpu.VMEM(placed.shape, F32)],
    )
    hiddens = [placed] + [partner(w, k * low_size) for k, w in enumerate(wanted, 1)]

    (c_third,) = last_parts((after(c_kept[0], d_sent_x), c_kept[1]), (c_second_x, c_second_y))
    c_last = relay(c_third, 4)

    def third_kernel(_, *refs):
        lowrank_ref, next_ref = refs[4], refs[9]
        for way in range(2):
            kept_ref, got_ref, sent_ref, rest_ref = refs[way], refs[2 + way], refs[5 + way], refs[7 + way]
            half = kept_ref.shape[0] // 2
            sent_ref[:half, :] = (
                kept_ref[half:, :] + got_ref[half : 2 * half, :].astype(F32)
            ).astype(BF16)
            rest_ref[...] = kept_ref[:half, :] + got_ref[:half, :].astype(F32)
            arrive(got_ref, 2 * half, way, lowrank_ref, next_ref)
            ride(sent_ref, half, way, next_ref)

    d_sent_x, d_sent_y, *d_kept, lowrank = small(
        third_kernel,
        [((half_rows + riding(way, n), n), BF16) for way, n in enumerate(d_counts)]
        + [((half_rows, n), F32) for n in d_counts]
        + [((rank, rows_total), F32)],
        d_kept_x,
        after(d_kept_y, own_last, c_third),
        d_first_x,
        d_first_y,
        lowrank,
    )
    d_second_x, d_second_y = partner(d_sent_x, 2), partner(d_sent_y, 1)
    (d_third,) = last_parts(
        (after(d_kept[0], *hiddens), d_kept[1]), (d_second_x, d_second_y)
    )
    d_last = relay(d_third, 4)

    def whole_kernel(_, lowrank_ref, got_x_ref, got_y_ref, out_ref):
        for way, got_ref in enumerate((got_x_ref, got_y_ref)):
            arrive(got_ref, half_rows, way, lowrank_ref, out_ref)

    (lowrank,) = small(
        whole_kernel,
        [((rank, rows_total), BF16)],
        after(lowrank, d_third),
        d_second_x,
        d_second_y,
    )

    all_grads, all_pieces = [], []
    for grads, pieces in chunks:
        all_pieces += [(tile + len(all_grads), *rest) for tile, *rest in pieces]
        all_grads += grads
    up_map_gradient = pl.pallas_call(
        functools.partial(
            up_body, low_size, tile_rows, all_pieces, len(all_grads), micro_count
        ),
        in_specs=[SMEM] * 3 + [VMEM] * (len(all_grads) + high_size),
        out_specs=VMEM,
        out_shape=jax.ShapeDtypeStruct(up_tile.shape, BF16),
        scratch_shapes=[pltpu.VMEM(up_tile.shape, F32)],
        compiler_params=PARAMS,
        cost_estimate=QUICK,
    )(*in_hbm(*scalars), *all_grads, after(hiddens[0], d_third), *hiddens[1:])

    down = adapter_down_maps[0]

    def adapter_kernel(groups, *refs):
        pos_ref, classes_ref, _, down_ref, lowrank_ref = refs[:5]
        sum_refs = refs[5 : 5 + 2 * groups]
        out_ref, total_ref = refs[5 + 2 * groups :]
        own = pos_ref[0] // low_size
        start = 0
        for g in range(groups):
            kept_ref, second_ref = sum_refs[2 * g : 2 * g + 2]
            half, count = kept_ref.shape[0] // 2, kept_ref.shape[1]
            total_ref[:, start : start + count] = (
                kept_ref[:half, :] + second_ref[:half, :].astype(F32)
            )
            start += count
        for at in range(start // size):
            piece = order[at]
            seg = segment_of(own, piece, tile_rows)
            rows = slice(at * size, (at + 1) * size)
            adapter = lax.dot_general(
                down_ref[classes_ref[piece[1], seg]],
                lowrank_ref[:, rows],
                TN,
                preferred_element_type=F32,
            )
            out_ref[:, rows] = (total_ref[:, rows] + adapter).astype(BF16)

    sums = own_sums + (
        (c_kept[0], c_second_x),
        (c_kept[1], c_second_y),
        (d_kept[0], d_second_x),
        (d_kept[1], d_second_y),
    )
    kept = pl.pallas_call(
        functools.partial(adapter_kernel, len(sums)),
        in_specs=[SMEM] * 3 + [VMEM] * (2 + 2 * len(sums)),
        out_specs=VMEM,
        out_shape=jax.ShapeDtypeStruct((portion, rows_total), BF16),
        scratch_shapes=[pltpu.VMEM((portion, rows_total), F32)],
        compiler_params=PARAMS,
        cost_estimate=QUICK,
    )(*in_hbm(*scalars, down), lowrank, *[a for two in sums for a in two])
    kept = relay(kept, 0)

    def finish_kernel(pos_ref, kept_ref, *refs):
        *got_refs, out_ref, total_ref, turned_ref, sem = refs
        own = pos_ref[0] // low_size
        start = 0
        for got_ref in got_refs:
            count = got_ref.shape[1]
            total_ref[:, start : start + count] = (
                kept_ref[:, start : start + count].astype(F32) + got_ref[...].astype(F32)
            ).astype(BF16)
            start += count
        copies = []
        for at in range(start // size):
            k, m, offset = order[at]
            base = pl.multiple_of((own ^ k) * tile_rows + offset, size)
            rows = slice(at * size, (at + 1) * size)
            turned_ref[rows, :] = total_ref[:, rows].T
            copies.append(
                pltpu.make_async_copy(
                    turned_ref.at[rows, :], out_ref.at[m, pl.ds(base, size), :], sem.at[at]
                )
            )
            copies[-1].start()
        for copy in copies:
            copy.wait()

    def down_kernel(pos_ref, classes_ref, live_ref, inputs_ref, lowrank_ref, out_ref, total_ref):
        own = pos_ref[0] // low_size
        total_ref[...] = jnp.zeros_like(total_ref)
        for at, piece in enumerate(order):
            k, m, offset = piece
            seg = segment_of(own, piece, tile_rows)

            @pl.when(seg < live_ref[m])
            def _():
                base = pl.multiple_of((own ^ k) * tile_rows + offset, size)
                total_ref[classes_ref[m, seg]] += jnp.dot(
                    lowrank_ref[:, at * size : (at + 1) * size],
                    inputs_ref[m, pl.ds(base, size), :],
                    preferred_element_type=F32,
                )

        out_ref[...] = total_ref[...].astype(BF16)

    down_map_gradient = pl.pallas_call(
        down_kernel,
        in_specs=[SMEM] * 3 + [VMEM] * 2,
        out_specs=VMEM,
        out_shape=jax.ShapeDtypeStruct(down.shape, BF16),
        scratch_shapes=[pltpu.VMEM(down.shape, F32)],
        compiler_params=PARAMS,
        cost_estimate=LONG,
    )(*in_hbm(*scalars, forward_input[0]), lowrank)

    got = [own_last, c_last, d_last]
    grad_prev = pl.pallas_call(
        finish_kernel,
        in_specs=[SMEM] + [VMEM] * (1 + len(got)),
        out_specs=pl.BlockSpec(memory_space=pltpu.HBM),
        out_shape=jax.ShapeDtypeStruct((micro_count, high_size * tile_rows, portion), BF16),
        scratch_shapes=[
            pltpu.VMEM((portion, rows_total), BF16),
            pltpu.VMEM((rows_total, portion), BF16),
            pltpu.SemaphoreType.DMA((rows_total // size,)),
        ],
        compiler_params=PARAMS,
        cost_estimate=QUICK,
    )(*in_hbm(after(scalars[0], up_map_gradient, down_map_gradient)), kept, *got)

    return (
        grad_prev[None],
        down_map_gradient[None],
        up_map_gradient[None, None],
    )


def solution(mesh):
    in_specs = (
        P("pipe", "tensor", None, None, None),
        P("pipe", None, None, "tensor"),
        P("pipe", None, "tensor", None),
        P("pipe", "tensor", None, None),
        P("pipe", None, None, "tensor"),
        P("pipe", "tensor", None, None, None),
        P("pipe", None, None),
        P("pipe", None),
    )
    out_specs = (
        P("pipe", None, None, "tensor"),
        P("pipe", None, None, "tensor"),
        P("pipe", "tensor", None, None, None),
    )
    return jax.shard_map(shards, mesh=mesh, in_specs=in_specs, out_specs=out_specs, check_vma=False)
```

```python
import functools

import jax
import jax.numpy as jnp
from jax import lax
from jax.experimental import pallas as pl
from jax.experimental.pallas import tpu as pltpu
from jax.sharding import PartitionSpec as P

SEG = 128
BF16 = jnp.bfloat16
F32 = jnp.float32
SMEM = pl.BlockSpec(memory_space=pltpu.SMEM)
VMEM = pl.BlockSpec(memory_space=pltpu.VMEM)
TN = (((0,), (0,)), ((), ()))
PARAMS = pltpu.CompilerParams(vmem_limit_bytes=16 * 2**20)
PRODUCT_PARAMS = pltpu.CompilerParams(vmem_limit_bytes=24 * 2**20)
QUICK = pl.CostEstimate(flops=1000, bytes_accessed=1000, transcendentals=0)
LONG = pl.CostEstimate(flops=4 * 10**10, bytes_accessed=1000, transcendentals=0)


def partner(value, mask):
    pairs = [(source, source ^ mask) for source in range(lax.axis_size("tensor"))]
    return lax.ppermute(value, "tensor", pairs)


def relay(value, mask):
    sections, tiles = lax.axis_size("pipe"), lax.axis_size("tensor")
    pairs = [
        (p * tiles + t, (p - 1) % sections * tiles + (t ^ mask))
        for p in range(sections)
        for t in range(tiles)
    ]
    return lax.ppermute(value, ("pipe", "tensor"), pairs)


def segment_of(high, piece, tile_rows):
    k, _, offset = piece
    return ((high ^ k) * tile_rows + offset) // SEG


def product_body(low_size, tile_rows, pieces, tiles, half, turns, sends, keeps, with_hidden, fetches, *refs):
    pos_ref, classes_ref, live_ref = refs[:3]
    grad_refs = refs[3 : 3 + tiles]
    weight_hbm = refs[3 + tiles]
    rows_ref, *scratch = refs[-3:] if fetches else refs[-1:]
    rest = list(refs[4 + tiles : -1 - len(scratch)])
    weight_ref, sems = scratch if fetches else (weight_hbm, None)
    up_ref = rest.pop(0) if keeps else None
    hidden_ref = rest.pop(0) if with_hidden else None
    sent_x, sent_y = (rest.pop(0), rest.pop(0)) if sends else (None, None)
    placed_ref = rest.pop(0) if with_hidden else None
    kept_x, kept_y, rank_ref = rest if keeps else (None, None, None)
    low, high = pos_ref[0] % low_size, pos_ref[0] // low_size
    total = rows_ref.shape[1]
    size = total // len(pieces)

    def weight_copy(block):
        return pltpu.make_async_copy(
            weight_hbm.at[block ^ low], weight_ref.at[block], sems.at[block]
        )

    jobs = []
    for x, y in ((1, 1), (1, 0), (0, 1), (0, 0)):
        to_x = (sent_x if x else kept_x, 2 * y, 1)
        to_y = (sent_y if y else kept_y, *((x, 2) if turns else (2 * x, 1)))
        start = 0 if to_x[0] is not None else half
        stop = total if to_y[0] is not None else half
        if start < stop:
            jobs.append((x + 2 * y, start, stop, to_x, to_y))
    if fetches:
        for block, *_ in jobs:
            for z in range(2):
                weight_copy(block + 4 * z).start()

    if with_hidden:
        micro_count, count, rank = hidden_ref.shape
        spot = lax.broadcasted_iota(jnp.int32, (count, half), 1)
        row = lax.broadcasted_iota(jnp.int32, (count, half), 0)
        chosen = (spot == low * count + row).astype(F32).astype(BF16)
        for m in range(micro_count):
            placed = lax.dot_general(
                hidden_ref[m], chosen, TN, preferred_element_type=F32
            ).astype(BF16)
            placed_ref[m * rank : (m + 1) * rank, :] = placed
            start = sent_x.shape[0] - (micro_count - m) * rank
            sent_x[start : start + rank, :] = placed

    for at, (tile, index, piece, first) in enumerate(pieces):
        seg = segment_of(high, piece, tile_rows)
        alive = seg < live_ref[piece[1]]
        place = slice(at * size, (at + 1) * size)

        @pl.when(alive)
        def _():
            rows = grad_refs[tile][index, first : first + size, :].T
            rows_ref[:, place] = rows
            if keeps:
                up = up_ref[classes_ref[piece[1], seg]]
                rank_ref[:, place] = jnp.dot(up, rows, preferred_element_type=F32)

        @pl.when(jnp.logical_not(alive))
        def _():
            rows_ref[:, place] = jnp.zeros((rows_ref.shape[0], size), rows_ref.dtype)
            if keeps:
                rank_ref[:, place] = jnp.zeros((rank_ref.shape[0], size), F32)

    for block, start, stop, to_x, to_y in jobs:

        @pl.loop(0, 2)
        def _(z):
            if fetches:
                weight_copy(block + 4 * z).wait()
            value = jnp.dot(
                weight_ref[block + 4 * z], rows_ref[:, start:stop], preferred_element_type=F32
            )
            for (ref, slot, step), part in (
                (to_x, value[:, : half - start]),
                (to_y, value[:, half - start :]),
            ):
                if ref is not None:
                    width = part.shape[0]
                    place = pl.ds(pl.multiple_of((slot + step * z) * width, width), width)
                    ref[place, :] = part.astype(ref.dtype)


def product(scalars, grads, pieces, tile_rows, weight_blocks, up_tile, low_size, turns, sends, keeps, cost, size, hidden=None, fetched=None):
    blocks, width, depth = weight_blocks.shape
    rows = len(pieces) * size
    half = rows // 2
    if rows > 128 and half % 128:
        half = half // 128 * 128 + 128
    outs = []
    extra = 0 if hidden is None else hidden.shape[0] * hidden.shape[2]
    for wanted, dtype in ((sends, BF16), (keeps, F32)):
        if wanted:
            for more, n in ((extra, half), (0, rows - half)):
                outs.append(jax.ShapeDtypeStruct((blocks // 2 * width + more, n), dtype))
    if extra:
        outs.append(jax.ShapeDtypeStruct((extra, half), BF16))
    if keeps:
        outs.append(jax.ShapeDtypeStruct((up_tile.shape[1], rows), F32))
    more = ([up_tile] if keeps else []) + ([] if hidden is None else [hidden])
    return pl.pallas_call(
        functools.partial(
            product_body, low_size, tile_rows, pieces, len(grads), half, turns, sends, keeps, extra > 0,
            fetched is None,
        ),
        in_specs=[SMEM] * 3
        + [VMEM] * len(grads)
        + [pl.BlockSpec(memory_space=pltpu.HBM) if fetched is None else VMEM]
        + [VMEM] * len(more),
        out_specs=[VMEM] * len(outs),
        out_shape=outs,
        scratch_shapes=[pltpu.VMEM((depth, rows), BF16)]
        + [pltpu.VMEM(weight_blocks.shape, BF16), pltpu.SemaphoreType.DMA((blocks,))]
        * (fetched is None),
        compiler_params=PRODUCT_PARAMS,
        cost_estimate=cost,
    )(
        *in_hbm(*scalars),
        *grads,
        *(in_hbm(weight_blocks) if fetched is None else [fetched]),
        *in_hbm(*more),
    )


def fetch_kernel(low_size, pos_ref, weight_ref, out_ref, sems):
    copies = [
        pltpu.make_async_copy(
            weight_ref.at[block ^ (pos_ref[0] % low_size)], out_ref.at[block], sems.at[block]
        )
        for block in range(low_size)
    ]
    for copy in copies:
        copy.start()
    for copy in copies:
        copy.wait()


def fetch(position, weight_blocks, low_size):
    return pl.pallas_call(
        functools.partial(fetch_kernel, low_size),
        in_specs=[SMEM, pl.BlockSpec(memory_space=pltpu.HBM)],
        out_specs=VMEM,
        out_shape=pltpu.VMEM(weight_blocks.shape, BF16),
        scratch_shapes=[pltpu.SemaphoreType.DMA((low_size,))],
        compiler_params=PARAMS,
        cost_estimate=QUICK,
    )(*in_hbm(position, weight_blocks))


def in_hbm(*arrays):
    return [pltpu.with_memory_space_constraint(array, pltpu.HBM) for array in arrays]


def after(value, *others):
    return lax.optimization_barrier((value, *others))[0]


def halve_kernel(ways, *refs):
    kept_refs, got_refs = refs[:ways], refs[ways : 2 * ways]
    placed_ref = refs[2 * ways] if len(refs) > 4 * ways else None
    outs = refs[-2 * ways - (placed_ref is not None) :]
    for way in range(ways):
        kept_ref, got_ref, sent_ref, rest_ref = kept_refs[way], got_refs[way], outs[way], outs[ways + way]
        half = kept_ref.shape[0] // 2
        sent_ref[:half, :] = (kept_ref[half:, :] + got_ref[half : 2 * half, :].astype(F32)).astype(BF16)
        rest_ref[...] = kept_ref[:half, :] + got_ref[:half, :].astype(F32)
        if way == 0 and placed_ref is not None:
            placed = placed_ref[...] + got_ref[2 * half :, :]
            sent_ref[half:, :] = placed
            outs[-1][...] = placed


def halve(kept, got, placed=None, cost=QUICK):
    placed = [] if placed is None else [placed]
    extra = [placed[0].shape[0] if placed and not way else 0 for way in range(len(kept))]
    shapes = [(k.shape[0] // 2, k.shape[1]) for k in kept]
    outs = pl.pallas_call(
        functools.partial(halve_kernel, len(kept)),
        in_specs=[VMEM] * (2 * len(kept) + len(placed)),
        out_specs=[VMEM] * (2 * len(kept) + len(placed)),
        out_shape=[jax.ShapeDtypeStruct((n + e, r), BF16) for (n, r), e in zip(shapes, extra)]
        + [jax.ShapeDtypeStruct(shape, F32) for shape in shapes]
        + [jax.ShapeDtypeStruct(p.shape, BF16) for p in placed],
        compiler_params=PARAMS,
        cost_estimate=cost,
    )(*kept, *got, *placed)
    ways = len(kept)
    return outs[:ways], outs[ways : 2 * ways], *outs[2 * ways :]


def last_kernel(ways, *refs):
    kept_refs, got_refs = refs[:ways], refs[ways : 2 * ways]
    placed_ref = refs[2 * ways] if len(refs) > 2 * ways + 1 else None
    out_ref = refs[2 * ways + (placed_ref is not None)]
    start = 0
    for kept_ref, got_ref in zip(kept_refs, got_refs):
        half, count = kept_ref.shape[0] // 2, kept_ref.shape[1]
        out_ref[:, start : start + count] = (
            kept_ref[half:, :] + got_ref[half : 2 * half, :].astype(F32)
        ).astype(BF16)
        start += count
    if placed_ref is not None:
        refs[-1][...] = placed_ref[...] + got_refs[0][2 * kept_refs[0].shape[0] // 2 :, :]


def last_parts(kept, got, placed=None, cost=QUICK):
    placed = [] if placed is None else [placed]
    shape = kept[0].shape[0] // 2, sum(k.shape[1] for k in kept)
    return pl.pallas_call(
        functools.partial(last_kernel, len(kept)),
        in_specs=[VMEM] * (2 * len(kept) + len(placed)),
        out_specs=[VMEM] * (1 + len(placed)),
        out_shape=[jax.ShapeDtypeStruct(shape, BF16)]
        + [jax.ShapeDtypeStruct(p.shape, BF16) for p in placed],
        compiler_params=PARAMS,
        cost_estimate=cost,
    )(*kept, *got, *placed)


def up_body(low_size, tile_rows, pieces, tiles, micro_count, *refs):
    pos_ref, classes_ref, live_ref = refs[:3]
    grad_refs = refs[3 : 3 + tiles]
    placed_ref, near_ref, *far_refs = refs[3 + tiles : -2]
    out_ref, total_ref = refs[-2:]
    high = pos_ref[0] // low_size
    total_ref[...] = jnp.zeros_like(total_ref)
    rank_part = total_ref.shape[1]
    skip = near_ref.shape[0] - placed_ref.shape[0]
    for tile, index, piece, first in pieces:
        k, m, offset = piece
        size = min(SEG, tile_rows)
        seg = segment_of(high, piece, tile_rows)
        lanes = slice(offset, offset + size)

        @pl.when(seg < live_ref[m])
        def _():
            if k == 0:
                start = pl.multiple_of(
                    m * (placed_ref.shape[0] // micro_count) + high * rank_part, rank_part
                )
                other = pl.multiple_of(skip + start, rank_part)
                hidden = (
                    placed_ref[pl.ds(start, rank_part), lanes]
                    + near_ref[pl.ds(other, rank_part), lanes]
                )
            else:
                rows = slice(skip + m * rank_part, skip + (m + 1) * rank_part)
                one_ref, other_ref = far_refs[2 * k - 2 : 2 * k]
                hidden = one_ref[rows, lanes] + other_ref[rows, lanes]
            total_ref[classes_ref[m, seg]] += jnp.dot(
                hidden,
                grad_refs[tile][index, first : first + size, :],
                preferred_element_type=F32,
            )

    out_ref[...] = total_ref[...].astype(BF16)


def shards(
    output_gradient,
    forward_input,
    saved_rank_outputs,
    projection_weight,
    adapter_down_maps,
    adapter_up_maps,
    segment_adapter_class,
    live_segment_table,
):
    grad_tile = output_gradient[0, 0]
    micro_count, tile_rows, tile_cols = grad_tile.shape
    up_tile = adapter_up_maps[0, 0]
    class_count, rank_part, _ = up_tile.shape
    rank, portion = adapter_down_maps.shape[2:]
    tiles = lax.axis_size("tensor")
    low_size = min(tiles, 8)
    high_size = tiles // low_size
    position = lax.axis_index("tensor")
    high = position // low_size
    weight_blocks = projection_weight[0, 0].reshape(low_size, portion, tile_cols)
    position, classes, live = lax.optimization_barrier(
        (position.astype(jnp.int32)[None], segment_adapter_class[0] + 0, live_segment_table[0] + 0)
    )
    scalars = position, classes, live
    position = position[0]
    size = min(SEG, tile_rows)
    offsets = range(0, tile_rows, size)

    own_pieces = [(0, m, (0, m, o), o) for m in range(micro_count) for o in offsets]

    def pieces_of(m, count=1):
        span = tile_rows // count
        return [
            ((k - 1) * count + o // span, 0, (k, m, o), o % span)
            for k in range(1, high_size)
            for o in offsets
        ]

    def produce(grads, pieces, turns, sends, keeps, cost, hidden=None, fetched=None):
        return product(
            scalars, grads, pieces, tile_rows, weight_blocks, up_tile, low_size, turns, sends, keeps,
            cost, size, hidden, fetched,
        )

    hidden = saved_rank_outputs[0]

    first_rows = lax.optimization_barrier(grad_tile[0])
    got0 = [partner(first_rows, k * low_size)[None] for k in range(1, high_size)]
    (own_grads,) = in_hbm(after(grad_tile, first_rows))
    sent_x, sent_y, placed = produce([own_grads], own_pieces, False, True, False, QUICK, hidden)
    first_x, first_y = partner(sent_x, 1), partner(sent_y, 2)
    (own_grads,) = in_hbm(after(grad_tile, sent_x, sent_y))
    kept_x, kept_y, part = produce([own_grads], own_pieces, False, False, True, QUICK)
    parts = [part]
    rows0 = after(got0[0], part), *got0[1:]
    c_sent_x, c_sent_y, c_kept_x, c_kept_y, part = produce(
        list(rows0), pieces_of(0), False, True, True, LONG
    )
    parts.append(part)
    second_rows = after(grad_tile[1], *got0)
    got1 = [partner(second_rows, k * low_size)[None] for k in range(1, high_size)]

    (sent_x, sent_y), (kept_x, kept_y), placed = halve(
        (after(kept_x, part), kept_y), (first_x, first_y), placed
    )
    second_x, second_y = partner(sent_x, 2), partner(sent_y, 1)
    c_first_x = partner(after(c_sent_x, sent_x, sent_y), 1)
    c_first_y = partner(after(c_sent_y, sent_x, sent_y), 2)

    fetched = fetch(after(scalars[0], sent_x, sent_y), weight_blocks, low_size)

    chunks = [([grad_tile], own_pieces), (got0, pieces_of(0)), (got1, pieces_of(1))]
    order = [piece for _, pieces in chunks for _, _, piece, _ in pieces]
    d_sent_x, d_sent_y, d_kept_x, d_kept_y, part = produce(
        got1, pieces_of(1), True, True, True, LONG, None, fetched
    )
    parts.append(part)
    own_third, placed = last_parts((after(kept_x, part), kept_y), (second_x, second_y), placed)
    own_last = relay(own_third, 4)
    own_sums = (kept_x, second_x), (kept_y, second_y)

    rows_total = len(order) * size
    blocks = rows_total // tile_rows

    def small(kernel, shapes, *operands, scratch=(), cost=QUICK):
        return pl.pallas_call(
            kernel,
            in_specs=[SMEM] + [VMEM] * len(operands),
            out_specs=[VMEM] * len(shapes),
            out_shape=[jax.ShapeDtypeStruct(*shape) for shape in shapes],
            scratch_shapes=list(scratch),
            compiler_params=PARAMS,
            cost_estimate=cost,
        )(*in_hbm(scalars[0]), *operands)

    def collect_kernel(pos_ref, *refs):
        part_refs, placed_ref = refs[: len(parts)], refs[len(parts)]
        *message_refs, wide_ref = refs[len(parts) + 1 :]
        own = pos_ref[0] // low_size
        block = 0
        for part_ref in part_refs:
            for start in range(0, part_ref.shape[1], tile_rows):
                value = part_ref[:, start : start + tile_rows].astype(BF16)
                for message_ref in message_refs:
                    message_ref[block * rank_part : (block + 1) * rank_part, :] = value
                block += 1
        wide_ref[...] = placed_ref[...].astype(F32)
        message_refs[0][block * rank_part :, :] = placed_ref[...]
        for k in range(1, high_size):
            for m in range(micro_count):
                start = pl.multiple_of(m * rank + (own ^ k) * rank_part, rank_part)
                first = (block + m) * rank_part
                message_refs[k][first : first + rank_part, :] = wide_ref[
                    pl.ds(start, rank_part), :
                ].astype(BF16)

    counts = [placed.shape[0]] + [micro_count * rank_part] * (high_size - 1)
    messages = small(
        collect_kernel,
        [((blocks * rank_part + n, tile_rows), BF16) for n in counts],
        *parts,
        placed,
        scratch=[pltpu.VMEM(placed.shape, F32)],
    )
    (c_sent_x, c_sent_y), c_kept = halve(
        (after(c_kept_x, messages[0]), c_kept_y), (c_first_x, c_first_y)
    )
    c_second_x, c_second_y = partner(c_sent_x, 2), partner(c_sent_y, 1)
    near = partner(messages[0], 4)
    far = []
    for k in range(1, high_size):
        far += [partner(messages[k], k * low_size), partner(messages[k], k * low_size + 4)]

    def columns_of(j, piece):
        k, m, offset = piece
        at = order.index((k ^ j, m, offset))
        return slice(at * size, (at + 1) * size)

    def block_of(message_ref, columns):
        block, start = columns.start // tile_rows, columns.start % tile_rows
        rows = slice(block * rank_part, (block + 1) * rank_part)
        return message_ref[rows, start : start + size].astype(F32)

    def lowrank_kernel(pos_ref, *refs):
        part_refs = refs[: len(parts)]
        near_ref, *far_refs = refs[len(parts) : -1]
        out_ref = refs[-1]
        whole = [(ref, start) for ref in part_refs for start in range(0, ref.shape[1], size)]
        for at, piece in enumerate(order):
            columns = slice(at * size, (at + 1) * size)
            for j in range(high_size):
                if j == 0:
                    part_ref, start = whole[at]
                    value = part_ref[:, start : start + size] + block_of(near_ref, columns)
                else:
                    other = columns_of(j, piece)
                    value = block_of(far_refs[2 * j - 2], other) + block_of(far_refs[2 * j - 1], other)
                start = pl.multiple_of(((pos_ref[0] // low_size) ^ j) * rank_part, rank_part)
                out_ref[pl.ds(start, rank_part), columns] = value

    (lowrank,) = small(lowrank_kernel, [((rank, rows_total), F32)], *parts, near, *far)

    halves = [range(0, len(order) // 2), range(len(order) // 2, len(order))]

    def riders(way, count):
        fit = count // size
        for i, at in enumerate(halves[way]):
            rows = slice(i // fit * rank, (i // fit + 1) * rank)
            yield rows, slice(i % fit * size, (i % fit + 1) * size), slice(at * size, (at + 1) * size)

    def riding(way, count):
        return -(-len(halves[way]) // (count // size)) * rank

    def ride(ref, first, way, lowrank_ref):
        for rows, there, whole in riders(way, ref.shape[1]):
            ref[first + rows.start : first + rows.stop, there] = lowrank_ref[:, whole].astype(BF16)

    def arrive(ref, first, way, lowrank_ref, out_ref):
        for rows, there, whole in riders(way, ref.shape[1]):
            got = ref[first + rows.start : first + rows.stop, there].astype(F32)
            out_ref[:, whole] = (lowrank_ref[:, whole] + got).astype(out_ref.dtype)

    half_rows = d_sent_x.shape[0] // 2
    d_counts = [d_sent_x.shape[1], d_sent_y.shape[1]]

    def append_kernel(_, *refs):
        for way in range(2):
            refs[3 + way][: 2 * half_rows, :] = refs[way][...]
            ride(refs[3 + way], 2 * half_rows, way, refs[2])

    d_sent_x, d_sent_y = small(
        append_kernel,
        [((2 * half_rows + riding(way, n), n), BF16) for way, n in enumerate(d_counts)],
        d_sent_x,
        d_sent_y,
        after(lowrank, *c_kept),
    )
    d_first_x, d_first_y = partner(d_sent_x, 1), partner(d_sent_y, 2)

    all_grads, all_pieces = [], []
    for grads, pieces in chunks:
        all_pieces += [(tile + len(all_grads), *rest) for tile, *rest in pieces]
        all_grads += grads
    up_map_gradient = pl.pallas_call(
        functools.partial(
            up_body, low_size, tile_rows, all_pieces, len(all_grads), micro_count
        ),
        in_specs=[SMEM] * 3 + [VMEM] * (len(all_grads) + 2 * high_size),
        out_specs=VMEM,
        out_shape=jax.ShapeDtypeStruct(up_tile.shape, BF16),
        scratch_shapes=[pltpu.VMEM(up_tile.shape, F32)],
        compiler_params=PARAMS,
        cost_estimate=LONG,
    )(*in_hbm(*scalars), *all_grads, placed, near, *far)

    (c_third,) = last_parts((after(c_kept[0], d_sent_x), c_kept[1]), (c_second_x, c_second_y))
    c_last = relay(c_third, 4)

    def third_kernel(_, *refs):
        lowrank_ref, next_ref, rider_ref = refs[4], refs[9], refs[10]
        for way in range(2):
            kept_ref, got_ref, sent_ref, rest_ref = refs[way], refs[2 + way], refs[5 + way], refs[7 + way]
            half = kept_ref.shape[0] // 2
            sent_ref[:half, :] = (
                kept_ref[half:, :] + got_ref[half : 2 * half, :].astype(F32)
            ).astype(BF16)
            rest_ref[...] = kept_ref[:half, :] + got_ref[:half, :].astype(F32)
            arrive(got_ref, 2 * half, way, lowrank_ref, next_ref)
        ride(refs[5], refs[0].shape[0] // 2, 0, next_ref)
        rider_ref[...] = next_ref[:, rows_total // 2 :].astype(BF16)

    d_sent_x, d_sent_y, *d_kept, lowrank, rider = small(
        third_kernel,
        [((half_rows + riding(0, d_counts[0]), d_counts[0]), BF16), ((half_rows, d_counts[1]), BF16)]
        + [((half_rows, n), F32) for n in d_counts]
        + [((rank, rows_total), F32), ((rank, rows_total // 2), BF16)],
        d_kept_x,
        after(d_kept_y, up_map_gradient, own_last, c_last),
        d_first_x,
        d_first_y,
        lowrank,
    )
    rider = partner(rider, 1)
    d_second_x, d_second_y = partner(d_sent_x, 2), partner(d_sent_y, 4)
    (d_third_x,) = last_parts((d_kept[0],), (d_second_x,))
    (d_third_y,) = last_parts((d_kept[1],), (d_second_y,))
    d_last = [relay(d_third_x, 4), relay(d_third_y, 1)]

    def whole_kernel(_, lowrank_ref, got_ref, rider_ref, out_ref):
        arrive(got_ref, half_rows, 0, lowrank_ref, out_ref)
        half = rows_total // 2
        out_ref[:, half:] = (lowrank_ref[:, half:] + rider_ref[...].astype(F32)).astype(BF16)

    (lowrank,) = small(
        whole_kernel,
        [((rank, rows_total), BF16)],
        after(lowrank, d_third_x, d_third_y),
        d_second_x,
        rider,
    )

    down = adapter_down_maps[0]

    def adapter_kernel(groups, *refs):
        pos_ref, classes_ref, _, down_ref, lowrank_ref = refs[:5]
        sum_refs = refs[5 : 5 + 2 * groups]
        out_ref, total_ref = refs[5 + 2 * groups :]
        own = pos_ref[0] // low_size
        start = 0
        for g in range(groups):
            kept_ref, second_ref = sum_refs[2 * g : 2 * g + 2]
            half, count = kept_ref.shape[0] // 2, kept_ref.shape[1]
            total_ref[:, start : start + count] = (
                kept_ref[:half, :] + second_ref[:half, :].astype(F32)
            )
            start += count
        for at in range(start // size):
            piece = order[at]
            seg = segment_of(own, piece, tile_rows)
            rows = slice(at * size, (at + 1) * size)
            adapter = lax.dot_general(
                down_ref[classes_ref[piece[1], seg]],
                lowrank_ref[:, rows],
                TN,
                preferred_element_type=F32,
            )
            out_ref[:, rows] = (total_ref[:, rows] + adapter).astype(BF16)

    sums = own_sums + (
        (c_kept[0], c_second_x),
        (c_kept[1], c_second_y),
        (d_kept[0], d_second_x),
        (d_kept[1], d_second_y),
    )
    kept = pl.pallas_call(
        functools.partial(adapter_kernel, len(sums)),
        in_specs=[SMEM] * 3 + [VMEM] * (2 + 2 * len(sums)),
        out_specs=VMEM,
        out_shape=jax.ShapeDtypeStruct((portion, rows_total), BF16),
        scratch_shapes=[pltpu.VMEM((portion, rows_total), F32)],
        compiler_params=PARAMS,
        cost_estimate=QUICK,
    )(*in_hbm(*scalars, down), lowrank, *[a for two in sums for a in two])
    kept = relay(kept, 0)

    def finish_kernel(pos_ref, kept_ref, *refs):
        *got_refs, out_ref, total_ref, turned_ref, sem = refs
        own = pos_ref[0] // low_size
        start = 0
        for got_ref in got_refs:
            count = got_ref.shape[1]
            total_ref[:, start : start + count] = (
                kept_ref[:, start : start + count].astype(F32) + got_ref[...].astype(F32)
            ).astype(BF16)
            start += count
        copies = []
        for at in range(start // size):
            k, m, offset = order[at]
            base = pl.multiple_of((own ^ k) * tile_rows + offset, size)
            rows = slice(at * size, (at + 1) * size)
            turned_ref[rows, :] = total_ref[:, rows].T
            copies.append(
                pltpu.make_async_copy(
                    turned_ref.at[rows, :], out_ref.at[m, pl.ds(base, size), :], sem.at[at]
                )
            )
            copies[-1].start()
        for copy in copies:
            copy.wait()

    got = [own_last, c_last, *d_last]
    grad_prev = pl.pallas_call(
        finish_kernel,
        in_specs=[SMEM] + [VMEM] * (1 + len(got)),
        out_specs=pl.BlockSpec(memory_space=pltpu.HBM),
        out_shape=jax.ShapeDtypeStruct((micro_count, high_size * tile_rows, portion), BF16),
        scratch_shapes=[
            pltpu.VMEM((portion, rows_total), BF16),
            pltpu.VMEM((rows_total, portion), BF16),
            pltpu.SemaphoreType.DMA((rows_total // size,)),
        ],
        compiler_params=PARAMS,
        cost_estimate=QUICK,
    )(*in_hbm(scalars[0]), kept, *got)

    def down_kernel(pos_ref, classes_ref, live_ref, inputs_ref, lowrank_ref, out_ref, total_ref):
        own = pos_ref[0] // low_size
        total_ref[...] = jnp.zeros_like(total_ref)
        for at, piece in enumerate(order):
            k, m, offset = piece
            seg = segment_of(own, piece, tile_rows)

            @pl.when(seg < live_ref[m])
            def _():
                base = pl.multiple_of((own ^ k) * tile_rows + offset, size)
                total_ref[classes_ref[m, seg]] += jnp.dot(
                    lowrank_ref[:, at * size : (at + 1) * size],
                    inputs_ref[m, pl.ds(base, size), :],
                    preferred_element_type=F32,
                )

        out_ref[...] = total_ref[...].astype(BF16)

    down_map_gradient = pl.pallas_call(
        down_kernel,
        in_specs=[SMEM] * 3 + [VMEM] * 2,
        out_specs=VMEM,
        out_shape=jax.ShapeDtypeStruct(down.shape, BF16),
        scratch_shapes=[pltpu.VMEM(down.shape, F32)],
        compiler_params=PARAMS,
        cost_estimate=LONG,
    )(*in_hbm(*scalars, forward_input[0]), lowrank)

    return (
        grad_prev[None],
        down_map_gradient[None],
        up_map_gradient[None, None],
    )


def solution(mesh):
    in_specs = (
        P("pipe", "tensor", None, None, None),
        P("pipe", None, None, "tensor"),
        P("pipe", None, "tensor", None),
        P("pipe", "tensor", None, None),
        P("pipe", None, None, "tensor"),
        P("pipe", "tensor", None, None, None),
        P("pipe", None, None),
        P("pipe", None),
    )
    out_specs = (
        P("pipe", None, None, "tensor"),
        P("pipe", None, None, "tensor"),
        P("pipe", "tensor", None, None, None),
    )
    return jax.shard_map(shards, mesh=mesh, in_specs=in_specs, out_specs=out_specs, check_vma=False)
```

```python
import functools

import jax
import jax.numpy as jnp
from jax import lax
from jax.experimental import pallas as pl
from jax.experimental.pallas import tpu as pltpu
from jax.sharding import PartitionSpec as P

SEG = 128
BF16 = jnp.bfloat16
F32 = jnp.float32
SMEM = pl.BlockSpec(memory_space=pltpu.SMEM)
VMEM = pl.BlockSpec(memory_space=pltpu.VMEM)
TN = (((0,), (0,)), ((), ()))
PARAMS = pltpu.CompilerParams(vmem_limit_bytes=16 * 2**20)
PRODUCT_PARAMS = pltpu.CompilerParams(vmem_limit_bytes=24 * 2**20)
QUICK = pl.CostEstimate(flops=1000, bytes_accessed=1000, transcendentals=0)
LONG = pl.CostEstimate(flops=4 * 10**10, bytes_accessed=1000, transcendentals=0)


def partner(value, mask):
    pairs = [(source, source ^ mask) for source in range(lax.axis_size("tensor"))]
    return lax.ppermute(value, "tensor", pairs)


def relay(value, mask):
    sections, tiles = lax.axis_size("pipe"), lax.axis_size("tensor")
    pairs = [
        (p * tiles + t, (p - 1) % sections * tiles + (t ^ mask))
        for p in range(sections)
        for t in range(tiles)
    ]
    return lax.ppermute(value, ("pipe", "tensor"), pairs)


def segment_of(high, piece, tile_rows):
    k, _, offset = piece
    return ((high ^ k) * tile_rows + offset) // SEG


def product_body(low_size, tile_rows, pieces, tiles, half, turns, sends, keeps, with_hidden, fetches, *refs):
    pos_ref, classes_ref, live_ref = refs[:3]
    grad_refs = refs[3 : 3 + tiles]
    weight_hbm = refs[3 + tiles]
    rows_ref, *scratch = refs[-3:] if fetches else refs[-1:]
    rest = list(refs[4 + tiles : -1 - len(scratch)])
    weight_ref, sems = scratch if fetches else (weight_hbm, None)
    up_ref = rest.pop(0) if keeps else None
    hidden_ref = rest.pop(0) if with_hidden else None
    sent_x, sent_y = (rest.pop(0), rest.pop(0)) if sends else (None, None)
    placed_ref = rest.pop(0) if with_hidden else None
    kept_x, kept_y, rank_ref = rest if keeps else (None, None, None)
    low, high = pos_ref[0] % low_size, pos_ref[0] // low_size
    total = rows_ref.shape[1]
    size = total // len(pieces)

    def weight_copy(block):
        return pltpu.make_async_copy(
            weight_hbm.at[block ^ low], weight_ref.at[block], sems.at[block]
        )

    jobs = []
    for x, y in ((1, 1), (1, 0), (0, 1), (0, 0)):
        to_x = (sent_x if x else kept_x, *((y, 2) if turns else (2 * y, 1)))
        to_y = (sent_y if y else kept_y, *((x, 2) if turns else (2 * x, 1)))
        start = 0 if to_x[0] is not None else half
        stop = total if to_y[0] is not None else half
        if start < stop:
            jobs.append((x + 2 * y, start, stop, to_x, to_y))
    if fetches:
        for block, *_ in jobs:
            for z in range(2):
                weight_copy(block + 4 * z).start()

    if with_hidden:
        micro_count, count, rank = hidden_ref.shape
        spot = lax.broadcasted_iota(jnp.int32, (count, half), 1)
        row = lax.broadcasted_iota(jnp.int32, (count, half), 0)
        chosen = (spot == low * count + row).astype(F32).astype(BF16)
        for m in range(micro_count):
            placed = lax.dot_general(
                hidden_ref[m], chosen, TN, preferred_element_type=F32
            ).astype(BF16)
            placed_ref[m * rank : (m + 1) * rank, :] = placed
            start = sent_x.shape[0] - (micro_count - m) * rank
            sent_x[start : start + rank, :] = placed

    for at, (tile, index, piece, first) in enumerate(pieces):
        seg = segment_of(high, piece, tile_rows)
        alive = seg < live_ref[piece[1]]
        place = slice(at * size, (at + 1) * size)

        @pl.when(alive)
        def _():
            rows = grad_refs[tile][index, first : first + size, :].T
            rows_ref[:, place] = rows
            if keeps:
                up = up_ref[classes_ref[piece[1], seg]]
                rank_ref[:, place] = jnp.dot(up, rows, preferred_element_type=F32)

        @pl.when(jnp.logical_not(alive))
        def _():
            rows_ref[:, place] = jnp.zeros((rows_ref.shape[0], size), rows_ref.dtype)
            if keeps:
                rank_ref[:, place] = jnp.zeros((rank_ref.shape[0], size), F32)

    for block, start, stop, to_x, to_y in jobs:

        @pl.loop(0, 2)
        def _(z):
            if fetches:
                weight_copy(block + 4 * z).wait()
            value = jnp.dot(
                weight_ref[block + 4 * z], rows_ref[:, start:stop], preferred_element_type=F32
            )
            for (ref, slot, step), part in (
                (to_x, value[:, : half - start]),
                (to_y, value[:, half - start :]),
            ):
                if ref is not None:
                    width = part.shape[0]
                    place = pl.ds(pl.multiple_of((slot + step * z) * width, width), width)
                    ref[place, :] = part.astype(ref.dtype)


def product(scalars, grads, pieces, tile_rows, weight_blocks, up_tile, low_size, turns, sends, keeps, cost, size, hidden=None, fetched=None):
    blocks, width, depth = weight_blocks.shape
    rows = len(pieces) * size
    half = rows // 2
    if rows > 128 and half % 128:
        half = half // 128 * 128 + 128
    outs = []
    extra = 0 if hidden is None else hidden.shape[0] * hidden.shape[2]
    for wanted, dtype in ((sends, BF16), (keeps, F32)):
        if wanted:
            for more, n in ((extra, half), (0, rows - half)):
                outs.append(jax.ShapeDtypeStruct((blocks // 2 * width + more, n), dtype))
    if extra:
        outs.append(jax.ShapeDtypeStruct((extra, half), BF16))
    if keeps:
        outs.append(jax.ShapeDtypeStruct((up_tile.shape[1], rows), F32))
    more = ([up_tile] if keeps else []) + ([] if hidden is None else [hidden])
    return pl.pallas_call(
        functools.partial(
            product_body, low_size, tile_rows, pieces, len(grads), half, turns, sends, keeps, extra > 0,
            fetched is None,
        ),
        in_specs=[SMEM] * 3
        + [VMEM] * len(grads)
        + [pl.BlockSpec(memory_space=pltpu.HBM) if fetched is None else VMEM]
        + [VMEM] * len(more),
        out_specs=[VMEM] * len(outs),
        out_shape=outs,
        scratch_shapes=[pltpu.VMEM((depth, rows), BF16)]
        + [pltpu.VMEM(weight_blocks.shape, BF16), pltpu.SemaphoreType.DMA((blocks,))]
        * (fetched is None),
        compiler_params=PRODUCT_PARAMS,
        cost_estimate=cost,
    )(
        *in_hbm(*scalars),
        *grads,
        *(in_hbm(weight_blocks) if fetched is None else [fetched]),
        *in_hbm(*more),
    )


def fetch_kernel(low_size, pos_ref, weight_ref, out_ref, sems):
    copies = [
        pltpu.make_async_copy(
            weight_ref.at[block ^ (pos_ref[0] % low_size)], out_ref.at[block], sems.at[block]
        )
        for block in range(low_size)
    ]
    for copy in copies:
        copy.start()
    for copy in copies:
        copy.wait()


def fetch(position, weight_blocks, low_size):
    return pl.pallas_call(
        functools.partial(fetch_kernel, low_size),
        in_specs=[SMEM, pl.BlockSpec(memory_space=pltpu.HBM)],
        out_specs=VMEM,
        out_shape=pltpu.VMEM(weight_blocks.shape, BF16),
        scratch_shapes=[pltpu.SemaphoreType.DMA((low_size,))],
        compiler_params=PARAMS,
        cost_estimate=QUICK,
    )(*in_hbm(position, weight_blocks))


def in_hbm(*arrays):
    return [pltpu.with_memory_space_constraint(array, pltpu.HBM) for array in arrays]


def after(value, *others):
    return lax.optimization_barrier((value, *others))[0]


def halve_kernel(ways, *refs):
    kept_refs, got_refs = refs[:ways], refs[ways : 2 * ways]
    placed_ref = refs[2 * ways] if len(refs) > 4 * ways else None
    outs = refs[-2 * ways - (placed_ref is not None) :]
    for way in range(ways):
        kept_ref, got_ref, sent_ref, rest_ref = kept_refs[way], got_refs[way], outs[way], outs[ways + way]
        half = kept_ref.shape[0] // 2
        sent_ref[:half, :] = (kept_ref[half:, :] + got_ref[half : 2 * half, :].astype(F32)).astype(BF16)
        rest_ref[...] = kept_ref[:half, :] + got_ref[:half, :].astype(F32)
        if way == 0 and placed_ref is not None:
            placed = placed_ref[...] + got_ref[2 * half :, :]
            sent_ref[half:, :] = placed
            outs[-1][...] = placed


def halve(kept, got, placed=None, cost=QUICK):
    placed = [] if placed is None else [placed]
    extra = [placed[0].shape[0] if placed and not way else 0 for way in range(len(kept))]
    shapes = [(k.shape[0] // 2, k.shape[1]) for k in kept]
    outs = pl.pallas_call(
        functools.partial(halve_kernel, len(kept)),
        in_specs=[VMEM] * (2 * len(kept) + len(placed)),
        out_specs=[VMEM] * (2 * len(kept) + len(placed)),
        out_shape=[jax.ShapeDtypeStruct((n + e, r), BF16) for (n, r), e in zip(shapes, extra)]
        + [jax.ShapeDtypeStruct(shape, F32) for shape in shapes]
        + [jax.ShapeDtypeStruct(p.shape, BF16) for p in placed],
        compiler_params=PARAMS,
        cost_estimate=cost,
    )(*kept, *got, *placed)
    ways = len(kept)
    return outs[:ways], outs[ways : 2 * ways], *outs[2 * ways :]


def last_kernel(ways, *refs):
    kept_refs, got_refs = refs[:ways], refs[ways : 2 * ways]
    placed_ref = refs[2 * ways] if len(refs) > 2 * ways + 1 else None
    out_ref = refs[2 * ways + (placed_ref is not None)]
    start = 0
    for kept_ref, got_ref in zip(kept_refs, got_refs):
        half, count = kept_ref.shape[0] // 2, kept_ref.shape[1]
        out_ref[:, start : start + count] = (
            kept_ref[half:, :] + got_ref[half : 2 * half, :].astype(F32)
        ).astype(BF16)
        start += count
    if placed_ref is not None:
        refs[-1][...] = placed_ref[...] + got_refs[0][2 * kept_refs[0].shape[0] // 2 :, :]


def last_parts(kept, got, placed=None, cost=QUICK):
    placed = [] if placed is None else [placed]
    shape = kept[0].shape[0] // 2, sum(k.shape[1] for k in kept)
    return pl.pallas_call(
        functools.partial(last_kernel, len(kept)),
        in_specs=[VMEM] * (2 * len(kept) + len(placed)),
        out_specs=[VMEM] * (1 + len(placed)),
        out_shape=[jax.ShapeDtypeStruct(shape, BF16)]
        + [jax.ShapeDtypeStruct(p.shape, BF16) for p in placed],
        compiler_params=PARAMS,
        cost_estimate=cost,
    )(*kept, *got, *placed)


def up_body(low_size, tile_rows, pieces, tiles, micro_count, *refs):
    pos_ref, classes_ref, live_ref = refs[:3]
    grad_refs = refs[3 : 3 + tiles]
    placed_ref, near_ref, *far_refs = refs[3 + tiles : -2]
    out_ref, total_ref = refs[-2:]
    high = pos_ref[0] // low_size
    total_ref[...] = jnp.zeros_like(total_ref)
    rank_part = total_ref.shape[1]
    skip = near_ref.shape[0] - placed_ref.shape[0]
    for tile, index, piece, first in pieces:
        k, m, offset = piece
        size = min(SEG, tile_rows)
        seg = segment_of(high, piece, tile_rows)
        lanes = slice(offset, offset + size)

        @pl.when(seg < live_ref[m])
        def _():
            if k == 0:
                start = pl.multiple_of(
                    m * (placed_ref.shape[0] // micro_count) + high * rank_part, rank_part
                )
                other = pl.multiple_of(skip + start, rank_part)
                hidden = (
                    placed_ref[pl.ds(start, rank_part), lanes]
                    + near_ref[pl.ds(other, rank_part), lanes]
                )
            else:
                rows = slice(skip + m * rank_part, skip + (m + 1) * rank_part)
                one_ref, other_ref = far_refs[2 * k - 2 : 2 * k]
                hidden = one_ref[rows, lanes] + other_ref[rows, lanes]
            total_ref[classes_ref[m, seg]] += jnp.dot(
                hidden,
                grad_refs[tile][index, first : first + size, :],
                preferred_element_type=F32,
            )

    out_ref[...] = total_ref[...].astype(BF16)


def shards(
    output_gradient,
    forward_input,
    saved_rank_outputs,
    projection_weight,
    adapter_down_maps,
    adapter_up_maps,
    segment_adapter_class,
    live_segment_table,
):
    grad_tile = output_gradient[0, 0]
    micro_count, tile_rows, tile_cols = grad_tile.shape
    up_tile = adapter_up_maps[0, 0]
    class_count, rank_part, _ = up_tile.shape
    rank, portion = adapter_down_maps.shape[2:]
    tiles = lax.axis_size("tensor")
    low_size = min(tiles, 8)
    high_size = tiles // low_size
    position = lax.axis_index("tensor")
    high = position // low_size
    weight_blocks = projection_weight[0, 0].reshape(low_size, portion, tile_cols)
    position, classes, live = lax.optimization_barrier(
        (position.astype(jnp.int32)[None], segment_adapter_class[0] + 0, live_segment_table[0] + 0)
    )
    scalars = position, classes, live
    position = position[0]
    size = min(SEG, tile_rows)
    offsets = range(0, tile_rows, size)

    own_pieces = [(0, m, (0, m, o), o) for m in range(micro_count) for o in offsets]

    def pieces_of(m, count=1):
        span = tile_rows // count
        return [
            ((k - 1) * count + o // span, 0, (k, m, o), o % span)
            for k in range(1, high_size)
            for o in offsets
        ]

    def produce(grads, pieces, turns, sends, keeps, cost, hidden=None, fetched=None):
        return product(
            scalars, grads, pieces, tile_rows, weight_blocks, up_tile, low_size, turns, sends, keeps,
            cost, size, hidden, fetched,
        )

    hidden = saved_rank_outputs[0]

    first_rows = lax.optimization_barrier(grad_tile[0])
    got0 = [partner(first_rows, k * low_size)[None] for k in range(1, high_size)]
    (own_grads,) = in_hbm(after(grad_tile, first_rows))
    sent_x, sent_y, placed = produce([own_grads], own_pieces, False, True, False, QUICK, hidden)
    first_x, first_y = partner(sent_x, 1), partner(sent_y, 2)
    (own_grads,) = in_hbm(after(grad_tile, sent_x, sent_y))
    kept_x, kept_y, part = produce([own_grads], own_pieces, False, False, True, QUICK)
    parts = [part]
    rows0 = after(got0[0], part), *got0[1:]
    c_sent_x, c_sent_y, c_kept_x, c_kept_y, part = produce(
        list(rows0), pieces_of(0), False, True, True, LONG
    )
    parts.append(part)
    second_rows = after(grad_tile[1], *got0)
    got1 = [partner(second_rows, k * low_size)[None] for k in range(1, high_size)]

    (sent_y,), (kept_y,) = halve((after(kept_y, part),), (first_y,))
    (sent_x,), (kept_x,), placed = halve((after(kept_x, part),), (first_x,), placed)
    second_x, second_y = partner(sent_x, 2), partner(sent_y, 1)
    c_first_x = partner(after(c_sent_x, sent_x, sent_y), 1)
    c_first_y = partner(after(c_sent_y, sent_x, sent_y), 2)

    fetched = fetch(after(scalars[0], sent_x, sent_y), weight_blocks, low_size)

    chunks = [([grad_tile], own_pieces), (got0, pieces_of(0)), (got1, pieces_of(1))]
    order = [piece for _, pieces in chunks for _, _, piece, _ in pieces]
    d_sent_x, d_sent_y, d_kept_x, d_kept_y, part = produce(
        got1, pieces_of(1), False, True, True, LONG, None, fetched
    )
    parts.append(part)
    own_third, placed = last_parts((after(kept_x, part), kept_y), (second_x, second_y), placed)
    own_last = relay(own_third, 4)
    own_sums = (kept_x, second_x), (kept_y, second_y)

    rows_total = len(order) * size
    blocks = rows_total // tile_rows

    def small(kernel, shapes, *operands, scratch=(), cost=QUICK):
        return pl.pallas_call(
            kernel,
            in_specs=[SMEM] + [VMEM] * len(operands),
            out_specs=[VMEM] * len(shapes),
            out_shape=[jax.ShapeDtypeStruct(*shape) for shape in shapes],
            scratch_shapes=list(scratch),
            compiler_params=PARAMS,
            cost_estimate=cost,
        )(*in_hbm(scalars[0]), *operands)

    def collect_kernel(pos_ref, *refs):
        part_refs, placed_ref = refs[: len(parts)], refs[len(parts)]
        *message_refs, wide_ref = refs[len(parts) + 1 :]
        own = pos_ref[0] // low_size
        block = 0
        for part_ref in part_refs:
            for start in range(0, part_ref.shape[1], tile_rows):
                value = part_ref[:, start : start + tile_rows].astype(BF16)
                for message_ref in message_refs:
                    message_ref[block * rank_part : (block + 1) * rank_part, :] = value
                block += 1
        wide_ref[...] = placed_ref[...].astype(F32)
        message_refs[0][block * rank_part :, :] = placed_ref[...]
        for k in range(1, high_size):
            for m in range(micro_count):
                start = pl.multiple_of(m * rank + (own ^ k) * rank_part, rank_part)
                first = (block + m) * rank_part
                message_refs[k][first : first + rank_part, :] = wide_ref[
                    pl.ds(start, rank_part), :
                ].astype(BF16)

    counts = [placed.shape[0]] + [micro_count * rank_part] * (high_size - 1)
    messages = small(
        collect_kernel,
        [((blocks * rank_part + n, tile_rows), BF16) for n in counts],
        *parts,
        placed,
        scratch=[pltpu.VMEM(placed.shape, F32)],
    )
    (c_sent_x, c_sent_y), c_kept = halve(
        (after(c_kept_x, messages[0]), c_kept_y), (c_first_x, c_first_y)
    )
    c_second_x, c_second_y = partner(c_sent_x, 2), partner(c_sent_y, 1)
    near = partner(messages[0], 4)
    far = []
    for k in range(1, high_size):
        far += [partner(messages[k], k * low_size), partner(messages[k], k * low_size + 4)]

    def columns_of(j, piece):
        k, m, offset = piece
        at = order.index((k ^ j, m, offset))
        return slice(at * size, (at + 1) * size)

    def block_of(message_ref, columns):
        block, start = columns.start // tile_rows, columns.start % tile_rows
        rows = slice(block * rank_part, (block + 1) * rank_part)
        return message_ref[rows, start : start + size].astype(F32)

    def lowrank_kernel(pos_ref, *refs):
        part_refs = refs[: len(parts)]
        near_ref, *far_refs = refs[len(parts) : -1]
        out_ref = refs[-1]
        whole = [(ref, start) for ref in part_refs for start in range(0, ref.shape[1], size)]
        for at, piece in enumerate(order):
            columns = slice(at * size, (at + 1) * size)
            for j in range(high_size):
                if j == 0:
                    part_ref, start = whole[at]
                    value = part_ref[:, start : start + size] + block_of(near_ref, columns)
                else:
                    other = columns_of(j, piece)
                    value = block_of(far_refs[2 * j - 2], other) + block_of(far_refs[2 * j - 1], other)
                start = pl.multiple_of(((pos_ref[0] // low_size) ^ j) * rank_part, rank_part)
                out_ref[pl.ds(start, rank_part), columns] = value

    (lowrank,) = small(lowrank_kernel, [((rank, rows_total), F32)], *parts, near, *far)

    halves = [range(0, len(order) // 2), range(len(order) // 2, len(order))]

    def riders(way, count):
        fit = count // size
        for i, at in enumerate(halves[way]):
            rows = slice(i // fit * rank, (i // fit + 1) * rank)
            yield rows, slice(i % fit * size, (i % fit + 1) * size), slice(at * size, (at + 1) * size)

    def riding(way, count):
        return -(-len(halves[way]) // (count // size)) * rank

    def ride(ref, first, way, lowrank_ref):
        for rows, there, whole in riders(way, ref.shape[1]):
            ref[first + rows.start : first + rows.stop, there] = lowrank_ref[:, whole].astype(BF16)

    def arrive(ref, first, way, lowrank_ref, out_ref):
        for rows, there, whole in riders(way, ref.shape[1]):
            got = ref[first + rows.start : first + rows.stop, there].astype(F32)
            out_ref[:, whole] = (lowrank_ref[:, whole] + got).astype(out_ref.dtype)

    half_rows = d_sent_x.shape[0] // 2
    d_counts = [d_sent_x.shape[1], d_sent_y.shape[1]]

    def append_kernel(_, *refs):
        for way in range(2):
            refs[3 + way][: 2 * half_rows, :] = refs[way][...]
            ride(refs[3 + way], 2 * half_rows, way, refs[2])

    d_sent_x, d_sent_y = small(
        append_kernel,
        [((2 * half_rows + riding(way, n), n), BF16) for way, n in enumerate(d_counts)],
        d_sent_x,
        d_sent_y,
        after(lowrank, *c_kept),
    )
    d_first_x, d_first_y = partner(d_sent_x, 1), partner(d_sent_y, 2)

    all_grads, all_pieces = [], []
    for grads, pieces in chunks:
        all_pieces += [(tile + len(all_grads), *rest) for tile, *rest in pieces]
        all_grads += grads
    up_map_gradient = pl.pallas_call(
        functools.partial(
            up_body, low_size, tile_rows, all_pieces, len(all_grads), micro_count
        ),
        in_specs=[SMEM] * 3 + [VMEM] * (len(all_grads) + 2 * high_size),
        out_specs=VMEM,
        out_shape=jax.ShapeDtypeStruct(up_tile.shape, BF16),
        scratch_shapes=[pltpu.VMEM(up_tile.shape, F32)],
        compiler_params=PARAMS,
        cost_estimate=LONG,
    )(*in_hbm(*scalars), *all_grads, placed, near, *far)

    (c_third,) = last_parts((after(c_kept[0], d_sent_x), c_kept[1]), (c_second_x, c_second_y))
    c_last = relay(c_third, 4)

    def third_kernel(_, *refs):
        lowrank_ref, next_ref = refs[4], refs[9]
        for way in range(2):
            kept_ref, got_ref, sent_ref, rest_ref = refs[way], refs[2 + way], refs[5 + way], refs[7 + way]
            half = kept_ref.shape[0] // 2
            sent_ref[:half, :] = (
                kept_ref[half:, :] + got_ref[half : 2 * half, :].astype(F32)
            ).astype(BF16)
            rest_ref[...] = kept_ref[:half, :] + got_ref[:half, :].astype(F32)
            arrive(got_ref, 2 * half, way, lowrank_ref, next_ref)
            ride(sent_ref, half, way, next_ref)

    d_sent_x, d_sent_y, *d_kept, lowrank = small(
        third_kernel,
        [((half_rows + riding(way, n), n), BF16) for way, n in enumerate(d_counts)]
        + [((half_rows, n), F32) for n in d_counts]
        + [((rank, rows_total), F32)],
        d_kept_x,
        after(d_kept_y, up_map_gradient, own_last, c_third),
        d_first_x,
        d_first_y,
        lowrank,
    )
    d_second_x, d_second_y = partner(d_sent_x, 2), partner(d_sent_y, 1)
    (d_third,) = last_parts(d_kept, (d_second_x, d_second_y))
    d_last = relay(d_third, 4)

    def whole_kernel(_, lowrank_ref, got_x_ref, got_y_ref, out_ref):
        for way, got_ref in enumerate((got_x_ref, got_y_ref)):
            arrive(got_ref, half_rows, way, lowrank_ref, out_ref)

    (lowrank,) = small(
        whole_kernel,
        [((rank, rows_total), BF16)],
        after(lowrank, d_third),
        d_second_x,
        d_second_y,
    )

    down = adapter_down_maps[0]

    def adapter_kernel(groups, *refs):
        pos_ref, classes_ref, _, down_ref, lowrank_ref = refs[:5]
        sum_refs = refs[5 : 5 + 2 * groups]
        out_ref, total_ref = refs[5 + 2 * groups :]
        own = pos_ref[0] // low_size
        start = 0
        for g in range(groups):
            kept_ref, second_ref = sum_refs[2 * g : 2 * g + 2]
            half, count = kept_ref.shape[0] // 2, kept_ref.shape[1]
            total_ref[:, start : start + count] = (
                kept_ref[:half, :] + second_ref[:half, :].astype(F32)
            )
            start += count
        for at in range(start // size):
            piece = order[at]
            seg = segment_of(own, piece, tile_rows)
            rows = slice(at * size, (at + 1) * size)
            adapter = lax.dot_general(
                down_ref[classes_ref[piece[1], seg]],
                lowrank_ref[:, rows],
                TN,
                preferred_element_type=F32,
            )
            out_ref[:, rows] = (total_ref[:, rows] + adapter).astype(BF16)

    sums = own_sums + (
        (c_kept[0], c_second_x),
        (c_kept[1], c_second_y),
        (d_kept[0], d_second_x),
        (d_kept[1], d_second_y),
    )
    kept = pl.pallas_call(
        functools.partial(adapter_kernel, len(sums)),
        in_specs=[SMEM] * 3 + [VMEM] * (2 + 2 * len(sums)),
        out_specs=VMEM,
        out_shape=jax.ShapeDtypeStruct((portion, rows_total), BF16),
        scratch_shapes=[pltpu.VMEM((portion, rows_total), F32)],
        compiler_params=PARAMS,
        cost_estimate=QUICK,
    )(*in_hbm(*scalars, down), lowrank, *[a for two in sums for a in two])
    kept = relay(kept, 0)

    def finish_kernel(pos_ref, kept_ref, *refs):
        *got_refs, out_ref, total_ref, turned_ref, sem = refs
        own = pos_ref[0] // low_size
        start = 0
        for got_ref in got_refs:
            count = got_ref.shape[1]
            total_ref[:, start : start + count] = (
                kept_ref[:, start : start + count].astype(F32) + got_ref[...].astype(F32)
            ).astype(BF16)
            start += count
        copies = []
        for at in range(start // size):
            k, m, offset = order[at]
            base = pl.multiple_of((own ^ k) * tile_rows + offset, size)
            rows = slice(at * size, (at + 1) * size)
            turned_ref[rows, :] = total_ref[:, rows].T
            copies.append(
                pltpu.make_async_copy(
                    turned_ref.at[rows, :], out_ref.at[m, pl.ds(base, size), :], sem.at[at]
                )
            )
            copies[-1].start()
        for copy in copies:
            copy.wait()

    got = [own_last, c_last, d_last]
    grad_prev = pl.pallas_call(
        finish_kernel,
        in_specs=[SMEM] + [VMEM] * (1 + len(got)),
        out_specs=pl.BlockSpec(memory_space=pltpu.HBM),
        out_shape=jax.ShapeDtypeStruct((micro_count, high_size * tile_rows, portion), BF16),
        scratch_shapes=[
            pltpu.VMEM((portion, rows_total), BF16),
            pltpu.VMEM((rows_total, portion), BF16),
            pltpu.SemaphoreType.DMA((rows_total // size,)),
        ],
        compiler_params=PARAMS,
        cost_estimate=QUICK,
    )(*in_hbm(scalars[0]), kept, *got)

    def down_kernel(pos_ref, classes_ref, live_ref, inputs_ref, lowrank_ref, out_ref, total_ref):
        own = pos_ref[0] // low_size
        total_ref[...] = jnp.zeros_like(total_ref)
        for at, piece in enumerate(order):
            k, m, offset = piece
            seg = segment_of(own, piece, tile_rows)

            @pl.when(seg < live_ref[m])
            def _():
                base = pl.multiple_of((own ^ k) * tile_rows + offset, size)
                total_ref[classes_ref[m, seg]] += jnp.dot(
                    lowrank_ref[:, at * size : (at + 1) * size],
                    inputs_ref[m, pl.ds(base, size), :],
                    preferred_element_type=F32,
                )

        out_ref[...] = total_ref[...].astype(BF16)

    down_map_gradient = pl.pallas_call(
        down_kernel,
        in_specs=[SMEM] * 3 + [VMEM] * 2,
        out_specs=VMEM,
        out_shape=jax.ShapeDtypeStruct(down.shape, BF16),
        scratch_shapes=[pltpu.VMEM(down.shape, F32)],
        compiler_params=PARAMS,
        cost_estimate=LONG,
    )(*in_hbm(*scalars, forward_input[0]), lowrank)

    return (
        grad_prev[None],
        down_map_gradient[None],
        up_map_gradient[None, None],
    )


def solution(mesh):
    in_specs = (
        P("pipe", "tensor", None, None, None),
        P("pipe", None, None, "tensor"),
        P("pipe", None, "tensor", None),
        P("pipe", "tensor", None, None),
        P("pipe", None, None, "tensor"),
        P("pipe", "tensor", None, None, None),
        P("pipe", None, None),
        P("pipe", None),
    )
    out_specs = (
        P("pipe", None, None, "tensor"),
        P("pipe", None, None, "tensor"),
        P("pipe", "tensor", None, None, None),
    )
    return jax.shard_map(shards, mesh=mesh, in_specs=in_specs, out_specs=out_specs, check_vma=False)
```
